32 devices in a mesh: page: 4 (over x, core), strip: 8 (over z, y).
Axes of the slice: x: 2, y: 2, z: 4, core: 2. Of those that a mesh axis runs over, the one named last changes fastest.
Arguments:
- visual_in: bfloat16 [8, 48, 96, 768], P('page', 'strip'), may hold values from -6 to 6
- query_in: bfloat16 [8, 1024, 768], P('page', 'strip'), may hold values from -6 to 6
- row_valid: int32 [8, 48], P('page', 'strip'), may hold values from 0 to 1, as said below
- segment_ids: int32 [8, 1024], P('page'), may hold values from 0 to 63, never falling along the last dimension, each value on 1 to 32 neighbouring positions
- slot_valid: int32 [8, 1024], P('page', 'strip'), may hold values from 0 to 1, as said below
- col_shift: int32 [8], P('page'), may hold values from 0 to 11
- row_shifted: int32 [8], P('page'), may hold values from 0 to 1, as said below
- norm_gains: float32 [768, 4], replicated, may hold values from 0.1 to 1.9
- w_vqkv: bfloat16 [768, 2304], replicated, may hold values from -0.21875 to 0.21875
- w_vout: bfloat16 [768, 768], replicated, may hold values from -1.5 to 1.5
- w_up: bfloat16 [768, 3072], replicated, may hold values from -0.21875 to 0.21875
- w_down: bfloat16 [3072, 768], replicated, may hold values from -0.109375 to 0.109375
- w_qqkv: bfloat16 [768, 2304], replicated, may hold values from -0.3125 to 0.3125
- w_xkv: bfloat16 [768, 1536], replicated, may hold values from -0.3125 to 0.3125
- w_qout: bfloat16 [768, 768], replicated, may hold values from -3 to 3
- w_qup: bfloat16 [768, 3072], replicated, may hold values from -0.21875 to 0.21875
- w_qdown: bfloat16 [3072, 768], replicated, may hold values from -0.109375 to 0.109375
- visual_cot: bfloat16 [8, 48, 96, 768], P('page', 'strip'), may hold values from -6 to 6
- query_cot: bfloat16 [8, 1024, 768], P('page', 'strip'), may hold values from -6 to 6
Outputs:
- visual_out: bfloat16 [8, 48, 96, 768], P('page', 'strip')
- query_out: bfloat16 [8, 1024, 768], P('page', 'strip')
- visual_in_grad: float32 [8, 48, 96, 768], P('page', 'strip')
- query_in_grad: float32 [8, 1024, 768], P('page', 'strip')
- gain_grads: float32 [768, 4], P('strip', 'page')
- w_vqkv_grad: float32 [768, 2304], P('strip', 'page')
- w_vout_grad: float32 [768, 768], P('strip', 'page')
- w_up_grad: float32 [768, 3072], P('strip', 'page')
- w_down_grad: float32 [3072, 768], P('strip', 'page')
- w_qqkv_grad: float32 [768, 2304], P('strip', 'page')
- w_xkv_grad: float32 [768, 1536], P('strip', 'page')
- w_qout_grad: float32 [768, 768], P('strip', 'page')
- w_qup_grad: float32 [768, 3072], P('strip', 'page')
- w_qdown_grad: float32 [3072, 768], P('strip', 'page')
The draws below stay inside these ranges and needn't reach their ends.
Inputs may be any that keep to these rules, and one draw needn't show every extreme that they name: `row_valid`: for each page, 1 on a leading run of patch rows and 0 after it; the run holds 24 rows or more. `slot_valid`: for each page, 1 on a leading run of slots and 0 after it; the run holds 512 slots or more. `segment_ids`: along a page's slots the ids never fall; a segment holds 1 to 32 slots. `row_shifted`: of pages 2k and 2k + 1, exactly one has 1.
All inputs are finite; a program needn't handle non-finite values.
Results may differ from the reference program's by a relative error of at most 0.0144.
Values may be sent and summed in bfloat16 or wider, within the bound.
A program may use at most 448 MiB of HBM per device.

```python
import math
import jax
import jax.numpy as jnp
import numpy as np
from jax import lax

D = 768
HEADS = 12
FF = 3072
HEAD_DIM = 64
WIN = 12
STRIP_ROWS = 6
COLS = 96
NQ = 1024
ROWS = 48
PAGES = 8


def draw_row_valid(key, part):
    lengths = jax.random.randint(key, (PAGES, 1), ROWS // 2, ROWS + 1)
    return (jnp.arange(ROWS)[None, :] < lengths).astype(jnp.int32)


def draw_slot_valid(key, part):
    lengths = jax.random.randint(key, (PAGES, 1), NQ // 2, NQ + 1)
    return (jnp.arange(NQ)[None, :] < lengths).astype(jnp.int32)


def draw_row_shifted(key, part):
    first = jax.random.randint(jax.random.fold_in(key, 7), (PAGES // 2,), 0, 2)
    return jnp.stack([first, 1 - first], axis=1).reshape(PAGES).astype(jnp.int32)


def touch_ends(drawn, key, least, largest):
    longest = drawn.shape.index(max(drawn.shape))
    spots = []
    for shift in (0, 1):
        where = [jax.random.randint(jax.random.fold_in(key, axis), (), 0, length) for axis, length in enumerate(drawn.shape)]
        where[longest] = (where[longest] + shift) % drawn.shape[longest]
        spots.append(tuple(where))
    return drawn.at[spots[0]].set(least).at[spots[1]].set(largest)


def level_of(stream_key, shape, shards, smallest, high):
    def one(axis_at, blocks):
        heights = jax.random.uniform(jax.random.fold_in(jax.random.fold_in(stream_key, 6), axis_at), (blocks,), jnp.float32, smallest / len(shards), high / len(shards))
        return jnp.repeat(jnp.exp(heights), shape[axis_at] // blocks).reshape((-1,) + (1,) * (len(shape) - axis_at - 1))

    factor_of = one(*shards[0])
    for cut in shards[1:]:
        factor_of = factor_of * one(*cut)
    return factor_of


def profile(count, total, bound, lean):
    loads = [(1 << 20) // math.isqrt(grade ** lean) + 1 for grade in range(2, count + 1)]
    spare, counts = total - bound - (count - 1), [1] * (count - 1)
    while spare > 0:
        candidates = [i for i in range(count - 1) if counts[i] < bound]
        mass, left = sum([loads[i] for i in candidates]), spare
        for i in candidates:
            addition = min(bound - counts[i], max(1, left * loads[i] // mass), spare)
            counts[i] = counts[i] + addition
            spare = spare - addition
    return np.array([bound] + counts)


def uneven_parts(key, count, total, limit, lean):
    if count == 2:
        one = jax.random.randint(key, (), max(1, total - limit), min(limit, total - 1) + 1)
        return jnp.stack([one, total - one])
    sizes = jnp.asarray(profile(count, total, limit, lean), jnp.int32)
    couples = (count - 1) // 2
    source_of, sink = sizes[1:1 + 2 * couples:2], sizes[2:2 + 2 * couples:2]
    slack = jnp.minimum(source_of - 1, limit - sink)
    passed = jax.random.randint(jax.random.fold_in(key, 1), (couples,), 0, 1 << 20) % (slack + 1)
    sizes = sizes.at[1:1 + 2 * couples:2].set(source_of - passed).at[2:2 + 2 * couples:2].set(sink + passed)
    return sizes[jax.random.permutation(jax.random.fold_in(key, 2), count)]


def scatter_about(own_key, shape, deviation, bound, shards=(), kind=jnp.bfloat16):
    array = jax.random.normal(own_key, shape, jnp.float32) * deviation
    if len(shards) > 0:
        array = level_of(own_key, shape, shards, -0.22, 0.18) * array
    return jnp.clip(array, min=-bound, max=bound).astype(kind)


def setup_inputs(seed: int = 0) -> dict:
    seeds = jax.random.split(jax.random.key(seed), 20)
    visual_in = scatter_about(seeds[0], (PAGES, ROWS, COLS, D), 1.0, 6.0, ((0, 4), (1, 8)))
    query_in = scatter_about(seeds[1], (PAGES, NQ, D), 1.0, 6.0, ((0, 4), (1, 8)))
    row_valid = draw_row_valid(jax.random.fold_in(seeds[19], 71), 0)
    segment_ids = jax.vmap(lambda own: jnp.searchsorted(jnp.cumsum(uneven_parts(own, NQ // 16, NQ, 32, 0)), jnp.arange(NQ), side="right"))(jax.random.split(seeds[3], PAGES)).reshape((PAGES, NQ)).astype(jnp.int32)
    slot_valid = draw_slot_valid(jax.random.fold_in(seeds[19], 71), 0)
    col_shift = touch_ends(jax.random.randint(seeds[5], (PAGES,), 0, WIN), jax.random.fold_in(seeds[5], 1), 0, WIN - 1).astype(jnp.int32)
    row_shifted = draw_row_shifted(jax.random.fold_in(seeds[19], 71), 0)
    norm_gains = jnp.clip(1.0 + 0.18 * jax.random.normal(seeds[7], (D, 4), jnp.float32), 0.1, 1.9)
    w_vqkv = scatter_about(seeds[8], (D, 3 * D), D ** -0.5, 0.21875)
    w_vout = scatter_about(seeds[9], (D, D), 16 ** -0.5, 1.5)
    w_up = scatter_about(seeds[10], (D, FF), D ** -0.5, 0.21875)
    w_down = scatter_about(seeds[11], (FF, D), FF ** -0.5, 0.109375)
    w_qqkv = scatter_about(seeds[12], (D, 3 * D), (D // 2) ** -0.5, 0.3125)
    w_xkv = scatter_about(seeds[13], (D, 2 * D), (D // 2) ** -0.5, 0.3125)
    w_qout = scatter_about(seeds[14], (D, D), 4 ** -0.5, 3.0)
    w_qup = scatter_about(seeds[15], (D, FF), D ** -0.5, 0.21875)
    w_qdown = scatter_about(seeds[16], (FF, D), FF ** -0.5, 0.109375)
    visual_cot = scatter_about(seeds[17], (PAGES, ROWS, COLS, D), 1.0, 6.0, ((0, 4), (1, 8)))
    query_cot = scatter_about(seeds[18], (PAGES, NQ, D), 1.0, 6.0, ((0, 4), (1, 8)))
    return dict(visual_in=visual_in, query_in=query_in, row_valid=row_valid, segment_ids=segment_ids, slot_valid=slot_valid, col_shift=col_shift, row_shifted=row_shifted, norm_gains=norm_gains, w_vqkv=w_vqkv, w_vout=w_vout, w_up=w_up, w_down=w_down, w_qqkv=w_qqkv, w_xkv=w_xkv, w_qout=w_qout, w_qup=w_qup, w_qdown=w_qdown, visual_cot=visual_cot, query_cot=query_cot)


@jax.custom_vjp
def low(v):
    return lax.optimization_barrier(v.astype(jnp.bfloat16)).astype(jnp.float32)

@jax.custom_vjp
def low_back(v):
    return v

def low_keep(v):
    return (low(v), None)

def low_pass(kept, grad):
    return (grad,)

def back_keep(v):
    return (v, None)

def back_low(kept, grad):
    return (low(grad),)
low.defvjp(low_keep, low_pass)
low_back.defvjp(back_keep, back_low)
norm_eps = 1e-05
masked_score = -1000000000.0
highest = lax.Precision.HIGHEST

def norm_rows(inputs, gain_row):
    centre = lax.optimization_barrier(jnp.mean(inputs, axis=-1, keepdims=True))
    offset = inputs - centre
    spread = lax.optimization_barrier(jnp.mean(offset * offset, axis=-1, keepdims=True))
    return offset * lax.rsqrt(spread + norm_eps) * gain_row

def matmul_high(left_rows, right_rows):
    return jnp.matmul(left_rows, right_rows, precision=highest)

def roll_columns(inputs, amounts, direction):
    return jax.vmap(lambda single, amount: jnp.roll(single, direction * amount, axis=1))(inputs, amounts)

def roll_rows(inputs, amounts, direction):
    return jax.vmap(lambda single, amount: jnp.roll(single, direction * amount, axis=0))(inputs, amounts)

def window_attention(projected, amounts, row_amounts):
    page_count = projected.shape[0]
    rolled = roll_rows(projected, row_amounts, -1)
    rolled = roll_columns(rolled, amounts, -1)
    blocks = rolled.reshape(page_count, ROWS // WIN, WIN, COLS // WIN, WIN, 3, HEADS, HEAD_DIM)
    blocks = blocks.transpose(5, 0, 1, 3, 6, 2, 4, 7).reshape(3, page_count, ROWS // WIN, COLS // WIN, HEADS, WIN * WIN, HEAD_DIM)
    scores = low_back(jnp.einsum('pabhid,pabhjd->pabhij', blocks[0], blocks[1], precision=highest) * HEAD_DIM ** (-0.5))
    weights = low(jax.nn.softmax(scores, axis=-1))
    mixed = jnp.einsum('pabhij,pabhjd->pabhid', weights, blocks[2], precision=highest)
    mixed = mixed.reshape(page_count, ROWS // WIN, COLS // WIN, HEADS, WIN, WIN, HEAD_DIM)
    mixed = mixed.transpose(0, 1, 4, 2, 5, 3, 6).reshape(page_count, ROWS, COLS, D)
    mixed = roll_columns(mixed, amounts, 1)
    return roll_rows(mixed, row_amounts, 1)

def page_queries(page_inputs):
    query_rows, key_rows, value_rows, segment_row, slot_row, patch_row = page_inputs
    key_heads = key_rows.reshape(-1, HEADS, HEAD_DIM)
    value_heads = value_rows.reshape(-1, HEADS, HEAD_DIM)
    is_patch = jnp.concatenate([jnp.zeros((NQ,), jnp.bool_), jnp.ones((ROWS * COLS,), jnp.bool_)])
    key_valid = jnp.concatenate([slot_row == 1, patch_row == 1])
    key_segment = jnp.concatenate([segment_row, jnp.zeros((ROWS * COLS,), jnp.int32)])

    def score_block(block_inputs):
        query_block, segment_block = block_inputs
        scores = jnp.einsum('ihd,jhd->hij', query_block.reshape(-1, HEADS, HEAD_DIM), key_heads, precision=highest)
        scores = low_back(scores * HEAD_DIM ** (-0.5))
        allowed = key_valid[None, :] & (is_patch[None, :] | (segment_block[:, None] == key_segment[None, :]))
        masked = jnp.where(allowed[None], scores, masked_score)
        weights = low(jax.nn.softmax(masked, axis=-1))
        return jnp.einsum('hij,jhd->ihd', weights, value_heads, precision=highest).reshape(-1, D)
    blocks = lax.map(jax.checkpoint(score_block), (query_rows.reshape(4, NQ // 4, D), segment_row.reshape(4, NQ // 4)))
    return blocks.reshape(NQ, D)

def reference(visual_in, query_in, row_valid, segment_ids, slot_valid, col_shift, row_shifted, norm_gains, w_vqkv, w_vout, w_up, w_down, w_qqkv, w_xkv, w_qout, w_qup, w_qdown, visual_cot, query_cot):
    patch_valid = jnp.repeat(row_valid, COLS, axis=1)
    row_amounts = (row_shifted * STRIP_ROWS).astype(jnp.int32)

    def forward(visual, queries, gains, vqkv, vout, upper, lower, qqkv, xkv, qout, qupper, qlower):
        page_count = visual.shape[0]
        normed_one = low(norm_rows(visual, gains[:, 0]))
        projected = low_back(low(matmul_high(normed_one, vqkv)))
        attended = low_back(low(window_attention(projected, col_shift, row_amounts)))
        after_attention = visual + low_back(matmul_high(attended, vout))
        normed_two = low(norm_rows(after_attention, gains[:, 1]))
        hidden = low(jax.nn.gelu(low_back(matmul_high(normed_two, upper)), approximate=True))
        visual_out = after_attention + low_back(matmul_high(hidden, lower))
        cross = low_back(low(matmul_high(normed_one, xkv)))
        normed_three = low(norm_rows(queries, gains[:, 2]))
        query_proj = low_back(low(matmul_high(normed_three, qqkv)))
        keys_all = jnp.concatenate([query_proj[..., D:2 * D], cross[..., :D].reshape(page_count, ROWS * COLS, D)], axis=1)
        values_all = jnp.concatenate([query_proj[..., 2 * D:], cross[..., D:].reshape(page_count, ROWS * COLS, D)], axis=1)
        attended_q = lax.map(page_queries, (query_proj[..., :D], keys_all, values_all, segment_ids, slot_valid, patch_valid))
        attended_q = low_back(low(attended_q))
        after_query = queries + low_back(matmul_high(attended_q, qout))
        normed_four = low(norm_rows(after_query, gains[:, 3]))
        hidden_q = low(jax.nn.gelu(low_back(matmul_high(normed_four, qupper)), approximate=True))
        query_out = after_query + low_back(matmul_high(hidden_q, qlower))
        return (visual_out, query_out)
    floats = [visual_in, query_in, norm_gains, w_vqkv, w_vout, w_up, w_down, w_qqkv, w_xkv, w_qout, w_qup, w_qdown]
    floats = [array_in.astype(jnp.float32) for array_in in floats]
    outputs, pullback = jax.vjp(forward, *floats)
    grads = pullback((visual_cot.astype(jnp.float32), query_cot.astype(jnp.float32)))
    return (outputs[0].astype(jnp.bfloat16), outputs[1].astype(jnp.bfloat16), grads[0], grads[1], grads[2], grads[3], grads[4], grads[5], grads[6], grads[7], grads[8], grads[9], grads[10], grads[11])
```

```python
import functools

import jax
import jax.numpy as jnp
from jax import lax
from jax.experimental import pallas as pl
from jax.experimental.pallas import tpu as pltpu
from jax.sharding import PartitionSpec as P

HEADS = 12
WIN = 12
EPS = 1e-05
MASKED = -1e9
SCALE = 0.125
BF = jnp.bfloat16
F32 = jnp.float32
LANES = 128
VMEM_BYTES = 60 * 1024 * 1024


def dot(left, right, left_dim=1, right_dim=0):
    return lax.dot_general(
        left, right, (((left_dim,), (right_dim,)), ((), ())), preferred_element_type=F32
    )


def iota(shape, dim):
    return lax.broadcasted_iota(jnp.int32, shape, dim)


def norm_stats(rows):
    offset = rows - jnp.mean(rows, axis=-1, keepdims=True)
    spread = lax.rsqrt(jnp.mean(offset * offset, axis=-1, keepdims=True) + EPS)
    return offset * spread, spread


def norm_back(unit, spread, gain, grad):
    product = grad * unit
    scaled = grad * gain
    centre = jnp.mean(scaled, axis=-1, keepdims=True)
    slope = jnp.mean(scaled * unit, axis=-1, keepdims=True)
    return spread * (scaled - centre - unit * slope), jnp.sum(product, axis=0, keepdims=True)


def gelu_pair(t):
    square = t * t
    th = jnp.tanh(0.7978845608 * (t + 0.044715 * t * square))
    plus = 0.5 * (1.0 + th)
    slope = plus + 0.5 * t * (1.0 - th * th) * (0.7978845608 * (1.0 + 0.134145 * square))
    return t * plus, slope


def three_parts(value):
    high = value.astype(BF).astype(F32)
    rest = value - high
    middle = rest.astype(BF).astype(F32)
    low = (rest - middle).astype(BF).astype(F32)
    return high, middle, low


def place_lanes(column, lane, first):
    high, middle, low = three_parts(column)
    return (
        jnp.where(lane == first, high, 0.0)
        + jnp.where(lane == first + 16, middle, 0.0)
        + jnp.where(lane == first + 32, low, 0.0)
    )


def join_lanes(stats, first):
    total = stats
    rolled = []
    for part in range(3):
        amount = (first + 16 * part) % LANES
        rolled.append(total if amount == 0 else pltpu.roll(total, LANES - amount, 1))
    return rolled[0] + rolled[1] + rolled[2]


def spread_heads(values, width):
    head_dim = width // HEADS
    pick = (iota((LANES, width), 0) == iota((LANES, width), 1) // head_dim).astype(BF)
    high, middle, low = three_parts(values)
    return dot(high.astype(BF), pick) + dot(middle.astype(BF), pick) + dot(low.astype(BF), pick)


def params(limit=VMEM_BYTES):
    return pltpu.CompilerParams(vmem_limit_bytes=limit)


def whole(shape):
    return pl.BlockSpec(shape, lambda *_: (0,) * len(shape))


def cost(flops, moved, exps=0):
    return pl.CostEstimate(flops=int(flops), bytes_accessed=int(moved), transcendentals=int(exps))


def sds(shape, kind):
    return jax.ShapeDtypeStruct(shape, kind)


def patch_in_kernel(src_ref, own_ref, other_ref, gain_ref, wq_ref, wx_ref, x_ref, n_ref, qkv_ref, cross_ref):
    half = own_ref.shape[0]
    part = src_ref.shape[0] // 2
    pieces = []
    for k in range(2):
        onehot = (iota((part, half), 1) == src_ref[k * part : (k + 1) * part, :]).astype(F32).astype(BF)
        pieces.append(dot(onehot, own_ref[...]))
        pieces.append(dot(onehot, other_ref[...]))
    x = jnp.concatenate(pieces, axis=0)
    x_ref[...] = x.astype(BF)
    unit, _ = norm_stats(x)
    normed = (unit * gain_ref[0:1, :]).astype(BF)
    n_ref[...] = normed
    qkv_ref[...] = dot(normed, wq_ref[...]).astype(BF)
    cross_ref[...] = dot(normed, wx_ref[...]).astype(BF)


def patch_in(src, own, other, gains, wq, wx):
    half, width = own.shape
    tokens = 2 * half
    step = 4 * half // (half // 72)
    rows = lambda w: pl.BlockSpec((step, w), lambda i: (i, 0))
    return pl.pallas_call(
        patch_in_kernel,
        grid=(tokens // step,),
        in_specs=[
            pl.BlockSpec((step // 2, 1), lambda i: (i, 0)),
            whole(own.shape),
            whole(own.shape),
            whole(gains.shape),
            whole(wq.shape),
            whole(wx.shape),
        ],
        out_specs=[rows(width), rows(width), rows(wq.shape[1]), rows(wx.shape[1])],
        out_shape=[
            sds((tokens, width), BF),
            sds((tokens, width), BF),
            sds((tokens, wq.shape[1]), BF),
            sds((tokens, wx.shape[1]), BF),
        ],
        compiler_params=params(),
        cost_estimate=cost(2 * tokens * width * (wq.shape[1] + wx.shape[1]), 2e7),
        name="patch_in",
    )(src, own, other, gains, wq, wx)


def window_kernel(qkv_ref, out_ref, stat_ref):
    tokens, width = out_ref.shape
    lane = iota((1, LANES), 1)
    left = lane < 64
    stats = jnp.zeros((tokens, LANES), F32)
    for pair in range(HEADS // 2):
        at = pair * LANES
        q = qkv_ref[:, at : at + LANES] * SCALE
        k = qkv_ref[:, width + at : width + at + LANES]
        v = qkv_ref[:, 2 * width + at : 2 * width + at + LANES]
        mixed = []
        for side in range(2):
            mine = left if side == 0 else ~left
            scores = dot(jnp.where(mine, q, 0).astype(BF), k, 1, 1)
            peak = jnp.max(scores, axis=-1, keepdims=True)
            raised = jnp.exp(scores - peak)
            total = jnp.sum(raised, axis=-1, keepdims=True)
            probs = (raised * (1.0 / total)).astype(BF)
            mixed.append(dot(probs, v))
            stats = stats + place_lanes(peak + jnp.log(total), lane, 2 * pair + side)
        out_ref[:, at : at + LANES] = jnp.where(left, mixed[0], mixed[1]).astype(BF)
    stat_ref[...] = stats.astype(BF)


def window_forward(qkv, tokens):
    total, width3 = qkv.shape
    width = width3 // 3
    return pl.pallas_call(
        window_kernel,
        grid=(total // tokens,),
        in_specs=[pl.BlockSpec((tokens, width3), lambda i: (i, 0))],
        out_specs=[
            pl.BlockSpec((tokens, width), lambda i: (i, 0)),
            pl.BlockSpec((tokens, LANES), lambda i: (i, 0)),
        ],
        out_shape=[sds((total, width), BF), sds((total, LANES), BF)],
        compiler_params=params(),
        cost_estimate=cost(16 * total * tokens * width, 8e6, total * tokens * HEADS),
        name="window_forward",
    )(qkv)


def stat_lanes(stats, head, first, base):
    row, col = iota((LANES, LANES), 0), iota((LANES, LANES), 1)
    hit = (row == first + head + 16 * (col - base)) & (col >= base) & (col < base + 3)
    return dot(stats, jnp.where(hit, -1.0, 0.0).astype(BF))


def window_back_kernel(qkv_ref, go_ref, stat_ref, out_ref):
    tokens, width = go_ref.shape
    lane = iota((1, LANES), 1)
    left = lane < 64
    stats = stat_ref[...]
    for pair in range(HEADS // 2):
        at = pair * LANES
        q = qkv_ref[:, at : at + LANES]
        k = qkv_ref[:, width + at : width + at + LANES]
        v = qkv_ref[:, 2 * width + at : 2 * width + at + LANES]
        g = go_ref[:, at : at + LANES]
        parts = []
        for side in range(2):
            mine = left if side == 0 else ~left
            base = 64 * (1 - side)
            ones = (lane >= base) & (lane < base + 3)
            shifted = jnp.where(mine, q.astype(F32) * SCALE, stat_lanes(stats, 2 * pair + side, 0, base))
            keys = jnp.where(mine, k.astype(F32), jnp.where(ones, 1.0, 0.0)).astype(BF)
            probs = jnp.exp(dot(keys, shifted.astype(BF), 1, 1))
            grads = dot(jnp.where(mine, v.astype(F32), 0.0).astype(BF), g, 1, 1)
            inner = jnp.sum(probs * grads, axis=0, keepdims=True)
            dscore = (probs * (grads - inner)).astype(BF)
            parts.append((dot(dscore, k, 0, 0), dot(dscore, q), dot(probs.astype(BF), g)))
        for index, factor in ((0, SCALE), (1, SCALE), (2, 1.0)):
            joined = jnp.where(left, parts[0][index], parts[1][index]) * factor
            out_ref[:, index * width + at : index * width + at + LANES] = joined.astype(BF)


def window_backward(qkv, go, stats, tokens):
    total, width3 = qkv.shape
    width = width3 // 3
    rows = lambda w: pl.BlockSpec((tokens, w), lambda i: (i, 0))
    return pl.pallas_call(
        window_back_kernel,
        grid=(total // tokens,),
        in_specs=[rows(width3), rows(width), rows(LANES)],
        out_specs=rows(width3),
        out_shape=sds((total, width3), BF),
        compiler_params=params(),
        cost_estimate=cost(40 * total * tokens * width, 1.3e7, total * tokens * HEADS),
        name="window_backward",
    )(qkv, go, stats)


def split_halves(rows, part):
    count = rows.shape[0] // (2 * part)
    return [
        jnp.concatenate([rows[(2 * w + s) * part : (2 * w + s + 1) * part] for w in range(count)], axis=0)
        for s in range(2)
    ]


def patch_ffn_kernel(
    src_ref, inv_ref, att_ref, x_ref, own_ref, other_ref, gain_ref, wo_ref, up_ref, down_ref,
    out_own_ref, out_other_ref, after_grad_ref, att_grad_ref, wo_grad_ref, up_grad_ref, down_grad_ref, gain_grad_ref,
    after, normed, cot, total, back, acts, dacts,
):
    step = pl.program_id(0)
    tokens, width = att_ref.shape
    half = own_ref.shape[0]
    part = 72
    block = 4 * part

    @pl.when(step == 0)
    def _():
        for b in range(tokens // block):
            rows = slice(b * block, (b + 1) * block)
            value = x_ref[rows, :].astype(F32) + dot(att_ref[rows, :], wo_ref[...])
            after[rows, :] = value
            unit, _ = norm_stats(value)
            normed[rows, :] = (unit * gain_ref[1:2, :]).astype(BF)
            pieces = []
            for k in range(2):
                table = src_ref[(2 * b + k) * part : (2 * b + k + 1) * part, :]
                onehot = (iota((part, half), 1) == table).astype(F32).astype(BF)
                pieces.append(dot(onehot, own_ref[...]))
                pieces.append(dot(onehot, other_ref[...]))
            cot[rows, :] = jnp.concatenate(pieces, axis=0).astype(BF)
        total[...] = jnp.zeros_like(total)
        back[...] = jnp.zeros_like(back)

    for b in range(tokens // block):
        rows = slice(b * block, (b + 1) * block)
        value, slope = gelu_pair(dot(normed[rows, :], up_ref[...]))
        act = value.astype(BF)
        acts[rows, :] = act
        total[rows, :] += dot(act, down_ref[...])
        dact = (slope * dot(cot[rows, :], down_ref[...], 1, 1)).astype(BF)
        dacts[rows, :] = dact
        back[rows, :] += dot(dact, up_ref[...], 1, 1)
    up_grad_ref[...] = dot(normed[...], dacts[...], 0, 0).astype(BF)
    down_grad_ref[...] = dot(acts[...], cot[...], 0, 0).astype(BF)

    @pl.when(step == pl.num_programs(0) - 1)
    def _():
        gain_sum = jnp.zeros((1, width), F32)
        for b in range(tokens // block):
            rows = slice(b * block, (b + 1) * block)
            unit, spread = norm_stats(after[rows, :])
            grad, gain_part = norm_back(unit, spread, gain_ref[1:2, :], back[rows, :])
            gain_sum = gain_sum + gain_part
            grad = cot[rows, :].astype(F32) + grad
            after_grad_ref[rows, :] = grad
            branch = grad.astype(BF)
            normed[rows, :] = branch
            att_grad_ref[rows, :] = dot(branch, wo_ref[...], 1, 1).astype(BF)
        gain_grad_ref[...] = jnp.broadcast_to(gain_sum, gain_grad_ref.shape)
        wo_grad_ref[...] = dot(att_ref[...], normed[...], 0, 0).astype(BF)
        halves = split_halves(after[...] + total[...], part)
        onehot = (iota((half, half), 1) == inv_ref[...]).astype(F32).astype(BF)
        out_own_ref[...] = dot(onehot, halves[0].astype(BF)).astype(BF)
        out_other_ref[...] = dot(onehot, halves[1].astype(BF)).astype(BF)


def patch_ffn(src, inv, att, x, own, other, gains, wo, up, down, chunk=384):
    tokens, width = att.shape
    half = tokens // 2
    hidden = up.shape[1]
    return pl.pallas_call(
        patch_ffn_kernel,
        grid=(hidden // chunk,),
        in_specs=[whole(a.shape) for a in (src, inv, att, x, own, other, gains, wo)]
        + [pl.BlockSpec((width, chunk), lambda j: (0, j)), pl.BlockSpec((chunk, width), lambda j: (j, 0))],
        out_specs=[
            whole((half, width)),
            whole((half, width)),
            whole((tokens, width)),
            whole((tokens, width)),
            whole((width, width)),
            pl.BlockSpec((width, chunk), lambda j: (0, j)),
            pl.BlockSpec((chunk, width), lambda j: (j, 0)),
            whole((8, width)),
        ],
        out_shape=[
            sds((half, width), BF),
            sds((half, width), BF),
            sds((tokens, width), F32),
            sds((tokens, width), BF),
            sds((width, width), BF),
            sds((width, hidden), BF),
            sds((hidden, width), BF),
            sds((8, width), F32),
        ],
        scratch_shapes=[
            pltpu.VMEM((tokens, width), F32),
            pltpu.VMEM((tokens, width), BF),
            pltpu.VMEM((tokens, width), BF),
            pltpu.VMEM((tokens, width), F32),
            pltpu.VMEM((tokens, width), F32),
            pltpu.VMEM((tokens, chunk), BF),
            pltpu.VMEM((tokens, chunk), BF),
        ],
        compiler_params=params(),
        cost_estimate=cost(12 * tokens * width * hidden, 4e7, tokens * hidden),
        name="patch_ffn",
    )(src, inv, att, x, own, other, gains, wo, up, down)


def patch_back_kernel(
    inv_ref, gp_ref, gk_ref, gv_ref, n_ref, x_ref, after_ref, gain_ref, wq_ref, wx_ref,
    own_ref, other_ref, wq_grad_ref, wx_grad_ref, gain_grad_ref, back,
    *, q_steps, k_steps,
):
    step = pl.program_id(0)
    half, width = own_ref.shape
    tokens = 2 * half
    part = 72
    block = 4 * part

    @pl.when(step == 0)
    def _():
        back[...] = jnp.zeros_like(back)

    def one(grad_ref, weight_ref, out_ref):
        back[...] += dot(grad_ref[...], weight_ref[...], 1, 1)
        out_ref[...] = dot(n_ref[...], grad_ref[...], 0, 0).astype(BF)

    @pl.when(step < q_steps)
    def _():
        one(gp_ref, wq_ref, wq_grad_ref)

    @pl.when((step >= q_steps) & (step < q_steps + k_steps))
    def _():
        one(gk_ref, wx_ref, wx_grad_ref)

    @pl.when(step >= q_steps + k_steps)
    def _():
        one(gv_ref, wx_ref, wx_grad_ref)

    @pl.when(step == pl.num_programs(0) - 1)
    def _():
        gain_sum = jnp.zeros((1, width), F32)
        for b in range(tokens // block):
            rows = slice(b * block, (b + 1) * block)
            unit, spread = norm_stats(x_ref[rows, :].astype(F32))
            grad, gain_part = norm_back(unit, spread, gain_ref[0:1, :], back[rows, :])
            gain_sum = gain_sum + gain_part
            back[rows, :] = after_ref[rows, :] + grad
        gain_grad_ref[...] = jnp.broadcast_to(gain_sum, gain_grad_ref.shape)
        halves = split_halves(back[...], part)
        onehot = (iota((half, half), 1) == inv_ref[...]).astype(F32).astype(BF)
        high = halves[0].astype(BF)
        low = (halves[0] - high.astype(F32)).astype(BF)
        own_ref[...] = dot(onehot, high) + dot(onehot, low)
        other_ref[...] = dot(onehot, halves[1].astype(BF)).astype(BF)


def patch_back(inv, gp, gk, gv, normed, x, after, gains, wq, wx, chunk=384):
    tokens, width = x.shape
    half = tokens // 2
    q_steps, k_steps = wq.shape[1] // chunk, width // chunk
    steps = q_steps + 2 * k_steps
    at_q = lambda j: jnp.minimum(j, q_steps - 1)
    at_x = lambda j: jnp.maximum(j - q_steps, 0)
    at_k = lambda j: jnp.clip(j - q_steps, 0, k_steps - 1)
    at_v = lambda j: jnp.clip(j - q_steps - k_steps, 0, k_steps - 1)
    return pl.pallas_call(
        functools.partial(patch_back_kernel, q_steps=q_steps, k_steps=k_steps),
        grid=(steps,),
        in_specs=[
            whole(inv.shape),
            pl.BlockSpec((tokens, chunk), lambda j: (0, at_q(j))),
            pl.BlockSpec((tokens, chunk), lambda j: (0, at_k(j))),
            pl.BlockSpec((tokens, chunk), lambda j: (0, at_v(j))),
            whole(normed.shape),
            whole(x.shape),
            whole(after.shape),
            whole(gains.shape),
            pl.BlockSpec((width, chunk), lambda j: (0, at_q(j))),
            pl.BlockSpec((width, chunk), lambda j: (0, at_x(j))),
        ],
        out_specs=[
            whole((half, width)),
            whole((half, width)),
            pl.BlockSpec((width, chunk), lambda j: (0, at_q(j))),
            pl.BlockSpec((width, chunk), lambda j: (0, at_x(j))),
            whole((8, width)),
        ],
        out_shape=[
            sds((half, width), F32),
            sds((half, width), BF),
            sds(wq.shape, BF),
            sds(wx.shape, BF),
            sds((8, width), F32),
        ],
        scratch_shapes=[pltpu.VMEM((tokens, width), F32)],
        compiler_params=params(),
        cost_estimate=cost(4 * tokens * width * (wq.shape[1] + wx.shape[1]), 4e7),
        name="patch_back",
    )(inv, gp, gk, gv, normed, x, after, gains, wq, wx)


def query_in_kernel(x_ref, gain_ref, w_ref, n_ref, q_ref, kv_ref):
    unit, _ = norm_stats(x_ref[...].astype(F32))
    normed = (unit * gain_ref[2:3, :]).astype(BF)
    n_ref[...] = normed
    width = x_ref.shape[1]
    q_ref[...] = dot(normed, w_ref[:, :width]).astype(BF)
    kv_ref[...] = dot(normed, w_ref[:, width:]).astype(BF)


def query_in_call(x, gains, w):
    slots, width = x.shape
    return pl.pallas_call(
        query_in_kernel,
        out_shape=[sds((slots, width), BF), sds((slots, width), BF), sds((slots, 2 * width), BF)],
        compiler_params=params(),
        cost_estimate=cost(2 * slots * width * w.shape[1], 5e6),
        name="query_in",
    )(x, gains, w)


def row_blocks(total, first, length, most=256):
    blocks = []
    for low, high in ((0, first), (first + length, total)):
        at = low
        while at < high:
            count = -(-(high - at) // most)
            size = min(high - at, -(-((high - at) // count) // 16) * 16)
            blocks.append((at, size, False))
            at += size
    blocks.append((first, length, True))
    return blocks


def query_forward_kernel(q_ref, k_ref, v_ref, sk_ref, sv_ref, kb_ref, qs_ref, ks_ref, out_ref, stat_ref, held, *, blocks):
    pair = pl.program_id(0)
    lane = iota((1, LANES), 1)
    left = lane < 64

    @pl.when(pair == 0)
    def _():
        held[...] = jnp.zeros_like(held)

    keys = []
    for side in range(2):
        keys.append(jnp.where(lane == 64 * (1 - side), kb_ref[...], k_ref[...]))
    for at, size, near in blocks:
        q = q_ref[at : at + size, :].astype(F32) * SCALE
        mixed, columns = [], jnp.zeros((size, LANES), F32)
        for side in range(2):
            mine = left if side == 0 else ~left
            own = jnp.where(mine, q, jnp.where(lane == 64 * (1 - side), 1.0, 0.0)).astype(BF)
            scores = dot(own, keys[side], 1, 1)
            peak = jnp.max(scores, axis=-1, keepdims=True)
            if near:
                extra = dot(jnp.where(mine, q, 0.0).astype(BF), sk_ref[...], 1, 1)
                extra = jnp.where(qs_ref[...] == ks_ref[...], extra, MASKED)
                peak = jnp.maximum(peak, jnp.max(extra, axis=-1, keepdims=True))
            raised = jnp.exp(scores - peak)
            total = jnp.sum(raised, axis=-1, keepdims=True)
            value = dot(raised.astype(BF), v_ref[...])
            if near:
                raised = jnp.exp(extra - peak)
                total = total + jnp.sum(raised, axis=-1, keepdims=True)
                value = value + dot(raised.astype(BF), sv_ref[...])
            mixed.append(value * (1.0 / total))
            columns = columns + place_lanes(peak + jnp.log(total), lane, 2 * pair + side)
        out_ref[at : at + size, :] = jnp.where(left, mixed[0], mixed[1]).astype(BF)
        held[at : at + size, :] += columns

    @pl.when(pair == pl.num_programs(0) - 1)
    def _():
        stat_ref[...] = held[...].astype(BF)


def query_forward(q, cross, slot_kv, key_bias, q_seg, k_seg, blocks):
    total, width = q.shape
    patches, slots = cross.shape[0], slot_kv.shape[0]
    pairs = HEADS // 2
    col = lambda rows, first: pl.BlockSpec((rows, LANES), lambda p: (0, first + p))
    return pl.pallas_call(
        functools.partial(query_forward_kernel, blocks=blocks),
        grid=(pairs,),
        in_specs=[
            col(total, 0), col(patches, 0), col(patches, pairs), col(slots, 0), col(slots, pairs),
            whole(key_bias.shape), whole(q_seg.shape), whole(k_seg.shape),
        ],
        out_specs=[col(total, 0), whole((total, LANES))],
        out_shape=[sds((total, width), BF), sds((total, LANES), BF)],
        scratch_shapes=[pltpu.VMEM((total, LANES), F32)],
        compiler_params=params(),
        cost_estimate=cost(16 * total * patches * width, 1e7, total * patches * HEADS),
        name="query_forward",
    )(q, cross, cross, slot_kv, slot_kv, key_bias, q_seg, k_seg)


def query_back_kernel(
    q_ref, go_ref, stat_ref, k_ref, v_ref, sk_ref, sv_ref, kb_ref, qs_ref, ks_ref,
    dq_ref, dk_ref, dv_ref, dsk_ref, dsv_ref, sum_k, sum_v,
    *, blocks,
):
    pair = pl.program_id(0)
    lane = iota((1, LANES), 1)
    left = lane < 64
    sides = []
    for side in range(2):
        mine = left if side == 0 else ~left
        base = 64 * (1 - side)
        ones = jnp.where((lane >= base) & (lane < base + 3), 1.0, 0.0)
        bias = lane == base + 3
        sides.append(
            (
                jnp.where(mine, k_ref[...].astype(F32), jnp.where(bias, kb_ref[...].astype(F32), ones)).astype(BF),
                jnp.where(mine, v_ref[...].astype(F32), ones).astype(BF),
                jnp.where(mine, sk_ref[...].astype(F32), ones).astype(BF),
                jnp.where(mine, sv_ref[...].astype(F32), ones).astype(BF),
            )
        )
    for number, (at, size, near) in enumerate(blocks):
        q = q_ref[at : at + size, :]
        g = go_ref[at : at + size, :]
        stats = stat_ref[at : at + size, :]
        dq, dk, dv, dsk, dsv = [], [], [], [], []
        for side in range(2):
            mine = left if side == 0 else ~left
            base = 64 * (1 - side)
            head = 2 * pair + side
            plain = jnp.where(lane == base + 3, 1.0, 0.0)
            shifted = jnp.where(mine, q.astype(F32) * SCALE, stat_lanes(stats, head, 0, base) + plain).astype(BF)
            lowered = jnp.where(mine, g.astype(F32), stat_lanes(stats, head, 48, base)).astype(BF)
            keys, values, slot_keys, slot_values = sides[side]
            probs = jnp.exp(dot(keys, shifted, 1, 1))
            dscore = (probs * dot(values, lowered, 1, 1)).astype(BF)
            dk.append(dot(dscore, q))
            dv.append(dot(probs.astype(BF), g))
            moved = dot(dscore, k_ref[...], 0, 0)
            if near:
                scores = jnp.where(ks_ref[...] == qs_ref[...], dot(slot_keys, shifted, 1, 1), MASKED)
                probs = jnp.exp(scores)
                dscore = (probs * dot(slot_values, lowered, 1, 1)).astype(BF)
                dsk.append(dot(dscore, q))
                dsv.append(dot(probs.astype(BF), g))
                moved = moved + dot(dscore, sk_ref[...], 0, 0)
            dq.append(moved)
        dq_ref[at : at + size, :] = (jnp.where(left, dq[0], dq[1]) * SCALE).astype(BF)
        if number == 0:
            sum_k[...] = jnp.where(left, dk[0], dk[1])
            sum_v[...] = jnp.where(left, dv[0], dv[1])
        else:
            sum_k[...] += jnp.where(left, dk[0], dk[1])
            sum_v[...] += jnp.where(left, dv[0], dv[1])
        if near:
            dsk_ref[...] = (jnp.where(left, dsk[0], dsk[1]) * SCALE).astype(BF)
            dsv_ref[...] = jnp.where(left, dsv[0], dsv[1]).astype(BF)
    dk_ref[...] = (sum_k[...] * SCALE).astype(BF)
    dv_ref[...] = sum_v[...].astype(BF)


def query_backward(q, go, stats, cross, slot_kv, key_bias, q_seg, k_seg, blocks):
    total, width = q.shape
    patches, slots = cross.shape[0], slot_kv.shape[0]
    pairs = HEADS // 2
    col = lambda rows, first: pl.BlockSpec((rows, LANES), lambda p: (0, first + p))
    return pl.pallas_call(
        functools.partial(query_back_kernel, blocks=blocks),
        grid=(pairs,),
        in_specs=[
            col(total, 0), col(total, 0), whole(stats.shape), col(patches, 0), col(patches, pairs),
            col(slots, 0), col(slots, pairs), whole(key_bias.shape), whole(q_seg.shape), whole(k_seg.shape),
        ],
        out_specs=[col(total, 0), col(patches, 0), col(patches, 0), col(slots, 0), col(slots, 0)],
        out_shape=[
            sds((total, width), BF),
            sds((patches, width), BF),
            sds((patches, width), BF),
            sds((slots, width), BF),
            sds((slots, width), BF),
        ],
        scratch_shapes=[pltpu.VMEM((patches, LANES), F32), pltpu.VMEM((patches, LANES), F32)],
        compiler_params=params(),
        cost_estimate=cost(40 * total * patches * width, 1.5e7, total * patches * HEADS),
        name="query_backward",
    )(q, go, stats, cross, cross, slot_kv, slot_kv, key_bias, q_seg, k_seg)


def query_ffn_kernel(*refs, parts):
    outs, stats = refs[:parts], refs[parts : 2 * parts]
    x_ref, cot_ref, gain_ref, wo_ref, up_ref, down_ref = refs[2 * parts : 2 * parts + 6]
    (
        out_ref, grad_ref, send_ref, stat_ref, att_ref, normed_ref, act_ref, dact_ref, branch_ref, gain_grad_ref,
        mixed, after, total, back, joint,
    ) = refs[2 * parts + 6 :]
    step = pl.program_id(0)
    width = x_ref.shape[1]

    @pl.when(step == 0)
    def _():
        each = [join_lanes(s[...].astype(F32), 0) for s in stats]
        peak = functools.reduce(jnp.maximum, each)
        weights = [jnp.exp(e - peak) for e in each]
        weight_sum = functools.reduce(jnp.add, weights)
        joint[...] = peak + jnp.log(weight_sum)
        value = None
        for o, w in zip(outs, weights):
            term = o[...].astype(F32) * spread_heads(w / weight_sum, width)
            value = term if value is None else value + term
        mixed[...] = value
        att_ref[...] = value.astype(BF)
        rows = x_ref[...].astype(F32) + dot(att_ref[...], wo_ref[...])
        after[...] = rows
        unit, _ = norm_stats(rows)
        normed_ref[...] = (unit * gain_ref[3:4, :]).astype(BF)
        total[...] = jnp.zeros_like(total)
        back[...] = jnp.zeros_like(back)

    value, slope = gelu_pair(dot(normed_ref[...], up_ref[...]))
    act = value.astype(BF)
    act_ref[...] = act
    total[...] += dot(act, down_ref[...])
    dact = (slope * dot(cot_ref[...], down_ref[...], 1, 1)).astype(BF)
    dact_ref[...] = dact
    back[...] += dot(dact, up_ref[...], 1, 1)

    @pl.when(step == pl.num_programs(0) - 1)
    def _():
        out_ref[...] = (after[...] + total[...]).astype(BF)
        unit, spread = norm_stats(after[...])
        grad, gain_part = norm_back(unit, spread, gain_ref[3:4, :], back[...])
        gain_grad_ref[...] = jnp.broadcast_to(gain_part, gain_grad_ref.shape)
        grad = cot_ref[...].astype(F32) + grad
        grad_ref[...] = grad
        branch = grad.astype(BF)
        branch_ref[...] = branch
        sent = dot(branch, wo_ref[...], 1, 1).astype(BF)
        send_ref[...] = sent
        pick = (iota((width, LANES), 0) // (width // HEADS) == iota((width, LANES), 1)).astype(F32).astype(BF)
        high, middle, low = three_parts(sent.astype(F32) * mixed[...])
        inner = dot(high.astype(BF), pick) + dot(middle.astype(BF), pick) + dot(low.astype(BF), pick)
        lane = iota((1, LANES), 1)
        packed = jnp.zeros(inner.shape, F32)
        for source, first in ((joint[...], 0), (inner, 48)):
            kept = jnp.where(lane < HEADS, source, 0.0)
            for number, piece in enumerate(three_parts(kept)):
                amount = first + 16 * number
                packed = packed + (piece if amount == 0 else pltpu.roll(piece, amount, 1))
        stat_ref[...] = packed.astype(BF)


def query_ffn(outs, stats, x, cot, gains, wo, up, down, chunk=768):
    slots, width = x.shape
    hidden = up.shape[1]
    parts = len(outs)
    rows = lambda kind: sds((slots, width), kind)
    return pl.pallas_call(
        functools.partial(query_ffn_kernel, parts=parts),
        grid=(hidden // chunk,),
        in_specs=[whole(a.shape) for a in (*outs, *stats, x, cot, gains, wo)]
        + [pl.BlockSpec((width, chunk), lambda j: (0, j)), pl.BlockSpec((chunk, width), lambda j: (j, 0))],
        out_specs=[
            whole((slots, width)),
            whole((slots, width)),
            whole((slots, width)),
            whole((slots, LANES)),
            whole((slots, width)),
            whole((slots, width)),
            pl.BlockSpec((slots, chunk), lambda j: (0, j)),
            pl.BlockSpec((slots, chunk), lambda j: (0, j)),
            whole((slots, width)),
            whole((8, width)),
        ],
        out_shape=[
            rows(BF), rows(F32), rows(BF), sds((slots, LANES), BF), rows(BF), rows(BF),
            sds((slots, hidden), BF), sds((slots, hidden), BF), rows(BF), sds((8, width), F32),
        ],
        scratch_shapes=[pltpu.VMEM((slots, width), F32)] * 4 + [pltpu.VMEM((slots, LANES), F32)],
        compiler_params=params(),
        cost_estimate=cost(8 * slots * width * hidden, 2e7, slots * hidden),
        name="query_ffn",
    )(*outs, *stats, x, cot, gains, wo, up, down)


def query_weights_kernel(normed_ref, cot_ref, att_ref, branch_ref, act_ref, dact_ref, up_ref, down_ref, wo_ref):
    up_ref[...] = dot(normed_ref[...], dact_ref[...], 0, 0).astype(BF)
    down_ref[...] = dot(act_ref[...], cot_ref[...], 0, 0).astype(BF)

    @pl.when(pl.program_id(0) == 0)
    def _():
        wo_ref[...] = dot(att_ref[...], branch_ref[...], 0, 0).astype(BF)


def query_weights(normed, cot, att, branch, act, dact, chunk=768):
    slots, width = normed.shape
    hidden = act.shape[1]
    return pl.pallas_call(
        query_weights_kernel,
        grid=(hidden // chunk,),
        in_specs=[whole((slots, width))] * 4 + [pl.BlockSpec((slots, chunk), lambda j: (0, j))] * 2,
        out_specs=[
            pl.BlockSpec((width, chunk), lambda j: (0, j)),
            pl.BlockSpec((chunk, width), lambda j: (j, 0)),
            whole((width, width)),
        ],
        out_shape=[sds((width, hidden), BF), sds((hidden, width), BF), sds((width, width), BF)],
        compiler_params=params(),
        cost_estimate=cost(4 * slots * width * hidden, 1.6e7),
        name="query_weights",
    )(normed, cot, att, branch, act, dact)


def query_out_kernel(*refs, parts):
    dqs = refs[:parts]
    dk_ref, dv_ref, n_ref, x_ref, grad_ref, gain_ref, w_ref = refs[parts : parts + 7]
    out_ref, w_grad_ref, gain_grad_ref = refs[parts + 7 :]
    width = x_ref.shape[1]
    value = dqs[0][...].astype(F32)
    for d in dqs[1:]:
        value = value + d[...].astype(F32)
    back = None
    for number, piece in enumerate((value.astype(BF), dk_ref[...], dv_ref[...])):
        cols = slice(number * width, (number + 1) * width)
        term = dot(piece, w_ref[:, cols], 1, 1)
        back = term if back is None else back + term
        w_grad_ref[:, cols] = dot(n_ref[...], piece, 0, 0).astype(BF)
    unit, spread = norm_stats(x_ref[...].astype(F32))
    grad, gain_part = norm_back(unit, spread, gain_ref[2:3, :], back)
    gain_grad_ref[...] = jnp.broadcast_to(gain_part, gain_grad_ref.shape)
    out_ref[...] = grad_ref[...] + grad


def query_out(dqs, dk, dv, normed, x, grad, gains, w):
    slots, width = x.shape
    return pl.pallas_call(
        functools.partial(query_out_kernel, parts=len(dqs)),
        out_shape=[sds((slots, width), F32), sds(w.shape, BF), sds((8, width), F32)],
        compiler_params=params(),
        cost_estimate=cost(4 * slots * width * w.shape[1], 1e7),
        name="query_out",
    )(*dqs, dk, dv, normed, x, grad, gains, w)


def from_ahead(array, count, distance):
    return lax.ppermute(array, "strip", [(i, (i - distance) % count) for i in range(count)])


def from_partner(array, count):
    return lax.ppermute(array, "strip", [(i, i ^ 1) for i in range(count)])


def scattered(grad):
    strips, pages = lax.axis_size("strip"), lax.axis_size("page")
    rows, cols = grad.shape
    part = lax.psum_scatter(grad, "strip", scatter_dimension=0, tiled=True)
    part = part.reshape(rows // strips, pages, cols // pages).transpose(1, 0, 2)
    return lax.psum_scatter(part, "page", scatter_dimension=0, tiled=False).astype(F32)


def local(
    visual_in, query_in, row_valid, segment_ids, slot_valid, col_shift, row_shifted, norm_gains,
    w_vqkv, w_vout, w_up, w_down, w_qqkv, w_xkv, w_qout, w_qup, w_qdown, visual_cot, query_cot,
):
    pages, strip_rows, columns, width = visual_in.shape
    own_slots, all_slots = query_in.shape[1], segment_ids.shape[1]
    count = lax.axis_size("strip")
    group = count // 2
    half = strip_rows * columns
    slots = 2 * own_slots
    window = WIN * WIN
    part = strip_rows * WIN
    place = lax.axis_index("strip")
    odd = place % 2 == 1
    up = jnp.where(odd, 1 - row_shifted[0], row_shifted[0])
    down = 1 - up
    pick = lambda array, which: lax.dynamic_index_in_dim(array, which, 0, keepdims=False)

    def put(own, other):
        first = jnp.where(up == 0, own, other)
        second = jnp.where(up == 0, other, own)
        return jnp.stack([first, second], axis=0)

    def pair_slots(array):
        mine, theirs = pick(array, up), from_partner(pick(array, down), count)
        return jnp.where(odd, jnp.concatenate([theirs, mine]), jnp.concatenate([mine, theirs]))

    gains = jnp.pad(norm_gains.T, ((0, 4), (0, 0)))
    shift = pick(col_shift, up)
    query_rows = pair_slots(query_in)
    patch_own = pick(visual_in, up).reshape(half, width)
    patch_other = from_ahead(pick(visual_in, down).reshape(half, width), count, 1)
    query_cots = pair_slots(query_cot)
    cot_own = pick(visual_cot, up).reshape(half, width)
    cot_other = from_ahead(pick(visual_cot, down).reshape(half, width), count, 1)
    rows_ok = jnp.concatenate([pick(row_valid, up), from_ahead(pick(row_valid, down), count, 1)])
    slots_ok = pair_slots(slot_valid)

    token = jnp.arange(half, dtype=jnp.int32)
    in_window = token % part
    src = (in_window // WIN) * columns + (token // part * WIN + in_window % WIN + shift) % columns
    turned = (token % columns - shift) % columns
    inv = (turned // WIN) * part + (token // columns) * WIN + turned % WIN
    src, inv = src[:, None], inv[:, None]
    key_bias = jnp.where(jnp.tile(jnp.repeat(rows_ok, WIN), 2 * half // window) == 1, 0.0, MASKED)
    key_bias = jnp.broadcast_to(key_bias.astype(BF)[:, None], (2 * half, LANES))

    order = [-1] + list(range(group - 1))
    near_first, near_length = slots - 32, slots + 64
    segments = pick(segment_ids, up)
    twice = jnp.concatenate([segments, segments, segments])
    base = (place // 2) * slots
    near_ids = lax.dynamic_slice_in_dim(twice, all_slots + base - 32, near_length)
    own_ids = lax.dynamic_slice_in_dim(segments, base, slots)
    own_ids = jnp.where(slots_ok == 1, own_ids, -1)
    blocks = row_blocks(all_slots, near_first, near_length)

    def gather(array):
        return jnp.concatenate(
            [array if k == 0 else from_ahead(array, count, 2 * k) for k in order], axis=0
        )

    def give_back(array):
        pieces = []
        for number, k in enumerate(order):
            piece = array[number * slots : (number + 1) * slots]
            pieces.append(piece if k == 0 else from_ahead(piece, count, -2 * k))
        return pieces

    normed_three, q_own, slot_kv = query_in_call(query_rows, gains, w_qqkv)
    q_all = gather(q_own)
    x, normed_one, qkv, cross = patch_in(src, patch_own, patch_other, gains, w_vqkv, w_xkv)
    att, win_stats = window_forward(qkv, window)
    q_out, q_stats = query_forward(q_all, cross, slot_kv, key_bias, near_ids[:, None], own_ids[None, :], blocks)
    out_parts, stat_parts = give_back(q_out), give_back(q_stats)
    (vis_own, vis_other, grad_after, grad_att, g_vout, g_up, g_down, gain_two) = patch_ffn(
        src, inv, att, x, cot_own, cot_other, gains, w_vout, w_up, w_down
    )
    (q_res, grad_q, send_q, send_stats, att_q, normed_four, act_q, dact_q, branch_q, gain_four) = query_ffn(
        out_parts, stat_parts, query_rows, query_cots, gains, w_qout, w_qup, w_qdown
    )
    go_all, stats_all = gather(send_q), gather(send_stats)
    g_qup, g_qdown, g_qout = query_weights(normed_four, query_cots, att_q, branch_q, act_q, dact_q)
    g_proj = window_backward(qkv, grad_att, win_stats, window)
    dq, dk, dv, dsk, dsv = query_backward(
        q_all, go_all, stats_all, cross, slot_kv, key_bias, near_ids[None, :], own_ids[:, None], blocks
    )
    dq_parts = give_back(dq)
    vin_own, vin_other, g_vqkv, g_xkv, gain_one = patch_back(
        inv, g_proj, dk, dv, normed_one, x, grad_after, gains, w_vqkv, w_xkv
    )
    qin_grad, g_qqkv, gain_three = query_out(dq_parts, dsk, dsv, normed_three, query_rows, grad_q, gains, w_qqkv)

    shape = (pages, strip_rows, columns, width)
    visual_out = put(vis_own, from_ahead(vis_other, count, -1)).reshape(shape)
    visual_in_grad = put(vin_own, from_ahead(vin_other, count, -1).astype(F32)).reshape(shape)

    def return_slots(pair, kind):
        low, high = pair[:own_slots], pair[own_slots:]
        mine = jnp.where(odd, high, low)
        theirs = from_partner(jnp.where(odd, low, high).astype(BF), count)
        return put(mine.astype(kind), theirs.astype(kind))

    query_out_rows = return_slots(q_res, BF)
    query_in_grad = return_slots(qin_grad, F32)

    gain_rows = jnp.stack([gain_one[0], gain_two[0], gain_three[0], gain_four[0]])
    gain_rows = lax.psum_scatter(gain_rows, "page", scatter_dimension=0, tiled=True)
    gain_part = lax.psum_scatter(gain_rows, "strip", scatter_dimension=1, tiled=True).reshape(-1, 1)
    return (
        visual_out, query_out_rows, visual_in_grad, query_in_grad, gain_part,
        scattered(g_vqkv), scattered(g_vout), scattered(g_up), scattered(g_down), scattered(g_qqkv),
        scattered(g_xkv), scattered(g_qout), scattered(g_qup), scattered(g_qdown),
    )


def solution(mesh):
    tokens, slots, table = P("page", "strip", None, None), P("page", "strip", None), P("page", "strip")
    tile = P("strip", "page")
    return jax.shard_map(
        local,
        mesh=mesh,
        in_specs=(tokens, slots, table, P("page", None), table, P("page"), P("page")) + (P(),) * 10 + (tokens, slots),
        out_specs=(tokens, slots, tokens, slots) + (tile,) * 10,
        check_vma=False,
    )
```

```python
import functools

import jax
import jax.numpy as jnp
from jax import lax
from jax.experimental import pallas as pl
from jax.experimental.pallas import tpu as pltpu
from jax.sharding import PartitionSpec as P

HEADS = 12
WIN = 12
EPS = 1e-05
MASKED = -1e9
SCALE = 0.125
BF = jnp.bfloat16
F32 = jnp.float32
LANES = 128
VMEM_BYTES = 60 * 1024 * 1024


def dot(left, right, left_dim=1, right_dim=0):
    return lax.dot_general(
        left, right, (((left_dim,), (right_dim,)), ((), ())), preferred_element_type=F32
    )


def iota(shape, dim):
    return lax.broadcasted_iota(jnp.int32, shape, dim)


def norm_stats(rows):
    offset = rows - jnp.mean(rows, axis=-1, keepdims=True)
    spread = lax.rsqrt(jnp.mean(offset * offset, axis=-1, keepdims=True) + EPS)
    return offset * spread, spread


def norm_back(unit, spread, gain, grad):
    product = grad * unit
    scaled = grad * gain
    centre = jnp.mean(scaled, axis=-1, keepdims=True)
    slope = jnp.mean(scaled * unit, axis=-1, keepdims=True)
    return spread * (scaled - centre - unit * slope), jnp.sum(product, axis=0, keepdims=True)


def gelu_pair(t):
    square = t * t
    th = jnp.tanh(0.7978845608 * (t + 0.044715 * t * square))
    plus = 0.5 * (1.0 + th)
    slope = plus + 0.5 * t * (1.0 - th * th) * (0.7978845608 * (1.0 + 0.134145 * square))
    return t * plus, slope


def three_parts(value):
    high = value.astype(BF).astype(F32)
    rest = value - high
    middle = rest.astype(BF).astype(F32)
    low = (rest - middle).astype(BF).astype(F32)
    return high, middle, low


def place_lanes(column, lane, first):
    high, middle, low = three_parts(column)
    return (
        jnp.where(lane == first, high, 0.0)
        + jnp.where(lane == first + 16, middle, 0.0)
        + jnp.where(lane == first + 32, low, 0.0)
    )


def join_lanes(stats, first):
    total = stats
    rolled = []
    for part in range(3):
        amount = (first + 16 * part) % LANES
        rolled.append(total if amount == 0 else pltpu.roll(total, LANES - amount, 1))
    return rolled[0] + rolled[1] + rolled[2]


def spread_heads(values, width):
    head_dim = width // HEADS
    pick = (iota((LANES, width), 0) == iota((LANES, width), 1) // head_dim).astype(BF)
    high, middle, low = three_parts(values)
    return dot(high.astype(BF), pick) + dot(middle.astype(BF), pick) + dot(low.astype(BF), pick)


def params(limit=VMEM_BYTES):
    return pltpu.CompilerParams(vmem_limit_bytes=limit)


def whole(shape):
    return pl.BlockSpec(shape, lambda *_: (0,) * len(shape))


def cost(flops, moved, exps=0):
    return pl.CostEstimate(flops=int(flops), bytes_accessed=int(moved), transcendentals=int(exps))


def sds(shape, kind):
    return jax.ShapeDtypeStruct(shape, kind)


def tile_index(strip, half, order):
    y = strip % 2
    lead = (y, half) if order == 0 else (half, y)
    return lead + ((strip // 2 % 2) * 2 + strip // 4,)


def tile_shape(rows, cols):
    return (2, 2, 2, 4, cols // 256 * (rows // 16), LANES)


def store_all(ref, value, order):
    rows, cols = value.shape
    size, tiles = rows // 16, cols // 256
    for strip in range(8):
        for core in range(2):
            at = (2 * strip + core) * size
            for half in range(2):
                lead = tile_index(strip, half, order)
                for t in range(tiles):
                    lanes = (half * tiles + t) * LANES
                    ref[(core, *lead, slice(t * size, (t + 1) * size), slice(None))] = value[at : at + size, lanes : lanes + LANES]


def store_columns(ref, value, order):
    size = value.shape[0] // 16
    for strip in range(8):
        for core in range(2):
            at = (2 * strip + core) * size
            lead = list(tile_index(strip, 0, order))
            for t in range(value.shape[1] // LANES):
                ref[(core, *lead, slice(t * size, (t + 1) * size), slice(None))] = value[at : at + size, t * LANES : (t + 1) * LANES]


def store_strip(ref, value, order):
    size, tiles = value.shape[0] // 2, value.shape[1] // 256
    for core in range(2):
        for half in range(2):
            lead = (0, half) if order == 0 else (half, 0)
            for t in range(tiles):
                lanes = (half * tiles + t) * LANES
                ref[(core, *lead, 0, slice(t * size, (t + 1) * size), slice(None))] = value[
                    core * size : (core + 1) * size, lanes : lanes + LANES
                ]


def columns_spec(rows, chunk, per_half, order, at):
    block = (2, 2, 1, 4) if order == 0 else (2, 1, 2, 4)
    lead = lambda half: (0, 0, half, 0) if order == 0 else (0, half, 0, 0)
    return pl.BlockSpec(
        (*block, chunk // LANES * (rows // 16), LANES), lambda j: (*lead(at(j) // per_half), at(j) % per_half, 0)
    )


def strip_spec(rows, cols, order):
    block = (2, 1, 2, 1) if order == 0 else (2, 2, 1, 1)
    lead = lambda y: (0, y, 0) if order == 0 else (0, 0, y)
    return pl.BlockSpec(
        (*block, cols // 256 * (rows // 16), LANES),
        lambda j: (*lead(j % 2), (j // 2 % 2) * 2 + j // 4, 0, 0),
    )


def patch_in_kernel(src_ref, own_ref, other_ref, gain_ref, wq_ref, wx_ref, x_ref, n_ref, qkv_ref, cross_ref):
    half = own_ref.shape[0]
    part = src_ref.shape[0] // 2
    pieces = []
    for k in range(2):
        onehot = (iota((part, half), 1) == src_ref[k * part : (k + 1) * part, :]).astype(F32).astype(BF)
        pieces.append(dot(onehot, own_ref[...]))
        pieces.append(dot(onehot, other_ref[...]))
    x = jnp.concatenate(pieces, axis=0)
    x_ref[...] = x.astype(BF)
    unit, _ = norm_stats(x)
    normed = (unit * gain_ref[0:1, :]).astype(BF)
    n_ref[...] = normed
    qkv_ref[...] = dot(normed, wq_ref[...]).astype(BF)
    cross_ref[...] = dot(normed, wx_ref[...]).astype(BF)


def patch_in(src, own, other, gains, wq, wx):
    half, width = own.shape
    tokens = 2 * half
    step = 4 * half // (half // 72)
    rows = lambda w: pl.BlockSpec((step, w), lambda i: (i, 0))
    return pl.pallas_call(
        patch_in_kernel,
        grid=(tokens // step,),
        in_specs=[
            pl.BlockSpec((step // 2, 1), lambda i: (i, 0)),
            whole(own.shape),
            whole(own.shape),
            whole(gains.shape),
            whole(wq.shape),
            whole(wx.shape),
        ],
        out_specs=[rows(width), rows(width), rows(wq.shape[1]), rows(wx.shape[1])],
        out_shape=[
            sds((tokens, width), BF),
            sds((tokens, width), BF),
            sds((tokens, wq.shape[1]), BF),
            sds((tokens, wx.shape[1]), BF),
        ],
        compiler_params=params(),
        cost_estimate=cost(2 * tokens * width * (wq.shape[1] + wx.shape[1]), 2e7),
        name="patch_in",
    )(src, own, other, gains, wq, wx)


def window_kernel(qkv_ref, out_ref, stat_ref):
    tokens, width = out_ref.shape
    lane = iota((1, LANES), 1)
    left = lane < 64
    stats = jnp.zeros((tokens, LANES), F32)
    for pair in range(HEADS // 2):
        at = pair * LANES
        q = qkv_ref[:, at : at + LANES] * SCALE
        k = qkv_ref[:, width + at : width + at + LANES]
        v = qkv_ref[:, 2 * width + at : 2 * width + at + LANES]
        mixed = []
        for side in range(2):
            mine = left if side == 0 else ~left
            scores = dot(jnp.where(mine, q, 0).astype(BF), k, 1, 1)
            peak = jnp.max(scores, axis=-1, keepdims=True)
            raised = jnp.exp(scores - peak)
            total = jnp.sum(raised, axis=-1, keepdims=True)
            probs = (raised * (1.0 / total)).astype(BF)
            mixed.append(dot(probs, v))
            stats = stats + place_lanes(peak + jnp.log(total), lane, 2 * pair + side)
        out_ref[:, at : at + LANES] = jnp.where(left, mixed[0], mixed[1]).astype(BF)
    stat_ref[...] = stats.astype(BF)


def window_forward(qkv, tokens):
    total, width3 = qkv.shape
    width = width3 // 3
    return pl.pallas_call(
        window_kernel,
        grid=(total // tokens,),
        in_specs=[pl.BlockSpec((tokens, width3), lambda i: (i, 0))],
        out_specs=[
            pl.BlockSpec((tokens, width), lambda i: (i, 0)),
            pl.BlockSpec((tokens, LANES), lambda i: (i, 0)),
        ],
        out_shape=[sds((total, width), BF), sds((total, LANES), BF)],
        compiler_params=params(),
        cost_estimate=cost(16 * total * tokens * width, 8e6, total * tokens * HEADS),
        name="window_forward",
    )(qkv)


def stat_lanes(stats, head, first, base):
    row, col = iota((LANES, LANES), 0), iota((LANES, LANES), 1)
    hit = (row == first + head + 16 * (col - base)) & (col >= base) & (col < base + 3)
    return dot(stats, jnp.where(hit, -1.0, 0.0).astype(BF))


def window_back_kernel(qkv_ref, go_ref, stat_ref, out_ref):
    tokens, width = go_ref.shape
    lane = iota((1, LANES), 1)
    left = lane < 64
    stats = stat_ref[...]
    for pair in range(HEADS // 2):
        at = pair * LANES
        q = qkv_ref[:, at : at + LANES]
        k = qkv_ref[:, width + at : width + at + LANES]
        v = qkv_ref[:, 2 * width + at : 2 * width + at + LANES]
        g = go_ref[:, at : at + LANES]
        parts = []
        for side in range(2):
            mine = left if side == 0 else ~left
            base = 64 * (1 - side)
            ones = (lane >= base) & (lane < base + 3)
            shifted = jnp.where(mine, q.astype(F32) * SCALE, stat_lanes(stats, 2 * pair + side, 0, base))
            keys = jnp.where(mine, k.astype(F32), jnp.where(ones, 1.0, 0.0)).astype(BF)
            probs = jnp.exp(dot(keys, shifted.astype(BF), 1, 1))
            grads = dot(jnp.where(mine, v.astype(F32), 0.0).astype(BF), g, 1, 1)
            inner = jnp.sum(probs * grads, axis=0, keepdims=True)
            dscore = (probs * (grads - inner)).astype(BF)
            parts.append((dot(dscore, k, 0, 0), dot(dscore, q), dot(probs.astype(BF), g)))
        for index, factor in ((0, SCALE), (1, SCALE), (2, 1.0)):
            joined = jnp.where(left, parts[0][index], parts[1][index]) * factor
            out_ref[:, index * width + at : index * width + at + LANES] = joined.astype(BF)


def window_backward(qkv, go, stats, tokens):
    total, width3 = qkv.shape
    width = width3 // 3
    rows = lambda w: pl.BlockSpec((tokens, w), lambda i: (i, 0))
    return pl.pallas_call(
        window_back_kernel,
        grid=(total // tokens,),
        in_specs=[rows(width3), rows(width), rows(LANES)],
        out_specs=rows(width3),
        out_shape=sds((total, width3), BF),
        compiler_params=params(),
        cost_estimate=cost(40 * total * tokens * width, 1.3e7, total * tokens * HEADS),
        name="window_backward",
    )(qkv, go, stats)


def split_halves(rows, part):
    count = rows.shape[0] // (2 * part)
    return [
        jnp.concatenate([rows[(2 * w + s) * part : (2 * w + s + 1) * part] for w in range(count)], axis=0)
        for s in range(2)
    ]


def patch_ffn_kernel(
    src_ref, inv_ref, att_ref, x_ref, own_ref, other_ref, gain_ref, wo_ref, up_ref, down_ref,
    out_own_ref, out_other_ref, after_grad_ref, att_grad_ref, wo_grad_ref, up_grad_ref, down_grad_ref, gain_grad_ref,
    after, normed, cot, total, back, acts, dacts,
    *, tiled,
):
    step = pl.program_id(0)
    tokens, width = att_ref.shape
    half = own_ref.shape[0]
    part = 72
    block = 4 * part

    @pl.when(step == 0)
    def _():
        for b in range(tokens // block):
            rows = slice(b * block, (b + 1) * block)
            value = x_ref[rows, :].astype(F32) + dot(att_ref[rows, :], wo_ref[...])
            after[rows, :] = value
            unit, _ = norm_stats(value)
            normed[rows, :] = (unit * gain_ref[1:2, :]).astype(BF)
            pieces = []
            for k in range(2):
                table = src_ref[(2 * b + k) * part : (2 * b + k + 1) * part, :]
                onehot = (iota((part, half), 1) == table).astype(F32).astype(BF)
                pieces.append(dot(onehot, own_ref[...]))
                pieces.append(dot(onehot, other_ref[...]))
            cot[rows, :] = jnp.concatenate(pieces, axis=0).astype(BF)
        total[...] = jnp.zeros_like(total)
        back[...] = jnp.zeros_like(back)

    for b in range(tokens // block):
        rows = slice(b * block, (b + 1) * block)
        value, slope = gelu_pair(dot(normed[rows, :], up_ref[...]))
        act = value.astype(BF)
        acts[rows, :] = act
        total[rows, :] += dot(act, down_ref[...])
        dact = (slope * dot(cot[rows, :], down_ref[...], 1, 1)).astype(BF)
        dacts[rows, :] = dact
        back[rows, :] += dot(dact, up_ref[...], 1, 1)
    up_grad = dot(normed[...], dacts[...], 0, 0).astype(BF)
    down_grad = dot(acts[...], cot[...], 0, 0).astype(BF)
    if tiled:
        store_columns(up_grad_ref, up_grad, 0)
        store_strip(down_grad_ref, down_grad, 1)
    else:
        up_grad_ref[...] = up_grad
        down_grad_ref[...] = down_grad

    @pl.when(step == pl.num_programs(0) - 1)
    def _():
        gain_sum = jnp.zeros((1, width), F32)
        for b in range(tokens // block):
            rows = slice(b * block, (b + 1) * block)
            unit, spread = norm_stats(after[rows, :])
            grad, gain_part = norm_back(unit, spread, gain_ref[1:2, :], back[rows, :])
            gain_sum = gain_sum + gain_part
            grad = cot[rows, :].astype(F32) + grad
            after_grad_ref[rows, :] = grad
            branch = grad.astype(BF)
            normed[rows, :] = branch
            att_grad_ref[rows, :] = dot(branch, wo_ref[...], 1, 1).astype(BF)
        gain_grad_ref[...] = jnp.broadcast_to(gain_sum, gain_grad_ref.shape)
        wo_grad = dot(att_ref[...], normed[...], 0, 0).astype(BF)
        if tiled:
            store_all(wo_grad_ref, wo_grad, 0)
        else:
            wo_grad_ref[...] = wo_grad
        halves = split_halves(after[...] + total[...], part)
        onehot = (iota((half, half), 1) == inv_ref[...]).astype(F32).astype(BF)
        out_own_ref[...] = dot(onehot, halves[0].astype(BF)).astype(BF)
        out_other_ref[...] = dot(onehot, halves[1].astype(BF)).astype(BF)


def grad_forms(width, hidden, chunk, tiled, wo_order, up_order, down_order):
    if not tiled:
        return (
            [whole((width, width)), pl.BlockSpec((width, chunk), lambda j: (0, j)), pl.BlockSpec((chunk, width), lambda j: (j, 0))],
            [sds((width, width), BF), sds((width, hidden), BF), sds((hidden, width), BF)],
        )
    shapes = [tile_shape(width, width), tile_shape(width, hidden), tile_shape(hidden, width)]
    per_half = hidden // 2 // chunk
    return (
        [whole(shapes[0]), columns_spec(width, chunk, per_half, up_order, lambda j: j), strip_spec(hidden, width, down_order)],
        [sds(shape, BF) for shape in shapes],
    )


def patch_ffn(src, inv, att, x, own, other, gains, wo, up, down, tiled, chunk=384):
    tokens, width = att.shape
    half = tokens // 2
    hidden = up.shape[1]
    grad_specs, grad_shapes = grad_forms(width, hidden, chunk, tiled, 0, 0, 1)
    return pl.pallas_call(
        functools.partial(patch_ffn_kernel, tiled=tiled),
        grid=(hidden // chunk,),
        in_specs=[whole(a.shape) for a in (src, inv, att, x, own, other, gains, wo)]
        + [pl.BlockSpec((width, chunk), lambda j: (0, j)), pl.BlockSpec((chunk, width), lambda j: (j, 0))],
        out_specs=[
            whole((half, width)),
            whole((half, width)),
            whole((tokens, width)),
            whole((tokens, width)),
            *grad_specs,
            whole((8, width)),
        ],
        out_shape=[
            sds((half, width), BF),
            sds((half, width), BF),
            sds((tokens, width), F32),
            sds((tokens, width), BF),
            *grad_shapes,
            sds((8, width), F32),
        ],
        scratch_shapes=[
            pltpu.VMEM((tokens, width), F32),
            pltpu.VMEM((tokens, width), BF),
            pltpu.VMEM((tokens, width), BF),
            pltpu.VMEM((tokens, width), F32),
            pltpu.VMEM((tokens, width), F32),
            pltpu.VMEM((tokens, chunk), BF),
            pltpu.VMEM((tokens, chunk), BF),
        ],
        compiler_params=params(),
        cost_estimate=cost(12 * tokens * width * hidden, 4e7, tokens * hidden),
        name="patch_ffn",
    )(src, inv, att, x, own, other, gains, wo, up, down)


def qkv_back_kernel(gp_ref, n_ref, w_ref, back_ref, w_grad_ref, *, tiled):
    @pl.when(pl.program_id(0) == 0)
    def _():
        back_ref[...] = jnp.zeros_like(back_ref)

    back_ref[...] += dot(gp_ref[...], w_ref[...], 1, 1)
    w_grad = dot(n_ref[...], gp_ref[...], 0, 0).astype(BF)
    if tiled:
        store_columns(w_grad_ref, w_grad, 0)
    else:
        w_grad_ref[...] = w_grad


def qkv_back(gp, normed, w, tiled, chunk=384):
    tokens, width = normed.shape
    cols = w.shape[1]
    natural = pl.BlockSpec((width, chunk), lambda j: (0, j))
    grad_spec = columns_spec(width, chunk, cols // 2 // chunk, 0, lambda j: j) if tiled else natural
    return pl.pallas_call(
        functools.partial(qkv_back_kernel, tiled=tiled),
        grid=(cols // chunk,),
        in_specs=[pl.BlockSpec((tokens, chunk), lambda j: (0, j)), whole(normed.shape), natural],
        out_specs=[whole((tokens, width)), grad_spec],
        out_shape=[sds((tokens, width), F32), sds(tile_shape(width, cols) if tiled else w.shape, BF)],
        compiler_params=params(),
        cost_estimate=cost(4 * tokens * width * cols, 2e7),
        name="qkv_back",
    )(gp, normed, w)


def cross_back_kernel(
    inv_ref, gk_ref, gv_ref, n_ref, x_ref, after_ref, part_ref, gain_ref, wx_ref, g2_ref, g4_ref,
    own_ref, other_ref, gain_grad_ref, *rest,
    tiled,
):
    step = pl.program_id(0)
    half, width = own_ref.shape
    tokens = 2 * half
    part = 72
    block = 4 * part
    back = rest[-1]

    @pl.when(step == 0)
    def _():
        back[...] = part_ref[...]

    def one(grad_ref):
        back[...] += dot(grad_ref[...], wx_ref[...], 1, 1)
        w_grad = dot(n_ref[...], grad_ref[...], 0, 0).astype(BF)
        if not tiled:
            rest[0][...] = w_grad
            return

        @pl.when(step % 2 == 0)
        def _():
            store_columns(rest[0], w_grad, 0)

        @pl.when(step % 2 == 1)
        def _():
            store_columns(rest[1], w_grad, 1)

    @pl.when(step < 2)
    def _():
        one(gk_ref)

    @pl.when(step >= 2)
    def _():
        one(gv_ref)

    @pl.when(step == pl.num_programs(0) - 1)
    def _():
        gain_sum = jnp.zeros((1, width), F32)
        for b in range(tokens // block):
            rows = slice(b * block, (b + 1) * block)
            unit, spread = norm_stats(x_ref[rows, :].astype(F32))
            grad, gain_part = norm_back(unit, spread, gain_ref[0:1, :], back[rows, :])
            gain_sum = gain_sum + gain_part
            back[rows, :] = after_ref[rows, :] + grad
        row = iota((8, width), 0)
        gain_grad_ref[...] = jnp.where(row == 0, gain_sum, jnp.where(row == 1, g2_ref[...], jnp.where(row == 3, g4_ref[...], 0.0)))
        halves = split_halves(back[...], part)
        onehot = (iota((half, half), 1) == inv_ref[...]).astype(F32).astype(BF)
        high = halves[0].astype(BF)
        low = (halves[0] - high.astype(F32)).astype(BF)
        own_ref[...] = dot(onehot, high) + dot(onehot, low)
        other_ref[...] = dot(onehot, halves[1].astype(BF)).astype(BF)


def cross_back(inv, gk, gv, normed, x, after, part, gains, wx, g2, g4, tiled):
    tokens, width = x.shape
    half = tokens // 2
    chunk = width // 2
    cols = wx.shape[1]
    if tiled:
        shape = tile_shape(width, cols // 2)
        grad_specs = [columns_spec(width, chunk, 1, order, lambda j: j // 2) for order in (0, 1)]
        grad_shapes = [sds(shape, BF)] * 2
    else:
        grad_specs = [pl.BlockSpec((width, chunk), lambda j: (0, j))]
        grad_shapes = [sds(wx.shape, BF)]
    return pl.pallas_call(
        functools.partial(cross_back_kernel, tiled=tiled),
        grid=(4,),
        in_specs=[
            whole(inv.shape),
            pl.BlockSpec((tokens, chunk), lambda j: (0, jnp.minimum(j, 1))),
            pl.BlockSpec((tokens, chunk), lambda j: (0, jnp.maximum(j - 2, 0))),
            *[whole(a.shape) for a in (normed, x, after, part, gains)],
            pl.BlockSpec((width, chunk), lambda j: (0, j)),
            whole(g2.shape),
            whole(g4.shape),
        ],
        out_specs=[whole((half, width)), whole((half, width)), whole((8, width)), *grad_specs],
        out_shape=[sds((half, width), F32), sds((half, width), BF), sds((8, width), F32), *grad_shapes],
        scratch_shapes=[pltpu.VMEM((tokens, width), F32)],
        compiler_params=params(),
        cost_estimate=cost(4 * tokens * width * cols, 2e7),
        name="cross_back",
    )(inv, gk, gv, normed, x, after, part, gains, wx, g2, g4)


def query_in_kernel(x_ref, gain_ref, w_ref, n_ref, q_ref, kv_ref):
    unit, _ = norm_stats(x_ref[...].astype(F32))
    normed = (unit * gain_ref[2:3, :]).astype(BF)
    n_ref[...] = normed
    width = x_ref.shape[1]
    q_ref[...] = dot(normed, w_ref[:, :width]).astype(BF)
    kv_ref[...] = dot(normed, w_ref[:, width:]).astype(BF)


def query_in_call(x, gains, w):
    slots, width = x.shape
    return pl.pallas_call(
        query_in_kernel,
        out_shape=[sds((slots, width), BF), sds((slots, width), BF), sds((slots, 2 * width), BF)],
        compiler_params=params(),
        cost_estimate=cost(2 * slots * width * w.shape[1], 5e6),
        name="query_in",
    )(x, gains, w)


def row_blocks(total, first, length, most=256):
    blocks = []
    for low, high in ((0, first), (first + length, total)):
        at = low
        while at < high:
            count = -(-(high - at) // most)
            size = min(high - at, -(-((high - at) // count) // 16) * 16)
            blocks.append((at, size, False))
            at += size
    blocks.append((first, length, True))
    return blocks


def query_forward_kernel(q_ref, k_ref, v_ref, sk_ref, sv_ref, kb_ref, qs_ref, ks_ref, out_ref, held, *, blocks):
    pair = pl.program_id(0)

    @pl.when(pair == 0)
    def _():
        held[...] = jnp.zeros_like(held)

    @pl.when(pair < HEADS // 2)
    def _():
        query_forward_pair(pair, q_ref, k_ref, v_ref, sk_ref, sv_ref, kb_ref, qs_ref, ks_ref, out_ref, held, blocks)

    @pl.when(pair == HEADS // 2)
    def _():
        out_ref[...] = held[...].astype(BF)


def query_forward_pair(pair, q_ref, k_ref, v_ref, sk_ref, sv_ref, kb_ref, qs_ref, ks_ref, out_ref, held, blocks):
    lane = iota((1, LANES), 1)
    left = lane < 64
    keys = []
    for side in range(2):
        keys.append(jnp.where(lane == 64 * (1 - side), kb_ref[...], k_ref[...]))
    for at, size, near in blocks:
        q = q_ref[at : at + size, :].astype(F32) * SCALE
        mixed, columns = [], jnp.zeros((size, LANES), F32)
        for side in range(2):
            mine = left if side == 0 else ~left
            own = jnp.where(mine, q, jnp.where(lane == 64 * (1 - side), 1.0, 0.0)).astype(BF)
            scores = dot(own, keys[side], 1, 1)
            peak = jnp.max(scores, axis=-1, keepdims=True)
            if near:
                extra = dot(jnp.where(mine, q, 0.0).astype(BF), sk_ref[...], 1, 1)
                extra = jnp.where(qs_ref[...] == ks_ref[...], extra, MASKED)
                peak = jnp.maximum(peak, jnp.max(extra, axis=-1, keepdims=True))
            raised = jnp.exp(scores - peak)
            total = jnp.sum(raised, axis=-1, keepdims=True)
            value = dot(raised.astype(BF), v_ref[...])
            if near:
                raised = jnp.exp(extra - peak)
                total = total + jnp.sum(raised, axis=-1, keepdims=True)
                value = value + dot(raised.astype(BF), sv_ref[...])
            mixed.append(value * (1.0 / total))
            columns = columns + place_lanes(peak + jnp.log(total), lane, 2 * pair + side)
        out_ref[at : at + size, :] = jnp.where(left, mixed[0], mixed[1]).astype(BF)
        held[at : at + size, :] += columns


def query_forward(q, cross, slot_kv, key_bias, q_seg, k_seg, blocks):
    total, width = q.shape
    patches, slots = cross.shape[0], slot_kv.shape[0]
    pairs = HEADS // 2
    col = lambda rows, first: pl.BlockSpec((rows, LANES), lambda p: (0, first + jnp.minimum(p, pairs - 1)))
    return pl.pallas_call(
        functools.partial(query_forward_kernel, blocks=blocks),
        grid=(pairs + 1,),
        in_specs=[
            col(total, 0), col(patches, 0), col(patches, pairs), col(slots, 0), col(slots, pairs),
            whole(key_bias.shape), whole(q_seg.shape), whole(k_seg.shape),
        ],
        out_specs=pl.BlockSpec((total, LANES), lambda p: (0, p)),
        out_shape=sds((total, width + LANES), BF),
        scratch_shapes=[pltpu.VMEM((total, LANES), F32)],
        compiler_params=params(),
        cost_estimate=cost(16 * total * patches * width, 1e7, total * patches * HEADS),
        name="query_forward",
    )(q, cross, cross, slot_kv, slot_kv, key_bias, q_seg, k_seg)


def query_back_kernel(
    q_ref, go_ref, stat_ref, k_ref, v_ref, sk_ref, sv_ref, kb_ref, qs_ref, ks_ref,
    dq_ref, dk_ref, dv_ref, dsk_ref, dsv_ref, sum_k, sum_v,
    *, blocks,
):
    pair = pl.program_id(0)
    lane = iota((1, LANES), 1)
    left = lane < 64
    sides = []
    for side in range(2):
        mine = left if side == 0 else ~left
        base = 64 * (1 - side)
        ones = jnp.where((lane >= base) & (lane < base + 3), 1.0, 0.0)
        bias = lane == base + 3
        sides.append(
            (
                jnp.where(mine, k_ref[...].astype(F32), jnp.where(bias, kb_ref[...].astype(F32), ones)).astype(BF),
                jnp.where(mine, v_ref[...].astype(F32), ones).astype(BF),
                jnp.where(mine, sk_ref[...].astype(F32), ones).astype(BF),
                jnp.where(mine, sv_ref[...].astype(F32), ones).astype(BF),
            )
        )
    for number, (at, size, near) in enumerate(blocks):
        q = q_ref[at : at + size, :]
        g = go_ref[at : at + size, :]
        stats = stat_ref[at : at + size, :]
        dq, dk, dv, dsk, dsv = [], [], [], [], []
        for side in range(2):
            mine = left if side == 0 else ~left
            base = 64 * (1 - side)
            head = 2 * pair + side
            plain = jnp.where(lane == base + 3, 1.0, 0.0)
            shifted = jnp.where(mine, q.astype(F32) * SCALE, stat_lanes(stats, head, 0, base) + plain).astype(BF)
            lowered = jnp.where(mine, g.astype(F32), stat_lanes(stats, head, 48, base)).astype(BF)
            keys, values, slot_keys, slot_values = sides[side]
            probs = jnp.exp(dot(keys, shifted, 1, 1))
            dscore = (probs * dot(values, lowered, 1, 1)).astype(BF)
            dk.append(dot(dscore, q))
            dv.append(dot(probs.astype(BF), g))
            moved = dot(dscore, k_ref[...], 0, 0)
            if near:
                scores = jnp.where(ks_ref[...] == qs_ref[...], dot(slot_keys, shifted, 1, 1), MASKED)
                probs = jnp.exp(scores)
                dscore = (probs * dot(slot_values, lowered, 1, 1)).astype(BF)
                dsk.append(dot(dscore, q))
                dsv.append(dot(probs.astype(BF), g))
                moved = moved + dot(dscore, sk_ref[...], 0, 0)
            dq.append(moved)
        dq_ref[at : at + size, :] = (jnp.where(left, dq[0], dq[1]) * SCALE).astype(BF)
        if number == 0:
            sum_k[...] = jnp.where(left, dk[0], dk[1])
            sum_v[...] = jnp.where(left, dv[0], dv[1])
        else:
            sum_k[...] += jnp.where(left, dk[0], dk[1])
            sum_v[...] += jnp.where(left, dv[0], dv[1])
        if near:
            dsk_ref[...] = (jnp.where(left, dsk[0], dsk[1]) * SCALE).astype(BF)
            dsv_ref[...] = jnp.where(left, dsv[0], dsv[1]).astype(BF)
    dk_ref[...] = (sum_k[...] * SCALE).astype(BF)
    dv_ref[...] = sum_v[...].astype(BF)


def query_backward(q, go, cross, slot_kv, key_bias, q_seg, k_seg, blocks):
    total, width = q.shape
    patches, slots = cross.shape[0], slot_kv.shape[0]
    pairs = HEADS // 2
    col = lambda rows, first: pl.BlockSpec((rows, LANES), lambda p: (0, first + p))
    return pl.pallas_call(
        functools.partial(query_back_kernel, blocks=blocks),
        grid=(pairs,),
        in_specs=[
            col(total, 0), col(total, 0), pl.BlockSpec((total, LANES), lambda p: (0, pairs)), col(patches, 0), col(patches, pairs),
            col(slots, 0), col(slots, pairs), whole(key_bias.shape), whole(q_seg.shape), whole(k_seg.shape),
        ],
        out_specs=[col(total, 0), col(patches, 0), col(patches, 0), col(slots, 0), col(slots, 0)],
        out_shape=[
            sds((total, width), BF),
            sds((patches, width), BF),
            sds((patches, width), BF),
            sds((slots, width), BF),
            sds((slots, width), BF),
        ],
        scratch_shapes=[pltpu.VMEM((patches, LANES), F32), pltpu.VMEM((patches, LANES), F32)],
        compiler_params=params(),
        cost_estimate=cost(40 * total * patches * width, 1.5e7, total * patches * HEADS),
        name="query_backward",
    )(q, go, go, cross, cross, slot_kv, slot_kv, key_bias, q_seg, k_seg)


def query_ffn_kernel(*refs, parts):
    outs = refs[:parts]
    x_ref, cot_ref, gain_ref, wo_ref, up_ref, down_ref = refs[parts : parts + 6]
    (
        out_ref, grad_ref, send_ref, att_ref, normed_ref, act_ref, dact_ref, branch_ref, gain_grad_ref,
        mixed, after, total, back, joint,
    ) = refs[parts + 6 :]
    step = pl.program_id(0)
    width = x_ref.shape[1]

    @pl.when(step == 0)
    def _():
        each = [join_lanes(o[:, width:].astype(F32), 0) for o in outs]
        peak = functools.reduce(jnp.maximum, each)
        weights = [jnp.exp(e - peak) for e in each]
        weight_sum = functools.reduce(jnp.add, weights)
        joint[...] = peak + jnp.log(weight_sum)
        value = None
        for o, w in zip(outs, weights):
            term = o[:, :width].astype(F32) * spread_heads(w / weight_sum, width)
            value = term if value is None else value + term
        mixed[...] = value
        att_ref[...] = value.astype(BF)
        rows = x_ref[...].astype(F32) + dot(att_ref[...], wo_ref[...])
        after[...] = rows
        unit, _ = norm_stats(rows)
        normed_ref[...] = (unit * gain_ref[3:4, :]).astype(BF)
        total[...] = jnp.zeros_like(total)
        back[...] = jnp.zeros_like(back)

    value, slope = gelu_pair(dot(normed_ref[...], up_ref[...]))
    act = value.astype(BF)
    act_ref[...] = act
    total[...] += dot(act, down_ref[...])
    dact = (slope * dot(cot_ref[...], down_ref[...], 1, 1)).astype(BF)
    dact_ref[...] = dact
    back[...] += dot(dact, up_ref[...], 1, 1)

    @pl.when(step == pl.num_programs(0) - 1)
    def _():
        out_ref[...] = (after[...] + total[...]).astype(BF)
        unit, spread = norm_stats(after[...])
        grad, gain_part = norm_back(unit, spread, gain_ref[3:4, :], back[...])
        gain_grad_ref[...] = jnp.broadcast_to(gain_part, gain_grad_ref.shape)
        grad = cot_ref[...].astype(F32) + grad
        grad_ref[...] = grad
        branch = grad.astype(BF)
        branch_ref[...] = branch
        sent = dot(branch, wo_ref[...], 1, 1).astype(BF)
        send_ref[:, :width] = sent
        pick = (iota((width, LANES), 0) // (width // HEADS) == iota((width, LANES), 1)).astype(F32).astype(BF)
        high, middle, low = three_parts(sent.astype(F32) * mixed[...])
        inner = dot(high.astype(BF), pick) + dot(middle.astype(BF), pick) + dot(low.astype(BF), pick)
        lane = iota((1, LANES), 1)
        packed = jnp.zeros(inner.shape, F32)
        for source, first in ((joint[...], 0), (inner, 48)):
            kept = jnp.where(lane < HEADS, source, 0.0)
            for number, piece in enumerate(three_parts(kept)):
                amount = first + 16 * number
                packed = packed + (piece if amount == 0 else pltpu.roll(piece, amount, 1))
        send_ref[:, width:] = packed.astype(BF)


def query_ffn(outs, x, cot, gains, wo, up, down, chunk=768):
    slots, width = x.shape
    hidden = up.shape[1]
    parts = len(outs)
    rows = lambda kind: sds((slots, width), kind)
    return pl.pallas_call(
        functools.partial(query_ffn_kernel, parts=parts),
        grid=(hidden // chunk,),
        in_specs=[whole(a.shape) for a in (*outs, x, cot, gains, wo)]
        + [pl.BlockSpec((width, chunk), lambda j: (0, j)), pl.BlockSpec((chunk, width), lambda j: (j, 0))],
        out_specs=[
            whole((slots, width)),
            whole((slots, width)),
            whole((slots, width + LANES)),
            whole((slots, width)),
            whole((slots, width)),
            pl.BlockSpec((slots, chunk), lambda j: (0, j)),
            pl.BlockSpec((slots, chunk), lambda j: (0, j)),
            whole((slots, width)),
            whole((8, width)),
        ],
        out_shape=[
            rows(BF), rows(F32), sds((slots, width + LANES), BF), rows(BF), rows(BF),
            sds((slots, hidden), BF), sds((slots, hidden), BF), rows(BF), sds((8, width), F32),
        ],
        scratch_shapes=[pltpu.VMEM((slots, width), F32)] * 4 + [pltpu.VMEM((slots, LANES), F32)],
        compiler_params=params(),
        cost_estimate=cost(8 * slots * width * hidden, 2e7, slots * hidden),
        name="query_ffn",
    )(*outs, x, cot, gains, wo, up, down)


def query_weights_kernel(normed_ref, cot_ref, att_ref, branch_ref, act_ref, dact_ref, wo_ref, up_ref, down_ref, *, tiled):
    up_grad = dot(normed_ref[...], dact_ref[...], 0, 0).astype(BF)
    down_grad = dot(act_ref[...], cot_ref[...], 0, 0).astype(BF)
    if tiled:
        store_columns(up_ref, up_grad, 0)
        store_strip(down_ref, down_grad, 1)
    else:
        up_ref[...] = up_grad
        down_ref[...] = down_grad

    @pl.when(pl.program_id(0) == 0)
    def _():
        wo_grad = dot(att_ref[...], branch_ref[...], 0, 0).astype(BF)
        if tiled:
            store_all(wo_ref, wo_grad, 1)
        else:
            wo_ref[...] = wo_grad


def query_weights(normed, cot, att, branch, act, dact, tiled, chunk=384):
    slots, width = normed.shape
    hidden = act.shape[1]
    grad_specs, grad_shapes = grad_forms(width, hidden, chunk, tiled, 1, 0, 1)
    return pl.pallas_call(
        functools.partial(query_weights_kernel, tiled=tiled),
        grid=(hidden // chunk,),
        in_specs=[whole((slots, width))] * 4 + [pl.BlockSpec((slots, chunk), lambda j: (0, j))] * 2,
        out_specs=grad_specs,
        out_shape=grad_shapes,
        compiler_params=params(),
        cost_estimate=cost(4 * slots * width * hidden, 1.6e7),
        name="query_weights",
    )(normed, cot, att, branch, act, dact)


def query_out_kernel(*refs, parts, tiled):
    dqs = refs[:parts]
    dk_ref, dv_ref, n_ref, x_ref, grad_ref, gain_ref, w_ref, rows_ref = refs[parts : parts + 8]
    out_ref, w_grad_ref, gain_grad_ref = refs[parts + 8 : parts + 11]
    width = x_ref.shape[1]
    value = dqs[0][...].astype(F32)
    for d in dqs[1:]:
        value = value + d[...].astype(F32)
    back = None
    for number, piece in enumerate((value.astype(BF), dk_ref[...], dv_ref[...])):
        cols = slice(number * width, (number + 1) * width)
        term = dot(piece, w_ref[:, cols], 1, 1)
        back = term if back is None else back + term
        (refs[-1] if tiled else w_grad_ref)[:, cols] = dot(n_ref[...], piece, 0, 0).astype(BF)
    if tiled:
        store_all(w_grad_ref, refs[-1][...], 1)
    unit, spread = norm_stats(x_ref[...].astype(F32))
    grad, gain_part = norm_back(unit, spread, gain_ref[2:3, :], back)
    out_ref[...] = grad_ref[...] + grad
    gain_rows = rows_ref[...] + jnp.where(iota((8, width), 0) == 2, gain_part, 0.0)
    if not tiled:
        gain_grad_ref[...] = gain_rows
        return
    turned = gain_rows.T
    size = width // 16
    lane = iota((1, LANES), 1)
    for half in range(2):
        tile = jnp.where(lane == 0, turned[:, 2 * half : 2 * half + 1], 0.0)
        tile = jnp.where(lane == 1, turned[:, 2 * half + 1 : 2 * half + 2], tile).astype(BF)
        for strip in range(8):
            for core in range(2):
                at = (2 * strip + core) * size
                gain_grad_ref[(core, *tile_index(strip, half, 0), slice(None), slice(None))] = tile[at : at + size]


def query_out(dqs, dk, dv, normed, x, grad, gains, w, gain_rows, tiled):
    slots, width = x.shape
    return pl.pallas_call(
        functools.partial(query_out_kernel, parts=len(dqs), tiled=tiled),
        out_shape=[
            sds((slots, width), F32),
            sds(tile_shape(width, w.shape[1]) if tiled else w.shape, BF),
            sds(tile_shape(width, 256), BF) if tiled else sds((8, width), F32),
        ],
        scratch_shapes=[pltpu.VMEM(w.shape, BF)] if tiled else [],
        compiler_params=params(),
        cost_estimate=cost(4 * slots * width * w.shape[1], 1e7),
        name="query_out",
    )(*dqs, dk, dv, normed, x, grad, gains, w, gain_rows)


PAIR = pl.DeviceIdType.MESH


def coordinates():
    page, strip = lax.axis_index("page"), lax.axis_index("strip")
    core, x = lax.rem(page, 2), page // 2
    y, z_low, z_high = lax.rem(strip, 2), lax.rem(strip // 2, 2), strip // 4
    flip = lambda index, bit, weight: index + weight - 2 * weight * bit
    core_mate = (flip(page, core, 1), strip)
    mates = {
        "x": (x, (flip(page, x, 2), strip)),
        "y": (y, (page, flip(strip, y, 1))),
        "low": (z_low, (page, flip(strip, z_low, 2))),
        "high": (z_high, (page, flip(strip, z_high, 4))),
    }
    return core, core_mate, [[mates[k] for k in ("y", "x", "low", "high")], [mates[k] for k in ("x", "y", "low", "high")]]


def meet(mates):
    barrier = pltpu.get_barrier_semaphore()
    for mate in mates:
        pl.semaphore_signal(barrier, inc=1, device_id=mate, device_id_type=PAIR)
    pl.semaphore_wait(barrier, len(mates))


def send(source, target, sems, number, mate):
    copy = pltpu.make_async_remote_copy(
        src_ref=source,
        dst_ref=target,
        send_sem=sems.at[0, number],
        recv_sem=sems.at[1, number],
        device_id=mate,
        device_id_type=PAIR,
    )
    copy.start()
    return copy


def add_into(target, first, source, start, length):
    def step(i, carry):
        target[first + i] = (target[first + i].astype(F32) + source[start + i].astype(F32)).astype(BF)
        return carry

    lax.fori_loop(0, length, step, 0)


def spans(arrays):
    at, found = 0, []
    for array in arrays:
        found.append((at, array.shape[2]))
        at += array.shape[2]
    return found


def core_sum_kernel(*refs, counts, sizes):
    total = sum(counts)
    grads = [refs[: counts[0]], refs[counts[0] : total]]
    outs = refs[total : total + 4]
    held, remote, near = refs[total + 4 : total + 6], refs[total + 6], refs[total + 7]
    core, core_mate, orders = coordinates()
    meet([core_mate])
    jobs, number = [], 0
    for order in range(2):
        bit = orders[order][0][0]
        for grad, (at, rows) in zip(grads[order], sizes[order]):
            target = held[order].at[:, pl.ds(at, rows), :]
            far = send(grad.at[1 - core], target, remote, number, core_mate)
            mine = []
            for which, out in enumerate((outs[2 * order], outs[2 * order + 1])):
                first = 8 * (bit if which else 1 - bit)
                copy = pltpu.make_async_copy(
                    grad.at[core, pl.ds(first, 8)], out.at[:, pl.ds(at, rows), :], near.at[2 * number + which]
                )
                copy.start()
                mine.append((copy, out, first))
            jobs.append((far, mine, order, at, rows))
            number += 1
    for far, mine, order, at, rows in jobs:
        far.wait()
        for copy, out, first in mine:
            copy.wait()

            def step(i, carry, out=out, first=first, order=order, at=at, rows=rows):
                span = pl.ds(at, rows)
                out[i, span, :] = (out[i, span, :].astype(F32) + held[order][first + i, span, :].astype(F32)).astype(BF)
                return carry

            lax.fori_loop(0, 8, step, 0)


def core_sum(grads, collective):
    grads = [[g.reshape(2, 16, *g.shape[-2:]) for g in group] for group in grads]
    sizes = [spans(group) for group in grads]
    rows = [sum(r for _, r in group) for group in sizes]
    counts = [len(group) for group in grads]
    total = sum(counts)
    return pl.pallas_call(
        functools.partial(core_sum_kernel, counts=counts, sizes=sizes),
        in_specs=[pl.BlockSpec(memory_space=pl.ANY)] * total,
        out_specs=[pl.BlockSpec(memory_space=pltpu.VMEM)] * 4,
        out_shape=[sds((8, rows[order], LANES), BF) for order in (0, 0, 1, 1)],
        scratch_shapes=[
            pltpu.VMEM((16, rows[0], LANES), BF),
            pltpu.VMEM((16, rows[1], LANES), BF),
            pltpu.SemaphoreType.DMA((2, total)),
            pltpu.SemaphoreType.DMA((2 * total,)),
        ],
        compiler_params=pltpu.CompilerParams(collective_id=collective, has_side_effects=True, vmem_limit_bytes=VMEM_BYTES),
        name="core_sum",
    )(*grads[0], *grads[1])


def halved_sum(pairs):
    page, strip = lax.axis_index("page"), lax.axis_index("strip")
    bits = {"x": page // 2, "y": strip % 2, "low": strip // 2 % 2, "high": strip // 4}
    weights = {"x": ("page", 2), "y": ("strip", 1), "low": ("strip", 2), "high": ("strip", 4)}
    results = []
    for (out, keep), order in zip(pairs, (("y", "x", "low", "high"), ("x", "y", "low", "high"))):
        for number, name in enumerate(order):
            axis, weight = weights[name]
            got = lax.ppermute(out, axis, [(i, i ^ weight) for i in range(lax.axis_size(axis))])
            if number == 3:
                results.append((keep + got)[0])
                break
            size = keep.shape[0] // 2
            bit = bits[order[number + 1]]
            cut = lambda array, which: lax.dynamic_slice_in_dim(array, which * size, size)
            out, keep = cut(keep, 1 - bit) + cut(got, 1 - bit), cut(keep, bit) + cut(got, bit)
    return results


def late_sum_kernel(*refs, counts, sizes, early_rows):
    total = sum(counts)
    grads = [refs[: counts[0]], refs[counts[0] : total]]
    early = refs[total : total + 2]
    own, got = refs[total + 2 : total + 4], refs[total + 4 : total + 6]
    sums, first_held = refs[total + 6 : total + 8], refs[total + 8 : total + 10]
    held = [refs[total + 10 : total + 14], refs[total + 14 : total + 18]]
    done, remote, near = refs[total + 18 : total + 20], refs[total + 20], refs[total + 21]
    core, core_mate, orders = coordinates()
    meet([core_mate] + [mate for _, mate in orders[0]])
    jobs, number = [], 0
    for order in range(2):
        for grad, (at, rows) in zip(grads[order], sizes[order]):
            span = pl.ds(at, rows)
            far = send(grad.at[1 - core], first_held[order].at[:, span, :], remote, number, core_mate)
            copy = pltpu.make_async_copy(grad.at[core], sums[order].at[:, span, :], near.at[number])
            copy.start()
            jobs.append((far, copy))
            number += 1
    loads = []
    for order in range(2):
        copy = pltpu.make_async_copy(early[order], own[order].at[pl.ds(0, early_rows), :], near.at[total + order])
        copy.start()
        loads.append(copy)
    for far, copy in jobs:
        far.wait()
        copy.wait()
    bases = [0, 0]
    flights = []
    for order in range(2):
        bit, mate = orders[order][0]
        out = 8 * (1 - bit)
        add_into(sums[order], out, first_held[order], out, 8)
        flights.append(send(sums[order].at[pl.ds(out, 8)], held[order][0], remote, number, mate))
        number += 1
    for order in range(2):
        bases[order] = 8 * orders[order][0][0]
        add_into(sums[order], bases[order], first_held[order], bases[order], 8)
    for stage in range(1, 5):
        size = 8 >> stage
        for order in range(2):
            flights[order].wait()
            base = bases[order]
            if stage == 4:
                value = sums[order][base].astype(F32) + held[order][3][0].astype(F32)
                own[order][early_rows:, :] = value.astype(BF)
                continue
            bit, mate = orders[order][stage]
            out, keep = size * (1 - bit), size * bit
            add_into(sums[order], base + out, held[order][stage - 1], out, size)
            flights[order] = send(sums[order].at[pl.ds(base + out, size)], held[order][stage], remote, number, mate)
            number += 1
            add_into(sums[order], base + keep, held[order][stage - 1], keep, size)
            bases[order] = base + keep
    for copy in loads:
        copy.wait()
    flights = []
    for order in range(2):
        flights.append(send(own[order], done[order], remote, number, core_mate))
        number += 1
    for order in range(2):
        flights[order].wait()
        got[order][...] = done[order][...]


def late_sum(grads, early, collective):
    grads = [[g.reshape(2, 16, *g.shape[-2:]) for g in group] for group in grads]
    sizes = [spans(group) for group in grads]
    rows = [sum(r for _, r in group) for group in sizes]
    counts = [len(group) for group in grads]
    total = sum(counts)
    early_rows = early[0].shape[0]
    share = [sds((early_rows + r, LANES), BF) for r in rows]
    vmem = lambda *shape: pltpu.VMEM(shape, BF)
    return pl.pallas_call(
        functools.partial(late_sum_kernel, counts=counts, sizes=sizes, early_rows=early_rows),
        in_specs=[pl.BlockSpec(memory_space=pl.ANY)] * (total + 2),
        out_specs=[pl.BlockSpec(memory_space=pltpu.VMEM)] * 4,
        out_shape=share + share,
        scratch_shapes=[
            *[vmem(16, r, LANES) for r in rows],
            *[vmem(16, r, LANES) for r in rows],
            *[vmem(8 >> k, rows[0], LANES) for k in range(4)],
            *[vmem(8 >> k, rows[1], LANES) for k in range(4)],
            *[vmem(early_rows + r, LANES) for r in rows],
            pltpu.SemaphoreType.DMA((2, total + 10)),
            pltpu.SemaphoreType.DMA((total + 2,)),
        ],
        compiler_params=pltpu.CompilerParams(collective_id=collective, has_side_effects=True, vmem_limit_bytes=VMEM_BYTES),
        name="late_sum",
    )(*grads[0], *grads[1], *early)


def finish_kernel(core_ref, own0, own1, got0, got1, gain_ref, *outs, plan):
    first = core_ref[0] == 0
    owns, gots = (own0, own1), (got0, got1)
    lane = iota((1, LANES), 1)
    left = lane < 64

    def tile(order, at, size, part):
        mine = owns[order][at : at + size, :].astype(F32)
        theirs = gots[order][at : at + size, :].astype(F32)
        return jnp.where(first == (part == 0), mine, theirs)

    for out, (size, tiles) in zip(outs, plan):
        count = len(tiles)
        for part in range(2):
            rows = slice(part * size, (part + 1) * size)
            values = [tile(order, at, size, part) for order, at in tiles]
            if count % 2 == 0:
                for t in range(count // 2):
                    out[rows, t * LANES : (t + 1) * LANES] = jnp.where(first, values[t], values[t + count // 2])
                continue
            turned = [pltpu.roll(v, 64, 1) for v in values[count // 2 :]]
            for t in range(count // 2):
                shifted = jnp.where(left, turned[t], turned[t + 1])
                out[rows, t * LANES : (t + 1) * LANES] = jnp.where(first, values[t], shifted)
            out[rows, count // 2 * LANES :] = jnp.where(first, values[count // 2], turned[-1])[:, :64]
    order, at, size = 0, own0.shape[0] - gain_ref.shape[0] // 2, gain_ref.shape[0] // 2
    for part in range(2):
        value = tile(order, at, size, part)
        gain_ref[part * size : (part + 1) * size, :] = jnp.where(first, value, pltpu.roll(value, LANES - 1, 1))[:, :1]


def finish(core, shares, shapes, plan, gain_rows):
    vmem = pl.BlockSpec(memory_space=pltpu.VMEM)
    return pl.pallas_call(
        functools.partial(finish_kernel, plan=plan),
        in_specs=[pl.BlockSpec(memory_space=pltpu.SMEM)] + [vmem] * 4,
        out_specs=[vmem] * (1 + len(shapes)),
        out_shape=[sds((gain_rows, 1), F32)] + [sds(shape, F32) for shape in shapes],
        compiler_params=params(),
        name="finish",
    )(core, *shares)


def from_ahead(array, count, distance):
    return lax.ppermute(array, "strip", [(i, (i - distance) % count) for i in range(count)])


def from_partner(array, count):
    return lax.ppermute(array, "strip", [(i, i ^ 1) for i in range(count)])


def scattered(grad):
    strips, pages = lax.axis_size("strip"), lax.axis_size("page")
    rows, cols = grad.shape
    part = lax.psum_scatter(grad, "strip", scatter_dimension=0, tiled=True)
    part = part.reshape(rows // strips, pages, cols // pages).transpose(1, 0, 2)
    return lax.psum_scatter(part, "page", scatter_dimension=0, tiled=False).astype(F32)


def local(
    visual_in, query_in, row_valid, segment_ids, slot_valid, col_shift, row_shifted, norm_gains,
    w_vqkv, w_vout, w_up, w_down, w_qqkv, w_xkv, w_qout, w_qup, w_qdown, visual_cot, query_cot,
):
    pages, strip_rows, columns, width = visual_in.shape
    own_slots, all_slots = query_in.shape[1], segment_ids.shape[1]
    count = lax.axis_size("strip")
    group = count // 2
    half = strip_rows * columns
    slots = 2 * own_slots
    window = WIN * WIN
    part = strip_rows * WIN
    place = lax.axis_index("strip")
    odd = place % 2 == 1
    up = jnp.where(odd, 1 - row_shifted[0], row_shifted[0])
    down = 1 - up
    pick = lambda array, which: lax.dynamic_index_in_dim(array, which, 0, keepdims=False)

    def put(own, other):
        first = jnp.where(up == 0, own, other)
        second = jnp.where(up == 0, other, own)
        return jnp.stack([first, second], axis=0)

    def pair_slots(array):
        mine, theirs = pick(array, up), from_partner(pick(array, down), count)
        return jnp.where(odd, jnp.concatenate([theirs, mine]), jnp.concatenate([mine, theirs]))

    gains = jnp.pad(norm_gains.T, ((0, 4), (0, 0)))
    shift = pick(col_shift, up)
    query_rows = pair_slots(query_in)
    patch_own = pick(visual_in, up).reshape(half, width)
    patch_other = from_ahead(pick(visual_in, down).reshape(half, width), count, 1)
    query_cots = pair_slots(query_cot)
    cot_own = pick(visual_cot, up).reshape(half, width)
    cot_other = from_ahead(pick(visual_cot, down).reshape(half, width), count, 1)
    rows_ok = jnp.concatenate([pick(row_valid, up), from_ahead(pick(row_valid, down), count, 1)])
    slots_ok = pair_slots(slot_valid)

    token = jnp.arange(half, dtype=jnp.int32)
    in_window = token % part
    src = (in_window // WIN) * columns + (token // part * WIN + in_window % WIN + shift) % columns
    turned = (token % columns - shift) % columns
    inv = (turned // WIN) * part + (token // columns) * WIN + turned % WIN
    src, inv = src[:, None], inv[:, None]
    key_bias = jnp.where(jnp.tile(jnp.repeat(rows_ok, WIN), 2 * half // window) == 1, 0.0, MASKED)
    key_bias = jnp.broadcast_to(key_bias.astype(BF)[:, None], (2 * half, LANES))

    order = [-1] + list(range(group - 1))
    near_first, near_length = slots - 32, slots + 64
    segments = pick(segment_ids, up)
    twice = jnp.concatenate([segments, segments, segments])
    base = (place // 2) * slots
    near_ids = lax.dynamic_slice_in_dim(twice, all_slots + base - 32, near_length)
    own_ids = lax.dynamic_slice_in_dim(segments, base, slots)
    own_ids = jnp.where(slots_ok == 1, own_ids, -1)
    blocks = row_blocks(all_slots, near_first, near_length)

    def gather(array):
        return jnp.concatenate(
            [array if k == 0 else from_ahead(array, count, 2 * k) for k in order], axis=0
        )

    def give_back(array):
        pieces = []
        for number, k in enumerate(order):
            piece = array[number * slots : (number + 1) * slots]
            pieces.append(piece if k == 0 else from_ahead(piece, count, -2 * k))
        return pieces

    tiled = count == 8
    after = lambda array, *others: lax.optimization_barrier((array, *others))[0]

    normed_three, q_own, slot_kv = query_in_call(query_rows, gains, w_qqkv)
    q_all = gather(q_own)
    x, normed_one, qkv, cross = patch_in(src, after(patch_own, q_own), patch_other, gains, w_vqkv, w_xkv)
    att, win_stats = window_forward(qkv, window)
    q_out = query_forward(after(q_all, att), cross, slot_kv, key_bias, near_ids[:, None], own_ids[None, :], blocks)
    out_parts = give_back(q_out)
    (vis_own, vis_other, grad_after, grad_att, g_vout, g_up, g_down, gain_two) = patch_ffn(
        src, inv, after(att, q_out), x, cot_own, cot_other, gains, w_vout, w_up, w_down, tiled
    )
    out_parts[0] = after(out_parts[0], grad_att)
    (q_res, grad_q, send_q, att_q, normed_four, act_q, dact_q, branch_q, gain_four) = query_ffn(
        out_parts, query_rows, query_cots, gains, w_qout, w_qup, w_qdown
    )
    go_all = gather(send_q)
    g_qout, g_qup, g_qdown = query_weights(normed_four, query_cots, att_q, branch_q, act_q, dact_q, tiled)
    if tiled:
        out_0, keep_0, out_1, keep_1 = core_sum([[g_up, g_qup, g_vout], [g_down, g_qdown, g_qout]], 0)
        early = halved_sum([(out_0, keep_0), (out_1, keep_1)])
        grad_att = after(grad_att, out_0)
    g_proj = window_backward(qkv, grad_att, win_stats, window)
    back_part, g_vqkv = qkv_back(g_proj, normed_one, w_vqkv, tiled)
    dq, dk, dv, dsk, dsv = query_backward(
        q_all, after(go_all, back_part), cross, slot_kv, key_bias, near_ids[None, :], own_ids[:, None], blocks
    )
    dq_parts = give_back(dq)
    vin_own, vin_other, gain_rows, *g_xkv = cross_back(
        inv, dk, dv, normed_one, x, grad_after, back_part, gains, w_xkv, gain_two, gain_four, tiled
    )
    dq_parts[0] = after(dq_parts[0], vin_own)
    qin_grad, g_qqkv, gain_grads = query_out(
        dq_parts, dsk, dsv, normed_three, query_rows, grad_q, gains, w_qqkv, gain_rows, tiled
    )

    shape = (pages, strip_rows, columns, width)
    visual_out = put(vis_own, from_ahead(vis_other, count, -1)).reshape(shape)
    visual_in_grad = put(vin_own, from_ahead(vin_other, count, -1).astype(F32)).reshape(shape)

    def return_slots(pair, kind):
        low, high = pair[:own_slots], pair[own_slots:]
        mine = jnp.where(odd, high, low)
        theirs = from_partner(jnp.where(odd, low, high).astype(BF), count)
        return put(mine.astype(kind), theirs.astype(kind))

    query_out_rows = return_slots(q_res, BF)
    query_in_grad = return_slots(qin_grad, F32)

    weights = (w_vqkv, w_vout, w_up, w_down, w_qqkv, w_xkv, w_qout, w_qup, w_qdown)
    if tiled:
        sets = [[g_up, g_qup, g_vout, g_vqkv, g_xkv[0], gain_grads], [g_down, g_qdown, g_qout, g_qqkv, g_xkv[1]]]
        shares = late_sum([sets[0][3:], sets[1][3:]], early, 1)
        starts = [[sum(g.shape[-2] for g in group[:k]) for k in range(len(group))] for group in sets]
        where = {w: (0, starts[0][k]) for k, w in enumerate((2, 7, 1, 0, 5))}
        where.update({w: (1, starts[1][k]) for k, w in enumerate((3, 8, 6, 4))})
        plan, shapes = [], []
        for number, weight in enumerate(weights):
            rows, cols = weight.shape
            size, tiles = rows // 16, cols // 256
            order, at = where[number]
            spots = [(order, at + t * size) for t in range(tiles)]
            if number == 5:
                spots = spots[:3] + [(1, starts[1][4] + t * size) for t in range(3)]
            plan.append((size, spots))
            shapes.append((rows // 8, cols // lax.axis_size("page")))
        core = (lax.axis_index("page") % 2).astype(jnp.int32).reshape(1)
        gain_part, *parts = finish(core, shares, shapes, plan, width // 8)
    else:
        grads = (g_vqkv, g_vout, g_up, g_down, g_qqkv, g_xkv[0], g_qout, g_qup, g_qdown)
        parts = [scattered(g) for g in grads]
        gain_part = lax.psum_scatter(gain_grads[:4], "page", scatter_dimension=0, tiled=True)
        gain_part = lax.psum_scatter(gain_part, "strip", scatter_dimension=1, tiled=True).reshape(-1, 1)
    return (visual_out, query_out_rows, visual_in_grad, query_in_grad, gain_part, *parts)


def solution(mesh):
    tokens, slots, table = P("page", "strip", None, None), P("page", "strip", None), P("page", "strip")
    tile = P("strip", "page")
    return jax.shard_map(
        local,
        mesh=mesh,
        in_specs=(tokens, slots, table, P("page", None), table, P("page"), P("page")) + (P(),) * 10 + (tokens, slots),
        out_specs=(tokens, slots, tokens, slots) + (tile,) * 10,
        check_vma=False,
    )
```

```python
import functools

import jax
import jax.numpy as jnp
from jax import lax
from jax.experimental import pallas as pl
from jax.experimental.pallas import tpu as pltpu
from jax.sharding import PartitionSpec as P

HEADS = 12
WIN = 12
EPS = 1e-05
MASKED = -1e9
SCALE = 0.125
BF = jnp.bfloat16
F32 = jnp.float32
LANES = 128
VMEM_BYTES = 60 * 1024 * 1024


def dot(left, right, left_dim=1, right_dim=0):
    return lax.dot_general(
        left, right, (((left_dim,), (right_dim,)), ((), ())), preferred_element_type=F32
    )


def iota(shape, dim):
    return lax.broadcasted_iota(jnp.int32, shape, dim)


def norm_stats(rows):
    offset = rows - jnp.mean(rows, axis=-1, keepdims=True)
    spread = lax.rsqrt(jnp.mean(offset * offset, axis=-1, keepdims=True) + EPS)
    return offset * spread, spread


def norm_back(unit, spread, gain, grad):
    product = grad * unit
    scaled = grad * gain
    centre = jnp.mean(scaled, axis=-1, keepdims=True)
    slope = jnp.mean(scaled * unit, axis=-1, keepdims=True)
    return spread * (scaled - centre - unit * slope), jnp.sum(product, axis=0, keepdims=True)


def gelu_pair(t):
    square = t * t
    plus = 0.5 * jnp.tanh(t * (0.7978845608 + 0.0356774081 * square)) + 0.5
    value = t * plus
    return value, plus + value * (1.0 - plus) * (1.5957691216 + 0.2140644488 * square)


def three_parts(value):
    high = value.astype(BF).astype(F32)
    rest = value - high
    middle = rest.astype(BF).astype(F32)
    low = (rest - middle).astype(BF).astype(F32)
    return high, middle, low


def place_lanes(column, lane, first):
    high, middle, low = three_parts(column)
    return (
        jnp.where(lane == first, high, 0.0)
        + jnp.where(lane == first + 16, middle, 0.0)
        + jnp.where(lane == first + 32, low, 0.0)
    )


def join_lanes(stats, first):
    total = stats
    rolled = []
    for part in range(3):
        amount = (first + 16 * part) % LANES
        rolled.append(total if amount == 0 else pltpu.roll(total, LANES - amount, 1))
    return rolled[0] + rolled[1] + rolled[2]


def spread_heads(values, width):
    head_dim = width // HEADS
    pick = (iota((LANES, width), 0) == iota((LANES, width), 1) // head_dim).astype(BF)
    high, middle, low = three_parts(values)
    return dot(high.astype(BF), pick) + dot(middle.astype(BF), pick) + dot(low.astype(BF), pick)


def whole(shape, single=False):
    mode = pl.Buffered(1) if single else None
    return pl.BlockSpec(shape, lambda *_: (0,) * len(shape), pipeline_mode=mode)


def sds(shape, kind):
    return jax.ShapeDtypeStruct(shape, kind)


ANY = pl.BlockSpec(memory_space=pl.ANY)


def call(kernel, name, ins, outs, grid=(1,), scratch=(), scalars=None, deps=(), work=(0, 0, 0), aliases={}):
    first = len(ins) + (scalars is not None)

    def body(*refs):
        kernel(*refs[:first], *refs[first + len(deps) :])

    return pl.pallas_call(
        body,
        grid_spec=pltpu.PrefetchScalarGridSpec(
            num_scalar_prefetch=int(scalars is not None),
            grid=grid,
            in_specs=[spec for _, spec in ins] + [ANY] * len(deps),
            out_specs=[spec for *_, spec in outs],
            scratch_shapes=list(scratch),
        ),
        out_shape=[sds(shape, kind) for shape, kind, _ in outs],
        input_output_aliases=aliases,
        compiler_params=pltpu.CompilerParams(vmem_limit_bytes=VMEM_BYTES),
        cost_estimate=pl.CostEstimate(flops=int(3 * work[0]), bytes_accessed=int(work[1]), transcendentals=int(work[2])),
        name=name,
    )(*([] if scalars is None else [scalars]), *[array for array, _ in ins], *deps)


UP, SHIFT, ODD, CORE, BIT_X, BIT_Y, BIT_LOW, BIT_HIGH, BASE = range(9)


def page_block(shape):
    return pl.BlockSpec((1, *shape[1:]), lambda *at: (at[-1][UP],) + (0,) * (len(shape) - 1))


def steps_below(value, size, count):
    total = jnp.zeros_like(value)
    for k in range(1, count):
        total = total + jnp.where(value >= size * k, 1, 0)
    return total


def into_windows(own, other, shift, strip_rows, columns):
    half, part = strip_rows * columns, strip_rows * WIN
    token = iota((half, 1), 0)
    window = steps_below(token, part, columns // WIN)
    inside = token - part * window
    row = steps_below(inside, WIN, strip_rows)
    column = inside - WIN * row + WIN * window + shift
    column = jnp.where(column >= columns, column - columns, column)
    onehot = (iota((half, half), 1) == row * columns + column).astype(F32).astype(BF)
    turned = [dot(onehot, own), dot(onehot, other)]
    pieces = [turned[side][w * part : (w + 1) * part] for w in range(columns // WIN) for side in range(2)]
    return jnp.concatenate(pieces, axis=0)


def out_of_windows(shift, strip_rows, columns):
    half = strip_rows * columns
    token = iota((half, 1), 0)
    row = steps_below(token, columns, strip_rows)
    column = token - columns * row - shift
    column = jnp.where(column < 0, column + columns, column)
    window = steps_below(column, WIN, columns // WIN)
    spot = window * (strip_rows * WIN) + row * WIN + column - WIN * window
    return (iota((half, half), 1) == spot).astype(F32).astype(BF)


def tile_index(strip, half, order):
    y = strip % 2
    lead = (y, half) if order == 0 else (half, y)
    return lead + ((strip // 2 % 2) * 2 + strip // 4,)


def tile_shape(rows, cols):
    return (2, 2, 2, 4, cols // 256 * (rows // 16), LANES)


def store_all(ref, value, order):
    rows, cols = value.shape
    size, tiles = rows // 16, cols // 256
    for strip in range(8):
        for core in range(2):
            at = (2 * strip + core) * size
            for half in range(2):
                lead = tile_index(strip, half, order)
                for t in range(tiles):
                    lanes = (half * tiles + t) * LANES
                    ref[(core, *lead, slice(t * size, (t + 1) * size), slice(None))] = value[at : at + size, lanes : lanes + LANES]


def store_columns(ref, value, order):
    size = value.shape[0] // 16
    for strip in range(8):
        for core in range(2):
            at = (2 * strip + core) * size
            lead = list(tile_index(strip, 0, order))
            for t in range(value.shape[1] // LANES):
                ref[(core, *lead, slice(t * size, (t + 1) * size), slice(None))] = value[at : at + size, t * LANES : (t + 1) * LANES]


def store_strips(ref, value, order):
    size, tiles = value.shape[0] // 4, value.shape[1] // 256
    for y in range(2):
        for core in range(2):
            for half in range(2):
                lead = (y, half) if order == 0 else (half, y)
                for t in range(tiles):
                    lanes = (half * tiles + t) * LANES
                    at = (2 * y + core) * size
                    ref[(core, *lead, 0, slice(t * size, (t + 1) * size), slice(None))] = value[at : at + size, lanes : lanes + LANES]


def columns_spec(rows, chunk, per_half, order, at):
    block = (2, 2, 1, 4) if order == 0 else (2, 1, 2, 4)
    lead = lambda half: (0, 0, half, 0) if order == 0 else (0, half, 0, 0)
    return pl.BlockSpec(
        (*block, chunk // LANES * (rows // 16), LANES), lambda j, *_: (*lead(at(j) // per_half), at(j) % per_half, 0)
    )


def strips_spec(rows, cols):
    return pl.BlockSpec(
        (2, 2, 2, 1, cols // 256 * (rows // 16), LANES), lambda j, *_: (0, 0, 0, (j % 2) * 2 + j // 2, 0, 0)
    )


def grad_forms(width, hidden, chunk, tiled, wo_order):
    if not tiled:
        return [
            ((width, width), BF, whole((width, width))),
            ((width, hidden), BF, pl.BlockSpec((width, chunk), lambda j, *_: (0, j))),
            ((hidden, width), BF, pl.BlockSpec((chunk, width), lambda j, *_: (j, 0))),
        ]
    shapes = [tile_shape(width, width), tile_shape(width, hidden), tile_shape(hidden, width)]
    specs = [
        whole(shapes[0]),
        columns_spec(width, chunk, hidden // 2 // chunk, 0, lambda j: j),
        strips_spec(hidden, width),
    ]
    return [(shape, BF, spec) for shape, spec in zip(shapes, specs)]


def put_grad(ref, value, store, order, tiled):
    if tiled:
        store(ref, value, order)
    else:
        ref[...] = value


def patch_in_kernel(s_ref, ok_ref, own_ref, other_ref, gain_ref, wq_ref, wx_ref, x_ref, n_ref, qkv_ref, cross_ref, bias_ref, turned, *, form):
    strip_rows, half = form[0], own_ref.shape[1]
    row = steps_below(iota((WIN * WIN, 1), 0), WIN, WIN)
    valid = jnp.zeros((WIN * WIN, 1), F32)
    for r in range(strip_rows):
        mine = jnp.where(ok_ref[s_ref[UP], r] == 1, 1.0, 0.0)
        theirs = other_ref[half : half + 1, r : r + 1].astype(F32)
        valid = valid + jnp.where(row == r, mine, 0.0) + jnp.where(row == strip_rows + r, theirs, 0.0)
    bias = jnp.broadcast_to(jnp.where(valid > 0.5, 0.0, MASKED).astype(BF), (WIN * WIN, LANES))
    for k in range(2):
        bias_ref[k * WIN * WIN : (k + 1) * WIN * WIN, :] = bias
    @pl.when(pl.program_id(0) == 0)
    def _():
        turned[...] = into_windows(own_ref[0], other_ref[:half, :], s_ref[SHIFT], *form).astype(BF)

    step = x_ref.shape[0]
    x = turned[pl.ds(pl.multiple_of(pl.program_id(0) * step, step), step), :].astype(F32)
    x_ref[...] = x.astype(BF)
    unit, _ = norm_stats(x)
    normed = (unit * gain_ref[0:1, :]).astype(BF)
    n_ref[...] = normed
    qkv_ref[...] = dot(normed, wq_ref[...]).astype(BF)
    cross_ref[...] = dot(normed, wx_ref[...]).astype(BF)


def patch_in(scalars, rows_ok, visual, other, gains, wq, wx, form, deps):
    _, half, width = visual.shape
    tokens = 2 * half
    step = 4 * form[0] * WIN
    rows = lambda w: ((tokens, w), BF, pl.BlockSpec((step, w), lambda i, *_: (i, 0)))
    return call(
        functools.partial(patch_in_kernel, form=form),
        "patch_in",
        [(rows_ok, pl.BlockSpec(memory_space=pltpu.SMEM)), (visual, page_block(visual.shape))]
        + [(a, whole(a.shape, True)) for a in (other, gains, wq, wx)],
        [rows(width), rows(width), rows(wq.shape[1]), rows(wx.shape[1]), rows(LANES)],
        grid=(tokens // step,),
        scratch=[pltpu.VMEM((tokens, width), BF)],
        scalars=scalars,
        deps=deps,
        work=(2 * tokens * width * (wq.shape[1] + wx.shape[1]), 2e7, 0),
    )


def pack_kernel(s_ref, ok_ref, rows_ref, out_ref):
    count, flags = rows_ref.shape[1], ok_ref.shape[1]
    out_ref[:count, :] = rows_ref[0]
    out_ref[count:, :] = jnp.zeros_like(out_ref[count:, :])
    theirs = jnp.where(s_ref[UP] == 0, ok_ref[1:2, :], ok_ref[0:1, :]).astype(F32).astype(BF)
    out_ref[count:, :flags] = jnp.broadcast_to(theirs, (out_ref.shape[0] - count, flags))


def other_page(shape):
    return pl.BlockSpec((1, *shape[1:]), lambda *at: (1 - at[-1][UP],) + (0,) * (len(shape) - 1))


def pack(scalars, rows, flags, deps):
    _, count, width = rows.shape
    shape = (count + 16, width)
    [out] = call(
        pack_kernel,
        "pack",
        [(flags, whole(flags.shape)), (rows, other_page(rows.shape))],
        [(shape, BF, whole(shape))],
        scalars=scalars,
        deps=deps,
    )
    return out


def pack_two_kernel(s_ref, a_ref, b_ref, a_out, b_out):
    a_out[...] = a_ref[0]
    b_out[...] = b_ref[0]


def pack_two(scalars, a, b, deps):
    return call(
        pack_two_kernel,
        "pack_two",
        [(x, other_page(x.shape)) for x in (a, b)],
        [(x.shape[1:], BF, whole(x.shape[1:])) for x in (a, b)],
        scalars=scalars,
        deps=deps,
    )


def put_two_kernel(s_ref, a_ref, b_ref, a_came, b_came, a_out, b_out):
    a_out[0] = a_came[...].astype(a_out.dtype)
    b_out[0] = b_came[...].astype(b_out.dtype)


def put_two(scalars, a, b, a_came, b_came, deps):
    return call(
        put_two_kernel,
        "put_two",
        [(a, ANY), (b, ANY)] + [(x, whole(x.shape)) for x in (a_came, b_came)],
        [(x.shape, x.dtype, other_page(x.shape)) for x in (a, b)],
        scalars=scalars,
        deps=deps,
        aliases={1: 0, 2: 1},
    )


def head_masks():
    lane = iota((1, LANES), 1)
    left = lane < 64
    return left, [left.astype(F32).astype(BF), (~left).astype(F32).astype(BF)]


def window_kernel(qkv_ref, out_ref):
    tokens, width = out_ref.shape
    left, masks = head_masks()
    for pair in range(HEADS // 2):
        at = pair * LANES
        q = qkv_ref[:, at : at + LANES] * SCALE
        k = qkv_ref[:, width + at : width + at + LANES]
        v = qkv_ref[:, 2 * width + at : 2 * width + at + LANES]
        all_scores = [dot(q * masks[side], k, 1, 1) for side in range(2)]
        mixed = []
        for scores in all_scores:
            raised = jnp.exp(scores - jnp.max(scores, axis=-1, keepdims=True))
            total = jnp.sum(raised, axis=-1, keepdims=True)
            mixed.append(dot(raised.astype(BF), v) * (1.0 / total))
        out_ref[:, at : at + LANES] = jnp.where(left, mixed[0], mixed[1]).astype(BF)


def window_forward(qkv, tokens, deps):
    total, width3 = qkv.shape
    width = width3 // 3
    rows = lambda w: pl.BlockSpec((tokens, w), lambda i: (i, 0))
    [att] = call(
        window_kernel,
        "window_forward",
        [(qkv, rows(width3))],
        [((total, width), BF, rows(width))],
        grid=(total // tokens,),
        deps=deps,
        work=(16 * total * tokens * width, 8e6, total * tokens * HEADS),
    )
    return att


def window_back_kernel(qkv_ref, go_ref, out_ref):
    tokens, width = go_ref.shape
    left, masks = head_masks()
    for pair in range(HEADS // 2):
        at = pair * LANES
        q = qkv_ref[:, at : at + LANES]
        k = qkv_ref[:, width + at : width + at + LANES]
        v = qkv_ref[:, 2 * width + at : 2 * width + at + LANES]
        g = go_ref[:, at : at + LANES]
        scaled = q * SCALE
        all_scores = [dot(k * masks[side], scaled, 1, 1) for side in range(2)]
        all_grads = [dot(v * masks[side], g, 1, 1) for side in range(2)]
        parts = []
        for scores, grads in zip(all_scores, all_grads):
            raised = jnp.exp(scores - jnp.max(scores, axis=0, keepdims=True))
            inverse = 1.0 / jnp.sum(raised, axis=0, keepdims=True)
            probs = raised * inverse
            inner = jnp.sum(probs * grads, axis=0, keepdims=True)
            dscore = (probs * (grads - inner)).astype(BF)
            parts.append((dot(dscore, k, 0, 0), dot(dscore, q), dot(probs.astype(BF), g)))
        for index, factor in ((0, SCALE), (1, SCALE), (2, 1.0)):
            joined = jnp.where(left, parts[0][index], parts[1][index]) * factor
            out_ref[:, index * width + at : index * width + at + LANES] = joined.astype(BF)


def window_backward(qkv, go, tokens, deps):
    total, width3 = qkv.shape
    width = width3 // 3
    rows = lambda w: pl.BlockSpec((tokens, w), lambda i: (i, 0))
    [out] = call(
        window_back_kernel,
        "window_backward",
        [(qkv, rows(width3)), (go, rows(width))],
        [((total, width3), BF, rows(width3))],
        grid=(total // tokens,),
        deps=deps,
        work=(40 * total * tokens * width, 1.3e7, total * tokens * HEADS),
    )
    return out


def split_halves(rows, part):
    count = rows.shape[0] // (2 * part)
    return [
        jnp.concatenate([rows[(2 * w + s) * part : (2 * w + s + 1) * part] for w in range(count)], axis=0)
        for s in range(2)
    ]


def patch_ffn_kernel(
    s_ref, att_ref, x_ref, own_ref, other_ref, gain_ref, wo_ref, up_ref, down_ref,
    out_own_ref, out_other_ref, after_grad_ref, att_grad_ref, wo_grad_ref, up_grad_ref, down_grad_ref, gain_grad_ref,
    after, normed, cot, total, acts, dacts,
    *, tiled, form,
):
    step = pl.program_id(0)
    tokens, width = att_ref.shape
    part = form[0] * WIN
    block = 4 * part
    back = after_grad_ref
    blocks = [slice(b * block, (b + 1) * block) for b in range(tokens // block)]

    @pl.when(step == 0)
    def _():
        cot[...] = into_windows(own_ref[0], other_ref[...], s_ref[SHIFT], *form).astype(BF)
        for rows in blocks:
            value = x_ref[rows, :].astype(F32) + dot(att_ref[rows, :], wo_ref[...])
            after[rows, :] = value
            unit, _ = norm_stats(value)
            normed[rows, :] = (unit * gain_ref[1:2, :]).astype(BF)

    def products(first):
        enter = lambda rows: (dot(normed[rows, :], up_ref[...]), dot(cot[rows, :], down_ref[...], 1, 1))
        ahead = enter(blocks[0])
        for b, rows in enumerate(blocks):
            pre, grads = ahead
            if b + 1 < len(blocks):
                ahead = enter(blocks[b + 1])
            value, slope = gelu_pair(pre)
            act = value.astype(BF)
            acts[rows, :] = act
            dact = (slope * grads).astype(BF)
            dacts[rows, :] = dact
            if first:
                total[rows, :] = dot(act, down_ref[...])
                back[rows, :] = dot(dact, up_ref[...], 1, 1)
            else:
                total[rows, :] += dot(act, down_ref[...])
                back[rows, :] += dot(dact, up_ref[...], 1, 1)

    @pl.when(step == 0)
    def _():
        products(True)

    @pl.when(step > 0)
    def _():
        products(False)

    put_grad(up_grad_ref, dot(normed[...], dacts[...], 0, 0).astype(BF), store_columns, 0, tiled)
    put_grad(down_grad_ref, dot(acts[...], cot[...], 0, 0).astype(BF), store_strips, 1, tiled)

    @pl.when(step == pl.num_programs(0) - 1)
    def _():
        gain_sum = jnp.zeros((1, width), F32)
        for rows in blocks:
            unit, spread = norm_stats(after[rows, :])
            grad, gain_part = norm_back(unit, spread, gain_ref[1:2, :], back[rows, :])
            gain_sum = gain_sum + gain_part
            grad = cot[rows, :].astype(F32) + grad
            after_grad_ref[rows, :] = grad
            branch = grad.astype(BF)
            normed[rows, :] = branch
            att_grad_ref[rows, :] = dot(branch, wo_ref[...], 1, 1).astype(BF)
        gain_grad_ref[...] = jnp.broadcast_to(gain_sum, gain_grad_ref.shape)
        put_grad(wo_grad_ref, dot(att_ref[...], normed[...], 0, 0).astype(BF), store_all, 0, tiled)
        halves = split_halves(after[...] + total[...], part)
        onehot = out_of_windows(s_ref[SHIFT], *form)
        out_own_ref[0] = dot(onehot, halves[0].astype(BF)).astype(BF)
        out_other_ref[...] = dot(onehot, halves[1].astype(BF)).astype(BF)


def patch_ffn(scalars, att, x, cot, cot_other, gains, wo, up, down, tiled, form, deps, chunk=768):
    tokens, width = att.shape
    half = tokens // 2
    hidden = up.shape[1]
    single = lambda a: (a, whole(a.shape, True))
    return call(
        functools.partial(patch_ffn_kernel, tiled=tiled, form=form),
        "patch_ffn",
        [
            single(att), single(x), (cot, page_block(cot.shape)), single(cot_other), single(gains), single(wo),
            (up, pl.BlockSpec((width, chunk), lambda j, *_: (0, j))),
            (down, pl.BlockSpec((chunk, width), lambda j, *_: (j, 0))),
        ],
        [
            (cot.shape, BF, page_block(cot.shape)),
            ((half, width), BF, whole((half, width))),
            ((tokens, width), F32, whole((tokens, width))),
            ((tokens, width), BF, whole((tokens, width))),
            *grad_forms(width, hidden, chunk, tiled, 0),
            ((8, width), F32, whole((8, width))),
        ],
        grid=(hidden // chunk,),
        scratch=[
            pltpu.VMEM((tokens, width), F32),
            pltpu.VMEM((tokens, width), BF),
            pltpu.VMEM((tokens, width), BF),
            pltpu.VMEM((tokens, width), F32),
            pltpu.VMEM((tokens, chunk), BF),
            pltpu.VMEM((tokens, chunk), BF),
        ],
        scalars=scalars,
        deps=deps,
        work=(12 * tokens * width * hidden, 4e7, tokens * hidden),
    )


def qkv_back_kernel(gp_ref, n_ref, w_ref, back_ref, w_grad_ref, *, tiled):
    first = dot(gp_ref[...], w_ref[...], 1, 1)

    @pl.when(pl.program_id(0) == 0)
    def _():
        back_ref[...] = first

    @pl.when(pl.program_id(0) > 0)
    def _():
        back_ref[...] += first

    put_grad(w_grad_ref, dot(n_ref[...], gp_ref[...], 0, 0).astype(BF), store_columns, 0, tiled)


def qkv_back(gp, normed, w, tiled, deps):
    tokens, width = normed.shape
    cols = w.shape[1]
    chunk = cols // 2
    natural = pl.BlockSpec((width, chunk), lambda j: (0, j))
    if tiled:
        form = (tile_shape(width, cols), BF, columns_spec(width, chunk, 1, 0, lambda j: j))
    else:
        form = (w.shape, BF, natural)
    return call(
        functools.partial(qkv_back_kernel, tiled=tiled),
        "qkv_back",
        [(gp, pl.BlockSpec((tokens, chunk), lambda j: (0, j))), (normed, whole(normed.shape, True)), (w, natural)],
        [((tokens, width), F32, whole((tokens, width))), form],
        grid=(2,),
        deps=deps,
        work=(4 * tokens * width * cols, 2e7, 0),
    )


def cross_back_kernel(
    s_ref, gk0_ref, gk1_ref, gv0_ref, gv1_ref, n_ref, x_ref, after_ref, part_ref, gain_ref, wx_ref, g2_ref, g4_ref,
    own_ref, other_ref, gain_grad_ref, *rest,
    tiled, form,
):
    step = pl.program_id(0)
    half, width = other_ref.shape
    tokens = 2 * half
    part = form[0] * WIN
    block = 4 * part
    back = rest[-1]

    def one(grad, base):
        back[...] = base[...] + dot(grad, wx_ref[...], 1, 1)
        w_grad = dot(n_ref[...], grad, 0, 0).astype(BF)
        if not tiled:
            rest[0][...] = w_grad
            return
        store_columns(rest[0], w_grad[:, : width // 2], 0)
        store_columns(rest[1], w_grad[:, width // 2 :], 1)

    @pl.when(step == 0)
    def _():
        one(jnp.concatenate([gk0_ref[...], gk1_ref[...]], axis=1), part_ref)

    @pl.when(step == 1)
    def _():
        one(jnp.concatenate([gv0_ref[...], gv1_ref[...]], axis=1), back)
        gain_sum = jnp.zeros((1, width), F32)
        for b in range(tokens // block):
            rows = slice(b * block, (b + 1) * block)
            unit, spread = norm_stats(x_ref[rows, :].astype(F32))
            grad, gain_part = norm_back(unit, spread, gain_ref[0:1, :], back[rows, :])
            gain_sum = gain_sum + gain_part
            back[rows, :] = after_ref[rows, :] + grad
        row = iota((8, width), 0)
        gain_grad_ref[...] = jnp.where(row == 0, gain_sum, jnp.where(row == 1, g2_ref[...], jnp.where(row == 3, g4_ref[...], 0.0)))
        halves = split_halves(back[...], part)
        onehot = out_of_windows(s_ref[SHIFT], *form)
        high = halves[0].astype(BF)
        low = (halves[0] - high.astype(F32)).astype(BF)
        own_ref[0] = dot(onehot, high) + dot(onehot, low)
        other_ref[...] = dot(onehot, halves[1].astype(BF)).astype(BF)


def cross_back(scalars, gks, gvs, normed, x, after, part, gains, wx, g2, g4, pages, tiled, form, deps):
    tokens, width = x.shape
    half = tokens // 2
    cols = wx.shape[1]
    if tiled:
        shape = tile_shape(width, cols // 2)
        grads = [(shape, BF, columns_spec(width, width // 2, 1, order, lambda j: j)) for order in (0, 1)]
    else:
        grads = [(wx.shape, BF, pl.BlockSpec((width, width), lambda j, *_: (0, j)))]
    single = lambda a: (a, whole(a.shape, True))
    own_shape = (pages, half, width)
    return call(
        functools.partial(cross_back_kernel, tiled=tiled, form=form),
        "cross_back",
        [single(a) for a in (*gks, *gvs, normed, x, after, part, gains)]
        + [(wx, pl.BlockSpec((width, width), lambda j, *_: (0, j))), single(g2), single(g4)],
        [
            (own_shape, F32, page_block(own_shape)),
            ((half, width), BF, whole((half, width))),
            ((8, width), F32, whole((8, width))),
            *grads,
        ],
        grid=(2,),
        scratch=[pltpu.VMEM((tokens, width), F32)],
        scalars=scalars,
        deps=deps,
        work=(4 * tokens * width * cols, 2e7, 0),
    )


def pair_rows(own, theirs, odd):
    return jnp.where(odd == 1, jnp.concatenate([theirs, own], axis=0), jnp.concatenate([own, theirs], axis=0))


def query_in_kernel(
    s_ref, seg_ref, ok_ref, own_ref, theirs_ref, gain_ref, w_ref, x_ref, n_ref, q_ref, kv_ref, same_ref, turned_ref
):
    own_slots = own_ref.shape[1]
    x = pair_rows(own_ref[0].astype(F32), theirs_ref[:own_slots, :].astype(F32), s_ref[ODD])
    slots, total = 2 * own_slots, seg_ref.shape[1]
    reach = slots + 64
    first = s_ref[UP] == 0
    segments = jnp.where(first, seg_ref[0:1, :], seg_ref[1:2, :]).astype(F32)
    amount = 32 - s_ref[BASE]
    near = pltpu.roll(jnp.broadcast_to(segments, (8, total)), jnp.where(amount < 0, amount + total, amount), 1)
    mine = jnp.where(first, ok_ref[0:1, :], ok_ref[1:2, :]).astype(F32)
    theirs = theirs_ref[own_slots : own_slots + 1, :own_slots].astype(F32)
    valid = jnp.where(s_ref[ODD] == 1, jnp.concatenate([theirs, mine], axis=1), jnp.concatenate([mine, theirs], axis=1))
    own = pltpu.roll(near, total - 32, 1)[0:1, :slots]
    own = jnp.where(valid > 0.5, own, -1.0)
    padded = -(-reach // LANES) * LANES
    column = near[:, :padded].T[:reach, 0:1]
    same = jnp.where(column == own, 1.0, 0.0)
    same_ref[...] = same.astype(BF)
    turned_ref[...] = same.T.astype(BF)
    x_ref[...] = x.astype(BF)
    unit, _ = norm_stats(x)
    normed = (unit * gain_ref[2:3, :]).astype(BF)
    n_ref[...] = normed
    width = x.shape[1]
    q_ref[...] = dot(normed, w_ref[:, :width]).astype(BF)
    kv_ref[...] = dot(normed, w_ref[:, width:]).astype(BF)


def query_in_call(scalars, segments, slots_ok, queries, theirs, gains, w):
    _, own_slots, width = queries.shape
    slots = 2 * own_slots
    reach = slots + 64
    rows = lambda w: ((slots, w), BF, whole((slots, w)))
    return call(
        query_in_kernel,
        "query_in",
        [(segments, whole(segments.shape)), (slots_ok, whole(slots_ok.shape)), (queries, page_block(queries.shape))]
        + [(a, whole(a.shape)) for a in (theirs, gains, w)],
        [rows(width), rows(width), rows(width), rows(2 * width)]
        + [(shape, BF, whole(shape)) for shape in ((reach, slots), (slots, reach))],
        scalars=scalars,
        work=(2 * slots * width * w.shape[1], 5e6, 0),
    )


def forward_blocks(pieces, slots, group):
    if pieces > 1:
        blocks = [([(0, 0, slots - 32)], False), ([(0, slots - 32, 32), (1, 0, slots), (2, 0, 32)], True)]
        blocks.append(([(2, 32, slots - 32)], False))
        return blocks + [([(k, 0, slots)], False) for k in range(3, pieces)]
    blocks = [([(0, slots - 32, slots + 64)], True)]
    if slots > 32:
        blocks.append(([(0, 0, slots - 32)], False))
    at, total = 2 * slots + 32, slots * group
    while at < total:
        size = min(256, total - at)
        blocks.append(([(0, at, size)], False))
        at += size
    return blocks


def take(refs, block):
    parts = [refs[p][at : at + size, :] for p, at, size in block]
    return parts[0] if len(parts) == 1 else jnp.concatenate([p.astype(F32) for p in parts], axis=0).astype(parts[0].dtype)


def give(refs, block, value):
    done = 0
    for p, at, size in block:
        refs[p][at : at + size, :] = value[done : done + size].astype(refs[p].dtype)
        done += size


def query_forward_kernel(*refs, pieces, blocks):
    qs = refs[:pieces]
    k_ref, v_ref, sk_ref, sv_ref, kb_ref, same_ref = refs[pieces : pieces + 6]
    outs, held = refs[pieces + 6 : 2 * pieces + 6], refs[2 * pieces + 6 :]
    pair = pl.program_id(0)
    left, masks = head_masks()
    lane = iota((1, LANES), 1)

    @pl.when(pair == 0)
    def _():
        for h in held:
            h[...] = jnp.zeros_like(h)

    @pl.when(pair < HEADS // 2)
    def _():
        keys = [jnp.where(lane == 64 * (1 - side), kb_ref[...], k_ref[...]) for side in range(2)]
        marks = [jnp.where(lane == 64 * (1 - side), 1.0, 0.0).astype(BF) for side in range(2)]
        for block, near in blocks:
            q = take(qs, block) * SCALE
            size = q.shape[0]
            all_scores = [dot(q * masks[side] + marks[side], keys[side], 1, 1) for side in range(2)]
            if near:
                same = same_ref[...].astype(F32) > 0.5
                extras = [jnp.where(same, dot(q * masks[side], sk_ref[...], 1, 1), MASKED) for side in range(2)]
            mixed, columns = [], jnp.zeros((size, LANES), F32)
            for side in range(2):
                scores = all_scores[side]
                peak = jnp.max(scores, axis=-1, keepdims=True)
                if near:
                    peak = jnp.maximum(peak, jnp.max(extras[side], axis=-1, keepdims=True))
                raised = jnp.exp(scores - peak)
                total = jnp.sum(raised, axis=-1, keepdims=True)
                value = dot(raised.astype(BF), v_ref[...])
                if near:
                    raised = jnp.exp(extras[side] - peak)
                    total = total + jnp.sum(raised, axis=-1, keepdims=True)
                    value = value + dot(raised.astype(BF), sv_ref[...])
                mixed.append(value * (1.0 / total))
                columns = columns + place_lanes(peak + jnp.log(total), lane, 2 * pair + side)
            give(outs, block, jnp.where(left, mixed[0], mixed[1]))
            done = 0
            for p, at, rows in block:
                held[p][at : at + rows, :] += columns[done : done + rows]
                done += rows

    @pl.when(pair == HEADS // 2)
    def _():
        for out, h in zip(outs, held):
            out[...] = h[...].astype(BF)


def query_forward(qs, cross, slot_kv, key_bias, same, blocks, deps):
    width = qs[0].shape[1]
    patches, slots = cross.shape[0], slot_kv.shape[0]
    pairs = HEADS // 2
    total = sum(q.shape[0] for q in qs)
    col = lambda rows, first: pl.BlockSpec((rows, LANES), lambda p: (0, first + jnp.minimum(p, pairs - 1)))
    return call(
        functools.partial(query_forward_kernel, pieces=len(qs), blocks=blocks),
        "query_forward",
        [(q, col(q.shape[0], 0)) for q in qs]
        + [(cross, col(patches, 0)), (cross, col(patches, pairs)), (slot_kv, col(slots, 0)), (slot_kv, col(slots, pairs))]
        + [(a, whole(a.shape)) for a in (key_bias, same)],
        [((q.shape[0], width + LANES), BF, pl.BlockSpec((q.shape[0], LANES), lambda p: (0, p))) for q in qs],
        grid=(pairs + 1,),
        scratch=[pltpu.VMEM((q.shape[0], LANES), F32) for q in qs],
        deps=deps,
        work=(16 * total * patches * width, 1e7, total * patches * HEADS),
    )


def stat_lanes(stats, head, first, base):
    row, col = iota((LANES, LANES), 0), iota((LANES, LANES), 1)
    hit = (row == first + head + 16 * (col - base)) & (col >= base) & (col < base + 3)
    return dot(stats, jnp.where(hit, -1.0, 0.0).astype(BF)).astype(BF)


def query_back_kernel(*refs, pieces, blocks, near_block, first_pair):
    qs, gos, stats = refs[:pieces], refs[pieces : 2 * pieces], refs[2 * pieces : 3 * pieces]
    k_ref, v_ref, sk_ref, sv_ref, kb_ref, same_ref = refs[3 * pieces : 3 * pieces + 6]
    dqs = refs[3 * pieces + 6 : 4 * pieces + 6]
    dk_ref, dv_ref, dsk_ref, dsv_ref, sum_k, sum_v = refs[4 * pieces + 6 : 4 * pieces + 12]
    near_dqs = refs[4 * pieces + 12 :]
    pair = pl.program_id(0) + first_pair
    left, masks = head_masks()
    lane = iota((1, LANES), 1)
    bases = (64, 0)
    ones = [jnp.where((lane >= b) & (lane < b + 3), 1.0, 0.0).astype(BF) for b in bases]
    plain = [jnp.where(lane == b + 3, 1.0, 0.0).astype(BF) for b in bases]
    keys = [jnp.where(lane == bases[s] + 3, kb_ref[...], k_ref[...] * masks[s] + ones[s]) for s in range(2)]
    values = [v_ref[...] * masks[s] + ones[s] for s in range(2)]

    def sides(block):
        q, g, st = take(qs, block), take(gos, block), take(stats, block)
        scaled = q * SCALE
        shifted = [scaled * masks[s] + (stat_lanes(st, 2 * pair + s, 0, bases[s]) + plain[s]) for s in range(2)]
        lowered = [g * masks[s] + stat_lanes(st, 2 * pair + s, 48, bases[s]) for s in range(2)]
        return q, g, shifted, lowered

    for ref in near_dqs:
        ref[...] = jnp.zeros_like(ref)
    q, g, shifted, lowered = sides(near_block)
    same = same_ref[...].astype(F32) > 0.5
    moved, dsk, dsv = [], [], []
    for s in range(2):
        scores = dot(sk_ref[...] * masks[s] + ones[s], shifted[s], 1, 1)
        probs = jnp.exp(jnp.where(same, scores, MASKED))
        dscore = (probs * dot(sv_ref[...] * masks[s] + ones[s], lowered[s], 1, 1)).astype(BF)
        dsk.append(dot(dscore, q))
        dsv.append(dot(probs.astype(BF), g))
        moved.append(dot(dscore, sk_ref[...], 0, 0))
    give(near_dqs, near_block, jnp.where(left, moved[0], moved[1]))
    dsk_ref[...] = (jnp.where(left, dsk[0], dsk[1]) * SCALE).astype(BF)
    dsv_ref[...] = jnp.where(left, dsv[0], dsv[1]).astype(BF)

    for number, block in enumerate(blocks):
        q, g, shifted, lowered = sides(block)
        scores = [dot(keys[s], shifted[s], 1, 1) for s in range(2)]
        grads = [dot(values[s], lowered[s], 1, 1) for s in range(2)]
        dq, dk, dv = [], [], []
        for s in range(2):
            probs = jnp.exp(scores[s])
            dscore = (probs * grads[s]).astype(BF)
            dv.append(dot(probs.astype(BF), g))
            dk.append(dot(dscore, q))
            dq.append(dot(dscore, k_ref[...], 0, 0))
        near = take(near_dqs, block)
        give(dqs, block, (jnp.where(left, dq[0], dq[1]) + near) * SCALE)
        if number == 0:
            sum_k[...] = jnp.where(left, dk[0], dk[1])
            sum_v[...] = jnp.where(left, dv[0], dv[1])
        else:
            sum_k[...] += jnp.where(left, dk[0], dk[1])
            sum_v[...] += jnp.where(left, dv[0], dv[1])
    dk_ref[...] = (sum_k[...] * SCALE).astype(BF)
    dv_ref[...] = sum_v[...].astype(BF)


def query_backward(qs, gos, cross, slot_kv, key_bias, same, near_block, part, deps):
    patches, slots = cross.shape[0], slot_kv.shape[0]
    pairs = HEADS // 2
    count = pairs // 2
    width = count * LANES
    total = sum(q.shape[0] for q in qs)
    blocks = []
    for number, q in enumerate(qs):
        step = min(256, q.shape[0])
        blocks += [[(number, at, step)] for at in range(0, q.shape[0], step)]
    col = lambda rows, first: pl.BlockSpec((rows, LANES), lambda p: (0, first + part * count + p))
    out = lambda rows: ((rows, width), BF, pl.BlockSpec((rows, LANES), lambda p: (0, p)))
    found = call(
        functools.partial(
            query_back_kernel, pieces=len(qs), blocks=blocks, near_block=near_block, first_pair=part * count
        ),
        "query_backward",
        [(q, col(q.shape[0], 0)) for q in qs]
        + [(g, col(g.shape[0], 0)) for g in gos]
        + [(g, pl.BlockSpec((g.shape[0], LANES), lambda p: (0, pairs))) for g in gos]
        + [(cross, col(patches, 0)), (cross, col(patches, pairs)), (slot_kv, col(slots, 0)), (slot_kv, col(slots, pairs))]
        + [(a, whole(a.shape)) for a in (key_bias, same)],
        [out(q.shape[0]) for q in qs] + [out(patches), out(patches), out(slots), out(slots)],
        grid=(count,),
        scratch=[pltpu.VMEM((patches, LANES), F32)] * 2 + [pltpu.VMEM((q.shape[0], LANES), F32) for q in qs],
        deps=deps,
        work=(20 * total * patches * width, 1.5e7, total * patches * HEADS // 2),
    )
    return found[: len(qs)], *found[len(qs) :]


def query_ffn_kernel(s_ref, *refs, parts, tiled):
    outs = refs[:parts]
    x_ref, own_ref, theirs_ref, gain_ref, wo_ref, up_ref, down_ref = refs[parts : parts + 7]
    (
        out_own_ref, out_other_ref, grad_ref, send_ref, att_ref, normed_ref, act_ref, dact_ref, branch_ref, cot_ref,
        gain_grad_ref, mixed, after, total, back, joint,
    ) = refs[parts + 7 :]
    step = pl.program_id(0)
    width = x_ref.shape[1]

    @pl.when(step == 0)
    def _():
        each = [join_lanes(o[:, width:].astype(F32), 0) for o in outs]
        peak = functools.reduce(jnp.maximum, each)
        weights = [jnp.exp(e - peak) for e in each]
        weight_sum = functools.reduce(jnp.add, weights)
        joint[...] = peak + jnp.log(weight_sum)
        value = None
        for o, w in zip(outs, weights):
            term = o[:, :width].astype(F32) * spread_heads(w / weight_sum, width)
            value = term if value is None else value + term
        mixed[...] = value
        att_ref[...] = value.astype(BF)
        rows = x_ref[...].astype(F32) + dot(att_ref[...], wo_ref[...])
        after[...] = rows
        unit, _ = norm_stats(rows)
        normed_ref[...] = (unit * gain_ref[3:4, :]).astype(BF)
        cot_ref[...] = pair_rows(own_ref[0].astype(F32), theirs_ref[...].astype(F32), s_ref[ODD]).astype(BF)
        total[...] = jnp.zeros_like(total)
        back[...] = jnp.zeros_like(back)

    grads = dot(cot_ref[...], down_ref[...], 1, 1)
    value, slope = gelu_pair(dot(normed_ref[...], up_ref[...]))
    dact = (slope * grads).astype(BF)
    dact_ref[...] = dact
    back[...] += dot(dact, up_ref[...], 1, 1)
    act = value.astype(BF)
    act_ref[...] = act
    total[...] += dot(act, down_ref[...])

    @pl.when(step == pl.num_programs(0) - 1)
    def _():
        rows = after[...] + total[...]
        own_slots = rows.shape[0] // 2
        low, high = rows[:own_slots], rows[own_slots:]
        odd = s_ref[ODD] == 1
        out_own_ref[0] = jnp.where(odd, high, low).astype(BF)
        out_other_ref[...] = jnp.where(odd, low, high).astype(BF)
        unit, spread = norm_stats(after[...])
        grad, gain_part = norm_back(unit, spread, gain_ref[3:4, :], back[...])
        gain_grad_ref[...] = jnp.broadcast_to(gain_part, gain_grad_ref.shape)
        grad = cot_ref[...].astype(F32) + grad
        grad_ref[...] = grad
        branch = grad.astype(BF)
        branch_ref[...] = branch
        sent = dot(branch, wo_ref[...], 1, 1).astype(BF)
        send_ref[:, :width] = sent
        pick = (iota((width, LANES), 0) // (width // HEADS) == iota((width, LANES), 1)).astype(F32).astype(BF)
        high, middle, low = three_parts(sent.astype(F32) * mixed[...])
        inner = dot(high.astype(BF), pick) + dot(middle.astype(BF), pick) + dot(low.astype(BF), pick)
        lane = iota((1, LANES), 1)
        packed = jnp.zeros(inner.shape, F32)
        for source, first in ((joint[...], 0), (inner, 48)):
            kept = jnp.where(lane < HEADS, source, 0.0)
            for number, piece in enumerate(three_parts(kept)):
                amount = first + 16 * number
                packed = packed + (piece if amount == 0 else pltpu.roll(piece, amount, 1))
        send_ref[:, width:] = packed.astype(BF)


def query_ffn(scalars, outs, x, cot, cot_theirs, gains, wo, up, down, tiled, deps, chunk=768):
    slots, width = x.shape
    hidden = up.shape[1]
    rows = lambda w, kind: ((slots, w), kind, whole((slots, w)))
    chunks = ((slots, hidden), BF, pl.BlockSpec((slots, chunk), lambda j, *_: (0, j)))
    half = (slots // 2, width)
    return call(
        functools.partial(query_ffn_kernel, parts=len(outs), tiled=tiled),
        "query_ffn",
        [(a, whole(a.shape)) for a in (*outs, x)]
        + [(cot, page_block(cot.shape))]
        + [(a, whole(a.shape)) for a in (cot_theirs, gains, wo)]
        + [
            (up, pl.BlockSpec((width, chunk), lambda j, *_: (0, j))),
            (down, pl.BlockSpec((chunk, width), lambda j, *_: (j, 0))),
        ],
        [
            (cot.shape, BF, page_block(cot.shape)), (half, BF, whole(half)), rows(width, F32), rows(width + LANES, BF),
            rows(width, BF), rows(width, BF), chunks, chunks, rows(width, BF), rows(width, BF), ((8, width), F32, whole((8, width))),
        ],
        grid=(hidden // chunk,),
        scratch=[pltpu.VMEM((slots, width), F32)] * 4 + [pltpu.VMEM((slots, LANES), F32)],
        scalars=scalars,
        deps=deps,
        work=(8 * slots * width * hidden, 2e7, slots * hidden),
    )


def query_weights_kernel(normed_ref, cot_ref, att_ref, branch_ref, act_ref, dact_ref, wo_ref, up_ref, down_ref, *, tiled):
    put_grad(up_ref, dot(normed_ref[...], dact_ref[...], 0, 0).astype(BF), store_columns, 0, tiled)
    put_grad(down_ref, dot(act_ref[...], cot_ref[...], 0, 0).astype(BF), store_strips, 1, tiled)

    @pl.when(pl.program_id(0) == 0)
    def _():
        put_grad(wo_ref, dot(att_ref[...], branch_ref[...], 0, 0).astype(BF), store_all, 1, tiled)


def query_weights(normed, cot, att, branch, act, dact, tiled, deps, chunk=768):
    slots, width = normed.shape
    hidden = act.shape[1]
    return call(
        functools.partial(query_weights_kernel, tiled=tiled),
        "query_weights",
        [(a, whole((slots, width))) for a in (normed, cot, att, branch)]
        + [(a, pl.BlockSpec((slots, chunk), lambda j: (0, j))) for a in (act, dact)],
        grad_forms(width, hidden, chunk, tiled, 1),
        grid=(hidden // chunk,),
        deps=deps,
        work=(4 * slots * width * hidden, 1.6e7, 0),
    )


def query_out_kernel(s_ref, *refs, parts, tiled):
    halves = [refs[:parts], refs[parts : 2 * parts]]
    others = refs[2 * parts : 2 * parts + 4]
    n_ref, x_ref, grad_ref, gain_ref, w_ref, rows_ref = refs[2 * parts + 4 : 2 * parts + 10]
    own_ref, other_ref, w_grad_ref, gain_grad_ref = refs[2 * parts + 10 : 2 * parts + 14]
    width = x_ref.shape[1]
    sums = []
    for dqs in halves:
        value = dqs[0][...].astype(F32)
        for d in dqs[1:]:
            value = value + d[...].astype(F32)
        sums.append(value.astype(BF))
    join = lambda a, b: jnp.concatenate([a, b], axis=1)
    pieces = [join(*sums), join(others[0][...], others[1][...]), join(others[2][...], others[3][...])]
    back = None
    for number, piece in enumerate(pieces):
        cols = slice(number * width, (number + 1) * width)
        term = dot(piece, w_ref[:, cols], 1, 1)
        back = term if back is None else back + term
        (refs[-1] if tiled else w_grad_ref)[:, cols] = dot(n_ref[...], piece, 0, 0).astype(BF)
    if tiled:
        store_all(w_grad_ref, refs[-1][...], 1)
    unit, spread = norm_stats(x_ref[...].astype(F32))
    grad, gain_part = norm_back(unit, spread, gain_ref[2:3, :], back)
    rows = grad_ref[...] + grad
    own_slots = rows.shape[0] // 2
    low, high = rows[:own_slots], rows[own_slots:]
    odd = s_ref[ODD] == 1
    own_ref[0] = jnp.where(odd, high, low)
    other_ref[...] = jnp.where(odd, low, high).astype(BF)
    gain_rows = rows_ref[...] + jnp.where(iota((8, width), 0) == 2, gain_part, 0.0)
    if not tiled:
        gain_grad_ref[...] = gain_rows
        return
    turned = gain_rows.T
    size = width // 16
    lane = iota((1, LANES), 1)
    for half in range(2):
        tile = jnp.where(lane == 0, turned[:, 2 * half : 2 * half + 1], 0.0)
        tile = jnp.where(lane == 1, turned[:, 2 * half + 1 : 2 * half + 2], tile).astype(BF)
        for strip in range(8):
            for core in range(2):
                at = (2 * strip + core) * size
                gain_grad_ref[(core, *tile_index(strip, half, 0), slice(None), slice(None))] = tile[at : at + size]


def query_out(scalars, dqs, dks, dvs, normed, x, grad, gains, w, gain_rows, pages, tiled, deps):
    slots, width = x.shape
    own_shape = (pages, slots // 2, width)
    w_shape = tile_shape(width, w.shape[1]) if tiled else w.shape
    g_shape, g_kind = (tile_shape(width, 256), BF) if tiled else ((8, width), F32)
    ins = (*dqs[0], *dqs[1], *dks, *dvs, normed, x, grad, gains, w, gain_rows)
    return call(
        functools.partial(query_out_kernel, parts=len(dqs[0]), tiled=tiled),
        "query_out",
        [(a, whole(a.shape, True)) for a in ins],
        [
            (own_shape, F32, page_block(own_shape)),
            ((slots // 2, width), BF, whole((slots // 2, width))),
            (w_shape, BF, whole(w_shape)),
            (g_shape, g_kind, whole(g_shape)),
        ],
        scratch=[pltpu.VMEM(w.shape, BF)] if tiled else [],
        scalars=scalars,
        deps=deps,
        work=(4 * slots * width * w.shape[1], 1e7, 0),
    )


PAIR = pl.DeviceIdType.MESH


def coordinates():
    page, strip = lax.axis_index("page"), lax.axis_index("strip")
    core, x = lax.rem(page, 2), page // 2
    y, z_low, z_high = lax.rem(strip, 2), lax.rem(strip // 2, 2), strip // 4
    flip = lambda index, bit, weight: index + weight - 2 * weight * bit
    core_mate = (flip(page, core, 1), strip)
    mates = {
        "x": (x, (flip(page, x, 2), strip)),
        "y": (y, (page, flip(strip, y, 1))),
        "low": (z_low, (page, flip(strip, z_low, 2))),
        "high": (z_high, (page, flip(strip, z_high, 4))),
    }
    return core, core_mate, [[mates[k] for k in ("y", "x", "low", "high")], [mates[k] for k in ("x", "y", "low", "high")]]


def meet(mates):
    barrier = pltpu.get_barrier_semaphore()
    for mate in mates:
        pl.semaphore_signal(barrier, inc=1, device_id=mate, device_id_type=PAIR)
    pl.semaphore_wait(barrier, len(mates))


def send(source, target, sems, number, mate):
    copy = pltpu.make_async_remote_copy(
        src_ref=source,
        dst_ref=target,
        send_sem=sems.at[0, number],
        recv_sem=sems.at[1, number],
        device_id=mate,
        device_id_type=PAIR,
    )
    copy.start()
    return copy


def add_rows(target, first, source, start, length, at, rows):
    span = pl.ds(at, rows)

    def step(i, carry):
        total = target[first + i, span, :].astype(F32) + source[start + i, span, :].astype(F32)
        target[first + i, span, :] = total.astype(BF)
        return carry

    lax.fori_loop(0, length, step, 0)


def spans(arrays):
    at, found = 0, []
    for array in arrays:
        found.append((at, array.shape[2]))
        at += array.shape[2]
    return found


def core_sum_kernel(*refs, counts, sizes):
    total = sum(counts)
    grads = [refs[: counts[0]], refs[counts[0] : total]]
    outs = refs[total : total + 4]
    held, remote, near = refs[total + 4 : total + 6], refs[total + 6], refs[total + 7]
    core, core_mate, orders = coordinates()
    meet([core_mate])
    jobs, number = [], 0
    for order in range(2):
        bit = orders[order][0][0]
        for grad, (at, rows) in zip(grads[order], sizes[order]):
            target = held[order].at[:, pl.ds(at, rows), :]
            far = send(grad.at[1 - core], target, remote, number, core_mate)
            mine = []
            for which, out in enumerate((outs[2 * order], outs[2 * order + 1])):
                first = 8 * (bit if which else 1 - bit)
                copy = pltpu.make_async_copy(
                    grad.at[core, pl.ds(first, 8)], out.at[:, pl.ds(at, rows), :], near.at[2 * number + which]
                )
                copy.start()
                mine.append((copy, out, first))
            jobs.append((far, mine, order, at, rows))
            number += 1
    for far, mine, order, at, rows in jobs:
        far.wait()
        for copy, out, first in mine:
            copy.wait()
            add_rows(out, 0, held[order], first, 8, at, rows)


def core_sum(grads, collective, deps):
    grads = [[g.reshape(2, 16, *g.shape[-2:]) for g in group] for group in grads]
    sizes = [spans(group) for group in grads]
    rows = [sum(r for _, r in group) for group in sizes]
    counts = [len(group) for group in grads]
    total = sum(counts)
    kernel = functools.partial(core_sum_kernel, counts=counts, sizes=sizes)
    return pl.pallas_call(
        lambda *refs: kernel(*refs[:total], *refs[total + len(deps) :]),
        in_specs=[ANY] * (total + len(deps)),
        out_specs=[pl.BlockSpec(memory_space=pltpu.VMEM)] * 4,
        out_shape=[sds((8, rows[order], LANES), BF) for order in (0, 0, 1, 1)],
        scratch_shapes=[
            pltpu.VMEM((16, rows[0], LANES), BF),
            pltpu.VMEM((16, rows[1], LANES), BF),
            pltpu.SemaphoreType.DMA((2, total)),
            pltpu.SemaphoreType.DMA((2 * total,)),
        ],
        compiler_params=pltpu.CompilerParams(collective_id=collective, has_side_effects=True, vmem_limit_bytes=VMEM_BYTES),
        name="core_sum",
    )(*grads[0], *grads[1], *deps)


ORDERS = (("y", "x", "low", "high"), ("x", "y", "low", "high"))
PLACES = {"x": BIT_X, "y": BIT_Y, "low": BIT_LOW, "high": BIT_HIGH}


def across(array, name):
    axis, weight = {"x": ("page", 2), "y": ("strip", 1), "low": ("strip", 2), "high": ("strip", 4)}[name]
    return lax.ppermute(array, axis, [(i, i ^ weight) for i in range(lax.axis_size(axis))])


def halve_add_kernel(s_ref, *refs):
    for k in range(4):
        keep, got, out = refs[2 * k], refs[2 * k + 1], refs[8 + k]
        out[...] = (keep[...].astype(F32) + got[...].astype(F32)).astype(BF)


def halve_add(scalars, kept, got, stage, deps):
    ins, outs = [], []
    for order in range(2):
        size = kept[order].shape[0] // 2
        shape = kept[order].shape[1:]
        place = PLACES[ORDERS[order][stage]]
        for flip in (1, 0):
            spec = pl.BlockSpec(
                (1, *shape),
                lambda i, s, place=place, flip=flip, size=size: ((1 - s[place] if flip else s[place]) * size + i, 0, 0),
            )
            ins += [(kept[order], spec), (got[order], spec)]
            outs.append(((size, *shape), BF, pl.BlockSpec((1, *shape), lambda i, s: (i, 0, 0))))
    return call(
        halve_add_kernel, "halve_add", ins, outs, grid=(size,), scalars=scalars, deps=deps, work=(1e6, 6 * size * 1296 * 512, 0)
    )


def late_sum_kernel(*refs, lots, arrays, early_rows):
    grads = refs[:arrays]
    early = refs[arrays : arrays + 4]
    own, got = refs[arrays + 4 : arrays + 6], refs[arrays + 6 : arrays + 8]
    sums, first_held = refs[arrays + 8 : arrays + 10], refs[arrays + 10 : arrays + 12]
    held = [refs[arrays + 12 : arrays + 16], refs[arrays + 16 : arrays + 20]]
    done, loaded, early_held = refs[arrays + 20 : arrays + 22], refs[arrays + 22 : arrays + 26], refs[arrays + 26 : arrays + 28]
    remote, near = refs[arrays + 28 :]
    core, core_mate, orders = coordinates()
    meet([core_mate] + [mate for _, mate in orders[0]])
    numbers, local_numbers = iter(range(1000)), iter(range(1000))
    jobs = []
    for order, at, members in lots:
        copies, first = [], at
        for member, start, rows in members:
            there, span = pl.ds(start, rows), pl.ds(first, rows)
            first += rows
            copies.append(
                send(grads[member].at[1 - core, :, there, :], first_held[order].at[:, span, :], remote, next(numbers), core_mate)
            )
            copy = pltpu.make_async_copy(
                grads[member].at[core, :, there, :], sums[order].at[:, span, :], near.at[next(local_numbers)]
            )
            copy.start()
            copies.append(copy)
        jobs.append((order, at, first - at, copies))
    loads = []
    for k in range(4):
        copy = pltpu.make_async_copy(early[k], loaded[k], near.at[next(local_numbers)])
        copy.start()
        loads.append(copy)
    for copy in loads:
        copy.wait()
    early_flights = []
    for order in range(2):
        bit, mate = orders[order][3]
        kept = loaded[2 * order]
        add_rows(kept, 1 - bit, loaded[2 * order + 1], 1 - bit, 1, 0, early_rows)
        early_flights.append(send(kept.at[1 - bit], early_held[order], remote, next(numbers), mate))
        add_rows(kept, bit, loaded[2 * order + 1], bit, 1, 0, early_rows)
    bases = [0] * len(jobs)
    flights = [None] * len(jobs)
    first_exchange = []
    for stage in range(4):
        size = 8 >> stage
        for n, (order, at, rows, copies) in enumerate(jobs):
            source = first_held[order] if stage == 0 else held[order][stage - 1]
            for copy in copies if stage == 0 else [flights[n]]:
                copy.wait()
            bit, mate = orders[order][stage]
            out, keep = size * (1 - bit), size * bit
            base = bases[n]
            add_rows(sums[order], base + out, source, out, size, at, rows)
            flights[n] = send(
                sums[order].at[pl.ds(base + out, size), pl.ds(at, rows), :],
                held[order][stage].at[:, pl.ds(at, rows), :],
                remote,
                next(numbers),
                mate,
            )
            add_rows(sums[order], base + keep, source, keep, size, at, rows)
            bases[n] = base + keep
        if stage == 2:
            for order in range(2):
                early_flights[order].wait()
                total = loaded[2 * order][orders[order][3][0]].astype(F32) + early_held[order][...].astype(F32)
                own[order][:early_rows, :] = total.astype(BF)
                span = pl.ds(0, early_rows)
                first_exchange.append(send(own[order].at[span, :], done[order].at[span, :], remote, next(numbers), core_mate))
    exchange = []
    for n, (order, at, rows, _) in enumerate(jobs):
        flights[n].wait()
        value = sums[order][bases[n], pl.ds(at, rows), :].astype(F32) + held[order][3][0, pl.ds(at, rows), :].astype(F32)
        span = pl.ds(early_rows + at, rows)
        own[order][span, :] = value.astype(BF)
        exchange.append(send(own[order].at[span, :], done[order].at[span, :], remote, next(numbers), core_mate))
    for copy in first_exchange + exchange:
        copy.wait()
    for order in range(2):
        got[order][...] = done[order][...]


def late_sum(grads, lots, rows, early, collective, deps):
    grads = [g.reshape(2, 16, *g.shape[-2:]) for g in grads]
    arrays = len(grads)
    members = sum(len(lot[2]) for lot in lots)
    early_rows = early[0].shape[1]
    share = [sds((early_rows + r, LANES), BF) for r in rows]
    vmem = lambda *shape: pltpu.VMEM(shape, BF)
    kernel = functools.partial(late_sum_kernel, lots=lots, arrays=arrays, early_rows=early_rows)
    first = arrays + 4
    return pl.pallas_call(
        lambda *refs: kernel(*refs[:first], *refs[first + len(deps) :]),
        in_specs=[ANY] * (first + len(deps)),
        out_specs=[pl.BlockSpec(memory_space=pltpu.VMEM)] * 4,
        out_shape=share + share,
        scratch_shapes=[
            *[vmem(16, r, LANES) for r in rows],
            *[vmem(16, r, LANES) for r in rows],
            *[vmem(8 >> k, rows[0], LANES) for k in range(4)],
            *[vmem(8 >> k, rows[1], LANES) for k in range(4)],
            *[vmem(early_rows + r, LANES) for r in rows],
            *[vmem(2, early_rows, LANES)] * 4,
            *[vmem(early_rows, LANES)] * 2,
            pltpu.SemaphoreType.DMA((2, members + 5 * len(lots) + 4)),
            pltpu.SemaphoreType.DMA((members + 4,)),
        ],
        compiler_params=pltpu.CompilerParams(collective_id=collective, has_side_effects=True, vmem_limit_bytes=VMEM_BYTES),
        name="late_sum",
    )(*grads, *early, *deps)


def finish_kernel(core_ref, own0, own1, got0, got1, gain_ref, *outs, plan):
    first = core_ref[0] == 0
    owns, gots = (own0, own1), (got0, got1)
    lane = iota((1, LANES), 1)
    left = lane < 64

    def tile(order, at, size, part):
        mine = owns[order][at : at + size, :].astype(F32)
        theirs = gots[order][at : at + size, :].astype(F32)
        return jnp.where(first == (part == 0), mine, theirs)

    for out, (size, tiles, flipped) in zip(outs, plan):
        count = len(tiles)
        for part in range(2):
            rows = slice(part * size, (part + 1) * size)
            values = [tile(order, at, size, part) for order, at in tiles]
            if count % 2 == 0:
                for t in range(count // 2):
                    out[rows, t * LANES : (t + 1) * LANES] = jnp.where(first, values[t], values[t + count // 2])
                continue
            turned = [pltpu.roll(v, 64, 1) for v in values[count // 2 :]]
            whole_tiles = [
                jnp.where(first, values[t], jnp.where(left, turned[t], turned[t + 1])) for t in range(count // 2)
            ]
            rest = jnp.where(first, values[count // 2], turned[-1])
            if flipped:
                for t, value in enumerate(whole_tiles):
                    for at in range(0, size, 64):
                        column = part * size + at
                        out[t * LANES : (t + 1) * LANES, column : column + 64] = value[at : at + 64].T
                for at in range(0, size, 64):
                    column = part * size + at
                    out[count // 2 * LANES :, column : column + 64] = rest[at : at + 64].T[:64]
                continue
            for t, value in enumerate(whole_tiles):
                out[rows, t * LANES : (t + 1) * LANES] = value
            out[rows, count // 2 * LANES :] = rest[:, :64]
    size = gain_ref.shape[1] // 2
    at = own0.shape[0] - size
    gain = jnp.concatenate([tile(0, at, size, part) for part in range(2)], axis=0).T
    gain_ref[...] = jnp.where(first, gain[0:1], gain[1:2])


def finish(core, shares, shapes, plan, gain_rows):
    vmem = pl.BlockSpec(memory_space=pltpu.VMEM)
    outs = [shape[::-1] if flipped else shape for shape, (_, _, flipped) in zip(shapes, plan)]
    gain, *found = pl.pallas_call(
        functools.partial(finish_kernel, plan=plan),
        in_specs=[pl.BlockSpec(memory_space=pltpu.SMEM)] + [vmem] * 4,
        out_specs=[vmem] * (1 + len(outs)),
        out_shape=[sds((1, gain_rows), F32)] + [sds(shape, F32) for shape in outs],
        compiler_params=pltpu.CompilerParams(vmem_limit_bytes=VMEM_BYTES),
        name="finish",
    )(core, *shares)
    return gain.T, *[f.T if flipped else f for f, (_, _, flipped) in zip(found, plan)]


def from_ahead(array, count, distance):
    return lax.ppermute(array, "strip", [(i, (i - distance) % count) for i in range(count)])


def from_partner(array, count):
    return lax.ppermute(array, "strip", [(i, i ^ 1) for i in range(count)])


def scattered(grad):
    strips, pages = lax.axis_size("strip"), lax.axis_size("page")
    rows, cols = grad.shape
    part = lax.psum_scatter(grad, "strip", scatter_dimension=0, tiled=True)
    part = part.reshape(rows // strips, pages, cols // pages).transpose(1, 0, 2)
    return lax.psum_scatter(part, "page", scatter_dimension=0, tiled=False).astype(F32)


def local(
    visual_in, query_in, row_valid, segment_ids, slot_valid, col_shift, row_shifted, norm_gains,
    w_vqkv, w_vout, w_up, w_down, w_qqkv, w_xkv, w_qout, w_qup, w_qdown, visual_cot, query_cot,
):
    pages, strip_rows, columns, width = visual_in.shape
    own_slots, all_slots = query_in.shape[1], segment_ids.shape[1]
    count = lax.axis_size("strip")
    tiled = count == 8
    group = count // 2
    half = strip_rows * columns
    slots = 2 * own_slots
    window = WIN * WIN
    form = (strip_rows, columns)
    place, page = lax.axis_index("strip"), lax.axis_index("page")
    odd = place % 2
    up = jnp.where(odd == 1, 1 - row_shifted[0], row_shifted[0])
    down = 1 - up
    pick = lambda array, which: lax.dynamic_index_in_dim(array, which, 0, keepdims=False)
    scalars = jnp.stack([up, pick(col_shift, up), odd, page % 2, page // 2, odd, place // 2 % 2, place // 4, (place // 2) * slots]).astype(jnp.int32)

    visual, cot = visual_in.reshape(pages, half, width), visual_cot.reshape(pages, half, width)
    query_sent = pack(scalars, query_in, slot_valid, [])
    query_theirs = from_partner(query_sent, count)
    patch_other = from_ahead(pack(scalars, visual, row_valid, [query_sent]), count, 1)
    gains = jnp.pad(norm_gains.T, ((0, 4), (0, 0)))

    order = [-1] + list(range(group - 1))
    blocks = forward_blocks(group if tiled else 1, slots, group)
    near_block = next(block for block, near in blocks if near)

    def gather(array):
        pieces = [array if k == 0 else from_ahead(array, count, 2 * k) for k in order]
        return pieces if tiled else [jnp.concatenate(pieces, axis=0)]

    def give_back(arrays):
        if not tiled:
            arrays = [arrays[0][n * slots : (n + 1) * slots] for n in range(group)]
        return [piece if k == 0 else from_ahead(piece, count, -2 * k) for piece, k in zip(arrays, order)]

    x_query, normed_three, q_own, slot_kv, same, turned = query_in_call(
        scalars, segment_ids, slot_valid, query_in, query_theirs, gains, w_qqkv
    )
    qs = gather(q_own)
    cot_sent, cot_q_sent = pack_two(scalars, cot, query_cot, [q_own])
    cot_other, cot_theirs = from_ahead(cot_sent, count, 1), from_partner(cot_q_sent, count)
    x, normed_one, qkv, cross, key_bias = patch_in(
        scalars, row_valid, visual, patch_other, gains, w_vqkv, w_xkv, form, [cot_q_sent]
    )
    att = window_forward(qkv, window, [])
    q_out = query_forward(qs, cross, slot_kv, key_bias, same, blocks, [att, cot_theirs])
    out_parts = give_back(q_out)
    (vis_own, vis_other, grad_after, grad_att, g_vout, g_up, g_down, gain_two) = patch_ffn(
        scalars, att, x, cot, cot_other, gains, w_vout, w_up, w_down, tiled, form, [q_out[0]]
    )
    vis_came = from_ahead(vis_other, count, -1)
    (q_res, q_res_other, grad_q, send_q, att_q, normed_four, act_q, dact_q, branch_q, cot_q, gain_four) = query_ffn(
        scalars, out_parts, x_query, query_cot, cot_theirs, gains, w_qout, w_qup, w_qdown, tiled, [gain_two]
    )
    gos = gather(send_q)
    res_came = from_partner(q_res_other, count)
    g_qout, g_qup, g_qdown = query_weights(normed_four, cot_q, att_q, branch_q, act_q, dact_q, tiled, [])
    last = g_qout
    if tiled:
        out_0, keep_0, out_1, keep_1 = core_sum([[g_up, g_qup, g_vout], [g_down, g_qdown, g_qout]], 0, [vis_came])
        got = [across(out_0, "y"), across(out_1, "x")]
        last = keep_0
    g_proj = window_backward(qkv, grad_att, window, [last])
    last = [g_proj, res_came]
    dqs, dks, dvs, dsks, dsvs = [], [], [], [], []
    for part in range(2):
        dq, dk, dv, dsk, dsv = query_backward(qs, gos, cross, slot_kv, key_bias, turned, near_block, part, last)
        last = [dk] if part == 0 else [dk, *dqs[0]]
        dqs.append(give_back(dq))
        dks.append(dk)
        dvs.append(dv)
        dsks.append(dsk)
        dsvs.append(dsv)
        if tiled:
            out_0, keep_0, out_1, keep_1 = halve_add(scalars, [keep_0, keep_1], got, part + 1, last)
            got = [across(out_0, ORDERS[0][part + 1]), across(out_1, ORDERS[1][part + 1])]
            last = [keep_0]
    back_part, g_vqkv = qkv_back(g_proj, normed_one, w_vqkv, tiled, last)
    vin_own, vin_other, gain_rows, *g_xkv = cross_back(
        scalars, dks, dvs, normed_one, x, grad_after, back_part, gains, w_xkv, gain_two, gain_four, pages, tiled, form, []
    )
    qin_own, qin_other, g_qqkv, gain_grads = query_out(
        scalars, dqs, dsks, dsvs, normed_three, x_query, grad_q, gains, w_qqkv, gain_rows, pages, tiled, got if tiled else []
    )

    def put(array, other):
        return lax.dynamic_update_index_in_dim(array, other.astype(array.dtype), down, 0)

    shape = (pages, strip_rows, columns, width)
    visual_out = put(vis_own, vis_came).reshape(shape)
    vin_came = from_ahead(vin_other, count, -1)
    query_out_rows = put(q_res, res_came)
    qin_came = from_partner(qin_other, count)

    weights = (w_vqkv, w_vout, w_up, w_down, w_qqkv, w_xkv, w_qout, w_qup, w_qdown)
    if tiled:
        sets = [[g_up, g_qup, g_vout, g_vqkv, g_xkv[0], gain_grads], [g_down, g_qdown, g_qout, g_qqkv, g_xkv[1]]]
        size = lambda g: g.shape[-2]
        a, b, c, d, e = g_vqkv, g_xkv[0], gain_grads, g_qqkv, g_xkv[1]
        cut = (size(a) // 2 + 15) // 16 * 16
        lots = [
            (0, 0, [(0, 0, cut)]),
            (1, 0, [(3, 0, cut)]),
            (0, cut, [(0, cut, size(a) - cut)]),
            (1, cut, [(3, cut, size(d) - cut)]),
            (0, size(a), [(1, 0, size(b)), (2, 0, size(c))]),
            (1, size(d), [(4, 0, size(e))]),
        ]
        late_rows = [size(a) + size(b) + size(c), size(d) + size(e)]
        shares = late_sum([a, b, c, d, e], lots, late_rows, [keep_0, got[0], keep_1, got[1]], 1, [])
        starts = [[sum(g.shape[-2] for g in group_[:k]) for k in range(len(group_))] for group_ in sets]
        where = {w: (0, starts[0][k]) for k, w in enumerate((2, 7, 1, 0, 5))}
        where.update({w: (1, starts[1][k]) for k, w in enumerate((3, 8, 6, 4))})
        plan, shapes = [], []
        for number, weight in enumerate(weights):
            rows, cols = weight.shape
            step, tiles = rows // 16, cols // 256
            which, at = where[number]
            spots = [(which, at + t * step) for t in range(tiles)]
            if number == 5:
                spots = spots[:3] + [(1, starts[1][4] + t * step) for t in range(3)]
            flipped = rows > 2 * cols and tiles % 2 == 1
            plan.append((step, spots, flipped))
            shapes.append((rows // 8, cols // lax.axis_size("page")))
        last = shares[0]
        gain_part, *parts = finish(scalars[CORE:CORE + 1], shares, shapes, plan, width // 8)
    else:
        last = gain_rows
        parts = [scattered(g) for g in (g_vqkv, g_vout, g_up, g_down, g_qqkv, g_xkv[0], g_qout, g_qup, g_qdown)]
        gain_part = lax.psum_scatter(gain_grads[:4], "page", scatter_dimension=0, tiled=True)
        gain_part = lax.psum_scatter(gain_part, "strip", scatter_dimension=1, tiled=True).reshape(-1, 1)
    visual_in_grad, query_in_grad = put_two(scalars, vin_own, qin_own, vin_came, qin_came, [last])
    visual_in_grad = visual_in_grad.reshape(shape)
    return (visual_out, query_out_rows, visual_in_grad, query_in_grad, gain_part, *parts)


def solution(mesh):
    tokens, slots, table = P("page", "strip", None, None), P("page", "strip", None), P("page", "strip")
    tile = P("strip", "page")
    return jax.shard_map(
        local,
        mesh=mesh,
        in_specs=(tokens, slots, table, P("page", None), table, P("page"), P("page")) + (P(),) * 10 + (tokens, slots),
        out_specs=(tokens, slots, tokens, slots) + (tile,) * 10,
        check_vma=False,
    )
```

```python
import functools

import jax
import jax.numpy as jnp
from jax import lax
from jax.experimental import pallas as pl
from jax.experimental.pallas import tpu as pltpu
from jax.sharding import PartitionSpec as P

HEADS = 12
WIN = 12
EPS = 1e-05
MASKED = -1e9
SCALE = 0.125
BF = jnp.bfloat16
F32 = jnp.float32
LANES = 128
VMEM_BYTES = 65400 * 1024


def dot(left, right, left_dim=1, right_dim=0):
    return lax.dot_general(
        left, right, (((left_dim,), (right_dim,)), ((), ())), preferred_element_type=F32
    )


def iota(shape, dim):
    return lax.broadcasted_iota(jnp.int32, shape, dim)


def norm_stats(rows):
    offset = rows - jnp.mean(rows, axis=-1, keepdims=True)
    spread = lax.rsqrt(jnp.mean(offset * offset, axis=-1, keepdims=True) + EPS)
    return offset * spread, spread


def norm_back(unit, spread, gain, grad):
    product = grad * unit
    scaled = grad * gain
    centre = jnp.mean(scaled, axis=-1, keepdims=True)
    slope = jnp.mean(scaled * unit, axis=-1, keepdims=True)
    return spread * (scaled - centre - unit * slope), jnp.sum(product, axis=0, keepdims=True)


def gelu_pair(t):
    square = t * t
    plus = 0.5 * jnp.tanh(t * (0.7978845608 + 0.0356774081 * square)) + 0.5
    value = t * plus
    return value, plus + value * (1.0 - plus) * (1.5957691216 + 0.2140644488 * square)


def three_parts(value):
    high = value.astype(BF).astype(F32)
    rest = value - high
    middle = rest.astype(BF).astype(F32)
    low = (rest - middle).astype(BF).astype(F32)
    return high, middle, low


def place_lanes(column, lane, first):
    high, middle, low = three_parts(column)
    return (
        jnp.where(lane == first, high, 0.0)
        + jnp.where(lane == first + 16, middle, 0.0)
        + jnp.where(lane == first + 32, low, 0.0)
    )


def join_lanes(stats, first):
    total = stats
    rolled = []
    for part in range(3):
        amount = (first + 16 * part) % LANES
        rolled.append(total if amount == 0 else pltpu.roll(total, LANES - amount, 1))
    return rolled[0] + rolled[1] + rolled[2]


def spread_heads(values, width):
    head_dim = width // HEADS
    pick = (iota((LANES, width), 0) == iota((LANES, width), 1) // head_dim).astype(BF)
    high, middle, low = three_parts(values)
    return dot(high.astype(BF), pick) + dot(middle.astype(BF), pick) + dot(low.astype(BF), pick)


def whole(shape, single=False):
    mode = pl.Buffered(1) if single else None
    return pl.BlockSpec(shape, lambda *_: (0,) * len(shape), pipeline_mode=mode)


def sds(shape, kind):
    return jax.ShapeDtypeStruct(shape, kind)


ANY = pl.BlockSpec(memory_space=pl.ANY)


def call(kernel, name, ins, outs, grid=(1,), scratch=(), scalars=None, deps=(), work=(0, 0, 0), aliases={}):
    first = len(ins) + (scalars is not None)

    def body(*refs):
        kernel(*refs[:first], *refs[first + len(deps) :])

    return pl.pallas_call(
        body,
        grid_spec=pltpu.PrefetchScalarGridSpec(
            num_scalar_prefetch=int(scalars is not None),
            grid=grid,
            in_specs=[spec for _, spec in ins] + [ANY] * len(deps),
            out_specs=[spec for *_, spec in outs],
            scratch_shapes=list(scratch),
        ),
        out_shape=[sds(shape, kind) for shape, kind, _ in outs],
        input_output_aliases=aliases,
        compiler_params=pltpu.CompilerParams(vmem_limit_bytes=VMEM_BYTES),
        cost_estimate=pl.CostEstimate(flops=int(3 * work[0]), bytes_accessed=int(work[1]), transcendentals=int(work[2])),
        name=name,
    )(*([] if scalars is None else [scalars]), *[array for array, _ in ins], *deps)


UP, SHIFT, ODD, CORE, BIT_X, BIT_Y, BIT_LOW, BIT_HIGH, BASE = range(9)


def page_block(shape):
    return pl.BlockSpec((1, *shape[1:]), lambda *at: (at[-1][UP],) + (0,) * (len(shape) - 1))


def steps_below(value, size, count):
    total = jnp.zeros_like(value)
    for k in range(1, count):
        total = total + jnp.where(value >= size * k, 1, 0)
    return total


def into_windows(own, other, shift, strip_rows, columns):
    half, part = strip_rows * columns, strip_rows * WIN
    token = iota((half, 1), 0)
    window = steps_below(token, part, columns // WIN)
    inside = token - part * window
    row = steps_below(inside, WIN, strip_rows)
    column = inside - WIN * row + WIN * window + shift
    column = jnp.where(column >= columns, column - columns, column)
    onehot = (iota((half, half), 1) == row * columns + column).astype(F32).astype(BF)
    turned = [dot(onehot, own), dot(onehot, other)]
    pieces = [turned[side][w * part : (w + 1) * part] for w in range(columns // WIN) for side in range(2)]
    return jnp.concatenate(pieces, axis=0)


def out_of_windows(shift, strip_rows, columns):
    half = strip_rows * columns
    token = iota((half, 1), 0)
    row = steps_below(token, columns, strip_rows)
    column = token - columns * row - shift
    column = jnp.where(column < 0, column + columns, column)
    window = steps_below(column, WIN, columns // WIN)
    spot = window * (strip_rows * WIN) + row * WIN + column - WIN * window
    return (iota((half, half), 1) == spot).astype(F32).astype(BF)


def tile_index(strip, half, order):
    y = strip % 2
    lead = (y, half) if order == 0 else (half, y)
    return lead + ((strip // 2 % 2) * 2 + strip // 4,)


def tile_shape(rows, cols):
    return (2, 2, 2, 4, cols // 256 * (rows // 16), LANES)


def store_all(ref, value, order):
    rows, cols = value.shape
    size, tiles = rows // 16, cols // 256
    for strip in range(8):
        for core in range(2):
            at = (2 * strip + core) * size
            for half in range(2):
                lead = tile_index(strip, half, order)
                for t in range(tiles):
                    lanes = (half * tiles + t) * LANES
                    ref[(core, *lead, slice(t * size, (t + 1) * size), slice(None))] = value[at : at + size, lanes : lanes + LANES]


def store_columns(ref, value, order, half=0, first=0):
    size = value.shape[0] // 16
    for strip in range(8):
        for core in range(2):
            at = (2 * strip + core) * size
            lead = tile_index(strip, half, order)
            for t in range(value.shape[1] // LANES):
                rows = slice((first + t) * size, (first + t + 1) * size)
                ref[(core, *lead, rows, slice(None))] = value[at : at + size, t * LANES : (t + 1) * LANES]


def store_strips(ref, value, order, z=0):
    size, tiles = value.shape[0] // 4, value.shape[1] // 256
    for y in range(2):
        for core in range(2):
            for half in range(2):
                lead = (y, half) if order == 0 else (half, y)
                for t in range(tiles):
                    lanes = (half * tiles + t) * LANES
                    at = (2 * y + core) * size
                    ref[(core, *lead, z, slice(t * size, (t + 1) * size), slice(None))] = value[at : at + size, lanes : lanes + LANES]


def columns_spec(rows, chunk, per_half, order, at):
    block = (2, 2, 1, 4) if order == 0 else (2, 1, 2, 4)
    lead = lambda half: (0, 0, half, 0) if order == 0 else (0, half, 0, 0)
    return pl.BlockSpec(
        (*block, chunk // LANES * (rows // 16), LANES), lambda j, *_: (*lead(at(j) // per_half), at(j) % per_half, 0)
    )


def strips_spec(rows, cols):
    return pl.BlockSpec(
        (2, 2, 2, 1, cols // 256 * (rows // 16), LANES), lambda j, *_: (0, 0, 0, (j % 2) * 2 + j // 2, 0, 0)
    )


def grad_forms(width, hidden, chunk, tiled, wo_order):
    if not tiled:
        return [
            ((width, width), BF, whole((width, width))),
            ((width, hidden), BF, pl.BlockSpec((width, chunk), lambda j, *_: (0, j))),
            ((hidden, width), BF, pl.BlockSpec((chunk, width), lambda j, *_: (j, 0))),
        ]
    shapes = [tile_shape(width, width), tile_shape(width, hidden), tile_shape(hidden, width)]
    specs = [
        whole(shapes[0]),
        columns_spec(width, chunk, hidden // 2 // chunk, 0, lambda j: j),
        strips_spec(hidden, width),
    ]
    return [(shape, BF, spec) for shape, spec in zip(shapes, specs)]


def put_grad(ref, value, store, order, tiled):
    if tiled:
        store(ref, value, order)
    else:
        ref[...] = value


def patch_in_kernel(s_ref, ok_ref, own_ref, other_ref, gain_ref, wq_ref, wx_ref, x_ref, n_ref, qkv_ref, cross_ref, bias_ref, turned, *, form):
    strip_rows, half = form[0], own_ref.shape[1]
    row = steps_below(iota((WIN * WIN, 1), 0), WIN, WIN)
    valid = jnp.zeros((WIN * WIN, 1), F32)
    for r in range(strip_rows):
        mine = jnp.where(ok_ref[s_ref[UP], r] == 1, 1.0, 0.0)
        theirs = other_ref[half : half + 1, r : r + 1].astype(F32)
        valid = valid + jnp.where(row == r, mine, 0.0) + jnp.where(row == strip_rows + r, theirs, 0.0)
    bias = jnp.broadcast_to(jnp.where(valid > 0.5, 0.0, MASKED).astype(BF), (WIN * WIN, LANES))
    for k in range(2):
        bias_ref[k * WIN * WIN : (k + 1) * WIN * WIN, :] = bias
    @pl.when(pl.program_id(0) == 0)
    def _():
        turned[...] = into_windows(own_ref[0], other_ref[:half, :], s_ref[SHIFT], *form).astype(BF)

    step = x_ref.shape[0]
    x = turned[pl.ds(pl.multiple_of(pl.program_id(0) * step, step), step), :].astype(F32)
    x_ref[...] = x.astype(BF)
    unit, _ = norm_stats(x)
    normed = (unit * gain_ref[0:1, :]).astype(BF)
    n_ref[...] = normed
    qkv_ref[...] = dot(normed, wq_ref[...]).astype(BF)
    cross_ref[...] = dot(normed, wx_ref[...]).astype(BF)


def patch_in(scalars, rows_ok, visual, other, gains, wq, wx, form, deps):
    _, half, width = visual.shape
    tokens = 2 * half
    step = 4 * form[0] * WIN
    rows = lambda w: ((tokens, w), BF, pl.BlockSpec((step, w), lambda i, *_: (i, 0)))
    return call(
        functools.partial(patch_in_kernel, form=form),
        "patch_in",
        [(rows_ok, pl.BlockSpec(memory_space=pltpu.SMEM)), (visual, page_block(visual.shape))]
        + [(a, whole(a.shape, True)) for a in (other, gains, wq, wx)],
        [rows(width), rows(width), rows(wq.shape[1]), rows(wx.shape[1]), rows(LANES)],
        grid=(tokens // step,),
        scratch=[pltpu.VMEM((tokens, width), BF)],
        scalars=scalars,
        deps=deps,
        work=(2 * tokens * width * (wq.shape[1] + wx.shape[1]), 2e7, 0),
    )


def pack_kernel(s_ref, ok_a_ref, a_ref, ok_b_ref, b_ref, a_out, b_out):
    for ok_ref, rows_ref, out_ref in ((ok_a_ref, a_ref, a_out), (ok_b_ref, b_ref, b_out)):
        count, flags = rows_ref.shape[1], ok_ref.shape[1]
        out_ref[:count, :] = rows_ref[0]
        out_ref[count:, :] = jnp.zeros_like(out_ref[count:, :])
        theirs = jnp.where(s_ref[UP] == 0, ok_ref[1:2, :], ok_ref[0:1, :]).astype(F32).astype(BF)
        out_ref[count:, :flags] = jnp.broadcast_to(theirs, (out_ref.shape[0] - count, flags))


def other_page(shape):
    return pl.BlockSpec((1, *shape[1:]), lambda *at: (1 - at[-1][UP],) + (0,) * (len(shape) - 1))


def pack(scalars, arrays):
    ins, outs = [], []
    for rows, flags in arrays:
        ins += [(flags, whole(flags.shape)), (rows, other_page(rows.shape))]
        shape = (rows.shape[1] + 16, rows.shape[2])
        outs.append((shape, BF, whole(shape)))
    return call(pack_kernel, "pack", ins, outs, scalars=scalars)


def held_back(array, deps):
    [out] = call(lambda a_ref, out_ref: None, "held_back", [(array, ANY)], [(array.shape, array.dtype, ANY)], deps=deps, aliases={0: 0})
    return out


def pack_two_kernel(s_ref, a_ref, b_ref, a_out, b_out):
    a_out[...] = a_ref[0]
    b_out[...] = b_ref[0]


def pack_two(scalars, a, b, deps):
    return call(
        pack_two_kernel,
        "pack_two",
        [(x, other_page(x.shape)) for x in (a, b)],
        [(x.shape[1:], BF, whole(x.shape[1:])) for x in (a, b)],
        scalars=scalars,
        deps=deps,
    )


def put_two_kernel(s_ref, a_ref, b_ref, a_came, b_came, a_out, b_out):
    a_out[0] = a_came[...].astype(a_out.dtype)
    b_out[0] = b_came[...].astype(b_out.dtype)


def put_two(scalars, a, b, a_came, b_came, deps):
    return call(
        put_two_kernel,
        "put_two",
        [(a, ANY), (b, ANY)] + [(x, whole(x.shape)) for x in (a_came, b_came)],
        [(x.shape, x.dtype, other_page(x.shape)) for x in (a, b)],
        scalars=scalars,
        deps=deps,
        aliases={1: 0, 2: 1},
    )


def head_masks():
    lane = iota((1, LANES), 1)
    left = lane < 64
    return left, [left.astype(F32).astype(BF), (~left).astype(F32).astype(BF)]


def window_kernel(qkv_ref, out_ref):
    tokens, width = out_ref.shape
    left, masks = head_masks()
    for pair in range(HEADS // 2):
        at = pair * LANES
        q = qkv_ref[:, at : at + LANES] * SCALE
        k = qkv_ref[:, width + at : width + at + LANES]
        v = qkv_ref[:, 2 * width + at : 2 * width + at + LANES]
        all_scores = [dot(q * masks[side], k, 1, 1) for side in range(2)]
        mixed = []
        for scores in all_scores:
            raised = jnp.exp(scores - jnp.max(scores, axis=-1, keepdims=True))
            total = jnp.sum(raised, axis=-1, keepdims=True)
            mixed.append(dot(raised.astype(BF), v) * (1.0 / total))
        out_ref[:, at : at + LANES] = jnp.where(left, mixed[0], mixed[1]).astype(BF)


def window_forward(qkv, tokens, deps):
    total, width3 = qkv.shape
    width = width3 // 3
    rows = lambda w: pl.BlockSpec((tokens, w), lambda i: (i, 0))
    [att] = call(
        window_kernel,
        "window_forward",
        [(qkv, rows(width3))],
        [((total, width), BF, rows(width))],
        grid=(total // tokens,),
        deps=deps,
        work=(16 * total * tokens * width, 8e6, total * tokens * HEADS),
    )
    return att


def window_back_kernel(qkv_ref, go_ref, out_ref):
    tokens, width = go_ref.shape
    left, masks = head_masks()
    for pair in range(HEADS // 2):
        at = pair * LANES
        q = qkv_ref[:, at : at + LANES]
        k = qkv_ref[:, width + at : width + at + LANES]
        v = qkv_ref[:, 2 * width + at : 2 * width + at + LANES]
        g = go_ref[:, at : at + LANES]
        scaled = q * SCALE
        all_scores = [dot(k * masks[side], scaled, 1, 1) for side in range(2)]
        all_grads = [dot(v * masks[side], g, 1, 1) for side in range(2)]
        parts = []
        for scores, grads in zip(all_scores, all_grads):
            raised = jnp.exp(scores - jnp.max(scores, axis=0, keepdims=True))
            inverse = 1.0 / jnp.sum(raised, axis=0, keepdims=True)
            probs = raised * inverse
            inner = jnp.sum(probs * grads, axis=0, keepdims=True)
            dscore = (probs * (grads - inner)).astype(BF)
            parts.append((dot(dscore, k, 0, 0), dot(dscore, q), dot(probs.astype(BF), g)))
        for index, factor in ((0, SCALE), (1, SCALE), (2, 1.0)):
            joined = jnp.where(left, parts[0][index], parts[1][index]) * factor
            out_ref[:, index * width + at : index * width + at + LANES] = joined.astype(BF)


def window_backward(qkv, go, tokens, deps):
    total, width3 = qkv.shape
    width = width3 // 3
    rows = lambda w: pl.BlockSpec((tokens, w), lambda i: (i, 0))
    [out] = call(
        window_back_kernel,
        "window_backward",
        [(qkv, rows(width3)), (go, rows(width))],
        [((total, width3), BF, rows(width3))],
        grid=(total // tokens,),
        deps=deps,
        work=(40 * total * tokens * width, 1.3e7, total * tokens * HEADS),
    )
    return out


def split_halves(rows, part):
    count = rows.shape[0] // (2 * part)
    return [
        jnp.concatenate([rows[(2 * w + s) * part : (2 * w + s + 1) * part] for w in range(count)], axis=0)
        for s in range(2)
    ]


def patch_ffn_kernel(
    s_ref, att_ref, x_ref, own_ref, other_ref, gain_ref, wo_ref, up_ref, down_ref,
    out_own_ref, out_other_ref, after_grad_ref, att_grad_ref, wo_grad_ref, up_grad_ref, down_grad_ref, gain_grad_ref,
    after, normed, cot, total, acts, dacts,
    *, tiled, form,
):
    step = pl.program_id(0)
    tokens, width = att_ref.shape
    part = form[0] * WIN
    block = 4 * part
    back = after_grad_ref
    blocks = [slice(b * block, (b + 1) * block) for b in range(tokens // block)]

    @pl.when(step == 0)
    def _():
        cot[...] = into_windows(own_ref[0], other_ref[...], s_ref[SHIFT], *form).astype(BF)
        for rows in blocks:
            value = x_ref[rows, :].astype(F32) + dot(att_ref[rows, :], wo_ref[...])
            after[rows, :] = value
            unit, _ = norm_stats(value)
            normed[rows, :] = (unit * gain_ref[1:2, :]).astype(BF)

    def products(first):
        enter = lambda rows: (dot(normed[rows, :], up_ref[...]), dot(cot[rows, :], down_ref[...], 1, 1))
        ahead = enter(blocks[0])
        for b, rows in enumerate(blocks):
            pre, grads = ahead
            if b + 1 < len(blocks):
                ahead = enter(blocks[b + 1])
            value, slope = gelu_pair(pre)
            act = value.astype(BF)
            acts[rows, :] = act
            dact = (slope * grads).astype(BF)
            dacts[rows, :] = dact
            if first:
                total[rows, :] = dot(act, down_ref[...])
                back[rows, :] = dot(dact, up_ref[...], 1, 1)
            else:
                total[rows, :] += dot(act, down_ref[...])
                back[rows, :] += dot(dact, up_ref[...], 1, 1)

    @pl.when(step == 0)
    def _():
        products(True)

    @pl.when(step > 0)
    def _():
        products(False)

    put_grad(up_grad_ref, dot(normed[...], dacts[...], 0, 0).astype(BF), store_columns, 0, tiled)
    put_grad(down_grad_ref, dot(acts[...], cot[...], 0, 0).astype(BF), store_strips, 1, tiled)

    @pl.when(step == pl.num_programs(0) - 1)
    def _():
        gain_sum = jnp.zeros((1, width), F32)
        for rows in blocks:
            unit, spread = norm_stats(after[rows, :])
            grad, gain_part = norm_back(unit, spread, gain_ref[1:2, :], back[rows, :])
            gain_sum = gain_sum + gain_part
            grad = cot[rows, :].astype(F32) + grad
            after_grad_ref[rows, :] = grad
            branch = grad.astype(BF)
            normed[rows, :] = branch
            att_grad_ref[rows, :] = dot(branch, wo_ref[...], 1, 1).astype(BF)
        gain_grad_ref[...] = jnp.broadcast_to(gain_sum, gain_grad_ref.shape)
        put_grad(wo_grad_ref, dot(att_ref[...], normed[...], 0, 0).astype(BF), store_all, 0, tiled)
        halves = split_halves(after[...] + total[...], part)
        onehot = out_of_windows(s_ref[SHIFT], *form)
        out_own_ref[0] = dot(onehot, halves[0].astype(BF)).astype(BF)
        out_other_ref[...] = dot(onehot, halves[1].astype(BF)).astype(BF)


def patch_ffn(scalars, att, x, cot, cot_other, gains, wo, up, down, tiled, form, deps, chunk=768):
    tokens, width = att.shape
    half = tokens // 2
    hidden = up.shape[1]
    single = lambda a: (a, whole(a.shape, True))
    return call(
        functools.partial(patch_ffn_kernel, tiled=tiled, form=form),
        "patch_ffn",
        [
            single(att), single(x), (cot, page_block(cot.shape)), single(cot_other), single(gains), single(wo),
            (up, pl.BlockSpec((width, chunk), lambda j, *_: (0, j))),
            (down, pl.BlockSpec((chunk, width), lambda j, *_: (j, 0))),
        ],
        [
            (cot.shape, BF, page_block(cot.shape)),
            ((half, width), BF, whole((half, width))),
            ((tokens, width), F32, whole((tokens, width))),
            ((tokens, width), BF, whole((tokens, width))),
            *grad_forms(width, hidden, chunk, tiled, 0),
            ((8, width), F32, whole((8, width))),
        ],
        grid=(hidden // chunk,),
        scratch=[
            pltpu.VMEM((tokens, width), F32),
            pltpu.VMEM((tokens, width), BF),
            pltpu.VMEM((tokens, width), BF),
            pltpu.VMEM((tokens, width), F32),
            pltpu.VMEM((tokens, chunk), BF),
            pltpu.VMEM((tokens, chunk), BF),
        ],
        scalars=scalars,
        deps=deps,
        work=(12 * tokens * width * hidden, 4e7, tokens * hidden),
    )


def qkv_back_kernel(gp_ref, n_ref, w_ref, back_ref, w_grad_ref, *, tiled):
    first = dot(gp_ref[...], w_ref[...], 1, 1)

    @pl.when(pl.program_id(0) == 0)
    def _():
        back_ref[...] = first

    @pl.when(pl.program_id(0) > 0)
    def _():
        back_ref[...] += first

    put_grad(w_grad_ref, dot(n_ref[...], gp_ref[...], 0, 0).astype(BF), store_columns, 0, tiled)


def qkv_back(gp, normed, w, tiled, deps):
    tokens, width = normed.shape
    cols = w.shape[1]
    chunk = cols // 2
    natural = pl.BlockSpec((width, chunk), lambda j: (0, j))
    if tiled:
        form = (tile_shape(width, cols), BF, columns_spec(width, chunk, 1, 0, lambda j: j))
    else:
        form = (w.shape, BF, natural)
    return call(
        functools.partial(qkv_back_kernel, tiled=tiled),
        "qkv_back",
        [(gp, pl.BlockSpec((tokens, chunk), lambda j: (0, j))), (normed, whole(normed.shape, True)), (w, natural)],
        [((tokens, width), F32, whole((tokens, width))), form],
        grid=(2,),
        deps=deps,
        work=(4 * tokens * width * cols, 2e7, 0),
    )


def cross_back_kernel(
    s_ref, gk0_ref, gk1_ref, gv0_ref, gv1_ref, n_ref, x_ref, after_ref, part_ref, gain_ref, wx_ref, g2_ref, g4_ref,
    own_ref, other_ref, gain_grad_ref, *rest,
    tiled, form,
):
    step = pl.program_id(0)
    half, width = other_ref.shape
    tokens = 2 * half
    part = form[0] * WIN
    block = 4 * part
    back = rest[-1]

    def one(grad, base):
        back[...] = base[...] + dot(grad, wx_ref[...], 1, 1)
        w_grad = dot(n_ref[...], grad, 0, 0).astype(BF)
        if not tiled:
            rest[0][...] = w_grad
            return
        store_columns(rest[0], w_grad[:, : width // 2], 0)
        store_columns(rest[1], w_grad[:, width // 2 :], 1)

    @pl.when(step == 0)
    def _():
        one(jnp.concatenate([gk0_ref[...], gk1_ref[...]], axis=1), part_ref)

    @pl.when(step == 1)
    def _():
        one(jnp.concatenate([gv0_ref[...], gv1_ref[...]], axis=1), back)
        gain_sum = jnp.zeros((1, width), F32)
        for b in range(tokens // block):
            rows = slice(b * block, (b + 1) * block)
            unit, spread = norm_stats(x_ref[rows, :].astype(F32))
            grad, gain_part = norm_back(unit, spread, gain_ref[0:1, :], back[rows, :])
            gain_sum = gain_sum + gain_part
            back[rows, :] = after_ref[rows, :] + grad
        row = iota((8, width), 0)
        gain_grad_ref[...] = jnp.where(row == 0, gain_sum, jnp.where(row == 1, g2_ref[...], jnp.where(row == 3, g4_ref[...], 0.0)))
        halves = split_halves(back[...], part)
        onehot = out_of_windows(s_ref[SHIFT], *form)
        high = halves[0].astype(BF)
        low = (halves[0] - high.astype(F32)).astype(BF)
        own_ref[0] = dot(onehot, high) + dot(onehot, low)
        other_ref[...] = dot(onehot, halves[1].astype(BF)).astype(BF)


def cross_back(scalars, gks, gvs, normed, x, after, part, gains, wx, g2, g4, pages, tiled, form, deps):
    tokens, width = x.shape
    half = tokens // 2
    cols = wx.shape[1]
    if tiled:
        shape = tile_shape(width, cols // 2)
        grads = [(shape, BF, columns_spec(width, width // 2, 1, order, lambda j: j)) for order in (0, 1)]
    else:
        grads = [(wx.shape, BF, pl.BlockSpec((width, width), lambda j, *_: (0, j)))]
    single = lambda a: (a, whole(a.shape, True))
    own_shape = (pages, half, width)
    return call(
        functools.partial(cross_back_kernel, tiled=tiled, form=form),
        "cross_back",
        [single(a) for a in (*gks, *gvs, normed, x, after, part, gains)]
        + [(wx, pl.BlockSpec((width, width), lambda j, *_: (0, j))), single(g2), single(g4)],
        [
            (own_shape, F32, page_block(own_shape)),
            ((half, width), BF, whole((half, width))),
            ((8, width), F32, whole((8, width))),
            *grads,
        ],
        grid=(2,),
        scratch=[pltpu.VMEM((tokens, width), F32)],
        scalars=scalars,
        deps=deps,
        work=(4 * tokens * width * cols, 2e7, 0),
    )


def pair_rows(own, theirs, odd):
    return jnp.where(odd == 1, jnp.concatenate([theirs, own], axis=0), jnp.concatenate([own, theirs], axis=0))


def query_in_kernel(
    s_ref, seg_ref, ok_ref, own_ref, theirs_ref, gain_ref, w_ref, x_ref, n_ref, q_ref, kv_ref, same_ref, turned_ref
):
    own_slots = own_ref.shape[1]
    x = pair_rows(own_ref[0].astype(F32), theirs_ref[:own_slots, :].astype(F32), s_ref[ODD])
    slots, total = 2 * own_slots, seg_ref.shape[1]
    reach = slots + 64
    first = s_ref[UP] == 0
    segments = jnp.where(first, seg_ref[0:1, :], seg_ref[1:2, :]).astype(F32)
    amount = 32 - s_ref[BASE]
    near = pltpu.roll(jnp.broadcast_to(segments, (8, total)), jnp.where(amount < 0, amount + total, amount), 1)
    mine = jnp.where(first, ok_ref[0:1, :], ok_ref[1:2, :]).astype(F32)
    theirs = theirs_ref[own_slots : own_slots + 1, :own_slots].astype(F32)
    valid = jnp.where(s_ref[ODD] == 1, jnp.concatenate([theirs, mine], axis=1), jnp.concatenate([mine, theirs], axis=1))
    own = pltpu.roll(near, total - 32, 1)[0:1, :slots]
    own = jnp.where(valid > 0.5, own, -1.0)
    padded = -(-reach // LANES) * LANES
    column = near[:, :padded].T[:reach, 0:1]
    same = jnp.where(column == own, 1.0, 0.0)
    same_ref[...] = same.astype(BF)
    turned_ref[...] = same.T.astype(BF)
    x_ref[...] = x.astype(BF)
    unit, _ = norm_stats(x)
    normed = (unit * gain_ref[2:3, :]).astype(BF)
    n_ref[...] = normed
    width = x.shape[1]
    q_ref[...] = dot(normed, w_ref[:, :width]).astype(BF)
    kv_ref[...] = dot(normed, w_ref[:, width:]).astype(BF)


def query_in_call(scalars, segments, slots_ok, queries, theirs, gains, w, deps):
    _, own_slots, width = queries.shape
    slots = 2 * own_slots
    reach = slots + 64
    rows = lambda w: ((slots, w), BF, whole((slots, w)))
    return call(
        query_in_kernel,
        "query_in",
        [(segments, whole(segments.shape)), (slots_ok, whole(slots_ok.shape)), (queries, page_block(queries.shape))]
        + [(a, whole(a.shape)) for a in (theirs, gains, w)],
        [rows(width), rows(width), rows(width), rows(2 * width)]
        + [(shape, BF, whole(shape)) for shape in ((reach, slots), (slots, reach))],
        deps=deps,
        scalars=scalars,
        work=(2 * slots * width * w.shape[1], 5e6, 0),
    )


def forward_blocks(pieces, slots, group):
    if pieces > 1:
        blocks = [([(0, 0, slots - 32)], False), ([(0, slots - 32, 32), (1, 0, slots), (2, 0, 32)], True)]
        blocks.append(([(2, 32, slots - 32)], False))
        return blocks + [([(k, 0, slots)], False) for k in range(3, pieces)]
    blocks = [([(0, slots - 32, slots + 64)], True)]
    if slots > 32:
        blocks.append(([(0, 0, slots - 32)], False))
    at, total = 2 * slots + 32, slots * group
    while at < total:
        size = min(256, total - at)
        blocks.append(([(0, at, size)], False))
        at += size
    return blocks


def take(refs, block):
    parts = [refs[p][at : at + size, :] for p, at, size in block]
    return parts[0] if len(parts) == 1 else jnp.concatenate([p.astype(F32) for p in parts], axis=0).astype(parts[0].dtype)


def give(refs, block, value):
    done = 0
    for p, at, size in block:
        refs[p][at : at + size, :] = value[done : done + size].astype(refs[p].dtype)
        done += size


def query_forward_kernel(*refs, pieces, blocks):
    qs = refs[:pieces]
    k_ref, v_ref, sk_ref, sv_ref, kb_ref, same_ref = refs[pieces : pieces + 6]
    outs, held = refs[pieces + 6 : 2 * pieces + 6], refs[2 * pieces + 6 :]
    pair = pl.program_id(0)
    left, masks = head_masks()
    lane = iota((1, LANES), 1)

    @pl.when(pair == 0)
    def _():
        for h in held:
            h[...] = jnp.zeros_like(h)

    @pl.when(pair < HEADS // 2)
    def _():
        keys = [jnp.where(lane == 64 * (1 - side), kb_ref[...], k_ref[...]) for side in range(2)]
        marks = [jnp.where(lane == 64 * (1 - side), 1.0, 0.0).astype(BF) for side in range(2)]
        for block, near in blocks:
            q = take(qs, block) * SCALE
            size = q.shape[0]
            all_scores = [dot(q * masks[side] + marks[side], keys[side], 1, 1) for side in range(2)]
            if near:
                same = same_ref[...].astype(F32) > 0.5
                extras = [jnp.where(same, dot(q * masks[side], sk_ref[...], 1, 1), MASKED) for side in range(2)]
            mixed, columns = [], jnp.zeros((size, LANES), F32)
            for side in range(2):
                scores = all_scores[side]
                peak = jnp.max(scores, axis=-1, keepdims=True)
                if near:
                    peak = jnp.maximum(peak, jnp.max(extras[side], axis=-1, keepdims=True))
                raised = jnp.exp(scores - peak)
                total = jnp.sum(raised, axis=-1, keepdims=True)
                value = dot(raised.astype(BF), v_ref[...])
                if near:
                    raised = jnp.exp(extras[side] - peak)
                    total = total + jnp.sum(raised, axis=-1, keepdims=True)
                    value = value + dot(raised.astype(BF), sv_ref[...])
                mixed.append(value * (1.0 / total))
                columns = columns + place_lanes(peak + jnp.log(total), lane, 2 * pair + side)
            give(outs, block, jnp.where(left, mixed[0], mixed[1]))
            done = 0
            for p, at, rows in block:
                held[p][at : at + rows, :] += columns[done : done + rows]
                done += rows

    @pl.when(pair == HEADS // 2)
    def _():
        for out, h in zip(outs, held):
            out[...] = h[...].astype(BF)


def query_forward(qs, cross, slot_kv, key_bias, same, blocks, deps):
    width = qs[0].shape[1]
    patches, slots = cross.shape[0], slot_kv.shape[0]
    pairs = HEADS // 2
    total = sum(q.shape[0] for q in qs)
    col = lambda rows, first: pl.BlockSpec((rows, LANES), lambda p: (0, first + jnp.minimum(p, pairs - 1)))
    return call(
        functools.partial(query_forward_kernel, pieces=len(qs), blocks=blocks),
        "query_forward",
        [(q, col(q.shape[0], 0)) for q in qs]
        + [(cross, col(patches, 0)), (cross, col(patches, pairs)), (slot_kv, col(slots, 0)), (slot_kv, col(slots, pairs))]
        + [(a, whole(a.shape)) for a in (key_bias, same)],
        [((q.shape[0], width + LANES), BF, pl.BlockSpec((q.shape[0], LANES), lambda p: (0, p))) for q in qs],
        grid=(pairs + 1,),
        scratch=[pltpu.VMEM((q.shape[0], LANES), F32) for q in qs],
        deps=deps,
        work=(16 * total * patches * width, 1e7, total * patches * HEADS),
    )


def stat_lanes(stats, head, first, base):
    row, col = iota((LANES, LANES), 0), iota((LANES, LANES), 1)
    hit = (row == first + head + 16 * (col - base)) & (col >= base) & (col < base + 3)
    return dot(stats, jnp.where(hit, -1.0, 0.0).astype(BF)).astype(BF)


def query_back_kernel(*refs, pieces, blocks, near_block, first_pair):
    qs, gos, stats = refs[:pieces], refs[pieces : 2 * pieces], refs[2 * pieces : 3 * pieces]
    k_ref, v_ref, sk_ref, sv_ref, kb_ref, same_ref = refs[3 * pieces : 3 * pieces + 6]
    dqs = refs[3 * pieces + 6 : 4 * pieces + 6]
    dk_ref, dv_ref, dsk_ref, dsv_ref, sum_k, sum_v = refs[4 * pieces + 6 : 4 * pieces + 12]
    near_dqs = refs[4 * pieces + 12 :]
    pair = pl.program_id(0) + first_pair
    left, masks = head_masks()
    lane = iota((1, LANES), 1)
    bases = (64, 0)
    ones = [jnp.where((lane >= b) & (lane < b + 3), 1.0, 0.0).astype(BF) for b in bases]
    plain = [jnp.where(lane == b + 3, 1.0, 0.0).astype(BF) for b in bases]
    keys = [jnp.where(lane == bases[s] + 3, kb_ref[...], k_ref[...] * masks[s] + ones[s]) for s in range(2)]
    values = [v_ref[...] * masks[s] + ones[s] for s in range(2)]

    def sides(block):
        q, g, st = take(qs, block), take(gos, block), take(stats, block)
        scaled = q * SCALE
        shifted = [scaled * masks[s] + (stat_lanes(st, 2 * pair + s, 0, bases[s]) + plain[s]) for s in range(2)]
        lowered = [g * masks[s] + stat_lanes(st, 2 * pair + s, 48, bases[s]) for s in range(2)]
        return q, g, shifted, lowered

    for ref in near_dqs:
        ref[...] = jnp.zeros_like(ref)
    q, g, shifted, lowered = sides(near_block)
    same = same_ref[...].astype(F32) > 0.5
    moved, dsk, dsv = [], [], []
    for s in range(2):
        scores = dot(sk_ref[...] * masks[s] + ones[s], shifted[s], 1, 1)
        probs = jnp.exp(jnp.where(same, scores, MASKED))
        dscore = (probs * dot(sv_ref[...] * masks[s] + ones[s], lowered[s], 1, 1)).astype(BF)
        dsk.append(dot(dscore, q))
        dsv.append(dot(probs.astype(BF), g))
        moved.append(dot(dscore, sk_ref[...], 0, 0))
    give(near_dqs, near_block, jnp.where(left, moved[0], moved[1]))
    dsk_ref[...] = (jnp.where(left, dsk[0], dsk[1]) * SCALE).astype(BF)
    dsv_ref[...] = jnp.where(left, dsv[0], dsv[1]).astype(BF)

    for number, block in enumerate(blocks):
        q, g, shifted, lowered = sides(block)
        scores = [dot(keys[s], shifted[s], 1, 1) for s in range(2)]
        grads = [dot(values[s], lowered[s], 1, 1) for s in range(2)]
        dq, dk, dv = [], [], []
        for s in range(2):
            probs = jnp.exp(scores[s])
            dscore = (probs * grads[s]).astype(BF)
            dv.append(dot(probs.astype(BF), g))
            dk.append(dot(dscore, q))
            dq.append(dot(dscore, k_ref[...], 0, 0))
        near = take(near_dqs, block)
        give(dqs, block, (jnp.where(left, dq[0], dq[1]) + near) * SCALE)
        if number == 0:
            sum_k[...] = jnp.where(left, dk[0], dk[1])
            sum_v[...] = jnp.where(left, dv[0], dv[1])
        else:
            sum_k[...] += jnp.where(left, dk[0], dk[1])
            sum_v[...] += jnp.where(left, dv[0], dv[1])
    dk_ref[...] = (sum_k[...] * SCALE).astype(BF)
    dv_ref[...] = sum_v[...].astype(BF)


def query_backward(qs, gos, cross, slot_kv, key_bias, same, near_block, part, deps):
    patches, slots = cross.shape[0], slot_kv.shape[0]
    pairs = HEADS // 2
    count = pairs // 2
    width = count * LANES
    total = sum(q.shape[0] for q in qs)
    blocks = []
    for number, q in enumerate(qs):
        step = min(256, q.shape[0])
        blocks += [[(number, at, step)] for at in range(0, q.shape[0], step)]
    col = lambda rows, first: pl.BlockSpec((rows, LANES), lambda p: (0, first + part * count + p))
    out = lambda rows: ((rows, width), BF, pl.BlockSpec((rows, LANES), lambda p: (0, p)))
    found = call(
        functools.partial(
            query_back_kernel, pieces=len(qs), blocks=blocks, near_block=near_block, first_pair=part * count
        ),
        "query_backward",
        [(q, col(q.shape[0], 0)) for q in qs]
        + [(g, col(g.shape[0], 0)) for g in gos]
        + [(g, pl.BlockSpec((g.shape[0], LANES), lambda p: (0, pairs))) for g in gos]
        + [(cross, col(patches, 0)), (cross, col(patches, pairs)), (slot_kv, col(slots, 0)), (slot_kv, col(slots, pairs))]
        + [(a, whole(a.shape)) for a in (key_bias, same)],
        [out(q.shape[0]) for q in qs] + [out(patches), out(patches), out(slots), out(slots)],
        grid=(count,),
        scratch=[pltpu.VMEM((patches, LANES), F32)] * 2 + [pltpu.VMEM((q.shape[0], LANES), F32) for q in qs],
        deps=deps,
        work=(20 * total * patches * width, 1.5e7, total * patches * HEADS // 2),
    )
    return found[: len(qs)], *found[len(qs) :]


def query_ffn_kernel(s_ref, *refs, parts, tiled):
    outs = refs[:parts]
    x_ref, own_ref, theirs_ref, gain_ref, wo_ref, up_ref, down_ref = refs[parts : parts + 7]
    (
        out_own_ref, out_other_ref, grad_ref, send_ref, att_ref, normed_ref, act_ref, dact_ref, branch_ref, cot_ref,
        gain_grad_ref, mixed, after, total, back, joint,
    ) = refs[parts + 7 :]
    step = pl.program_id(0)
    width = x_ref.shape[1]

    @pl.when(step == 0)
    def _():
        each = [join_lanes(o[:, width:].astype(F32), 0) for o in outs]
        peak = functools.reduce(jnp.maximum, each)
        weights = [jnp.exp(e - peak) for e in each]
        weight_sum = functools.reduce(jnp.add, weights)
        joint[...] = peak + jnp.log(weight_sum)
        value = None
        for o, w in zip(outs, weights):
            term = o[:, :width].astype(F32) * spread_heads(w / weight_sum, width)
            value = term if value is None else value + term
        mixed[...] = value
        att_ref[...] = value.astype(BF)
        rows = x_ref[...].astype(F32) + dot(att_ref[...], wo_ref[...])
        after[...] = rows
        unit, _ = norm_stats(rows)
        normed_ref[...] = (unit * gain_ref[3:4, :]).astype(BF)
        cot_ref[...] = pair_rows(own_ref[0].astype(F32), theirs_ref[...].astype(F32), s_ref[ODD]).astype(BF)
        total[...] = jnp.zeros_like(total)
        back[...] = jnp.zeros_like(back)

    grads = dot(cot_ref[...], down_ref[...], 1, 1)
    value, slope = gelu_pair(dot(normed_ref[...], up_ref[...]))
    dact = (slope * grads).astype(BF)
    dact_ref[...] = dact
    back[...] += dot(dact, up_ref[...], 1, 1)
    act = value.astype(BF)
    act_ref[...] = act
    total[...] += dot(act, down_ref[...])

    @pl.when(step == pl.num_programs(0) - 1)
    def _():
        rows = after[...] + total[...]
        own_slots = rows.shape[0] // 2
        low, high = rows[:own_slots], rows[own_slots:]
        odd = s_ref[ODD] == 1
        out_own_ref[0] = jnp.where(odd, high, low).astype(BF)
        out_other_ref[...] = jnp.where(odd, low, high).astype(BF)
        unit, spread = norm_stats(after[...])
        grad, gain_part = norm_back(unit, spread, gain_ref[3:4, :], back[...])
        gain_grad_ref[...] = jnp.broadcast_to(gain_part, gain_grad_ref.shape)
        grad = cot_ref[...].astype(F32) + grad
        grad_ref[...] = grad
        branch = grad.astype(BF)
        branch_ref[...] = branch
        sent = dot(branch, wo_ref[...], 1, 1).astype(BF)
        send_ref[:, :width] = sent
        pick = (iota((width, LANES), 0) // (width // HEADS) == iota((width, LANES), 1)).astype(F32).astype(BF)
        high, middle, low = three_parts(sent.astype(F32) * mixed[...])
        inner = dot(high.astype(BF), pick) + dot(middle.astype(BF), pick) + dot(low.astype(BF), pick)
        lane = iota((1, LANES), 1)
        packed = jnp.zeros(inner.shape, F32)
        for source, first in ((joint[...], 0), (inner, 48)):
            kept = jnp.where(lane < HEADS, source, 0.0)
            for number, piece in enumerate(three_parts(kept)):
                amount = first + 16 * number
                packed = packed + (piece if amount == 0 else pltpu.roll(piece, amount, 1))
        send_ref[:, width:] = packed.astype(BF)


def query_ffn(scalars, outs, x, cot, cot_theirs, gains, wo, up, down, tiled, deps, chunk=768):
    slots, width = x.shape
    hidden = up.shape[1]
    rows = lambda w, kind: ((slots, w), kind, whole((slots, w)))
    chunks = ((slots, hidden), BF, pl.BlockSpec((slots, chunk), lambda j, *_: (0, j)))
    half = (slots // 2, width)
    return call(
        functools.partial(query_ffn_kernel, parts=len(outs), tiled=tiled),
        "query_ffn",
        [(a, whole(a.shape)) for a in (*outs, x)]
        + [(cot, page_block(cot.shape))]
        + [(a, whole(a.shape)) for a in (cot_theirs, gains, wo)]
        + [
            (up, pl.BlockSpec((width, chunk), lambda j, *_: (0, j))),
            (down, pl.BlockSpec((chunk, width), lambda j, *_: (j, 0))),
        ],
        [
            (cot.shape, BF, page_block(cot.shape)), (half, BF, whole(half)), rows(width, F32), rows(width + LANES, BF),
            rows(width, BF), rows(width, BF), chunks, chunks, rows(width, BF), rows(width, BF), ((8, width), F32, whole((8, width))),
        ],
        grid=(hidden // chunk,),
        scratch=[pltpu.VMEM((slots, width), F32)] * 4 + [pltpu.VMEM((slots, LANES), F32)],
        scalars=scalars,
        deps=deps,
        work=(8 * slots * width * hidden, 2e7, slots * hidden),
    )


def query_weights_kernel(normed_ref, cot_ref, att_ref, branch_ref, act_ref, dact_ref, wo_ref, up_ref, down_ref, *, tiled):
    put_grad(up_ref, dot(normed_ref[...], dact_ref[...], 0, 0).astype(BF), store_columns, 0, tiled)
    put_grad(down_ref, dot(act_ref[...], cot_ref[...], 0, 0).astype(BF), store_strips, 1, tiled)

    @pl.when(pl.program_id(0) == 0)
    def _():
        put_grad(wo_ref, dot(att_ref[...], branch_ref[...], 0, 0).astype(BF), store_all, 1, tiled)


def query_weights(normed, cot, att, branch, act, dact, tiled, deps, chunk=768):
    slots, width = normed.shape
    hidden = act.shape[1]
    return call(
        functools.partial(query_weights_kernel, tiled=tiled),
        "query_weights",
        [(a, whole((slots, width))) for a in (normed, cot, att, branch)]
        + [(a, pl.BlockSpec((slots, chunk), lambda j: (0, j))) for a in (act, dact)],
        grad_forms(width, hidden, chunk, tiled, 1),
        grid=(hidden // chunk,),
        deps=deps,
        work=(4 * slots * width * hidden, 1.6e7, 0),
    )


def query_out_kernel(s_ref, *refs, parts, tiled):
    halves = [refs[:parts], refs[parts : 2 * parts]]
    others = refs[2 * parts : 2 * parts + 4]
    n_ref, x_ref, grad_ref, gain_ref, w_ref, rows_ref = refs[2 * parts + 4 : 2 * parts + 10]
    own_ref, other_ref, w_grad_ref, gain_grad_ref = refs[2 * parts + 10 : 2 * parts + 14]
    width = x_ref.shape[1]
    sums = []
    for dqs in halves:
        value = dqs[0][...].astype(F32)
        for d in dqs[1:]:
            value = value + d[...].astype(F32)
        sums.append(value.astype(BF))
    join = lambda a, b: jnp.concatenate([a, b], axis=1)
    pieces = [join(*sums), join(others[0][...], others[1][...]), join(others[2][...], others[3][...])]
    back = None
    for number, piece in enumerate(pieces):
        cols = slice(number * width, (number + 1) * width)
        term = dot(piece, w_ref[:, cols], 1, 1)
        back = term if back is None else back + term
        (refs[-1] if tiled else w_grad_ref)[:, cols] = dot(n_ref[...], piece, 0, 0).astype(BF)
    if tiled:
        store_all(w_grad_ref, refs[-1][...], 1)
    unit, spread = norm_stats(x_ref[...].astype(F32))
    grad, gain_part = norm_back(unit, spread, gain_ref[2:3, :], back)
    rows = grad_ref[...] + grad
    own_slots = rows.shape[0] // 2
    low, high = rows[:own_slots], rows[own_slots:]
    odd = s_ref[ODD] == 1
    own_ref[0] = jnp.where(odd, high, low)
    other_ref[...] = jnp.where(odd, low, high).astype(BF)
    gain_rows = rows_ref[...] + jnp.where(iota((8, width), 0) == 2, gain_part, 0.0)
    if not tiled:
        gain_grad_ref[...] = gain_rows
        return
    turned = gain_rows.T
    size = width // 16
    lane = iota((1, LANES), 1)
    for half in range(2):
        tile = jnp.where(lane == 0, turned[:, 2 * half : 2 * half + 1], 0.0)
        tile = jnp.where(lane == 1, turned[:, 2 * half + 1 : 2 * half + 2], tile).astype(BF)
        for strip in range(8):
            for core in range(2):
                at = (2 * strip + core) * size
                gain_grad_ref[(core, *tile_index(strip, half, 0), slice(None), slice(None))] = tile[at : at + size]


def query_out(scalars, dqs, dks, dvs, normed, x, grad, gains, w, gain_rows, pages, tiled, deps):
    slots, width = x.shape
    own_shape = (pages, slots // 2, width)
    w_shape = tile_shape(width, w.shape[1]) if tiled else w.shape
    g_shape, g_kind = (tile_shape(width, 256), BF) if tiled else ((8, width), F32)
    ins = (*dqs[0], *dqs[1], *dks, *dvs, normed, x, grad, gains, w, gain_rows)
    return call(
        functools.partial(query_out_kernel, parts=len(dqs[0]), tiled=tiled),
        "query_out",
        [(a, whole(a.shape, True)) for a in ins],
        [
            (own_shape, F32, page_block(own_shape)),
            ((slots // 2, width), BF, whole((slots // 2, width))),
            (w_shape, BF, whole(w_shape)),
            (g_shape, g_kind, whole(g_shape)),
        ],
        scratch=[pltpu.VMEM(w.shape, BF)] if tiled else [],
        scalars=scalars,
        deps=deps,
        work=(4 * slots * width * w.shape[1], 1e7, 0),
    )


PAIR = pl.DeviceIdType.MESH


def coordinates():
    page, strip = lax.axis_index("page"), lax.axis_index("strip")
    core, x = lax.rem(page, 2), page // 2
    y, z_low, z_high = lax.rem(strip, 2), lax.rem(strip // 2, 2), strip // 4
    flip = lambda index, bit, weight: index + weight - 2 * weight * bit
    core_mate = (flip(page, core, 1), strip)
    mates = {
        "x": (x, (flip(page, x, 2), strip)),
        "y": (y, (page, flip(strip, y, 1))),
        "low": (z_low, (page, flip(strip, z_low, 2))),
        "high": (z_high, (page, flip(strip, z_high, 4))),
    }
    return core, core_mate, [[mates[k] for k in ("y", "x", "low", "high")], [mates[k] for k in ("x", "y", "low", "high")]]


def meet(mates):
    barrier = pltpu.get_barrier_semaphore()
    for mate in mates:
        pl.semaphore_signal(barrier, inc=1, device_id=mate, device_id_type=PAIR)
    pl.semaphore_wait(barrier, len(mates))


def send(source, target, sems, number, mate):
    copy = pltpu.make_async_remote_copy(
        src_ref=source,
        dst_ref=target,
        send_sem=sems.at[0, number],
        recv_sem=sems.at[1, number],
        device_id=mate,
        device_id_type=PAIR,
    )
    copy.start()
    return copy


def add_rows(target, first, source, start, length, at, rows):
    span = pl.ds(at, rows)

    def step(i, carry):
        total = target[first + i, span, :].astype(F32) + source[start + i, span, :].astype(F32)
        target[first + i, span, :] = total.astype(BF)
        return carry

    lax.fori_loop(0, length, step, 0)


def query_sum_kernel(*refs, rows):
    up_ref, down_ref, wo_ref, normed_ref, cot_ref, att_ref, branch_ref, act_ref, dact_ref = refs[:9]
    outs = refs[9:13]
    own_up, own_down, own_wo, held_0, held_1, remote, near = refs[13:]
    held = (held_0, held_1)
    core, core_mate, orders = coordinates()
    meet([core_mate])
    wide, small = rows
    far, mine = [], []
    for number, (grad, order, at, size) in enumerate(((up_ref, 0, 0, wide), (down_ref, 1, 0, wide), (wo_ref, 0, 2 * wide, small))):
        span, bit = pl.ds(at, size), orders[order][0][0]
        far.append(send(grad.at[1 - core], held[order].at[:, :, :, span, :], remote, number, core_mate))
        for which in range(2):
            first = bit if which else 1 - bit
            copy = pltpu.make_async_copy(
                grad.at[core, first], outs[2 * order + which].at[:, :, span, :], near.at[2 * number + which]
            )
            copy.start()
            mine.append(copy)
    width = normed_ref.shape[1]
    own_rows = ((own_up, 0, wide, wide), (own_down, 1, wide, wide), (own_wo, 1, 2 * wide, small))
    store_all(own_wo, dot(att_ref[...], branch_ref[...], 0, 0).astype(BF), 1)
    for j in range(act_ref.shape[1] // width):
        cols = slice(j * width, (j + 1) * width)
        store_columns(own_up, dot(normed_ref[...], dact_ref[:, cols], 0, 0).astype(BF), 0, j // 2, (j % 2) * (width // LANES))
        store_strips(own_down, dot(act_ref[:, cols], cot_ref[...], 0, 0).astype(BF), 1, (j % 2) * 2 + j // 2)
    later = []
    for number, (grad, order, at, size) in enumerate(own_rows):
        later.append(send(grad.at[1 - core], held[order].at[:, :, :, pl.ds(at, size), :], remote, 3 + number, core_mate))
    for copy in far + mine:
        copy.wait()

    def add(order, at, size, own):
        bit = orders[order][0][0]
        span = pl.ds(at, size)
        for which in range(2):
            out, first = outs[2 * order + which], bit if which else 1 - bit
            for i in range(2):

                def step(z, carry, out=out, first=first, i=i):
                    mine = out[i, z, span, :] if own is None else own[core, first, i, z]
                    out[i, z, span, :] = (mine.astype(F32) + held[order][first, i, z, span, :].astype(F32)).astype(BF)
                    return carry

                lax.fori_loop(0, 4, step, 0)

    for order, at, size in ((0, 0, wide), (1, 0, wide), (0, 2 * wide, small)):
        add(order, at, size, None)
    for copy, (grad, order, at, size) in zip(later, own_rows):
        copy.wait()
        add(order, at, size, grad)


def query_sum(patch_grads, normed, cot, att, branch, act, dact, collective, deps):
    width, hidden = normed.shape[1], act.shape[1]
    shapes = [tile_shape(width, hidden), tile_shape(hidden, width), tile_shape(width, width)]
    rows = (shapes[0][-2], shapes[2][-2])
    total = 2 * rows[0] + rows[1]
    vmem = pl.BlockSpec(memory_space=pltpu.VMEM)
    kernel = functools.partial(query_sum_kernel, rows=rows)
    outs = pl.pallas_call(
        lambda *refs: kernel(*refs[:9], *refs[9 + len(deps) :]),
        in_specs=[ANY] * 3 + [vmem] * 6 + [ANY] * len(deps),
        out_specs=[vmem] * 4,
        out_shape=[sds((2, 4, total, LANES), BF)] * 4,
        scratch_shapes=[
            *[pltpu.VMEM(shape, BF) for shape in shapes],
            pltpu.VMEM((2, 2, 4, total, LANES), BF),
            pltpu.VMEM((2, 2, 4, total, LANES), BF),
            pltpu.SemaphoreType.DMA((2, 6)),
            pltpu.SemaphoreType.DMA((6,)),
        ],
        compiler_params=pltpu.CompilerParams(collective_id=collective, has_side_effects=True, vmem_limit_bytes=VMEM_BYTES),
        name="query_sum",
    )(*patch_grads, normed, cot, att, branch, act, dact, *deps)
    return [out.reshape(8, total, LANES) for out in outs]


ORDERS = (("y", "x", "low", "high"), ("x", "y", "low", "high"))
PLACES = {"x": BIT_X, "y": BIT_Y, "low": BIT_LOW, "high": BIT_HIGH}


def across(array, name):
    axis, weight = {"x": ("page", 2), "y": ("strip", 1), "low": ("strip", 2), "high": ("strip", 4)}[name]
    return lax.ppermute(array, axis, [(i, i ^ weight) for i in range(lax.axis_size(axis))])


def halve_add_kernel(s_ref, *refs):
    for k in range(4):
        keep, got, out = refs[2 * k], refs[2 * k + 1], refs[8 + k]
        out[...] = (keep[...].astype(F32) + got[...].astype(F32)).astype(BF)


def halve_add(scalars, kept, got, stage, deps):
    ins, outs = [], []
    for order in range(2):
        size = kept[order].shape[0] // 2
        shape = kept[order].shape[1:]
        place = PLACES[ORDERS[order][stage]]
        for flip in (1, 0):
            spec = pl.BlockSpec(
                (1, *shape),
                lambda i, s, place=place, flip=flip, size=size: ((1 - s[place] if flip else s[place]) * size + i, 0, 0),
            )
            ins += [(kept[order], spec), (got[order], spec)]
            outs.append(((size, *shape), BF, pl.BlockSpec((1, *shape), lambda i, s: (i, 0, 0))))
    return call(
        halve_add_kernel, "halve_add", ins, outs, grid=(size,), scalars=scalars, deps=deps, work=(1e6, 6 * size * 1296 * 512, 0)
    )


def late_sum_kernel(*refs, lots, arrays, early_rows):
    grads = refs[:arrays]
    early = refs[arrays : arrays + 4]
    own, got = refs[arrays + 4 : arrays + 6], refs[arrays + 6 : arrays + 8]
    sums, first_held = refs[arrays + 8 : arrays + 10], refs[arrays + 10 : arrays + 12]
    held = [refs[arrays + 12 : arrays + 16], refs[arrays + 16 : arrays + 20]]
    done, loaded, early_held = refs[arrays + 20 : arrays + 22], refs[arrays + 22 : arrays + 26], refs[arrays + 26 : arrays + 28]
    remote, near = refs[arrays + 28 :]
    core, core_mate, orders = coordinates()
    meet([core_mate] + [mate for _, mate in orders[0]])
    numbers, local_numbers = iter(range(1000)), iter(range(1000))
    jobs = []
    for order, at, members in lots:
        copies, first = [], at
        for member, start, rows in members:
            there, span = pl.ds(start, rows), pl.ds(first, rows)
            first += rows
            copies.append(
                send(grads[member].at[1 - core, :, there, :], first_held[order].at[:, span, :], remote, next(numbers), core_mate)
            )
            copy = pltpu.make_async_copy(
                grads[member].at[core, :, there, :], sums[order].at[:, span, :], near.at[next(local_numbers)]
            )
            copy.start()
            copies.append(copy)
        jobs.append((order, at, first - at, copies))
    loads = []
    for k in range(4):
        copy = pltpu.make_async_copy(early[k], loaded[k], near.at[next(local_numbers)])
        copy.start()
        loads.append(copy)
    for copy in loads:
        copy.wait()
    early_flights = []
    for order in range(2):
        bit, mate = orders[order][3]
        kept = loaded[2 * order]
        add_rows(kept, 1 - bit, loaded[2 * order + 1], 1 - bit, 1, 0, early_rows)
        early_flights.append(send(kept.at[1 - bit], early_held[order], remote, next(numbers), mate))
        add_rows(kept, bit, loaded[2 * order + 1], bit, 1, 0, early_rows)
    bases = [0] * len(jobs)
    flights = [None] * len(jobs)
    first_exchange = []
    for stage in range(4):
        size = 8 >> stage
        for n, (order, at, rows, copies) in enumerate(jobs):
            source = first_held[order] if stage == 0 else held[order][stage - 1]
            for copy in copies if stage == 0 else [flights[n]]:
                copy.wait()
            bit, mate = orders[order][stage]
            out, keep = size * (1 - bit), size * bit
            base = bases[n]
            add_rows(sums[order], base + out, source, out, size, at, rows)
            flights[n] = send(
                sums[order].at[pl.ds(base + out, size), pl.ds(at, rows), :],
                held[order][stage].at[:, pl.ds(at, rows), :],
                remote,
                next(numbers),
                mate,
            )
            add_rows(sums[order], base + keep, source, keep, size, at, rows)
            bases[n] = base + keep
        if stage == 2:
            for order in range(2):
                early_flights[order].wait()
                total = loaded[2 * order][orders[order][3][0]].astype(F32) + early_held[order][...].astype(F32)
                own[order][:early_rows, :] = total.astype(BF)
                span = pl.ds(0, early_rows)
                first_exchange.append(send(own[order].at[span, :], done[order].at[span, :], remote, next(numbers), core_mate))
    exchange = []
    for n, (order, at, rows, _) in enumerate(jobs):
        flights[n].wait()
        value = sums[order][bases[n], pl.ds(at, rows), :].astype(F32) + held[order][3][0, pl.ds(at, rows), :].astype(F32)
        span = pl.ds(early_rows + at, rows)
        own[order][span, :] = value.astype(BF)
        exchange.append(send(own[order].at[span, :], done[order].at[span, :], remote, next(numbers), core_mate))
    for copy in first_exchange + exchange:
        copy.wait()
    for order in range(2):
        got[order][...] = done[order][...]


def late_sum(grads, lots, rows, early, collective, deps):
    grads = [g.reshape(2, 16, *g.shape[-2:]) for g in grads]
    arrays = len(grads)
    members = sum(len(lot[2]) for lot in lots)
    early_rows = early[0].shape[1]
    share = [sds((early_rows + r, LANES), BF) for r in rows]
    vmem = lambda *shape: pltpu.VMEM(shape, BF)
    kernel = functools.partial(late_sum_kernel, lots=lots, arrays=arrays, early_rows=early_rows)
    first = arrays + 4
    return pl.pallas_call(
        lambda *refs: kernel(*refs[:first], *refs[first + len(deps) :]),
        in_specs=[ANY] * (first + len(deps)),
        out_specs=[pl.BlockSpec(memory_space=pltpu.VMEM)] * 4,
        out_shape=share + share,
        scratch_shapes=[
            *[vmem(16, r, LANES) for r in rows],
            *[vmem(16, r, LANES) for r in rows],
            *[vmem(8 >> k, rows[0], LANES) for k in range(4)],
            *[vmem(8 >> k, rows[1], LANES) for k in range(4)],
            *[vmem(early_rows + r, LANES) for r in rows],
            *[vmem(2, early_rows, LANES)] * 4,
            *[vmem(early_rows, LANES)] * 2,
            pltpu.SemaphoreType.DMA((2, members + 5 * len(lots) + 4)),
            pltpu.SemaphoreType.DMA((members + 4,)),
        ],
        compiler_params=pltpu.CompilerParams(collective_id=collective, has_side_effects=True, vmem_limit_bytes=VMEM_BYTES),
        name="late_sum",
    )(*grads, *early, *deps)


def finish_kernel(core_ref, own0, own1, got0, got1, gain_ref, *outs, plan):
    first = core_ref[0] == 0
    owns, gots = (own0, own1), (got0, got1)
    lane = iota((1, LANES), 1)
    left = lane < 64

    def tile(order, at, size, part):
        mine = owns[order][at : at + size, :].astype(F32)
        theirs = gots[order][at : at + size, :].astype(F32)
        return jnp.where(first == (part == 0), mine, theirs)

    for out, (size, tiles, flipped) in zip(outs, plan):
        count = len(tiles)
        for part in range(2):
            rows = slice(part * size, (part + 1) * size)
            values = [tile(order, at, size, part) for order, at in tiles]
            if count % 2 == 0:
                for t in range(count // 2):
                    out[rows, t * LANES : (t + 1) * LANES] = jnp.where(first, values[t], values[t + count // 2])
                continue
            turned = [pltpu.roll(v, 64, 1) for v in values[count // 2 :]]
            whole_tiles = [
                jnp.where(first, values[t], jnp.where(left, turned[t], turned[t + 1])) for t in range(count // 2)
            ]
            rest = jnp.where(first, values[count // 2], turned[-1])
            if flipped:
                for t, value in enumerate(whole_tiles):
                    for at in range(0, size, 64):
                        column = part * size + at
                        out[t * LANES : (t + 1) * LANES, column : column + 64] = value[at : at + 64].T
                for at in range(0, size, 64):
                    column = part * size + at
                    out[count // 2 * LANES :, column : column + 64] = rest[at : at + 64].T[:64]
                continue
            for t, value in enumerate(whole_tiles):
                out[rows, t * LANES : (t + 1) * LANES] = value
            out[rows, count // 2 * LANES :] = rest[:, :64]
    size = gain_ref.shape[1] // 2
    at = own0.shape[0] - size
    gain = jnp.concatenate([tile(0, at, size, part) for part in range(2)], axis=0).T
    gain_ref[...] = jnp.where(first, gain[0:1], gain[1:2])


def finish(core, shares, shapes, plan, gain_rows):
    vmem = pl.BlockSpec(memory_space=pltpu.VMEM)
    outs = [shape[::-1] if flipped else shape for shape, (_, _, flipped) in zip(shapes, plan)]
    gain, *found = pl.pallas_call(
        functools.partial(finish_kernel, plan=plan),
        in_specs=[pl.BlockSpec(memory_space=pltpu.SMEM)] + [vmem] * 4,
        out_specs=[vmem] * (1 + len(outs)),
        out_shape=[sds((1, gain_rows), F32)] + [sds(shape, F32) for shape in outs],
        compiler_params=pltpu.CompilerParams(vmem_limit_bytes=VMEM_BYTES),
        name="finish",
    )(core, *shares)
    return gain.T, *[f.T if flipped else f for f, (_, _, flipped) in zip(found, plan)]


def from_ahead(array, count, distance):
    return lax.ppermute(array, "strip", [(i, (i - distance) % count) for i in range(count)])


def from_partner(array, count):
    return lax.ppermute(array, "strip", [(i, i ^ 1) for i in range(count)])


def scattered(grad):
    strips, pages = lax.axis_size("strip"), lax.axis_size("page")
    rows, cols = grad.shape
    part = lax.psum_scatter(grad, "strip", scatter_dimension=0, tiled=True)
    part = part.reshape(rows // strips, pages, cols // pages).transpose(1, 0, 2)
    return lax.psum_scatter(part, "page", scatter_dimension=0, tiled=False).astype(F32)


def local(
    visual_in, query_in, row_valid, segment_ids, slot_valid, col_shift, row_shifted, norm_gains,
    w_vqkv, w_vout, w_up, w_down, w_qqkv, w_xkv, w_qout, w_qup, w_qdown, visual_cot, query_cot,
):
    pages, strip_rows, columns, width = visual_in.shape
    own_slots, all_slots = query_in.shape[1], segment_ids.shape[1]
    count = lax.axis_size("strip")
    tiled = count == 8
    group = count // 2
    half = strip_rows * columns
    slots = 2 * own_slots
    window = WIN * WIN
    form = (strip_rows, columns)
    place, page = lax.axis_index("strip"), lax.axis_index("page")
    odd = place % 2
    up = jnp.where(odd == 1, 1 - row_shifted[0], row_shifted[0])
    down = 1 - up
    pick = lambda array, which: lax.dynamic_index_in_dim(array, which, 0, keepdims=False)
    scalars = jnp.stack([up, pick(col_shift, up), odd, page % 2, page // 2, odd, place // 2 % 2, place // 4, (place // 2) * slots]).astype(jnp.int32)

    visual, cot = visual_in.reshape(pages, half, width), visual_cot.reshape(pages, half, width)
    query_sent, patch_sent = pack(scalars, [(query_in, slot_valid), (visual, row_valid)])
    query_theirs = from_partner(query_sent, count)
    patch_sent = held_back(patch_sent, [query_theirs])
    patch_other = from_ahead(patch_sent, count, 1)
    gains = jnp.pad(norm_gains.T, ((0, 4), (0, 0)))

    order = [-1] + list(range(group - 1))
    blocks = forward_blocks(group if tiled else 1, slots, group)
    near_block = next(block for block, near in blocks if near)

    def gather(array):
        pieces = [array if k == 0 else from_ahead(array, count, 2 * k) for k in order]
        return pieces if tiled else [jnp.concatenate(pieces, axis=0)]

    def give_back(arrays):
        if not tiled:
            arrays = [arrays[0][n * slots : (n + 1) * slots] for n in range(group)]
        return [piece if k == 0 else from_ahead(piece, count, -2 * k) for piece, k in zip(arrays, order)]

    x_query, normed_three, q_own, slot_kv, same, turned = query_in_call(
        scalars, segment_ids, slot_valid, query_in, query_theirs, gains, w_qqkv, [patch_sent]
    )
    qs = gather(q_own)
    cot_sent, cot_q_sent = pack_two(scalars, cot, query_cot, [q_own])
    cot_other, cot_theirs = from_ahead(cot_sent, count, 1), from_partner(cot_q_sent, count)
    x, normed_one, qkv, cross, key_bias = patch_in(
        scalars, row_valid, visual, patch_other, gains, w_vqkv, w_xkv, form, [cot_q_sent]
    )
    att = window_forward(qkv, window, [])
    q_out = query_forward(qs, cross, slot_kv, key_bias, same, blocks, [att, cot_theirs])
    out_parts = give_back(q_out)
    (vis_own, vis_other, grad_after, grad_att, g_vout, g_up, g_down, gain_two) = patch_ffn(
        scalars, att, x, cot, cot_other, gains, w_vout, w_up, w_down, tiled, form, [q_out[0]]
    )
    vis_came = from_ahead(vis_other, count, -1)
    (q_res, q_res_other, grad_q, send_q, att_q, normed_four, act_q, dact_q, branch_q, cot_q, gain_four) = query_ffn(
        scalars, out_parts, x_query, query_cot, cot_theirs, gains, w_qout, w_qup, w_qdown, tiled, [gain_two]
    )
    gos = gather(send_q)
    res_came = from_partner(q_res_other, count)
    if tiled:
        out_0, keep_0, out_1, keep_1 = query_sum(
            [g_up, g_down, g_vout], normed_four, cot_q, att_q, branch_q, act_q, dact_q, 0, []
        )
        got = [across(out_0, "y"), across(out_1, "x")]
        last = keep_0
    else:
        g_qout, g_qup, g_qdown = query_weights(normed_four, cot_q, att_q, branch_q, act_q, dact_q, tiled, [])
        last = g_qout
    g_proj = window_backward(qkv, grad_att, window, [last, vis_came])
    last = [g_proj, res_came]
    dqs, dks, dvs, dsks, dsvs = [], [], [], [], []
    for part in range(2):
        dq, dk, dv, dsk, dsv = query_backward(qs, gos, cross, slot_kv, key_bias, turned, near_block, part, last)
        last = [dk] if part == 0 else [dk, *dqs[0]]
        dqs.append(give_back(dq))
        dks.append(dk)
        dvs.append(dv)
        dsks.append(dsk)
        dsvs.append(dsv)
        if tiled:
            out_0, keep_0, out_1, keep_1 = halve_add(scalars, [keep_0, keep_1], got, part + 1, last)
            got = [across(out_0, ORDERS[0][part + 1]), across(out_1, ORDERS[1][part + 1])]
            last = [keep_0]
    back_part, g_vqkv = qkv_back(g_proj, normed_one, w_vqkv, tiled, last)
    vin_own, vin_other, gain_rows, *g_xkv = cross_back(
        scalars, dks, dvs, normed_one, x, grad_after, back_part, gains, w_xkv, gain_two, gain_four, pages, tiled, form, []
    )
    qin_own, qin_other, g_qqkv, gain_grads = query_out(
        scalars, dqs, dsks, dsvs, normed_three, x_query, grad_q, gains, w_qqkv, gain_rows, pages, tiled, got if tiled else []
    )

    def put(array, other):
        return lax.dynamic_update_index_in_dim(array, other.astype(array.dtype), down, 0)

    shape = (pages, strip_rows, columns, width)
    visual_out = put(vis_own, vis_came).reshape(shape)
    vin_came = from_ahead(vin_other, count, -1)
    query_out_rows = put(q_res, res_came)
    qin_came = from_partner(qin_other, count)

    weights = (w_vqkv, w_vout, w_up, w_down, w_qqkv, w_xkv, w_qout, w_qup, w_qdown)
    if tiled:
        size = lambda g: g.shape[-2]
        a, b, c, d, e = g_vqkv, g_xkv[0], gain_grads, g_qqkv, g_xkv[1]
        cut = (size(a) // 2 + 15) // 16 * 16
        lots = [
            (0, 0, [(0, 0, cut)]),
            (1, 0, [(3, 0, cut)]),
            (0, cut, [(0, cut, size(a) - cut)]),
            (1, cut, [(3, cut, size(d) - cut)]),
            (0, size(a), [(1, 0, size(b)), (2, 0, size(c))]),
            (1, size(d), [(4, 0, size(e))]),
        ]
        late_rows = [size(a) + size(b) + size(c), size(d) + size(e)]
        shares = late_sum([a, b, c, d, e], lots, late_rows, [keep_0, got[0], keep_1, got[1]], 1, [])
        tall, flat = g_up.shape[-2], g_vout.shape[-2]
        end = 2 * tall + flat
        where = {2: (0, 0), 7: (0, tall), 1: (0, 2 * tall), 0: (0, end), 5: (0, end + size(a))}
        where.update({3: (1, 0), 8: (1, tall), 6: (1, 2 * tall), 4: (1, end)})
        plan, shapes = [], []
        for number, weight in enumerate(weights):
            rows, cols = weight.shape
            step, tiles = rows // 16, cols // 256
            which, at = where[number]
            spots = [(which, at + t * step) for t in range(tiles)]
            if number == 5:
                spots = spots[:3] + [(1, end + size(d) + t * step) for t in range(3)]
            flipped = rows > 2 * cols and tiles % 2 == 1
            plan.append((step, spots, flipped))
            shapes.append((rows // 8, cols // lax.axis_size("page")))
        last = shares[0]
        gain_part, *parts = finish(scalars[CORE:CORE + 1], shares, shapes, plan, width // 8)
    else:
        last = gain_rows
        parts = [scattered(g) for g in (g_vqkv, g_vout, g_up, g_down, g_qqkv, g_xkv[0], g_qout, g_qup, g_qdown)]
        gain_part = lax.psum_scatter(gain_grads[:4], "page", scatter_dimension=0, tiled=True)
        gain_part = lax.psum_scatter(gain_part, "strip", scatter_dimension=1, tiled=True).reshape(-1, 1)
    visual_in_grad, query_in_grad = put_two(scalars, vin_own, qin_own, vin_came, qin_came, [last])
    visual_in_grad = visual_in_grad.reshape(shape)
    return (visual_out, query_out_rows, visual_in_grad, query_in_grad, gain_part, *parts)


def solution(mesh):
    tokens, slots, table = P("page", "strip", None, None), P("page", "strip", None), P("page", "strip")
    tile = P("strip", "page")
    return jax.shard_map(
        local,
        mesh=mesh,
        in_specs=(tokens, slots, table, P("page", None), table, P("page"), P("page")) + (P(),) * 10 + (tokens, slots),
        out_specs=(tokens, slots, tokens, slots) + (tile,) * 10,
        check_vma=False,
    )
```

```python
import functools

import jax
import jax.numpy as jnp
from jax import lax
from jax.experimental import pallas as pl
from jax.experimental.pallas import tpu as pltpu
from jax.sharding import PartitionSpec as P

HEADS = 12
WIN = 12
EPS = 1e-05
MASKED = -1e9
SCALE = 0.125
BF = jnp.bfloat16
F32 = jnp.float32
LANES = 128
VMEM_BYTES = 65400 * 1024


def dot(left, right, left_dim=1, right_dim=0):
    return lax.dot_general(
        left, right, (((left_dim,), (right_dim,)), ((), ())), preferred_element_type=F32
    )


def iota(shape, dim):
    return lax.broadcasted_iota(jnp.int32, shape, dim)


def norm_stats(rows):
    offset = rows - jnp.mean(rows, axis=-1, keepdims=True)
    spread = lax.rsqrt(jnp.mean(offset * offset, axis=-1, keepdims=True) + EPS)
    return offset * spread, spread


def norm_back(unit, spread, gain, grad):
    product = grad * unit
    scaled = grad * gain
    centre = jnp.mean(scaled, axis=-1, keepdims=True)
    slope = jnp.mean(scaled * unit, axis=-1, keepdims=True)
    return spread * (scaled - centre - unit * slope), jnp.sum(product, axis=0, keepdims=True)


def gelu_pair(t):
    square = t * t
    plus = 0.5 * jnp.tanh(t * (0.7978845608 + 0.0356774081 * square)) + 0.5
    value = t * plus
    return value, plus + value * (1.0 - plus) * (1.5957691216 + 0.2140644488 * square)


def three_parts(value):
    high = value.astype(BF).astype(F32)
    rest = value - high
    middle = rest.astype(BF).astype(F32)
    low = (rest - middle).astype(BF).astype(F32)
    return high, middle, low


def place_lanes(column, lane, first):
    high, middle, low = three_parts(column)
    return (
        jnp.where(lane == first, high, 0.0)
        + jnp.where(lane == first + 16, middle, 0.0)
        + jnp.where(lane == first + 32, low, 0.0)
    )


def join_lanes(stats, first):
    total = stats
    rolled = []
    for part in range(3):
        amount = (first + 16 * part) % LANES
        rolled.append(total if amount == 0 else pltpu.roll(total, LANES - amount, 1))
    return rolled[0] + rolled[1] + rolled[2]


def spread_heads(values, width):
    head_dim = width // HEADS
    pick = (iota((LANES, width), 0) == iota((LANES, width), 1) // head_dim).astype(BF)
    high, middle, low = three_parts(values)
    return dot(high.astype(BF), pick) + dot(middle.astype(BF), pick) + dot(low.astype(BF), pick)


def whole(shape, single=False):
    mode = pl.Buffered(1) if single else None
    return pl.BlockSpec(shape, lambda *_: (0,) * len(shape), pipeline_mode=mode)


def sds(shape, kind):
    return jax.ShapeDtypeStruct(shape, kind)


ANY = pl.BlockSpec(memory_space=pl.ANY)


def call(kernel, name, ins, outs, grid=(1,), scratch=(), scalars=None, deps=(), work=(0, 0, 0), aliases={}):
    first = len(ins) + (scalars is not None)

    def body(*refs):
        kernel(*refs[:first], *refs[first + len(deps) :])

    return pl.pallas_call(
        body,
        grid_spec=pltpu.PrefetchScalarGridSpec(
            num_scalar_prefetch=int(scalars is not None),
            grid=grid,
            in_specs=[spec for _, spec in ins] + [ANY] * len(deps),
            out_specs=[spec for *_, spec in outs],
            scratch_shapes=list(scratch),
        ),
        out_shape=[sds(shape, kind) for shape, kind, _ in outs],
        input_output_aliases=aliases,
        compiler_params=pltpu.CompilerParams(vmem_limit_bytes=VMEM_BYTES),
        cost_estimate=pl.CostEstimate(flops=int(3 * work[0]), bytes_accessed=int(work[1]), transcendentals=int(work[2])),
        name=name,
    )(*([] if scalars is None else [scalars]), *[array for array, _ in ins], *deps)


UP, SHIFT, ODD, CORE, BIT_X, BIT_Y, BIT_LOW, BIT_HIGH, BASE = range(9)


def page_block(shape):
    return pl.BlockSpec((1, *shape[1:]), lambda *at: (at[-1][UP],) + (0,) * (len(shape) - 1))


def steps_below(value, size, count):
    total = jnp.zeros_like(value)
    for k in range(1, count):
        total = total + jnp.where(value >= size * k, 1, 0)
    return total


def into_windows(own, other, shift, strip_rows, columns):
    half, part = strip_rows * columns, strip_rows * WIN
    token = iota((half, 1), 0)
    window = steps_below(token, part, columns // WIN)
    inside = token - part * window
    row = steps_below(inside, WIN, strip_rows)
    column = inside - WIN * row + WIN * window + shift
    column = jnp.where(column >= columns, column - columns, column)
    onehot = (iota((half, half), 1) == row * columns + column).astype(F32).astype(BF)
    turned = [dot(onehot, own), dot(onehot, other)]
    pieces = [turned[side][w * part : (w + 1) * part] for w in range(columns // WIN) for side in range(2)]
    return jnp.concatenate(pieces, axis=0)


def out_of_windows(shift, strip_rows, columns):
    half = strip_rows * columns
    token = iota((half, 1), 0)
    row = steps_below(token, columns, strip_rows)
    column = token - columns * row - shift
    column = jnp.where(column < 0, column + columns, column)
    window = steps_below(column, WIN, columns // WIN)
    spot = window * (strip_rows * WIN) + row * WIN + column - WIN * window
    return (iota((half, half), 1) == spot).astype(F32).astype(BF)


def tile_index(strip, half, order):
    y = strip % 2
    lead = (y, half) if order == 0 else (half, y)
    return lead + ((strip // 2 % 2) * 2 + strip // 4,)


def tile_shape(rows, cols):
    return (2, 2, 2, 4, cols // 256 * (rows // 16), LANES)


def store_all(ref, value, order):
    rows, cols = value.shape
    size, tiles = rows // 16, cols // 256
    for strip in range(8):
        for core in range(2):
            at = (2 * strip + core) * size
            for half in range(2):
                lead = tile_index(strip, half, order)
                for t in range(tiles):
                    lanes = (half * tiles + t) * LANES
                    ref[(core, *lead, slice(t * size, (t + 1) * size), slice(None))] = value[at : at + size, lanes : lanes + LANES]


def store_columns(ref, value, order, half=0, first=0):
    size = value.shape[0] // 16
    for strip in range(8):
        for core in range(2):
            at = (2 * strip + core) * size
            lead = tile_index(strip, half, order)
            for t in range(value.shape[1] // LANES):
                rows = slice((first + t) * size, (first + t + 1) * size)
                ref[(core, *lead, rows, slice(None))] = value[at : at + size, t * LANES : (t + 1) * LANES]


def store_strips(ref, value, order, z=0):
    size, tiles = value.shape[0] // 4, value.shape[1] // 256
    for y in range(2):
        for core in range(2):
            for half in range(2):
                lead = (y, half) if order == 0 else (half, y)
                for t in range(tiles):
                    lanes = (half * tiles + t) * LANES
                    at = (2 * y + core) * size
                    ref[(core, *lead, z, slice(t * size, (t + 1) * size), slice(None))] = value[at : at + size, lanes : lanes + LANES]


def columns_spec(rows, chunk, per_half, order, at):
    block = (2, 2, 1, 4) if order == 0 else (2, 1, 2, 4)
    lead = lambda half: (0, 0, half, 0) if order == 0 else (0, half, 0, 0)
    return pl.BlockSpec(
        (*block, chunk // LANES * (rows // 16), LANES), lambda j, *_: (*lead(at(j) // per_half), at(j) % per_half, 0)
    )


def strips_spec(rows, cols):
    return pl.BlockSpec(
        (2, 2, 2, 1, cols // 256 * (rows // 16), LANES), lambda j, *_: (0, 0, 0, (j % 2) * 2 + j // 2, 0, 0)
    )


def grad_forms(width, hidden, chunk, tiled, wo_order):
    if not tiled:
        return [
            ((width, width), BF, whole((width, width))),
            ((width, hidden), BF, pl.BlockSpec((width, chunk), lambda j, *_: (0, j))),
            ((hidden, width), BF, pl.BlockSpec((chunk, width), lambda j, *_: (j, 0))),
        ]
    shapes = [tile_shape(width, width), tile_shape(width, hidden), tile_shape(hidden, width)]
    specs = [
        whole(shapes[0]),
        columns_spec(width, chunk, hidden // 2 // chunk, 0, lambda j: j),
        strips_spec(hidden, width),
    ]
    return [(shape, BF, spec) for shape, spec in zip(shapes, specs)]


def put_grad(ref, value, store, order, tiled):
    if tiled:
        store(ref, value, order)
    else:
        ref[...] = value


def patch_in_kernel(s_ref, ok_ref, own_ref, other_ref, gain_ref, wq_ref, wx_ref, x_ref, n_ref, qkv_ref, cross_ref, bias_ref, turned, *, form):
    strip_rows, half = form[0], own_ref.shape[1]
    row = steps_below(iota((WIN * WIN, 1), 0), WIN, WIN)
    valid = jnp.zeros((WIN * WIN, 1), F32)
    for r in range(strip_rows):
        mine = jnp.where(ok_ref[s_ref[UP], r] == 1, 1.0, 0.0)
        theirs = other_ref[half : half + 1, r : r + 1].astype(F32)
        valid = valid + jnp.where(row == r, mine, 0.0) + jnp.where(row == strip_rows + r, theirs, 0.0)
    bias = jnp.broadcast_to(jnp.where(valid > 0.5, 0.0, MASKED).astype(BF), (WIN * WIN, LANES))
    for k in range(2):
        bias_ref[k * WIN * WIN : (k + 1) * WIN * WIN, :] = bias
    @pl.when(pl.program_id(0) == 0)
    def _():
        turned[...] = into_windows(own_ref[0], other_ref[:half, :], s_ref[SHIFT], *form).astype(BF)

    step = x_ref.shape[0]
    x = turned[pl.ds(pl.multiple_of(pl.program_id(0) * step, step), step), :].astype(F32)
    x_ref[...] = x.astype(BF)
    unit, _ = norm_stats(x)
    normed = (unit * gain_ref[0:1, :]).astype(BF)
    n_ref[...] = normed
    qkv_ref[...] = dot(normed, wq_ref[...]).astype(BF)
    cross_ref[...] = dot(normed, wx_ref[...]).astype(BF)


def patch_in(scalars, rows_ok, visual, other, gains, wq, wx, form, deps):
    _, half, width = visual.shape
    tokens = 2 * half
    step = 4 * form[0] * WIN
    rows = lambda w: ((tokens, w), BF, pl.BlockSpec((step, w), lambda i, *_: (i, 0)))
    return call(
        functools.partial(patch_in_kernel, form=form),
        "patch_in",
        [(rows_ok, pl.BlockSpec(memory_space=pltpu.SMEM)), (visual, page_block(visual.shape))]
        + [(a, whole(a.shape, True)) for a in (other, gains, wq, wx)],
        [rows(width), rows(width), rows(wq.shape[1]), rows(wx.shape[1]), rows(LANES)],
        grid=(tokens // step,),
        scratch=[pltpu.VMEM((tokens, width), BF)],
        scalars=scalars,
        deps=deps,
        work=(2 * tokens * width * (wq.shape[1] + wx.shape[1]), 2e7, 0),
    )


def pack_kernel(s_ref, ok_a_ref, a_ref, ok_b_ref, b_ref, a_out, b_out):
    for ok_ref, rows_ref, out_ref in ((ok_a_ref, a_ref, a_out), (ok_b_ref, b_ref, b_out)):
        count, flags = rows_ref.shape[1], ok_ref.shape[1]
        out_ref[:count, :] = rows_ref[0]
        out_ref[count:, :] = jnp.zeros_like(out_ref[count:, :])
        theirs = jnp.where(s_ref[UP] == 0, ok_ref[1:2, :], ok_ref[0:1, :]).astype(F32).astype(BF)
        out_ref[count:, :flags] = jnp.broadcast_to(theirs, (out_ref.shape[0] - count, flags))


def other_page(shape):
    return pl.BlockSpec((1, *shape[1:]), lambda *at: (1 - at[-1][UP],) + (0,) * (len(shape) - 1))


def pack(scalars, arrays):
    ins, outs = [], []
    for rows, flags in arrays:
        ins += [(flags, whole(flags.shape)), (rows, other_page(rows.shape))]
        shape = (rows.shape[1] + 16, rows.shape[2])
        outs.append((shape, BF, whole(shape)))
    return call(pack_kernel, "pack", ins, outs, scalars=scalars)


def held_back(array, deps):
    [out] = call(lambda a_ref, out_ref: None, "held_back", [(array, ANY)], [(array.shape, array.dtype, ANY)], deps=deps, aliases={0: 0})
    return out


def pack_two_kernel(s_ref, a_ref, b_ref, a_out, b_out):
    a_out[...] = a_ref[0]
    b_out[...] = b_ref[0]


def pack_two(scalars, a, b, deps):
    return call(
        pack_two_kernel,
        "pack_two",
        [(x, other_page(x.shape)) for x in (a, b)],
        [(x.shape[1:], BF, whole(x.shape[1:])) for x in (a, b)],
        scalars=scalars,
        deps=deps,
    )


def put_two_kernel(s_ref, a_ref, b_ref, a_came, b_came, a_out, b_out):
    a_out[0] = a_came[...].astype(a_out.dtype)
    b_out[0] = b_came[...].astype(b_out.dtype)


def put_two(scalars, a, b, a_came, b_came, deps):
    return call(
        put_two_kernel,
        "put_two",
        [(a, ANY), (b, ANY)] + [(x, whole(x.shape)) for x in (a_came, b_came)],
        [(x.shape, x.dtype, other_page(x.shape)) for x in (a, b)],
        scalars=scalars,
        deps=deps,
        aliases={1: 0, 2: 1},
    )


def head_masks():
    lane = iota((1, LANES), 1)
    left = lane < 64
    return left, [left.astype(F32).astype(BF), (~left).astype(F32).astype(BF)]


def window_kernel(qkv_ref, out_ref):
    tokens, width = out_ref.shape
    left, masks = head_masks()
    for pair in range(HEADS // 2):
        at = pair * LANES
        q = qkv_ref[:, at : at + LANES] * SCALE
        k = qkv_ref[:, width + at : width + at + LANES]
        v = qkv_ref[:, 2 * width + at : 2 * width + at + LANES]
        all_scores = [dot(q * masks[side], k, 1, 1) for side in range(2)]
        mixed = []
        for scores in all_scores:
            raised = jnp.exp(scores - jnp.max(scores, axis=-1, keepdims=True))
            total = jnp.sum(raised, axis=-1, keepdims=True)
            mixed.append(dot(raised.astype(BF), v) * (1.0 / total))
        out_ref[:, at : at + LANES] = jnp.where(left, mixed[0], mixed[1]).astype(BF)


def window_forward(qkv, tokens, deps):
    total, width3 = qkv.shape
    width = width3 // 3
    rows = lambda w: pl.BlockSpec((tokens, w), lambda i: (i, 0))
    [att] = call(
        window_kernel,
        "window_forward",
        [(qkv, rows(width3))],
        [((total, width), BF, rows(width))],
        grid=(total // tokens,),
        deps=deps,
        work=(16 * total * tokens * width, 8e6, total * tokens * HEADS),
    )
    return att


def window_back_kernel(qkv_ref, go_ref, out_ref):
    tokens, width = go_ref.shape
    left, masks = head_masks()
    for pair in range(HEADS // 2):
        at = pair * LANES
        q = qkv_ref[:, at : at + LANES]
        k = qkv_ref[:, width + at : width + at + LANES]
        v = qkv_ref[:, 2 * width + at : 2 * width + at + LANES]
        g = go_ref[:, at : at + LANES]
        scaled = q * SCALE
        all_scores = [dot(k * masks[side], scaled, 1, 1) for side in range(2)]
        all_grads = [dot(v * masks[side], g, 1, 1) for side in range(2)]
        parts = []
        for scores, grads in zip(all_scores, all_grads):
            raised = jnp.exp(scores - jnp.max(scores, axis=0, keepdims=True))
            inverse = 1.0 / jnp.sum(raised, axis=0, keepdims=True)
            probs = raised * inverse
            inner = jnp.sum(probs * grads, axis=0, keepdims=True)
            dscore = (probs * (grads - inner)).astype(BF)
            parts.append((dot(dscore, k, 0, 0), dot(dscore, q), dot(probs.astype(BF), g)))
        for index, factor in ((0, SCALE), (1, SCALE), (2, 1.0)):
            joined = jnp.where(left, parts[0][index], parts[1][index]) * factor
            out_ref[:, index * width + at : index * width + at + LANES] = joined.astype(BF)


def window_backward(qkv, go, tokens, deps):
    total, width3 = qkv.shape
    width = width3 // 3
    rows = lambda w: pl.BlockSpec((tokens, w), lambda i: (i, 0))
    [out] = call(
        window_back_kernel,
        "window_backward",
        [(qkv, rows(width3)), (go, rows(width))],
        [((total, width3), BF, rows(width3))],
        grid=(total // tokens,),
        deps=deps,
        work=(40 * total * tokens * width, 1.3e7, total * tokens * HEADS),
    )
    return out


def split_halves(rows, part):
    count = rows.shape[0] // (2 * part)
    return [
        jnp.concatenate([rows[(2 * w + s) * part : (2 * w + s + 1) * part] for w in range(count)], axis=0)
        for s in range(2)
    ]


def patch_ffn_kernel(
    s_ref, att_ref, x_ref, own_ref, other_ref, gain_ref, wo_ref, up_ref, down_ref,
    out_own_ref, out_other_ref, after_grad_ref, att_grad_ref, wo_grad_ref, up_grad_ref, down_grad_ref, gain_grad_ref,
    after, normed, cot, total, acts, dacts,
    *, tiled, form,
):
    step = pl.program_id(0)
    tokens, width = att_ref.shape
    part = form[0] * WIN
    block = 4 * part
    back = after_grad_ref
    blocks = [slice(b * block, (b + 1) * block) for b in range(tokens // block)]

    @pl.when(step == 0)
    def _():
        cot[...] = into_windows(own_ref[0], other_ref[...], s_ref[SHIFT], *form).astype(BF)
        for rows in blocks:
            value = x_ref[rows, :].astype(F32) + dot(att_ref[rows, :], wo_ref[...])
            after[rows, :] = value
            unit, _ = norm_stats(value)
            normed[rows, :] = (unit * gain_ref[1:2, :]).astype(BF)

    def products(first):
        enter = lambda rows: (dot(normed[rows, :], up_ref[...]), dot(cot[rows, :], down_ref[...], 1, 1))
        ahead = enter(blocks[0])
        for b, rows in enumerate(blocks):
            pre, grads = ahead
            if b + 1 < len(blocks):
                ahead = enter(blocks[b + 1])
            value, slope = gelu_pair(pre)
            act = value.astype(BF)
            acts[rows, :] = act
            dact = (slope * grads).astype(BF)
            dacts[rows, :] = dact
            if first:
                total[rows, :] = dot(act, down_ref[...])
                back[rows, :] = dot(dact, up_ref[...], 1, 1)
            else:
                total[rows, :] += dot(act, down_ref[...])
                back[rows, :] += dot(dact, up_ref[...], 1, 1)

    @pl.when(step == 0)
    def _():
        products(True)

    @pl.when(step > 0)
    def _():
        products(False)

    put_grad(up_grad_ref, dot(normed[...], dacts[...], 0, 0).astype(BF), store_columns, 0, tiled)
    put_grad(down_grad_ref, dot(acts[...], cot[...], 0, 0).astype(BF), store_strips, 1, tiled)

    @pl.when(step == pl.num_programs(0) - 1)
    def _():
        gain_sum = jnp.zeros((1, width), F32)
        for rows in blocks:
            unit, spread = norm_stats(after[rows, :])
            grad, gain_part = norm_back(unit, spread, gain_ref[1:2, :], back[rows, :])
            gain_sum = gain_sum + gain_part
            grad = cot[rows, :].astype(F32) + grad
            after_grad_ref[rows, :] = grad
            branch = grad.astype(BF)
            normed[rows, :] = branch
            att_grad_ref[rows, :] = dot(branch, wo_ref[...], 1, 1).astype(BF)
        gain_grad_ref[...] = jnp.broadcast_to(gain_sum, gain_grad_ref.shape)
        put_grad(wo_grad_ref, dot(att_ref[...], normed[...], 0, 0).astype(BF), store_all, 0, tiled)
        halves = split_halves(after[...] + total[...], part)
        onehot = out_of_windows(s_ref[SHIFT], *form)
        out_own_ref[0] = dot(onehot, halves[0].astype(BF)).astype(BF)
        out_other_ref[...] = dot(onehot, halves[1].astype(BF)).astype(BF)


def patch_ffn(scalars, att, x, cot, cot_other, gains, wo, up, down, tiled, form, deps, chunk=768):
    tokens, width = att.shape
    half = tokens // 2
    hidden = up.shape[1]
    single = lambda a: (a, whole(a.shape, True))
    return call(
        functools.partial(patch_ffn_kernel, tiled=tiled, form=form),
        "patch_ffn",
        [
            single(att), single(x), (cot, page_block(cot.shape)), single(cot_other), single(gains), single(wo),
            (up, pl.BlockSpec((width, chunk), lambda j, *_: (0, j))),
            (down, pl.BlockSpec((chunk, width), lambda j, *_: (j, 0))),
        ],
        [
            (cot.shape, BF, page_block(cot.shape)),
            ((half, width), BF, whole((half, width))),
            ((tokens, width), F32, whole((tokens, width))),
            ((tokens, width), BF, whole((tokens, width))),
            *grad_forms(width, hidden, chunk, tiled, 0),
            ((8, width), F32, whole((8, width))),
        ],
        grid=(hidden // chunk,),
        scratch=[
            pltpu.VMEM((tokens, width), F32),
            pltpu.VMEM((tokens, width), BF),
            pltpu.VMEM((tokens, width), BF),
            pltpu.VMEM((tokens, width), F32),
            pltpu.VMEM((tokens, chunk), BF),
            pltpu.VMEM((tokens, chunk), BF),
        ],
        scalars=scalars,
        deps=deps,
        work=(12 * tokens * width * hidden, 4e7, tokens * hidden),
    )


def patch_back_kernel(
    s_ref, gp_ref, wq_ref, gk0_ref, gk1_ref, gv0_ref, gv1_ref, n_ref, x_ref, after_ref, gain_ref, wx_ref, g2_ref, g4_ref,
    own_ref, other_ref, gain_grad_ref, wq_grad_ref, *rest,
    tiled, form,
):
    step = pl.program_id(0)
    half, width = other_ref.shape
    tokens = 2 * half
    part = form[0] * WIN
    block = 4 * part
    back = rest[-1]

    def query_part(first):
        term = dot(gp_ref[...], wq_ref[...], 1, 1)
        back[...] = term if first else back[...] + term
        put_grad(wq_grad_ref, dot(n_ref[...], gp_ref[...], 0, 0).astype(BF), store_columns, 0, tiled)

    def cross_part(grad):
        back[...] += dot(grad, wx_ref[...], 1, 1)
        w_grad = dot(n_ref[...], grad, 0, 0).astype(BF)
        if not tiled:
            rest[0][...] = w_grad
            return
        store_columns(rest[0], w_grad[:, : width // 2], 0)
        store_columns(rest[1], w_grad[:, width // 2 :], 1)

    @pl.when(step == 0)
    def _():
        query_part(True)

    @pl.when(step == 1)
    def _():
        query_part(False)

    @pl.when(step == 2)
    def _():
        cross_part(jnp.concatenate([gk0_ref[...], gk1_ref[...]], axis=1))

    @pl.when(step == 3)
    def _():
        cross_part(jnp.concatenate([gv0_ref[...], gv1_ref[...]], axis=1))
        gain_sum = jnp.zeros((1, width), F32)
        for b in range(tokens // block):
            rows = slice(b * block, (b + 1) * block)
            unit, spread = norm_stats(x_ref[rows, :].astype(F32))
            grad, gain_part = norm_back(unit, spread, gain_ref[0:1, :], back[rows, :])
            gain_sum = gain_sum + gain_part
            back[rows, :] = after_ref[rows, :] + grad
        row = iota((8, width), 0)
        gain_grad_ref[...] = jnp.where(row == 0, gain_sum, jnp.where(row == 1, g2_ref[...], jnp.where(row == 3, g4_ref[...], 0.0)))
        halves = split_halves(back[...], part)
        onehot = out_of_windows(s_ref[SHIFT], *form)
        high = halves[0].astype(BF)
        low = (halves[0] - high.astype(F32)).astype(BF)
        own_ref[0] = dot(onehot, high) + dot(onehot, low)
        other_ref[...] = dot(onehot, halves[1].astype(BF)).astype(BF)


def patch_back(scalars, gp, wq, gks, gvs, normed, x, after, gains, wx, g2, g4, pages, tiled, form, deps):
    tokens, width = x.shape
    half = tokens // 2
    cols = wx.shape[1]
    chunk = wq.shape[1] // 2
    at_q, at_x = (lambda j: jnp.minimum(j, 1)), (lambda j: jnp.maximum(j - 2, 0))
    if tiled:
        shape = tile_shape(width, cols // 2)
        grads = [(tile_shape(width, wq.shape[1]), BF, columns_spec(width, chunk, 1, 0, at_q))]
        grads += [(shape, BF, columns_spec(width, width // 2, 1, order, at_x)) for order in (0, 1)]
    else:
        grads = [
            (wq.shape, BF, pl.BlockSpec((width, chunk), lambda j, *_: (0, at_q(j)))),
            (wx.shape, BF, pl.BlockSpec((width, width), lambda j, *_: (0, at_x(j)))),
        ]
    single = lambda a: (a, whole(a.shape, True))
    own_shape = (pages, half, width)
    return call(
        functools.partial(patch_back_kernel, tiled=tiled, form=form),
        "patch_back",
        [
            (gp, pl.BlockSpec((tokens, chunk), lambda j, *_: (0, at_q(j)))),
            (wq, pl.BlockSpec((width, chunk), lambda j, *_: (0, at_q(j)))),
            *[single(a) for a in (*gks, *gvs, normed, x, after, gains)],
            (wx, pl.BlockSpec((width, width), lambda j, *_: (0, at_x(j)))),
            single(g2),
            single(g4),
        ],
        [
            (own_shape, F32, page_block(own_shape)),
            ((half, width), BF, whole((half, width))),
            ((8, width), F32, whole((8, width))),
            *grads,
        ],
        grid=(4,),
        scratch=[pltpu.VMEM((tokens, width), F32)],
        scalars=scalars,
        deps=deps,
        work=(4 * tokens * width * (cols + wq.shape[1]), 4e7, 0),
    )


def pair_rows(own, theirs, odd):
    return jnp.where(odd == 1, jnp.concatenate([theirs, own], axis=0), jnp.concatenate([own, theirs], axis=0))


def query_in_kernel(
    s_ref, seg_ref, ok_ref, own_ref, theirs_ref, gain_ref, w_ref, x_ref, n_ref, q_ref, kv_ref, same_ref, turned_ref
):
    own_slots = own_ref.shape[1]
    x = pair_rows(own_ref[0].astype(F32), theirs_ref[:own_slots, :].astype(F32), s_ref[ODD])
    slots, total = 2 * own_slots, seg_ref.shape[1]
    reach = slots + 64
    first = s_ref[UP] == 0
    segments = jnp.where(first, seg_ref[0:1, :], seg_ref[1:2, :]).astype(F32)
    amount = 32 - s_ref[BASE]
    near = pltpu.roll(jnp.broadcast_to(segments, (8, total)), jnp.where(amount < 0, amount + total, amount), 1)
    mine = jnp.where(first, ok_ref[0:1, :], ok_ref[1:2, :]).astype(F32)
    theirs = theirs_ref[own_slots : own_slots + 1, :own_slots].astype(F32)
    valid = jnp.where(s_ref[ODD] == 1, jnp.concatenate([theirs, mine], axis=1), jnp.concatenate([mine, theirs], axis=1))
    own = pltpu.roll(near, total - 32, 1)[0:1, :slots]
    own = jnp.where(valid > 0.5, own, -1.0)
    padded = -(-reach // LANES) * LANES
    column = near[:, :padded].T[:reach, 0:1]
    same = jnp.where(column == own, 1.0, 0.0)
    same_ref[...] = same.astype(BF)
    turned_ref[...] = same.T.astype(BF)
    x_ref[...] = x.astype(BF)
    unit, _ = norm_stats(x)
    normed = (unit * gain_ref[2:3, :]).astype(BF)
    n_ref[...] = normed
    width = x.shape[1]
    q_ref[...] = dot(normed, w_ref[:, :width]).astype(BF)
    kv_ref[...] = dot(normed, w_ref[:, width:]).astype(BF)


def query_in_call(scalars, segments, slots_ok, queries, theirs, gains, w, deps):
    _, own_slots, width = queries.shape
    slots = 2 * own_slots
    reach = slots + 64
    rows = lambda w: ((slots, w), BF, whole((slots, w)))
    return call(
        query_in_kernel,
        "query_in",
        [(segments, whole(segments.shape)), (slots_ok, whole(slots_ok.shape)), (queries, page_block(queries.shape))]
        + [(a, whole(a.shape)) for a in (theirs, gains, w)],
        [rows(width), rows(width), rows(width), rows(2 * width)]
        + [(shape, BF, whole(shape)) for shape in ((reach, slots), (slots, reach))],
        deps=deps,
        scalars=scalars,
        work=(2 * slots * width * w.shape[1], 5e6, 0),
    )


def forward_blocks(pieces, slots, group):
    if pieces > 1:
        blocks = [([(0, 0, slots - 32)], False), ([(0, slots - 32, 32), (1, 0, slots), (2, 0, 32)], True)]
        blocks.append(([(2, 32, slots - 32)], False))
        return blocks + [([(k, 0, slots)], False) for k in range(3, pieces)]
    blocks = [([(0, slots - 32, slots + 64)], True)]
    if slots > 32:
        blocks.append(([(0, 0, slots - 32)], False))
    at, total = 2 * slots + 32, slots * group
    while at < total:
        size = min(256, total - at)
        blocks.append(([(0, at, size)], False))
        at += size
    return blocks


def take(refs, block):
    parts = [refs[p][at : at + size, :] for p, at, size in block]
    return parts[0] if len(parts) == 1 else jnp.concatenate([p.astype(F32) for p in parts], axis=0).astype(parts[0].dtype)


def give(refs, block, value):
    done = 0
    for p, at, size in block:
        refs[p][at : at + size, :] = value[done : done + size].astype(refs[p].dtype)
        done += size


def query_forward_kernel(*refs, pieces, blocks):
    qs = refs[:pieces]
    k_ref, v_ref, sk_ref, sv_ref, kb_ref, same_ref = refs[pieces : pieces + 6]
    outs, held = refs[pieces + 6 : 2 * pieces + 6], refs[2 * pieces + 6 :]
    pair = pl.program_id(0)
    left, masks = head_masks()
    lane = iota((1, LANES), 1)

    @pl.when(pair == 0)
    def _():
        for h in held:
            h[...] = jnp.zeros_like(h)

    @pl.when(pair < HEADS // 2)
    def _():
        keys = [jnp.where(lane == 64 * (1 - side), kb_ref[...], k_ref[...]) for side in range(2)]
        marks = [jnp.where(lane == 64 * (1 - side), 1.0, 0.0).astype(BF) for side in range(2)]
        for block, near in blocks:
            q = take(qs, block) * SCALE
            size = q.shape[0]
            all_scores = [dot(q * masks[side] + marks[side], keys[side], 1, 1) for side in range(2)]
            if near:
                same = same_ref[...].astype(F32) > 0.5
                extras = [jnp.where(same, dot(q * masks[side], sk_ref[...], 1, 1), MASKED) for side in range(2)]
            mixed, columns = [], jnp.zeros((size, LANES), F32)
            for side in range(2):
                scores = all_scores[side]
                peak = jnp.max(scores, axis=-1, keepdims=True)
                if near:
                    peak = jnp.maximum(peak, jnp.max(extras[side], axis=-1, keepdims=True))
                raised = jnp.exp(scores - peak)
                total = jnp.sum(raised, axis=-1, keepdims=True)
                value = dot(raised.astype(BF), v_ref[...])
                if near:
                    raised = jnp.exp(extras[side] - peak)
                    total = total + jnp.sum(raised, axis=-1, keepdims=True)
                    value = value + dot(raised.astype(BF), sv_ref[...])
                mixed.append(value * (1.0 / total))
                columns = columns + place_lanes(peak + jnp.log(total), lane, 2 * pair + side)
            give(outs, block, jnp.where(left, mixed[0], mixed[1]))
            done = 0
            for p, at, rows in block:
                held[p][at : at + rows, :] += columns[done : done + rows]
                done += rows

    @pl.when(pair == HEADS // 2)
    def _():
        for out, h in zip(outs, held):
            out[...] = h[...].astype(BF)


def query_forward(qs, cross, slot_kv, key_bias, same, blocks, deps):
    width = qs[0].shape[1]
    patches, slots = cross.shape[0], slot_kv.shape[0]
    pairs = HEADS // 2
    total = sum(q.shape[0] for q in qs)
    col = lambda rows, first: pl.BlockSpec((rows, LANES), lambda p: (0, first + jnp.minimum(p, pairs - 1)))
    return call(
        functools.partial(query_forward_kernel, pieces=len(qs), blocks=blocks),
        "query_forward",
        [(q, col(q.shape[0], 0)) for q in qs]
        + [(cross, col(patches, 0)), (cross, col(patches, pairs)), (slot_kv, col(slots, 0)), (slot_kv, col(slots, pairs))]
        + [(a, whole(a.shape)) for a in (key_bias, same)],
        [((q.shape[0], width + LANES), BF, pl.BlockSpec((q.shape[0], LANES), lambda p: (0, p))) for q in qs],
        grid=(pairs + 1,),
        scratch=[pltpu.VMEM((q.shape[0], LANES), F32) for q in qs],
        deps=deps,
        work=(16 * total * patches * width, 1e7, total * patches * HEADS),
    )


def stat_lanes(stats, pair, bases):
    shape = (LANES, 4 * LANES)
    row, col = iota(shape, 0), iota(shape, 1)
    group, lane = col // LANES, col % LANES
    side = group % 2
    place = lane - jnp.where(side == 0, bases[0], bases[1])
    hit = (row == 48 * (group // 2) + 2 * pair + side + 16 * place) & (place >= 0) & (place < 3)
    return dot(stats, jnp.where(hit, -1.0, 0.0).astype(BF)).astype(BF)


def query_back_kernel(*refs, pieces, blocks, near_block, first_pair):
    qs, gos, stats = refs[:pieces], refs[pieces : 2 * pieces], refs[2 * pieces : 3 * pieces]
    k_ref, v_ref, sk_ref, sv_ref, kb_ref, same_ref = refs[3 * pieces : 3 * pieces + 6]
    dqs = refs[3 * pieces + 6 : 4 * pieces + 6]
    dk_ref, dv_ref, dsk_ref, dsv_ref, sum_k, sum_v = refs[4 * pieces + 6 : 4 * pieces + 12]
    near_dqs = refs[4 * pieces + 12 :]
    pair = pl.program_id(0) + first_pair
    left, masks = head_masks()
    lane = iota((1, LANES), 1)
    bases = (64, 0)
    ones = [jnp.where((lane >= b) & (lane < b + 3), 1.0, 0.0).astype(BF) for b in bases]
    plain = [jnp.where(lane == b + 3, 1.0, 0.0).astype(BF) for b in bases]
    keys = [jnp.where(lane == bases[s] + 3, kb_ref[...], k_ref[...] * masks[s] + ones[s]) for s in range(2)]
    values = [v_ref[...] * masks[s] + ones[s] for s in range(2)]

    def sides(block):
        q, g, st = take(qs, block), take(gos, block), take(stats, block)
        scaled = q * SCALE
        lanes = stat_lanes(st, pair, bases)
        part = lambda k: lanes[:, k * LANES : (k + 1) * LANES]
        shifted = [scaled * masks[s] + (part(s) + plain[s]) for s in range(2)]
        lowered = [g * masks[s] + part(2 + s) for s in range(2)]
        return q, g, shifted, lowered

    for ref in near_dqs:
        ref[...] = jnp.zeros_like(ref)
    q, g, shifted, lowered = sides(near_block)
    same = same_ref[...].astype(F32) > 0.5
    moved, dsk, dsv = [], [], []
    for s in range(2):
        scores = dot(sk_ref[...] * masks[s] + ones[s], shifted[s], 1, 1)
        probs = jnp.exp(jnp.where(same, scores, MASKED))
        dscore = (probs * dot(sv_ref[...] * masks[s] + ones[s], lowered[s], 1, 1)).astype(BF)
        dsk.append(dot(dscore, q))
        dsv.append(dot(probs.astype(BF), g))
        moved.append(dot(dscore, sk_ref[...], 0, 0))
    give(near_dqs, near_block, jnp.where(left, moved[0], moved[1]))
    dsk_ref[...] = (jnp.where(left, dsk[0], dsk[1]) * SCALE).astype(BF)
    dsv_ref[...] = jnp.where(left, dsv[0], dsv[1]).astype(BF)

    for number, block in enumerate(blocks):
        q, g, shifted, lowered = sides(block)
        scores = [dot(keys[s], shifted[s], 1, 1) for s in range(2)]
        grads = [dot(values[s], lowered[s], 1, 1) for s in range(2)]
        dq, dk, dv = [], [], []
        for s in range(2):
            probs = jnp.exp(scores[s])
            dscore = (probs * grads[s]).astype(BF)
            dv.append(dot(probs.astype(BF), g))
            dk.append(dot(dscore, q))
            dq.append(dot(dscore, k_ref[...], 0, 0))
        near = take(near_dqs, block)
        give(dqs, block, (jnp.where(left, dq[0], dq[1]) + near) * SCALE)
        if number == 0:
            sum_k[...] = jnp.where(left, dk[0], dk[1])
            sum_v[...] = jnp.where(left, dv[0], dv[1])
        else:
            sum_k[...] += jnp.where(left, dk[0], dk[1])
            sum_v[...] += jnp.where(left, dv[0], dv[1])
    dk_ref[...] = (sum_k[...] * SCALE).astype(BF)
    dv_ref[...] = sum_v[...].astype(BF)


def query_backward(qs, gos, cross, slot_kv, key_bias, same, near_block, part, deps):
    patches, slots = cross.shape[0], slot_kv.shape[0]
    pairs = HEADS // 2
    count = pairs // 2
    width = count * LANES
    total = sum(q.shape[0] for q in qs)
    blocks = []
    for number, q in enumerate(qs):
        step = min(256, q.shape[0])
        blocks += [[(number, at, step)] for at in range(0, q.shape[0], step)]
    col = lambda rows, first: pl.BlockSpec((rows, LANES), lambda p: (0, first + part * count + p))
    out = lambda rows: ((rows, width), BF, pl.BlockSpec((rows, LANES), lambda p: (0, p)))
    found = call(
        functools.partial(
            query_back_kernel, pieces=len(qs), blocks=blocks, near_block=near_block, first_pair=part * count
        ),
        "query_backward",
        [(q, col(q.shape[0], 0)) for q in qs]
        + [(g, col(g.shape[0], 0)) for g in gos]
        + [(g, pl.BlockSpec((g.shape[0], LANES), lambda p: (0, pairs))) for g in gos]
        + [(cross, col(patches, 0)), (cross, col(patches, pairs)), (slot_kv, col(slots, 0)), (slot_kv, col(slots, pairs))]
        + [(a, whole(a.shape)) for a in (key_bias, same)],
        [out(q.shape[0]) for q in qs] + [out(patches), out(patches), out(slots), out(slots)],
        grid=(count,),
        scratch=[pltpu.VMEM((patches, LANES), F32)] * 2 + [pltpu.VMEM((q.shape[0], LANES), F32) for q in qs],
        deps=deps,
        work=(20 * total * patches * width, 1.5e7, total * patches * HEADS // 2),
    )
    return found[: len(qs)], *found[len(qs) :]


def query_ffn_kernel(s_ref, *refs, parts, tiled):
    outs = refs[:parts]
    x_ref, own_ref, theirs_ref, gain_ref, wo_ref, up_ref, down_ref = refs[parts : parts + 7]
    (
        out_own_ref, out_other_ref, grad_ref, send_ref, att_ref, normed_ref, act_ref, dact_ref, branch_ref, cot_ref,
        gain_grad_ref, mixed, after, total, back, joint,
    ) = refs[parts + 7 :]
    step = pl.program_id(0)
    width = x_ref.shape[1]

    @pl.when(step == 0)
    def _():
        each = [join_lanes(o[:, width:].astype(F32), 0) for o in outs]
        peak = functools.reduce(jnp.maximum, each)
        weights = [jnp.exp(e - peak) for e in each]
        weight_sum = functools.reduce(jnp.add, weights)
        joint[...] = peak + jnp.log(weight_sum)
        value = None
        for o, w in zip(outs, weights):
            term = o[:, :width].astype(F32) * spread_heads(w / weight_sum, width)
            value = term if value is None else value + term
        mixed[...] = value
        att_ref[...] = value.astype(BF)
        rows = x_ref[...].astype(F32) + dot(att_ref[...], wo_ref[...])
        after[...] = rows
        unit, _ = norm_stats(rows)
        normed_ref[...] = (unit * gain_ref[3:4, :]).astype(BF)
        cot_ref[...] = pair_rows(own_ref[0].astype(F32), theirs_ref[...].astype(F32), s_ref[ODD]).astype(BF)
        total[...] = jnp.zeros_like(total)
        back[...] = jnp.zeros_like(back)

    grads = dot(cot_ref[...], down_ref[...], 1, 1)
    value, slope = gelu_pair(dot(normed_ref[...], up_ref[...]))
    dact = (slope * grads).astype(BF)
    dact_ref[...] = dact
    back[...] += dot(dact, up_ref[...], 1, 1)
    act = value.astype(BF)
    act_ref[...] = act
    total[...] += dot(act, down_ref[...])

    @pl.when(step == pl.num_programs(0) - 1)
    def _():
        rows = after[...] + total[...]
        own_slots = rows.shape[0] // 2
        low, high = rows[:own_slots], rows[own_slots:]
        odd = s_ref[ODD] == 1
        out_own_ref[0] = jnp.where(odd, high, low).astype(BF)
        out_other_ref[...] = jnp.where(odd, low, high).astype(BF)
        unit, spread = norm_stats(after[...])
        grad, gain_part = norm_back(unit, spread, gain_ref[3:4, :], back[...])
        gain_grad_ref[...] = jnp.broadcast_to(gain_part, gain_grad_ref.shape)
        grad = cot_ref[...].astype(F32) + grad
        grad_ref[...] = grad
        branch = grad.astype(BF)
        branch_ref[...] = branch
        sent = dot(branch, wo_ref[...], 1, 1).astype(BF)
        send_ref[:, :width] = sent
        pick = (iota((width, LANES), 0) // (width // HEADS) == iota((width, LANES), 1)).astype(F32).astype(BF)
        high, middle, low = three_parts(sent.astype(F32) * mixed[...])
        inner = dot(high.astype(BF), pick) + dot(middle.astype(BF), pick) + dot(low.astype(BF), pick)
        lane = iota((1, LANES), 1)
        packed = jnp.zeros(inner.shape, F32)
        for source, first in ((joint[...], 0), (inner, 48)):
            kept = jnp.where(lane < HEADS, source, 0.0)
            for number, piece in enumerate(three_parts(kept)):
                amount = first + 16 * number
                packed = packed + (piece if amount == 0 else pltpu.roll(piece, amount, 1))
        send_ref[:, width:] = packed.astype(BF)


def query_ffn(scalars, outs, x, cot, cot_theirs, gains, wo, up, down, tiled, deps, chunk=768):
    slots, width = x.shape
    hidden = up.shape[1]
    rows = lambda w, kind: ((slots, w), kind, whole((slots, w)))
    chunks = ((slots, hidden), BF, pl.BlockSpec((slots, chunk), lambda j, *_: (0, j)))
    half = (slots // 2, width)
    return call(
        functools.partial(query_ffn_kernel, parts=len(outs), tiled=tiled),
        "query_ffn",
        [(a, whole(a.shape)) for a in (*outs, x)]
        + [(cot, page_block(cot.shape))]
        + [(a, whole(a.shape)) for a in (cot_theirs, gains, wo)]
        + [
            (up, pl.BlockSpec((width, chunk), lambda j, *_: (0, j))),
            (down, pl.BlockSpec((chunk, width), lambda j, *_: (j, 0))),
        ],
        [
            (cot.shape, BF, page_block(cot.shape)), (half, BF, whole(half)), rows(width, F32), rows(width + LANES, BF),
            rows(width, BF), rows(width, BF), chunks, chunks, rows(width, BF), rows(width, BF), ((8, width), F32, whole((8, width))),
        ],
        grid=(hidden // chunk,),
        scratch=[pltpu.VMEM((slots, width), F32)] * 4 + [pltpu.VMEM((slots, LANES), F32)],
        scalars=scalars,
        deps=deps,
        work=(8 * slots * width * hidden, 2e7, slots * hidden),
    )


def query_weights_kernel(normed_ref, cot_ref, att_ref, branch_ref, act_ref, dact_ref, wo_ref, up_ref, down_ref, *, tiled):
    put_grad(up_ref, dot(normed_ref[...], dact_ref[...], 0, 0).astype(BF), store_columns, 0, tiled)
    put_grad(down_ref, dot(act_ref[...], cot_ref[...], 0, 0).astype(BF), store_strips, 1, tiled)

    @pl.when(pl.program_id(0) == 0)
    def _():
        put_grad(wo_ref, dot(att_ref[...], branch_ref[...], 0, 0).astype(BF), store_all, 1, tiled)


def query_weights(normed, cot, att, branch, act, dact, tiled, deps, chunk=768):
    slots, width = normed.shape
    hidden = act.shape[1]
    return call(
        functools.partial(query_weights_kernel, tiled=tiled),
        "query_weights",
        [(a, whole((slots, width))) for a in (normed, cot, att, branch)]
        + [(a, pl.BlockSpec((slots, chunk), lambda j: (0, j))) for a in (act, dact)],
        grad_forms(width, hidden, chunk, tiled, 1),
        grid=(hidden // chunk,),
        deps=deps,
        work=(4 * slots * width * hidden, 1.6e7, 0),
    )


def query_out_kernel(s_ref, *refs, parts, tiled):
    halves = [refs[:parts], refs[parts : 2 * parts]]
    others = refs[2 * parts : 2 * parts + 4]
    n_ref, x_ref, grad_ref, gain_ref, w_ref, rows_ref = refs[2 * parts + 4 : 2 * parts + 10]
    own_ref, other_ref, w_grad_ref, gain_grad_ref = refs[2 * parts + 10 : 2 * parts + 14]
    width = x_ref.shape[1]
    sums = []
    for dqs in halves:
        value = dqs[0][...].astype(F32)
        for d in dqs[1:]:
            value = value + d[...].astype(F32)
        sums.append(value.astype(BF))
    join = lambda a, b: jnp.concatenate([a, b], axis=1)
    pieces = [join(*sums), join(others[0][...], others[1][...]), join(others[2][...], others[3][...])]
    back = None
    for number, piece in enumerate(pieces):
        cols = slice(number * width, (number + 1) * width)
        term = dot(piece, w_ref[:, cols], 1, 1)
        back = term if back is None else back + term
        (refs[-1] if tiled else w_grad_ref)[:, cols] = dot(n_ref[...], piece, 0, 0).astype(BF)
    if tiled:
        store_all(w_grad_ref, refs[-1][...], 1)
    unit, spread = norm_stats(x_ref[...].astype(F32))
    grad, gain_part = norm_back(unit, spread, gain_ref[2:3, :], back)
    rows = grad_ref[...] + grad
    own_slots = rows.shape[0] // 2
    low, high = rows[:own_slots], rows[own_slots:]
    odd = s_ref[ODD] == 1
    own_ref[0] = jnp.where(odd, high, low)
    other_ref[...] = jnp.where(odd, low, high).astype(BF)
    gain_rows = rows_ref[...] + jnp.where(iota((8, width), 0) == 2, gain_part, 0.0)
    if not tiled:
        gain_grad_ref[...] = gain_rows
        return
    turned = gain_rows.T
    size = width // 16
    lane = iota((1, LANES), 1)
    for half in range(2):
        tile = jnp.where(lane == 0, turned[:, 2 * half : 2 * half + 1], 0.0)
        tile = jnp.where(lane == 1, turned[:, 2 * half + 1 : 2 * half + 2], tile).astype(BF)
        for strip in range(8):
            for core in range(2):
                at = (2 * strip + core) * size
                gain_grad_ref[(core, *tile_index(strip, half, 0), slice(None), slice(None))] = tile[at : at + size]


def query_out(scalars, dqs, dks, dvs, normed, x, grad, gains, w, gain_rows, pages, tiled, deps):
    slots, width = x.shape
    own_shape = (pages, slots // 2, width)
    w_shape = tile_shape(width, w.shape[1]) if tiled else w.shape
    g_shape, g_kind = (tile_shape(width, 256), BF) if tiled else ((8, width), F32)
    ins = (*dqs[0], *dqs[1], *dks, *dvs, normed, x, grad, gains, w, gain_rows)
    return call(
        functools.partial(query_out_kernel, parts=len(dqs[0]), tiled=tiled),
        "query_out",
        [(a, whole(a.shape, True)) for a in ins],
        [
            (own_shape, F32, page_block(own_shape)),
            ((slots // 2, width), BF, whole((slots // 2, width))),
            (w_shape, BF, whole(w_shape)),
            (g_shape, g_kind, whole(g_shape)),
        ],
        scratch=[pltpu.VMEM(w.shape, BF)] if tiled else [],
        scalars=scalars,
        deps=deps,
        work=(4 * slots * width * w.shape[1], 1e7, 0),
    )


PAIR = pl.DeviceIdType.MESH


def coordinates():
    page, strip = lax.axis_index("page"), lax.axis_index("strip")
    core, x = lax.rem(page, 2), page // 2
    y, z_low, z_high = lax.rem(strip, 2), lax.rem(strip // 2, 2), strip // 4
    flip = lambda index, bit, weight: index + weight - 2 * weight * bit
    core_mate = (flip(page, core, 1), strip)
    mates = {
        "x": (x, (flip(page, x, 2), strip)),
        "y": (y, (page, flip(strip, y, 1))),
        "low": (z_low, (page, flip(strip, z_low, 2))),
        "high": (z_high, (page, flip(strip, z_high, 4))),
    }
    return core, core_mate, [[mates[k] for k in ("y", "x", "low", "high")], [mates[k] for k in ("x", "y", "low", "high")]]


def meet(mates):
    barrier = pltpu.get_barrier_semaphore()
    for mate in mates:
        pl.semaphore_signal(barrier, inc=1, device_id=mate, device_id_type=PAIR)
    pl.semaphore_wait(barrier, len(mates))


def send(source, target, sems, number, mate):
    copy = pltpu.make_async_remote_copy(
        src_ref=source,
        dst_ref=target,
        send_sem=sems.at[0, number],
        recv_sem=sems.at[1, number],
        device_id=mate,
        device_id_type=PAIR,
    )
    copy.start()
    return copy


def add_rows(target, first, source, start, length, at, rows):
    span = pl.ds(at, rows)

    def step(i, carry):
        total = target[first + i, span, :].astype(F32) + source[start + i, span, :].astype(F32)
        target[first + i, span, :] = total.astype(BF)
        return carry

    lax.fori_loop(0, length, step, 0)


def query_sum_kernel(*refs, rows):
    up_ref, down_ref, wo_ref, normed_ref, cot_ref, att_ref, branch_ref, act_ref, dact_ref = refs[:9]
    outs = refs[9:13]
    own_up, own_down, own_wo, held_0, held_1, remote, near = refs[13:]
    held = (held_0, held_1)
    core, core_mate, orders = coordinates()
    meet([core_mate])
    wide, small = rows
    far, mine = [], []
    for number, (grad, order, at, size) in enumerate(((up_ref, 0, 0, wide), (down_ref, 1, 0, wide), (wo_ref, 0, 2 * wide, small))):
        span, bit = pl.ds(at, size), orders[order][0][0]
        far.append(send(grad.at[1 - core], held[order].at[:, :, :, span, :], remote, number, core_mate))
        for which in range(2):
            first = bit if which else 1 - bit
            copy = pltpu.make_async_copy(
                grad.at[core, first], outs[2 * order + which].at[:, :, span, :], near.at[2 * number + which]
            )
            copy.start()
            mine.append(copy)
    width = normed_ref.shape[1]
    own_rows = ((own_up, 0, wide, wide), (own_down, 1, wide, wide), (own_wo, 1, 2 * wide, small))
    store_all(own_wo, dot(att_ref[...], branch_ref[...], 0, 0).astype(BF), 1)
    for j in range(act_ref.shape[1] // width):
        cols = slice(j * width, (j + 1) * width)
        store_columns(own_up, dot(normed_ref[...], dact_ref[:, cols], 0, 0).astype(BF), 0, j // 2, (j % 2) * (width // LANES))
        store_strips(own_down, dot(act_ref[:, cols], cot_ref[...], 0, 0).astype(BF), 1, (j % 2) * 2 + j // 2)
    later = []
    for number, (grad, order, at, size) in enumerate(own_rows):
        later.append(send(grad.at[1 - core], held[order].at[:, :, :, pl.ds(at, size), :], remote, 3 + number, core_mate))
    for copy in far + mine:
        copy.wait()

    def add(order, at, size, own):
        bit = orders[order][0][0]
        span = pl.ds(at, size)
        for which in range(2):
            out, first = outs[2 * order + which], bit if which else 1 - bit
            for i in range(2):

                def step(z, carry, out=out, first=first, i=i):
                    mine = out[i, z, span, :] if own is None else own[core, first, i, z]
                    out[i, z, span, :] = (mine.astype(F32) + held[order][first, i, z, span, :].astype(F32)).astype(BF)
                    return carry

                lax.fori_loop(0, 4, step, 0)

    for order, at, size in ((0, 0, wide), (1, 0, wide), (0, 2 * wide, small)):
        add(order, at, size, None)
    for copy, (grad, order, at, size) in zip(later, own_rows):
        copy.wait()
        add(order, at, size, grad)


def query_sum(patch_grads, normed, cot, att, branch, act, dact, collective, deps):
    width, hidden = normed.shape[1], act.shape[1]
    shapes = [tile_shape(width, hidden), tile_shape(hidden, width), tile_shape(width, width)]
    rows = (shapes[0][-2], shapes[2][-2])
    total = 2 * rows[0] + rows[1]
    vmem = pl.BlockSpec(memory_space=pltpu.VMEM)
    kernel = functools.partial(query_sum_kernel, rows=rows)
    outs = pl.pallas_call(
        lambda *refs: kernel(*refs[:9], *refs[9 + len(deps) :]),
        in_specs=[ANY] * 3 + [vmem] * 6 + [ANY] * len(deps),
        out_specs=[vmem] * 4,
        out_shape=[sds((2, 4, total, LANES), BF)] * 4,
        scratch_shapes=[
            *[pltpu.VMEM(shape, BF) for shape in shapes],
            pltpu.VMEM((2, 2, 4, total, LANES), BF),
            pltpu.VMEM((2, 2, 4, total, LANES), BF),
            pltpu.SemaphoreType.DMA((2, 6)),
            pltpu.SemaphoreType.DMA((6,)),
        ],
        compiler_params=pltpu.CompilerParams(collective_id=collective, has_side_effects=True, vmem_limit_bytes=VMEM_BYTES),
        name="query_sum",
    )(*patch_grads, normed, cot, att, branch, act, dact, *deps)
    return [out.reshape(8, total, LANES) for out in outs]


ORDERS = (("y", "x", "low", "high"), ("x", "y", "low", "high"))
PLACES = {"x": BIT_X, "y": BIT_Y, "low": BIT_LOW, "high": BIT_HIGH}


def across(array, name):
    axis, weight = {"x": ("page", 2), "y": ("strip", 1), "low": ("strip", 2), "high": ("strip", 4)}[name]
    return lax.ppermute(array, axis, [(i, i ^ weight) for i in range(lax.axis_size(axis))])


def halve_add_kernel(s_ref, *refs):
    for k in range(4):
        keep, got, out = refs[2 * k], refs[2 * k + 1], refs[8 + k]
        out[...] = (keep[...].astype(F32) + got[...].astype(F32)).astype(BF)


def halve_add(scalars, kept, got, stage, deps):
    ins, outs = [], []
    for order in range(2):
        size = kept[order].shape[0] // 2
        shape = kept[order].shape[1:]
        place = PLACES[ORDERS[order][stage]]
        for flip in (1, 0):
            spec = pl.BlockSpec(
                (1, *shape),
                lambda i, s, place=place, flip=flip, size=size: ((1 - s[place] if flip else s[place]) * size + i, 0, 0),
            )
            ins += [(kept[order], spec), (got[order], spec)]
            outs.append(((size, *shape), BF, pl.BlockSpec((1, *shape), lambda i, s: (i, 0, 0))))
    return call(
        halve_add_kernel, "halve_add", ins, outs, grid=(size,), scalars=scalars, deps=deps, work=(1e6, 6 * size * 1296 * 512, 0)
    )


def late_sum_kernel(*refs, lots, arrays, early_rows):
    grads = refs[:arrays]
    early = refs[arrays : arrays + 4]
    own, got = refs[arrays + 4 : arrays + 6], refs[arrays + 6 : arrays + 8]
    sums, first_held = refs[arrays + 8 : arrays + 10], refs[arrays + 10 : arrays + 12]
    held = [refs[arrays + 12 : arrays + 16], refs[arrays + 16 : arrays + 20]]
    done, loaded, early_held = refs[arrays + 20 : arrays + 22], refs[arrays + 22 : arrays + 26], refs[arrays + 26 : arrays + 28]
    remote, near = refs[arrays + 28 :]
    core, core_mate, orders = coordinates()
    meet([core_mate] + [mate for _, mate in orders[0]])
    numbers, local_numbers = iter(range(1000)), iter(range(1000))
    jobs = []
    for order, at, members in lots:
        copies, first = [], at
        for member, start, rows in members:
            there, span = pl.ds(start, rows), pl.ds(first, rows)
            first += rows
            copies.append(
                send(grads[member].at[1 - core, :, there, :], first_held[order].at[:, span, :], remote, next(numbers), core_mate)
            )
            copy = pltpu.make_async_copy(
                grads[member].at[core, :, there, :], sums[order].at[:, span, :], near.at[next(local_numbers)]
            )
            copy.start()
            copies.append(copy)
        jobs.append((order, at, first - at, copies))
    loads = []
    for k in range(4):
        copy = pltpu.make_async_copy(early[k], loaded[k], near.at[next(local_numbers)])
        copy.start()
        loads.append(copy)
    for copy in loads:
        copy.wait()
    early_flights = []
    for order in range(2):
        bit, mate = orders[order][3]
        kept = loaded[2 * order]
        add_rows(kept, 1 - bit, loaded[2 * order + 1], 1 - bit, 1, 0, early_rows)
        early_flights.append(send(kept.at[1 - bit], early_held[order], remote, next(numbers), mate))
        add_rows(kept, bit, loaded[2 * order + 1], bit, 1, 0, early_rows)
    bases = [0] * len(jobs)
    flights = [None] * len(jobs)
    first_exchange = []
    for stage in range(4):
        size = 8 >> stage
        for n, (order, at, rows, copies) in enumerate(jobs):
            source = first_held[order] if stage == 0 else held[order][stage - 1]
            for copy in copies if stage == 0 else [flights[n]]:
                copy.wait()
            bit, mate = orders[order][stage]
            out, keep = size * (1 - bit), size * bit
            base = bases[n]
            add_rows(sums[order], base + out, source, out, size, at, rows)
            flights[n] = send(
                sums[order].at[pl.ds(base + out, size), pl.ds(at, rows), :],
                held[order][stage].at[:, pl.ds(at, rows), :],
                remote,
                next(numbers),
                mate,
            )
            add_rows(sums[order], base + keep, source, keep, size, at, rows)
            bases[n] = base + keep
        if stage == 2:
            for order in range(2):
                early_flights[order].wait()
                total = loaded[2 * order][orders[order][3][0]].astype(F32) + early_held[order][...].astype(F32)
                own[order][:early_rows, :] = total.astype(BF)
                span = pl.ds(0, early_rows)
                first_exchange.append(send(own[order].at[span, :], done[order].at[span, :], remote, next(numbers), core_mate))
    exchange = []
    for n, (order, at, rows, _) in enumerate(jobs):
        flights[n].wait()
        value = sums[order][bases[n], pl.ds(at, rows), :].astype(F32) + held[order][3][0, pl.ds(at, rows), :].astype(F32)
        span = pl.ds(early_rows + at, rows)
        own[order][span, :] = value.astype(BF)
        exchange.append(send(own[order].at[span, :], done[order].at[span, :], remote, next(numbers), core_mate))
    for copy in first_exchange + exchange:
        copy.wait()
    for order in range(2):
        got[order][...] = done[order][...]


def late_sum(grads, lots, rows, early, collective, deps):
    grads = [g.reshape(2, 16, *g.shape[-2:]) for g in grads]
    arrays = len(grads)
    members = sum(len(lot[2]) for lot in lots)
    early_rows = early[0].shape[1]
    share = [sds((early_rows + r, LANES), BF) for r in rows]
    vmem = lambda *shape: pltpu.VMEM(shape, BF)
    kernel = functools.partial(late_sum_kernel, lots=lots, arrays=arrays, early_rows=early_rows)
    first = arrays + 4
    return pl.pallas_call(
        lambda *refs: kernel(*refs[:first], *refs[first + len(deps) :]),
        in_specs=[ANY] * (first + len(deps)),
        out_specs=[pl.BlockSpec(memory_space=pltpu.VMEM)] * 4,
        out_shape=share + share,
        scratch_shapes=[
            *[vmem(16, r, LANES) for r in rows],
            *[vmem(16, r, LANES) for r in rows],
            *[vmem(8 >> k, rows[0], LANES) for k in range(4)],
            *[vmem(8 >> k, rows[1], LANES) for k in range(4)],
            *[vmem(early_rows + r, LANES) for r in rows],
            *[vmem(2, early_rows, LANES)] * 4,
            *[vmem(early_rows, LANES)] * 2,
            pltpu.SemaphoreType.DMA((2, members + 5 * len(lots) + 4)),
            pltpu.SemaphoreType.DMA((members + 4,)),
        ],
        compiler_params=pltpu.CompilerParams(collective_id=collective, has_side_effects=True, vmem_limit_bytes=VMEM_BYTES),
        name="late_sum",
    )(*grads, *early, *deps)


def finish_kernel(core_ref, own0, own1, got0, got1, gain_ref, *outs, plan):
    first = core_ref[0] == 0
    owns, gots = (own0, own1), (got0, got1)
    lane = iota((1, LANES), 1)
    left = lane < 64

    def tile(order, at, size, part):
        mine = owns[order][at : at + size, :].astype(F32)
        theirs = gots[order][at : at + size, :].astype(F32)
        return jnp.where(first == (part == 0), mine, theirs)

    for out, (size, tiles, flipped) in zip(outs, plan):
        count = len(tiles)
        for part in range(2):
            rows = slice(part * size, (part + 1) * size)
            values = [tile(order, at, size, part) for order, at in tiles]
            if count % 2 == 0:
                for t in range(count // 2):
                    out[rows, t * LANES : (t + 1) * LANES] = jnp.where(first, values[t], values[t + count // 2])
                continue
            turned = [pltpu.roll(v, 64, 1) for v in values[count // 2 :]]
            whole_tiles = [
                jnp.where(first, values[t], jnp.where(left, turned[t], turned[t + 1])) for t in range(count // 2)
            ]
            rest = jnp.where(first, values[count // 2], turned[-1])
            if flipped:
                for t, value in enumerate(whole_tiles):
                    for at in range(0, size, 64):
                        column = part * size + at
                        out[t * LANES : (t + 1) * LANES, column : column + 64] = value[at : at + 64].T
                for at in range(0, size, 64):
                    column = part * size + at
                    out[count // 2 * LANES :, column : column + 64] = rest[at : at + 64].T[:64]
                continue
            for t, value in enumerate(whole_tiles):
                out[rows, t * LANES : (t + 1) * LANES] = value
            out[rows, count // 2 * LANES :] = rest[:, :64]
    size = gain_ref.shape[1] // 2
    at = own0.shape[0] - size
    gain = jnp.concatenate([tile(0, at, size, part) for part in range(2)], axis=0).T
    gain_ref[...] = jnp.where(first, gain[0:1], gain[1:2])


def finish(core, shares, shapes, plan, gain_rows):
    vmem = pl.BlockSpec(memory_space=pltpu.VMEM)
    outs = [shape[::-1] if flipped else shape for shape, (_, _, flipped) in zip(shapes, plan)]
    gain, *found = pl.pallas_call(
        functools.partial(finish_kernel, plan=plan),
        in_specs=[pl.BlockSpec(memory_space=pltpu.SMEM)] + [vmem] * 4,
        out_specs=[vmem] * (1 + len(outs)),
        out_shape=[sds((1, gain_rows), F32)] + [sds(shape, F32) for shape in outs],
        compiler_params=pltpu.CompilerParams(vmem_limit_bytes=VMEM_BYTES),
        name="finish",
    )(core, *shares)
    return gain.T, *[f.T if flipped else f for f, (_, _, flipped) in zip(found, plan)]


def from_ahead(array, count, distance):
    return lax.ppermute(array, "strip", [(i, (i - distance) % count) for i in range(count)])


def from_partner(array, count):
    return lax.ppermute(array, "strip", [(i, i ^ 1) for i in range(count)])


def scattered(grad):
    strips, pages = lax.axis_size("strip"), lax.axis_size("page")
    rows, cols = grad.shape
    part = lax.psum_scatter(grad, "strip", scatter_dimension=0, tiled=True)
    part = part.reshape(rows // strips, pages, cols // pages).transpose(1, 0, 2)
    return lax.psum_scatter(part, "page", scatter_dimension=0, tiled=False).astype(F32)


def local(
    visual_in, query_in, row_valid, segment_ids, slot_valid, col_shift, row_shifted, norm_gains,
    w_vqkv, w_vout, w_up, w_down, w_qqkv, w_xkv, w_qout, w_qup, w_qdown, visual_cot, query_cot,
):
    pages, strip_rows, columns, width = visual_in.shape
    own_slots, all_slots = query_in.shape[1], segment_ids.shape[1]
    count = lax.axis_size("strip")
    tiled = count == 8
    group = count // 2
    half = strip_rows * columns
    slots = 2 * own_slots
    window = WIN * WIN
    form = (strip_rows, columns)
    place, page = lax.axis_index("strip"), lax.axis_index("page")
    odd = place % 2
    up = jnp.where(odd == 1, 1 - row_shifted[0], row_shifted[0])
    down = 1 - up
    pick = lambda array, which: lax.dynamic_index_in_dim(array, which, 0, keepdims=False)
    scalars = jnp.stack([up, pick(col_shift, up), odd, page % 2, page // 2, odd, place // 2 % 2, place // 4, (place // 2) * slots]).astype(jnp.int32)

    visual, cot = visual_in.reshape(pages, half, width), visual_cot.reshape(pages, half, width)
    query_sent, patch_sent = pack(scalars, [(query_in, slot_valid), (visual, row_valid)])
    query_theirs = from_partner(query_sent, count)
    patch_sent = held_back(patch_sent, [query_theirs])
    patch_other = from_ahead(patch_sent, count, 1)
    gains = jnp.pad(norm_gains.T, ((0, 4), (0, 0)))

    order = [-1] + list(range(group - 1))
    blocks = forward_blocks(group if tiled else 1, slots, group)
    near_block = next(block for block, near in blocks if near)

    def gather(array):
        pieces = [array if k == 0 else from_ahead(array, count, 2 * k) for k in order]
        return pieces if tiled else [jnp.concatenate(pieces, axis=0)]

    def give_back(arrays):
        if not tiled:
            arrays = [arrays[0][n * slots : (n + 1) * slots] for n in range(group)]
        return [piece if k == 0 else from_ahead(piece, count, -2 * k) for piece, k in zip(arrays, order)]

    x_query, normed_three, q_own, slot_kv, same, turned = query_in_call(
        scalars, segment_ids, slot_valid, query_in, query_theirs, gains, w_qqkv, [patch_sent]
    )
    qs = gather(q_own)
    x, normed_one, qkv, cross, key_bias = patch_in(
        scalars, row_valid, visual, patch_other, gains, w_vqkv, w_xkv, form, [q_own]
    )
    att = window_forward(qkv, window, [])
    cot_sent, cot_q_sent = pack_two(scalars, cot, query_cot, [att])
    cot_other, cot_theirs = from_ahead(cot_sent, count, 1), from_partner(cot_q_sent, count)
    q_out = query_forward(qs, cross, slot_kv, key_bias, same, blocks, [cot_q_sent])
    out_parts = give_back(q_out)
    (vis_own, vis_other, grad_after, grad_att, g_vout, g_up, g_down, gain_two) = patch_ffn(
        scalars, att, x, cot, cot_other, gains, w_vout, w_up, w_down, tiled, form, [q_out[0]]
    )
    vis_came = from_ahead(vis_other, count, -1)
    (q_res, q_res_other, grad_q, send_q, att_q, normed_four, act_q, dact_q, branch_q, cot_q, gain_four) = query_ffn(
        scalars, out_parts, x_query, query_cot, cot_theirs, gains, w_qout, w_qup, w_qdown, tiled, [gain_two]
    )
    gos = gather(send_q)
    res_came = from_partner(q_res_other, count)
    if tiled:
        out_0, keep_0, out_1, keep_1 = query_sum(
            [g_up, g_down, g_vout], normed_four, cot_q, att_q, branch_q, act_q, dact_q, 0, []
        )
        got = [across(out_0, "y"), across(out_1, "x")]
        last = keep_0
    else:
        g_qout, g_qup, g_qdown = query_weights(normed_four, cot_q, att_q, branch_q, act_q, dact_q, tiled, [])
        last = g_qout
    g_proj = window_backward(qkv, grad_att, window, [last, vis_came])
    last = [g_proj, res_came]
    dqs, dks, dvs, dsks, dsvs = [], [], [], [], []
    for part in range(2):
        dq, dk, dv, dsk, dsv = query_backward(qs, gos, cross, slot_kv, key_bias, turned, near_block, part, last)
        last = [dk] if part == 0 else [dk, *dqs[0]]
        dqs.append(give_back(dq))
        dks.append(dk)
        dvs.append(dv)
        dsks.append(dsk)
        dsvs.append(dsv)
        if tiled:
            out_0, keep_0, out_1, keep_1 = halve_add(scalars, [keep_0, keep_1], got, part + 1, last)
            got = [across(out_0, ORDERS[0][part + 1]), across(out_1, ORDERS[1][part + 1])]
            last = [keep_0]
    vin_own, vin_other, gain_rows, g_vqkv, *g_xkv = patch_back(
        scalars, g_proj, w_vqkv, dks, dvs, normed_one, x, grad_after, gains, w_xkv, gain_two, gain_four, pages, tiled, form, last
    )
    qin_own, qin_other, g_qqkv, gain_grads = query_out(
        scalars, dqs, dsks, dsvs, normed_three, x_query, grad_q, gains, w_qqkv, gain_rows, pages, tiled, got if tiled else []
    )

    def put(array, other):
        return lax.dynamic_update_index_in_dim(array, other.astype(array.dtype), down, 0)

    shape = (pages, strip_rows, columns, width)
    visual_out = put(vis_own, vis_came).reshape(shape)
    vin_came = from_ahead(vin_other, count, -1)
    query_out_rows = put(q_res, res_came)
    qin_came = from_partner(qin_other, count)

    weights = (w_vqkv, w_vout, w_up, w_down, w_qqkv, w_xkv, w_qout, w_qup, w_qdown)
    if tiled:
        size = lambda g: g.shape[-2]
        a, b, c, d, e = g_vqkv, g_xkv[0], gain_grads, g_qqkv, g_xkv[1]
        cut = (size(a) // 2 + 15) // 16 * 16
        lots = [
            (0, 0, [(0, 0, cut)]),
            (1, 0, [(3, 0, cut)]),
            (0, cut, [(0, cut, size(a) - cut)]),
            (1, cut, [(3, cut, size(d) - cut)]),
            (0, size(a), [(1, 0, size(b)), (2, 0, size(c))]),
            (1, size(d), [(4, 0, size(e))]),
        ]
        late_rows = [size(a) + size(b) + size(c), size(d) + size(e)]
        shares = late_sum([a, b, c, d, e], lots, late_rows, [keep_0, got[0], keep_1, got[1]], 1, [])
        tall, flat = g_up.shape[-2], g_vout.shape[-2]
        end = 2 * tall + flat
        where = {2: (0, 0), 7: (0, tall), 1: (0, 2 * tall), 0: (0, end), 5: (0, end + size(a))}
        where.update({3: (1, 0), 8: (1, tall), 6: (1, 2 * tall), 4: (1, end)})
        plan, shapes = [], []
        for number, weight in enumerate(weights):
            rows, cols = weight.shape
            step, tiles = rows // 16, cols // 256
            which, at = where[number]
            spots = [(which, at + t * step) for t in range(tiles)]
            if number == 5:
                spots = spots[:3] + [(1, end + size(d) + t * step) for t in range(3)]
            flipped = rows > 2 * cols and tiles % 2 == 1
            plan.append((step, spots, flipped))
            shapes.append((rows // 8, cols // lax.axis_size("page")))
        last = shares[0]
        gain_part, *parts = finish(scalars[CORE:CORE + 1], shares, shapes, plan, width // 8)
    else:
        last = gain_rows
        parts = [scattered(g) for g in (g_vqkv, g_vout, g_up, g_down, g_qqkv, g_xkv[0], g_qout, g_qup, g_qdown)]
        gain_part = lax.psum_scatter(gain_grads[:4], "page", scatter_dimension=0, tiled=True)
        gain_part = lax.psum_scatter(gain_part, "strip", scatter_dimension=1, tiled=True).reshape(-1, 1)
    visual_in_grad, query_in_grad = put_two(scalars, vin_own, qin_own, vin_came, qin_came, [last])
    visual_in_grad = visual_in_grad.reshape(shape)
    return (visual_out, query_out_rows, visual_in_grad, query_in_grad, gain_part, *parts)


def solution(mesh):
    tokens, slots, table = P("page", "strip", None, None), P("page", "strip", None), P("page", "strip")
    tile = P("strip", "page")
    return jax.shard_map(
        local,
        mesh=mesh,
        in_specs=(tokens, slots, table, P("page", None), table, P("page"), P("page")) + (P(),) * 10 + (tokens, slots),
        out_specs=(tokens, slots, tokens, slots) + (tile,) * 10,
        check_vma=False,
    )
```

```python
import functools

import jax
import jax.numpy as jnp
from jax import lax
from jax.experimental import pallas as pl
from jax.experimental.pallas import tpu as pltpu
from jax.sharding import PartitionSpec as P

HEADS = 12
WIN = 12
EPS = 1e-05
MASKED = -1e9
SCALE = 0.125
BF = jnp.bfloat16
F32 = jnp.float32
LANES = 128
VMEM_BYTES = 65400 * 1024


def dot(left, right, left_dim=1, right_dim=0):
    return lax.dot_general(
        left, right, (((left_dim,), (right_dim,)), ((), ())), preferred_element_type=F32
    )


def iota(shape, dim):
    return lax.broadcasted_iota(jnp.int32, shape, dim)


def norm_stats(rows):
    offset = rows - jnp.mean(rows, axis=-1, keepdims=True)
    spread = lax.rsqrt(jnp.mean(offset * offset, axis=-1, keepdims=True) + EPS)
    return offset * spread, spread


def norm_back(unit, spread, gain, grad):
    product = grad * unit
    scaled = grad * gain
    centre = jnp.mean(scaled, axis=-1, keepdims=True)
    slope = jnp.mean(scaled * unit, axis=-1, keepdims=True)
    return spread * (scaled - centre - unit * slope), jnp.sum(product, axis=0, keepdims=True)


def gelu_pair(t):
    square = t * t
    plus = 0.5 * jnp.tanh(t * (0.7978845608 + 0.0356774081 * square)) + 0.5
    value = t * plus
    return value, plus + value * (1.0 - plus) * (1.5957691216 + 0.2140644488 * square)


def three_parts(value):
    high = value.astype(BF).astype(F32)
    rest = value - high
    middle = rest.astype(BF).astype(F32)
    low = (rest - middle).astype(BF).astype(F32)
    return high, middle, low


def place_lanes(column, lane, first):
    high, middle, low = three_parts(column)
    return (
        jnp.where(lane == first, high, 0.0)
        + jnp.where(lane == first + 16, middle, 0.0)
        + jnp.where(lane == first + 32, low, 0.0)
    )


def join_lanes(stats, first):
    total = stats
    rolled = []
    for part in range(3):
        amount = (first + 16 * part) % LANES
        rolled.append(total if amount == 0 else pltpu.roll(total, LANES - amount, 1))
    return rolled[0] + rolled[1] + rolled[2]


def spread_heads(values, width):
    head_dim = width // HEADS
    pick = (iota((LANES, width), 0) == iota((LANES, width), 1) // head_dim).astype(BF)
    high, middle, low = three_parts(values)
    return dot(high.astype(BF), pick) + dot(middle.astype(BF), pick) + dot(low.astype(BF), pick)


def whole(shape, single=False):
    mode = pl.Buffered(1) if single else None
    return pl.BlockSpec(shape, lambda *_: (0,) * len(shape), pipeline_mode=mode)


def sds(shape, kind):
    return jax.ShapeDtypeStruct(shape, kind)


ANY = pl.BlockSpec(memory_space=pl.ANY)


def call(kernel, name, ins, outs, grid=(1,), scratch=(), scalars=None, deps=(), work=(0, 0, 0), aliases={}):
    first = len(ins) + (scalars is not None)

    def body(*refs):
        kernel(*refs[:first], *refs[first + len(deps) :])

    return pl.pallas_call(
        body,
        grid_spec=pltpu.PrefetchScalarGridSpec(
            num_scalar_prefetch=int(scalars is not None),
            grid=grid,
            in_specs=[spec for _, spec in ins] + [ANY] * len(deps),
            out_specs=[spec for *_, spec in outs],
            scratch_shapes=list(scratch),
        ),
        out_shape=[sds(shape, kind) for shape, kind, _ in outs],
        input_output_aliases=aliases,
        compiler_params=pltpu.CompilerParams(vmem_limit_bytes=VMEM_BYTES),
        cost_estimate=pl.CostEstimate(flops=int(3 * work[0]), bytes_accessed=int(work[1]), transcendentals=int(work[2])),
        name=name,
    )(*([] if scalars is None else [scalars]), *[array for array, _ in ins], *deps)


UP, SHIFT, ODD, CORE, BIT_X, BIT_Y, BIT_LOW, BIT_HIGH, BASE = range(9)


def page_block(shape):
    return pl.BlockSpec((1, *shape[1:]), lambda *at: (at[-1][UP],) + (0,) * (len(shape) - 1))


def steps_below(value, size, count):
    total = jnp.zeros_like(value)
    for k in range(1, count):
        total = total + jnp.where(value >= size * k, 1, 0)
    return total


def into_windows(own, other, shift, strip_rows, columns):
    half, part = strip_rows * columns, strip_rows * WIN
    token = iota((half, 1), 0)
    window = steps_below(token, part, columns // WIN)
    inside = token - part * window
    row = steps_below(inside, WIN, strip_rows)
    column = inside - WIN * row + WIN * window + shift
    column = jnp.where(column >= columns, column - columns, column)
    onehot = (iota((half, half), 1) == row * columns + column).astype(F32).astype(BF)
    turned = [dot(onehot, own), dot(onehot, other)]
    pieces = [turned[side][w * part : (w + 1) * part] for w in range(columns // WIN) for side in range(2)]
    return jnp.concatenate(pieces, axis=0)


def out_of_windows(shift, strip_rows, columns):
    half = strip_rows * columns
    token = iota((half, 1), 0)
    row = steps_below(token, columns, strip_rows)
    column = token - columns * row - shift
    column = jnp.where(column < 0, column + columns, column)
    window = steps_below(column, WIN, columns // WIN)
    spot = window * (strip_rows * WIN) + row * WIN + column - WIN * window
    return (iota((half, half), 1) == spot).astype(F32).astype(BF)


def tile_index(strip, half, order):
    y = strip % 2
    lead = (y, half) if order == 0 else (half, y)
    return lead + ((strip // 2 % 2) * 2 + strip // 4,)


def tile_shape(rows, cols):
    return (2, 2, 2, 4, cols // 256 * (rows // 16), LANES)


def store_all(ref, value, order):
    rows, cols = value.shape
    size, tiles = rows // 16, cols // 256
    for strip in range(8):
        for core in range(2):
            at = (2 * strip + core) * size
            for half in range(2):
                lead = tile_index(strip, half, order)
                for t in range(tiles):
                    lanes = (half * tiles + t) * LANES
                    ref[(core, *lead, slice(t * size, (t + 1) * size), slice(None))] = value[at : at + size, lanes : lanes + LANES]


def store_columns(ref, value, order, half=0, first=0):
    size = value.shape[0] // 16
    for strip in range(8):
        for core in range(2):
            at = (2 * strip + core) * size
            lead = tile_index(strip, half, order)
            for t in range(value.shape[1] // LANES):
                rows = slice((first + t) * size, (first + t + 1) * size)
                ref[(core, *lead, rows, slice(None))] = value[at : at + size, t * LANES : (t + 1) * LANES]


def store_strips(ref, value, order, z=0):
    size, tiles = value.shape[0] // 4, value.shape[1] // 256
    for y in range(2):
        for core in range(2):
            for half in range(2):
                lead = (y, half) if order == 0 else (half, y)
                for t in range(tiles):
                    lanes = (half * tiles + t) * LANES
                    at = (2 * y + core) * size
                    ref[(core, *lead, z, slice(t * size, (t + 1) * size), slice(None))] = value[at : at + size, lanes : lanes + LANES]


def columns_spec(rows, chunk, per_half, order, at):
    block = (2, 2, 1, 4) if order == 0 else (2, 1, 2, 4)
    lead = lambda half: (0, 0, half, 0) if order == 0 else (0, half, 0, 0)
    return pl.BlockSpec(
        (*block, chunk // LANES * (rows // 16), LANES), lambda j, *_: (*lead(at(j) // per_half), at(j) % per_half, 0)
    )


def strips_spec(rows, cols):
    return pl.BlockSpec(
        (2, 2, 2, 1, cols // 256 * (rows // 16), LANES), lambda j, *_: (0, 0, 0, (j % 2) * 2 + j // 2, 0, 0)
    )


def grad_forms(width, hidden, chunk, tiled, wo_order):
    if not tiled:
        return [
            ((width, width), BF, whole((width, width))),
            ((width, hidden), BF, pl.BlockSpec((width, chunk), lambda j, *_: (0, j))),
            ((hidden, width), BF, pl.BlockSpec((chunk, width), lambda j, *_: (j, 0))),
        ]
    shapes = [tile_shape(width, width), tile_shape(width, hidden), tile_shape(hidden, width)]
    specs = [
        whole(shapes[0]),
        columns_spec(width, chunk, hidden // 2 // chunk, 0, lambda j: j),
        strips_spec(hidden, width),
    ]
    return [(shape, BF, spec) for shape, spec in zip(shapes, specs)]


def put_grad(ref, value, store, order, tiled):
    if tiled:
        store(ref, value, order)
    else:
        ref[...] = value


def patch_in_kernel(s_ref, ok_ref, own_ref, other_ref, gain_ref, wq_ref, wx_ref, x_ref, n_ref, qkv_ref, cross_ref, bias_ref, turned, *, form):
    strip_rows, half = form[0], own_ref.shape[1]
    row = steps_below(iota((WIN * WIN, 1), 0), WIN, WIN)
    valid = jnp.zeros((WIN * WIN, 1), F32)
    for r in range(strip_rows):
        mine = jnp.where(ok_ref[s_ref[UP], r] == 1, 1.0, 0.0)
        theirs = other_ref[half : half + 1, r : r + 1].astype(F32)
        valid = valid + jnp.where(row == r, mine, 0.0) + jnp.where(row == strip_rows + r, theirs, 0.0)
    bias = jnp.broadcast_to(jnp.where(valid > 0.5, 0.0, MASKED).astype(BF), (WIN * WIN, LANES))
    for k in range(2):
        bias_ref[k * WIN * WIN : (k + 1) * WIN * WIN, :] = bias
    @pl.when(pl.program_id(0) == 0)
    def _():
        turned[...] = into_windows(own_ref[0], other_ref[:half, :], s_ref[SHIFT], *form).astype(BF)

    step = x_ref.shape[0]
    x = turned[pl.ds(pl.multiple_of(pl.program_id(0) * step, step), step), :].astype(F32)
    x_ref[...] = x.astype(BF)
    unit, _ = norm_stats(x)
    normed = (unit * gain_ref[0:1, :]).astype(BF)
    n_ref[...] = normed
    qkv_ref[...] = dot(normed, wq_ref[...]).astype(BF)
    cross_ref[...] = dot(normed, wx_ref[...]).astype(BF)


def patch_in(scalars, rows_ok, visual, other, gains, wq, wx, form, deps):
    _, half, width = visual.shape
    tokens = 2 * half
    step = 4 * form[0] * WIN
    rows = lambda w: ((tokens, w), BF, pl.BlockSpec((step, w), lambda i, *_: (i, 0)))
    return call(
        functools.partial(patch_in_kernel, form=form),
        "patch_in",
        [(rows_ok, pl.BlockSpec(memory_space=pltpu.SMEM)), (visual, page_block(visual.shape))]
        + [(a, whole(a.shape, True)) for a in (other, gains, wq, wx)],
        [rows(width), rows(width), rows(wq.shape[1]), rows(wx.shape[1]), rows(LANES)],
        grid=(tokens // step,),
        scratch=[pltpu.VMEM((tokens, width), BF)],
        scalars=scalars,
        deps=deps,
        work=(2 * tokens * width * (wq.shape[1] + wx.shape[1]), 2e7, 0),
    )


def pack_kernel(s_ref, ok_a_ref, a_ref, ok_b_ref, b_ref, a_out, b_out):
    for ok_ref, rows_ref, out_ref in ((ok_a_ref, a_ref, a_out), (ok_b_ref, b_ref, b_out)):
        count, flags = rows_ref.shape[1], ok_ref.shape[1]
        out_ref[:count, :] = rows_ref[0]
        out_ref[count:, :] = jnp.zeros_like(out_ref[count:, :])
        theirs = jnp.where(s_ref[UP] == 0, ok_ref[1:2, :], ok_ref[0:1, :]).astype(F32).astype(BF)
        out_ref[count:, :flags] = jnp.broadcast_to(theirs, (out_ref.shape[0] - count, flags))


def other_page(shape):
    return pl.BlockSpec((1, *shape[1:]), lambda *at: (1 - at[-1][UP],) + (0,) * (len(shape) - 1))


def pack(scalars, arrays):
    ins, outs = [], []
    for rows, flags in arrays:
        ins += [(flags, whole(flags.shape)), (rows, other_page(rows.shape))]
        shape = (rows.shape[1] + 16, rows.shape[2])
        outs.append((shape, BF, whole(shape)))
    return call(pack_kernel, "pack", ins, outs, scalars=scalars)


def held_back(array, deps):
    [out] = call(lambda a_ref, out_ref: None, "held_back", [(array, ANY)], [(array.shape, array.dtype, ANY)], deps=deps, aliases={0: 0})
    return out


def pack_two_kernel(s_ref, a_ref, b_ref, a_out, b_out):
    a_out[...] = a_ref[0]
    b_out[...] = b_ref[0]


def pack_two(scalars, a, b, deps):
    return call(
        pack_two_kernel,
        "pack_two",
        [(x, other_page(x.shape)) for x in (a, b)],
        [(x.shape[1:], BF, whole(x.shape[1:])) for x in (a, b)],
        scalars=scalars,
        deps=deps,
    )


def put_kernel(s_ref, *refs):
    count = len(refs) // 3
    for came, out in zip(refs[count : 2 * count], refs[2 * count :]):
        out[0] = came[...].astype(out.dtype)


def put(scalars, arrays, came, deps):
    return call(
        put_kernel,
        "put",
        [(a, ANY) for a in arrays] + [(c, whole(c.shape)) for c in came],
        [(a.shape, a.dtype, other_page(a.shape)) for a in arrays],
        scalars=scalars,
        deps=deps,
        aliases={k + 1: k for k in range(len(arrays))},
    )


def head_masks():
    lane = iota((1, LANES), 1)
    left = lane < 64
    return left, [left.astype(F32).astype(BF), (~left).astype(F32).astype(BF)]


def stack(parts, axis=0):
    return jnp.concatenate(parts, axis=axis)


def window_kernel(qkv_ref, out_ref):
    tokens, width = out_ref.shape
    left, masks = head_masks()
    for pair in range(HEADS // 2):
        at = pair * LANES
        q = qkv_ref[:, at : at + LANES] * SCALE
        k = qkv_ref[:, width + at : width + at + LANES]
        v = qkv_ref[:, 2 * width + at : 2 * width + at + LANES]
        scores = dot(stack([q * masks[0], q * masks[1]]), k, 1, 1)
        raised = jnp.exp(scores - jnp.max(scores, axis=-1, keepdims=True))
        total = jnp.sum(raised, axis=-1, keepdims=True)
        mixed = dot(raised.astype(BF), v) * (1.0 / total)
        out_ref[:, at : at + LANES] = jnp.where(left, mixed[:tokens], mixed[tokens:]).astype(BF)


def window_forward(qkv, tokens, deps):
    total, width3 = qkv.shape
    width = width3 // 3
    rows = lambda w: pl.BlockSpec((tokens, w), lambda i: (i, 0))
    [att] = call(
        window_kernel,
        "window_forward",
        [(qkv, rows(width3))],
        [((total, width), BF, rows(width))],
        grid=(total // tokens,),
        deps=deps,
        work=(16 * total * tokens * width, 8e6, total * tokens * HEADS),
    )
    return att


def window_back_kernel(qkv_ref, go_ref, out_ref):
    tokens, width = go_ref.shape
    left, masks = head_masks()
    for pair in range(HEADS // 2):
        at = pair * LANES
        q = qkv_ref[:, at : at + LANES]
        k = qkv_ref[:, width + at : width + at + LANES]
        v = qkv_ref[:, 2 * width + at : 2 * width + at + LANES]
        g = go_ref[:, at : at + LANES]
        scaled = q * SCALE
        all_scores = [dot(k * masks[side], scaled, 1, 1) for side in range(2)]
        all_grads = [dot(v * masks[side], g, 1, 1) for side in range(2)]
        parts = []
        for scores, grads in zip(all_scores, all_grads):
            raised = jnp.exp(scores - jnp.max(scores, axis=0, keepdims=True))
            inverse = 1.0 / jnp.sum(raised, axis=0, keepdims=True)
            probs = raised * inverse
            inner = jnp.sum(probs * grads, axis=0, keepdims=True)
            dscore = (probs * (grads - inner)).astype(BF)
            parts.append((dot(dscore, k, 0, 0), dot(dscore, q), dot(probs.astype(BF), g)))
        for index, factor in ((0, SCALE), (1, SCALE), (2, 1.0)):
            joined = jnp.where(left, parts[0][index], parts[1][index]) * factor
            out_ref[:, index * width + at : index * width + at + LANES] = joined.astype(BF)


def window_backward(qkv, go, tokens, deps):
    total, width3 = qkv.shape
    width = width3 // 3
    rows = lambda w: pl.BlockSpec((tokens, w), lambda i: (i, 0))
    [out] = call(
        window_back_kernel,
        "window_backward",
        [(qkv, rows(width3)), (go, rows(width))],
        [((total, width3), BF, rows(width3))],
        grid=(total // tokens,),
        deps=deps,
        work=(40 * total * tokens * width, 1.3e7, total * tokens * HEADS),
    )
    return out


def split_halves(rows, part):
    count = rows.shape[0] // (2 * part)
    return [
        jnp.concatenate([rows[(2 * w + s) * part : (2 * w + s + 1) * part] for w in range(count)], axis=0)
        for s in range(2)
    ]


def patch_ffn_kernel(
    s_ref, att_ref, x_ref, own_ref, other_ref, gain_ref, wo_ref, up_ref, down_ref,
    out_own_ref, out_other_ref, after_grad_ref, att_grad_ref, wo_grad_ref, up_grad_ref, down_grad_ref, gain_grad_ref,
    after, normed, cot, total, acts, dacts,
    *, tiled, form,
):
    step = pl.program_id(0)
    tokens, width = att_ref.shape
    part = form[0] * WIN
    block = 4 * part
    back = after_grad_ref
    blocks = [slice(b * block, (b + 1) * block) for b in range(tokens // block)]

    @pl.when(step == 0)
    def _():
        cot[...] = into_windows(own_ref[0], other_ref[...], s_ref[SHIFT], *form).astype(BF)
        for rows in blocks:
            value = x_ref[rows, :].astype(F32) + dot(att_ref[rows, :], wo_ref[...])
            after[rows, :] = value
            unit, _ = norm_stats(value)
            normed[rows, :] = (unit * gain_ref[1:2, :]).astype(BF)

    def products(first):
        enter = lambda rows: (dot(normed[rows, :], up_ref[...]), dot(cot[rows, :], down_ref[...], 1, 1))
        ahead = enter(blocks[0])
        for b, rows in enumerate(blocks):
            pre, grads = ahead
            if b + 1 < len(blocks):
                ahead = enter(blocks[b + 1])
            value, slope = gelu_pair(pre)
            act = value.astype(BF)
            acts[rows, :] = act
            dact = (slope * grads).astype(BF)
            dacts[rows, :] = dact
            if first:
                total[rows, :] = dot(act, down_ref[...])
                back[rows, :] = dot(dact, up_ref[...], 1, 1)
            else:
                total[rows, :] += dot(act, down_ref[...])
                back[rows, :] += dot(dact, up_ref[...], 1, 1)

    @pl.when(step == 0)
    def _():
        products(True)

    @pl.when(step > 0)
    def _():
        products(False)

    put_grad(up_grad_ref, dot(normed[...], dacts[...], 0, 0).astype(BF), store_columns, 0, tiled)
    put_grad(down_grad_ref, dot(acts[...], cot[...], 0, 0).astype(BF), store_strips, 1, tiled)

    @pl.when(step == pl.num_programs(0) - 1)
    def _():
        gain_sum = jnp.zeros((1, width), F32)
        for rows in blocks:
            unit, spread = norm_stats(after[rows, :])
            grad, gain_part = norm_back(unit, spread, gain_ref[1:2, :], back[rows, :])
            gain_sum = gain_sum + gain_part
            grad = cot[rows, :].astype(F32) + grad
            after_grad_ref[rows, :] = grad
            branch = grad.astype(BF)
            normed[rows, :] = branch
            att_grad_ref[rows, :] = dot(branch, wo_ref[...], 1, 1).astype(BF)
        gain_grad_ref[...] = jnp.broadcast_to(gain_sum, gain_grad_ref.shape)
        put_grad(wo_grad_ref, dot(att_ref[...], normed[...], 0, 0).astype(BF), store_all, 0, tiled)
        halves = split_halves(after[...] + total[...], part)
        onehot = out_of_windows(s_ref[SHIFT], *form)
        out_own_ref[0] = dot(onehot, halves[0].astype(BF)).astype(BF)
        out_other_ref[...] = dot(onehot, halves[1].astype(BF)).astype(BF)


def patch_ffn(scalars, att, x, cot, cot_other, gains, wo, up, down, tiled, form, deps, chunk=768):
    tokens, width = att.shape
    half = tokens // 2
    hidden = up.shape[1]
    single = lambda a: (a, whole(a.shape, True))
    return call(
        functools.partial(patch_ffn_kernel, tiled=tiled, form=form),
        "patch_ffn",
        [
            single(att), single(x), (cot, page_block(cot.shape)), single(cot_other), single(gains), single(wo),
            (up, pl.BlockSpec((width, chunk), lambda j, *_: (0, j))),
            (down, pl.BlockSpec((chunk, width), lambda j, *_: (j, 0))),
        ],
        [
            (cot.shape, BF, page_block(cot.shape)),
            ((half, width), BF, whole((half, width))),
            ((tokens, width), F32, whole((tokens, width))),
            ((tokens, width), BF, whole((tokens, width))),
            *grad_forms(width, hidden, chunk, tiled, 0),
            ((8, width), F32, whole((8, width))),
        ],
        grid=(hidden // chunk,),
        scratch=[
            pltpu.VMEM((tokens, width), F32),
            pltpu.VMEM((tokens, width), BF),
            pltpu.VMEM((tokens, width), BF),
            pltpu.VMEM((tokens, width), F32),
            pltpu.VMEM((tokens, chunk), BF),
            pltpu.VMEM((tokens, chunk), BF),
        ],
        scalars=scalars,
        deps=deps,
        work=(12 * tokens * width * hidden, 4e7, tokens * hidden),
    )


def patch_back_kernel(
    s_ref, gp_ref, wq_ref, gk0_ref, gk1_ref, gv0_ref, gv1_ref, n_ref, x_ref, after_ref, gain_ref, wx_ref, g2_ref, g4_ref,
    own_ref, other_ref, gain_grad_ref, wq_grad_ref, *rest,
    tiled, form,
):
    step = pl.program_id(0)
    half, width = other_ref.shape
    tokens = 2 * half
    part = form[0] * WIN
    block = 4 * part
    back = rest[-1]

    def query_part(first):
        term = dot(gp_ref[...], wq_ref[...], 1, 1)
        back[...] = term if first else back[...] + term
        put_grad(wq_grad_ref, dot(n_ref[...], gp_ref[...], 0, 0).astype(BF), store_columns, 0, tiled)

    def cross_part(grad):
        back[...] += dot(grad, wx_ref[...], 1, 1)
        w_grad = dot(n_ref[...], grad, 0, 0).astype(BF)
        if not tiled:
            rest[0][...] = w_grad
            return
        store_columns(rest[0], w_grad[:, : width // 2], 0)
        store_columns(rest[1], w_grad[:, width // 2 :], 1)

    @pl.when(step == 0)
    def _():
        query_part(True)

    @pl.when(step == 1)
    def _():
        query_part(False)

    @pl.when(step == 2)
    def _():
        cross_part(jnp.concatenate([gk0_ref[...], gk1_ref[...]], axis=1))

    @pl.when(step == 3)
    def _():
        cross_part(jnp.concatenate([gv0_ref[...], gv1_ref[...]], axis=1))
        gain_sum = jnp.zeros((1, width), F32)
        for b in range(tokens // block):
            rows = slice(b * block, (b + 1) * block)
            unit, spread = norm_stats(x_ref[rows, :].astype(F32))
            grad, gain_part = norm_back(unit, spread, gain_ref[0:1, :], back[rows, :])
            gain_sum = gain_sum + gain_part
            back[rows, :] = after_ref[rows, :] + grad
        row = iota((8, width), 0)
        gain_grad_ref[...] = jnp.where(row == 0, gain_sum, jnp.where(row == 1, g2_ref[...], jnp.where(row == 3, g4_ref[...], 0.0)))
        halves = split_halves(back[...], part)
        onehot = out_of_windows(s_ref[SHIFT], *form)
        high = halves[0].astype(BF)
        low = (halves[0] - high.astype(F32)).astype(BF)
        own_ref[0] = dot(onehot, high) + dot(onehot, low)
        other_ref[...] = dot(onehot, halves[1].astype(BF)).astype(BF)


def patch_back(scalars, gp, wq, gks, gvs, normed, x, after, gains, wx, g2, g4, pages, tiled, form, deps):
    tokens, width = x.shape
    half = tokens // 2
    cols = wx.shape[1]
    chunk = wq.shape[1] // 2
    at_q, at_x = (lambda j: jnp.minimum(j, 1)), (lambda j: jnp.maximum(j - 2, 0))
    if tiled:
        shape = tile_shape(width, cols // 2)
        grads = [(tile_shape(width, wq.shape[1]), BF, columns_spec(width, chunk, 1, 0, at_q))]
        grads += [(shape, BF, columns_spec(width, width // 2, 1, order, at_x)) for order in (0, 1)]
    else:
        grads = [
            (wq.shape, BF, pl.BlockSpec((width, chunk), lambda j, *_: (0, at_q(j)))),
            (wx.shape, BF, pl.BlockSpec((width, width), lambda j, *_: (0, at_x(j)))),
        ]
    single = lambda a: (a, whole(a.shape, True))
    own_shape = (pages, half, width)
    return call(
        functools.partial(patch_back_kernel, tiled=tiled, form=form),
        "patch_back",
        [
            (gp, pl.BlockSpec((tokens, chunk), lambda j, *_: (0, at_q(j)))),
            (wq, pl.BlockSpec((width, chunk), lambda j, *_: (0, at_q(j)))),
            *[single(a) for a in (*gks, *gvs, normed, x, after, gains)],
            (wx, pl.BlockSpec((width, width), lambda j, *_: (0, at_x(j)))),
            single(g2),
            single(g4),
        ],
        [
            (own_shape, F32, page_block(own_shape)),
            ((half, width), BF, whole((half, width))),
            ((8, width), F32, whole((8, width))),
            *grads,
        ],
        grid=(4,),
        scratch=[pltpu.VMEM((tokens, width), F32)],
        scalars=scalars,
        deps=deps,
        work=(4 * tokens * width * (cols + wq.shape[1]), 4e7, 0),
    )


def pair_rows(own, theirs, odd):
    return jnp.where(odd == 1, jnp.concatenate([theirs, own], axis=0), jnp.concatenate([own, theirs], axis=0))


def query_in_kernel(
    s_ref, seg_ref, ok_ref, own_ref, theirs_ref, gain_ref, w_ref, x_ref, n_ref, q_ref, kv_ref, same_ref, turned_ref
):
    own_slots = own_ref.shape[1]
    x = pair_rows(own_ref[0].astype(F32), theirs_ref[:own_slots, :].astype(F32), s_ref[ODD])
    slots, total = 2 * own_slots, seg_ref.shape[1]
    reach = slots + 64
    first = s_ref[UP] == 0
    segments = jnp.where(first, seg_ref[0:1, :], seg_ref[1:2, :]).astype(F32)
    amount = 32 - s_ref[BASE]
    near = pltpu.roll(jnp.broadcast_to(segments, (8, total)), jnp.where(amount < 0, amount + total, amount), 1)
    mine = jnp.where(first, ok_ref[0:1, :], ok_ref[1:2, :]).astype(F32)
    theirs = theirs_ref[own_slots : own_slots + 1, :own_slots].astype(F32)
    valid = jnp.where(s_ref[ODD] == 1, jnp.concatenate([theirs, mine], axis=1), jnp.concatenate([mine, theirs], axis=1))
    own = pltpu.roll(near, total - 32, 1)[0:1, :slots]
    own = jnp.where(valid > 0.5, own, -1.0)
    padded = -(-reach // LANES) * LANES
    column = near[:, :padded].T[:reach, 0:1]
    same = jnp.where(column == own, 1.0, 0.0)
    same_ref[...] = same.astype(BF)
    turned_ref[...] = same.T.astype(BF)
    x_ref[...] = x.astype(BF)
    unit, _ = norm_stats(x)
    normed = (unit * gain_ref[2:3, :]).astype(BF)
    n_ref[...] = normed
    width = x.shape[1]
    q_ref[...] = dot(normed, w_ref[:, :width]).astype(BF)
    kv_ref[...] = dot(normed, w_ref[:, width:]).astype(BF)


def query_in_call(scalars, segments, slots_ok, queries, theirs, gains, w, deps):
    _, own_slots, width = queries.shape
    slots = 2 * own_slots
    reach = slots + 64
    rows = lambda w: ((slots, w), BF, whole((slots, w)))
    return call(
        query_in_kernel,
        "query_in",
        [(segments, whole(segments.shape)), (slots_ok, whole(slots_ok.shape)), (queries, page_block(queries.shape))]
        + [(a, whole(a.shape)) for a in (theirs, gains, w)],
        [rows(width), rows(width), rows(width), rows(2 * width)]
        + [(shape, BF, whole(shape)) for shape in ((reach, slots), (slots, reach))],
        deps=deps,
        scalars=scalars,
        work=(2 * slots * width * w.shape[1], 5e6, 0),
    )


def forward_blocks(pieces, slots, group):
    if pieces > 1:
        blocks = [([(0, 0, slots - 32)], False), ([(0, slots - 32, 32), (1, 0, slots), (2, 0, 32)], True)]
        blocks.append(([(2, 32, slots - 32)], False))
        return blocks + [([(k, 0, slots)], False) for k in range(3, pieces)]
    blocks = [([(0, slots - 32, slots + 64)], True)]
    if slots > 32:
        blocks.append(([(0, 0, slots - 32)], False))
    at, total = 2 * slots + 32, slots * group
    while at < total:
        size = min(256, total - at)
        blocks.append(([(0, at, size)], False))
        at += size
    return blocks


def take(refs, block):
    parts = [refs[p][at : at + size, :] for p, at, size in block]
    return parts[0] if len(parts) == 1 else jnp.concatenate([p.astype(F32) for p in parts], axis=0).astype(parts[0].dtype)


def give(refs, block, value):
    done = 0
    for p, at, size in block:
        refs[p][at : at + size, :] = value[done : done + size].astype(refs[p].dtype)
        done += size


def query_forward_kernel(*refs, pieces, blocks):
    qs = refs[:pieces]
    k_ref, v_ref, sk_ref, sv_ref, kb_ref, same_ref = refs[pieces : pieces + 6]
    outs, held = refs[pieces + 6 : 2 * pieces + 6], refs[2 * pieces + 6 :]
    pair = pl.program_id(0)
    left, masks = head_masks()
    lane = iota((1, LANES), 1)

    @pl.when(pair == 0)
    def _():
        for h in held:
            h[...] = jnp.zeros_like(h)

    @pl.when(pair < HEADS // 2)
    def _():
        keys = [jnp.where(lane == 64 * (1 - side), kb_ref[...], k_ref[...]) for side in range(2)]
        marks = [jnp.where(lane == 64 * (1 - side), 1.0, 0.0).astype(BF) for side in range(2)]
        for block, near in blocks:
            q = take(qs, block) * SCALE
            size = q.shape[0]
            all_scores = [dot(q * masks[side] + marks[side], keys[side], 1, 1) for side in range(2)]
            if near:
                same = same_ref[...].astype(F32) > 0.5
                extras = [jnp.where(same, dot(q * masks[side], sk_ref[...], 1, 1), MASKED) for side in range(2)]
            mixed, columns = [], jnp.zeros((size, LANES), F32)
            for side in range(2):
                scores = all_scores[side]
                peak = jnp.max(scores, axis=-1, keepdims=True)
                if near:
                    peak = jnp.maximum(peak, jnp.max(extras[side], axis=-1, keepdims=True))
                raised = jnp.exp(scores - peak)
                total = jnp.sum(raised, axis=-1, keepdims=True)
                value = dot(raised.astype(BF), v_ref[...])
                if near:
                    raised = jnp.exp(extras[side] - peak)
                    total = total + jnp.sum(raised, axis=-1, keepdims=True)
                    value = value + dot(raised.astype(BF), sv_ref[...])
                mixed.append(value * (1.0 / total))
                columns = columns + place_lanes(peak + jnp.log(total), lane, 2 * pair + side)
            give(outs, block, jnp.where(left, mixed[0], mixed[1]))
            done = 0
            for p, at, rows in block:
                held[p][at : at + rows, :] += columns[done : done + rows]
                done += rows

    @pl.when(pair == HEADS // 2)
    def _():
        for out, h in zip(outs, held):
            out[...] = h[...].astype(BF)


def query_forward(qs, cross, slot_kv, key_bias, same, blocks, deps):
    width = qs[0].shape[1]
    patches, slots = cross.shape[0], slot_kv.shape[0]
    pairs = HEADS // 2
    total = sum(q.shape[0] for q in qs)
    col = lambda rows, first: pl.BlockSpec((rows, LANES), lambda p: (0, first + jnp.minimum(p, pairs - 1)))
    return call(
        functools.partial(query_forward_kernel, pieces=len(qs), blocks=blocks),
        "query_forward",
        [(q, col(q.shape[0], 0)) for q in qs]
        + [(cross, col(patches, 0)), (cross, col(patches, pairs)), (slot_kv, col(slots, 0)), (slot_kv, col(slots, pairs))]
        + [(a, whole(a.shape)) for a in (key_bias, same)],
        [((q.shape[0], width + LANES), BF, pl.BlockSpec((q.shape[0], LANES), lambda p: (0, p))) for q in qs],
        grid=(pairs + 1,),
        scratch=[pltpu.VMEM((q.shape[0], LANES), F32) for q in qs],
        deps=deps,
        work=(16 * total * patches * width, 1e7, total * patches * HEADS),
    )


def stat_lanes(stats, pair):
    shape = (LANES, 2 * LANES)
    row, col = iota(shape, 0), iota(shape, 1)
    group, lane = col // LANES, col % LANES
    side, place = lane // 4, lane % 4
    hit = (row == 48 * group + 2 * pair + side + 16 * place) & (side < 2) & (place < 3)
    return dot(stats, jnp.where(hit, -1.0, 0.0).astype(BF)).astype(BF)


def query_back_kernel(*refs, pieces, blocks, near_block, first_pair):
    qs, gos, stats = refs[:pieces], refs[pieces : 2 * pieces], refs[2 * pieces : 3 * pieces]
    k_ref, v_ref, sk_ref, sv_ref, kb_ref, same_ref = refs[3 * pieces : 3 * pieces + 6]
    dqs = refs[3 * pieces + 6 : 4 * pieces + 6]
    dk_ref, dv_ref, dsk_ref, dsv_ref, sum_k, sum_v = refs[4 * pieces + 6 : 4 * pieces + 12]
    near_dqs = refs[4 * pieces + 12 :]
    pair = pl.program_id(0) + first_pair
    left, masks = head_masks()
    lane = iota((1, LANES), 1)
    patches, slots = k_ref.shape[0], sk_ref.shape[0]
    ones = [jnp.where((lane >= 4 * k) & (lane < 4 * k + 3), 1.0, 0.0).astype(BF) for k in range(2)]
    plain = jnp.where(lane == 8, 1.0, 0.0).astype(BF)

    def both_heads(rows, bias=None):
        extra = [jnp.broadcast_to(ones[k], rows.shape) for k in range(2)]
        if bias is not None:
            extra = [jnp.where(lane == 8, bias, e) for e in extra]
        return stack([stack([rows * masks[k], extra[k]], 1) for k in range(2)])

    keys, values = both_heads(k_ref[...], kb_ref[...]), both_heads(v_ref[...])

    def sides(block):
        q, g, st = take(qs, block), take(gos, block), take(stats, block)
        lanes = stat_lanes(st, pair)
        return q, g, stack([q * SCALE, lanes[:, :LANES] + plain], 1), stack([g, lanes[:, LANES:]], 1)

    for ref in near_dqs:
        ref[...] = jnp.zeros_like(ref)
    q, g, shifted, lowered = sides(near_block)
    same = same_ref[...].astype(F32)
    scores = dot(both_heads(sk_ref[...]), shifted, 1, 1)
    probs = jnp.exp(jnp.where(stack([same, same]) > 0.5, scores, MASKED))
    dscore = (probs * dot(both_heads(sv_ref[...]), lowered, 1, 1)).astype(BF)
    dsk, dsv = dot(dscore, q), dot(probs.astype(BF), g)
    moved = [dot(dscore[k * slots : (k + 1) * slots], sk_ref[...], 0, 0) for k in range(2)]
    give(near_dqs, near_block, jnp.where(left, moved[0], moved[1]))
    dsk_ref[...] = (jnp.where(left, dsk[:slots], dsk[slots:]) * SCALE).astype(BF)
    dsv_ref[...] = jnp.where(left, dsv[:slots], dsv[slots:]).astype(BF)

    for number, block in enumerate(blocks):
        q, g, shifted, lowered = sides(block)
        size = q.shape[0]
        probs = jnp.exp(dot(keys, shifted, 1, 1))
        dscore = (probs * dot(values, lowered, 1, 1)).astype(BF)
        dv = dot(probs.astype(BF), g)
        dk = dot(dscore, q)
        dq = dot(stack([dscore[:patches], dscore[patches:]], 1), k_ref[...], 0, 0)
        near = take(near_dqs, block)
        give(dqs, block, (jnp.where(left, dq[:size], dq[size:]) + near) * SCALE)
        if number == 0:
            sum_k[...] = jnp.where(left, dk[:patches], dk[patches:])
            sum_v[...] = jnp.where(left, dv[:patches], dv[patches:])
        else:
            sum_k[...] += jnp.where(left, dk[:patches], dk[patches:])
            sum_v[...] += jnp.where(left, dv[:patches], dv[patches:])
    dk_ref[...] = (sum_k[...] * SCALE).astype(BF)
    dv_ref[...] = sum_v[...].astype(BF)


def query_backward(qs, gos, cross, slot_kv, key_bias, same, near_block, part, deps):
    patches, slots = cross.shape[0], slot_kv.shape[0]
    pairs = HEADS // 2
    count = pairs // 2
    width = count * LANES
    total = sum(q.shape[0] for q in qs)
    blocks = []
    for number, q in enumerate(qs):
        step = min(256, q.shape[0])
        blocks += [[(number, at, step)] for at in range(0, q.shape[0], step)]
    col = lambda rows, first: pl.BlockSpec((rows, LANES), lambda p: (0, first + part * count + p))
    out = lambda rows: ((rows, width), BF, pl.BlockSpec((rows, LANES), lambda p: (0, p)))
    found = call(
        functools.partial(
            query_back_kernel, pieces=len(qs), blocks=blocks, near_block=near_block, first_pair=part * count
        ),
        "query_backward",
        [(q, col(q.shape[0], 0)) for q in qs]
        + [(g, col(g.shape[0], 0)) for g in gos]
        + [(g, pl.BlockSpec((g.shape[0], LANES), lambda p: (0, pairs))) for g in gos]
        + [(cross, col(patches, 0)), (cross, col(patches, pairs)), (slot_kv, col(slots, 0)), (slot_kv, col(slots, pairs))]
        + [(a, whole(a.shape)) for a in (key_bias, same)],
        [out(q.shape[0]) for q in qs] + [out(patches), out(patches), out(slots), out(slots)],
        grid=(count,),
        scratch=[pltpu.VMEM((patches, LANES), F32)] * 2 + [pltpu.VMEM((q.shape[0], LANES), F32) for q in qs],
        deps=deps,
        work=(20 * total * patches * width, 1.5e7, total * patches * HEADS // 2),
    )
    return found[: len(qs)], *found[len(qs) :]


def query_ffn_kernel(s_ref, *refs, parts, tiled):
    outs = refs[:parts]
    x_ref, own_ref, theirs_ref, gain_ref, wo_ref, up_ref, down_ref = refs[parts : parts + 7]
    (
        out_own_ref, out_other_ref, grad_ref, send_ref, att_ref, normed_ref, act_ref, dact_ref, branch_ref, cot_ref,
        gain_grad_ref, mixed, after, total, back, joint,
    ) = refs[parts + 7 :]
    step = pl.program_id(0)
    width = x_ref.shape[1]

    @pl.when(step == 0)
    def _():
        each = [join_lanes(o[:, width:].astype(F32), 0) for o in outs]
        peak = functools.reduce(jnp.maximum, each)
        weights = [jnp.exp(e - peak) for e in each]
        weight_sum = functools.reduce(jnp.add, weights)
        joint[...] = peak + jnp.log(weight_sum)
        value = None
        for o, w in zip(outs, weights):
            term = o[:, :width].astype(F32) * spread_heads(w / weight_sum, width)
            value = term if value is None else value + term
        mixed[...] = value
        att_ref[...] = value.astype(BF)
        rows = x_ref[...].astype(F32) + dot(att_ref[...], wo_ref[...])
        after[...] = rows
        unit, _ = norm_stats(rows)
        normed_ref[...] = (unit * gain_ref[3:4, :]).astype(BF)
        cot_ref[...] = pair_rows(own_ref[0].astype(F32), theirs_ref[...].astype(F32), s_ref[ODD]).astype(BF)
        total[...] = jnp.zeros_like(total)
        back[...] = jnp.zeros_like(back)

    grads = dot(cot_ref[...], down_ref[...], 1, 1)
    value, slope = gelu_pair(dot(normed_ref[...], up_ref[...]))
    dact = (slope * grads).astype(BF)
    dact_ref[...] = dact
    back[...] += dot(dact, up_ref[...], 1, 1)
    act = value.astype(BF)
    act_ref[...] = act
    total[...] += dot(act, down_ref[...])

    @pl.when(step == pl.num_programs(0) - 1)
    def _():
        rows = after[...] + total[...]
        own_slots = rows.shape[0] // 2
        low, high = rows[:own_slots], rows[own_slots:]
        odd = s_ref[ODD] == 1
        out_own_ref[0] = jnp.where(odd, high, low).astype(BF)
        out_other_ref[...] = jnp.where(odd, low, high).astype(BF)
        unit, spread = norm_stats(after[...])
        grad, gain_part = norm_back(unit, spread, gain_ref[3:4, :], back[...])
        gain_grad_ref[...] = jnp.broadcast_to(gain_part, gain_grad_ref.shape)
        grad = cot_ref[...].astype(F32) + grad
        grad_ref[...] = grad
        branch = grad.astype(BF)
        branch_ref[...] = branch
        sent = dot(branch, wo_ref[...], 1, 1).astype(BF)
        send_ref[:, :width] = sent
        pick = (iota((width, LANES), 0) // (width // HEADS) == iota((width, LANES), 1)).astype(F32).astype(BF)
        high, middle, low = three_parts(sent.astype(F32) * mixed[...])
        inner = dot(high.astype(BF), pick) + dot(middle.astype(BF), pick) + dot(low.astype(BF), pick)
        lane = iota((1, LANES), 1)
        packed = jnp.zeros(inner.shape, F32)
        for source, first in ((joint[...], 0), (inner, 48)):
            kept = jnp.where(lane < HEADS, source, 0.0)
            for number, piece in enumerate(three_parts(kept)):
                amount = first + 16 * number
                packed = packed + (piece if amount == 0 else pltpu.roll(piece, amount, 1))
        send_ref[:, width:] = packed.astype(BF)


def query_ffn(scalars, outs, x, cot, cot_theirs, gains, wo, up, down, tiled, deps, chunk=768):
    slots, width = x.shape
    hidden = up.shape[1]
    rows = lambda w, kind: ((slots, w), kind, whole((slots, w)))
    chunks = ((slots, hidden), BF, pl.BlockSpec((slots, chunk), lambda j, *_: (0, j)))
    half = (slots // 2, width)
    return call(
        functools.partial(query_ffn_kernel, parts=len(outs), tiled=tiled),
        "query_ffn",
        [(a, whole(a.shape)) for a in (*outs, x)]
        + [(cot, page_block(cot.shape))]
        + [(a, whole(a.shape)) for a in (cot_theirs, gains, wo)]
        + [
            (up, pl.BlockSpec((width, chunk), lambda j, *_: (0, j))),
            (down, pl.BlockSpec((chunk, width), lambda j, *_: (j, 0))),
        ],
        [
            (cot.shape, BF, page_block(cot.shape)), (half, BF, whole(half)), rows(width, F32), rows(width + LANES, BF),
            rows(width, BF), rows(width, BF), chunks, chunks, rows(width, BF), rows(width, BF), ((8, width), F32, whole((8, width))),
        ],
        grid=(hidden // chunk,),
        scratch=[pltpu.VMEM((slots, width), F32)] * 4 + [pltpu.VMEM((slots, LANES), F32)],
        scalars=scalars,
        deps=deps,
        work=(8 * slots * width * hidden, 2e7, slots * hidden),
    )


def query_weights_kernel(normed_ref, cot_ref, att_ref, branch_ref, act_ref, dact_ref, wo_ref, up_ref, down_ref, *, tiled):
    put_grad(up_ref, dot(normed_ref[...], dact_ref[...], 0, 0).astype(BF), store_columns, 0, tiled)
    put_grad(down_ref, dot(act_ref[...], cot_ref[...], 0, 0).astype(BF), store_strips, 1, tiled)

    @pl.when(pl.program_id(0) == 0)
    def _():
        put_grad(wo_ref, dot(att_ref[...], branch_ref[...], 0, 0).astype(BF), store_all, 1, tiled)


def query_weights(normed, cot, att, branch, act, dact, tiled, deps, chunk=768):
    slots, width = normed.shape
    hidden = act.shape[1]
    return call(
        functools.partial(query_weights_kernel, tiled=tiled),
        "query_weights",
        [(a, whole((slots, width))) for a in (normed, cot, att, branch)]
        + [(a, pl.BlockSpec((slots, chunk), lambda j: (0, j))) for a in (act, dact)],
        grad_forms(width, hidden, chunk, tiled, 1),
        grid=(hidden // chunk,),
        deps=deps,
        work=(4 * slots * width * hidden, 1.6e7, 0),
    )


def query_out_kernel(s_ref, *refs, parts, tiled):
    halves = [refs[:parts], refs[parts : 2 * parts]]
    others = refs[2 * parts : 2 * parts + 4]
    n_ref, x_ref, grad_ref, gain_ref, w_ref, rows_ref = refs[2 * parts + 4 : 2 * parts + 10]
    own_ref, other_ref, w_grad_ref, gain_grad_ref = refs[2 * parts + 10 : 2 * parts + 14]
    width = x_ref.shape[1]
    sums = []
    for dqs in halves:
        value = dqs[0][...].astype(F32)
        for d in dqs[1:]:
            value = value + d[...].astype(F32)
        sums.append(value.astype(BF))
    join = lambda a, b: jnp.concatenate([a, b], axis=1)
    pieces = [join(*sums), join(others[0][...], others[1][...]), join(others[2][...], others[3][...])]
    back = None
    for number, piece in enumerate(pieces):
        cols = slice(number * width, (number + 1) * width)
        term = dot(piece, w_ref[:, cols], 1, 1)
        back = term if back is None else back + term
        (refs[-1] if tiled else w_grad_ref)[:, cols] = dot(n_ref[...], piece, 0, 0).astype(BF)
    if tiled:
        store_all(w_grad_ref, refs[-1][...], 1)
    unit, spread = norm_stats(x_ref[...].astype(F32))
    grad, gain_part = norm_back(unit, spread, gain_ref[2:3, :], back)
    rows = grad_ref[...] + grad
    own_slots = rows.shape[0] // 2
    low, high = rows[:own_slots], rows[own_slots:]
    odd = s_ref[ODD] == 1
    own_ref[0] = jnp.where(odd, high, low)
    other_ref[...] = jnp.where(odd, low, high).astype(BF)
    gain_rows = rows_ref[...] + jnp.where(iota((8, width), 0) == 2, gain_part, 0.0)
    if not tiled:
        gain_grad_ref[...] = gain_rows
        return
    turned = gain_rows.T
    size = width // 16
    lane = iota((1, LANES), 1)
    for half in range(2):
        tile = jnp.where(lane == 0, turned[:, 2 * half : 2 * half + 1], 0.0)
        tile = jnp.where(lane == 1, turned[:, 2 * half + 1 : 2 * half + 2], tile).astype(BF)
        for strip in range(8):
            for core in range(2):
                at = (2 * strip + core) * size
                gain_grad_ref[(core, *tile_index(strip, half, 0), slice(None), slice(None))] = tile[at : at + size]


def query_out(scalars, dqs, dks, dvs, normed, x, grad, gains, w, gain_rows, pages, tiled, deps):
    slots, width = x.shape
    own_shape = (pages, slots // 2, width)
    w_shape = tile_shape(width, w.shape[1]) if tiled else w.shape
    g_shape, g_kind = (tile_shape(width, 256), BF) if tiled else ((8, width), F32)
    ins = (*dqs[0], *dqs[1], *dks, *dvs, normed, x, grad, gains, w, gain_rows)
    return call(
        functools.partial(query_out_kernel, parts=len(dqs[0]), tiled=tiled),
        "query_out",
        [(a, whole(a.shape, True)) for a in ins],
        [
            (own_shape, F32, page_block(own_shape)),
            ((slots // 2, width), BF, whole((slots // 2, width))),
            (w_shape, BF, whole(w_shape)),
            (g_shape, g_kind, whole(g_shape)),
        ],
        scratch=[pltpu.VMEM(w.shape, BF)] if tiled else [],
        scalars=scalars,
        deps=deps,
        work=(4 * slots * width * w.shape[1], 1e7, 0),
    )


PAIR = pl.DeviceIdType.MESH


def coordinates():
    page, strip = lax.axis_index("page"), lax.axis_index("strip")
    core, x = lax.rem(page, 2), page // 2
    y, z_low, z_high = lax.rem(strip, 2), lax.rem(strip // 2, 2), strip // 4
    flip = lambda index, bit, weight: index + weight - 2 * weight * bit
    core_mate = (flip(page, core, 1), strip)
    mates = {
        "x": (x, (flip(page, x, 2), strip)),
        "y": (y, (page, flip(strip, y, 1))),
        "low": (z_low, (page, flip(strip, z_low, 2))),
        "high": (z_high, (page, flip(strip, z_high, 4))),
    }
    return core, core_mate, [[mates[k] for k in ("y", "x", "low", "high")], [mates[k] for k in ("x", "y", "low", "high")]]


def meet(mates):
    barrier = pltpu.get_barrier_semaphore()
    for mate in mates:
        pl.semaphore_signal(barrier, inc=1, device_id=mate, device_id_type=PAIR)
    pl.semaphore_wait(barrier, len(mates))


def send(source, target, sems, number, mate):
    copy = pltpu.make_async_remote_copy(
        src_ref=source,
        dst_ref=target,
        send_sem=sems.at[0, number],
        recv_sem=sems.at[1, number],
        device_id=mate,
        device_id_type=PAIR,
    )
    copy.start()
    return copy


def add_rows(target, first, source, start, length, at, rows):
    span = pl.ds(at, rows)

    def step(i, carry):
        total = target[first + i, span, :].astype(F32) + source[start + i, span, :].astype(F32)
        target[first + i, span, :] = total.astype(BF)
        return carry

    lax.fori_loop(0, length, step, 0)


def query_sum_kernel(*refs, rows):
    up_ref, down_ref, wo_ref, normed_ref, cot_ref, att_ref, branch_ref, act_ref, dact_ref = refs[:9]
    outs = refs[9:13]
    own_up, own_down, own_wo, held_0, held_1, remote, near = refs[13:]
    held = (held_0, held_1)
    core, core_mate, orders = coordinates()
    meet([core_mate])
    wide, small = rows
    far, mine = [], []
    for number, (grad, order, at, size) in enumerate(((up_ref, 0, 0, wide), (down_ref, 1, 0, wide), (wo_ref, 0, 2 * wide, small))):
        span, bit = pl.ds(at, size), orders[order][0][0]
        far.append(send(grad.at[1 - core], held[order].at[:, :, :, span, :], remote, number, core_mate))
        for which in range(2):
            first = bit if which else 1 - bit
            copy = pltpu.make_async_copy(
                grad.at[core, first], outs[2 * order + which].at[:, :, span, :], near.at[2 * number + which]
            )
            copy.start()
            mine.append(copy)
    width = normed_ref.shape[1]
    own_rows = ((own_up, 0, wide, wide), (own_down, 1, wide, wide), (own_wo, 1, 2 * wide, small))
    store_all(own_wo, dot(att_ref[...], branch_ref[...], 0, 0).astype(BF), 1)
    for j in range(act_ref.shape[1] // width):
        cols = slice(j * width, (j + 1) * width)
        store_columns(own_up, dot(normed_ref[...], dact_ref[:, cols], 0, 0).astype(BF), 0, j // 2, (j % 2) * (width // LANES))
        store_strips(own_down, dot(act_ref[:, cols], cot_ref[...], 0, 0).astype(BF), 1, (j % 2) * 2 + j // 2)
    later = []
    for number, (grad, order, at, size) in enumerate(own_rows):
        later.append(send(grad.at[1 - core], held[order].at[:, :, :, pl.ds(at, size), :], remote, 3 + number, core_mate))
    for copy in far + mine:
        copy.wait()

    def add(order, at, size, own):
        bit = orders[order][0][0]
        span = pl.ds(at, size)
        for which in range(2):
            out, first = outs[2 * order + which], bit if which else 1 - bit
            for i in range(2):

                def step(z, carry, out=out, first=first, i=i):
                    mine = out[i, z, span, :] if own is None else own[core, first, i, z]
                    out[i, z, span, :] = (mine.astype(F32) + held[order][first, i, z, span, :].astype(F32)).astype(BF)
                    return carry

                lax.fori_loop(0, 4, step, 0)

    for order, at, size in ((0, 0, wide), (1, 0, wide), (0, 2 * wide, small)):
        add(order, at, size, None)
    for copy, (grad, order, at, size) in zip(later, own_rows):
        copy.wait()
        add(order, at, size, grad)


def query_sum(patch_grads, normed, cot, att, branch, act, dact, collective, deps):
    width, hidden = normed.shape[1], act.shape[1]
    shapes = [tile_shape(width, hidden), tile_shape(hidden, width), tile_shape(width, width)]
    rows = (shapes[0][-2], shapes[2][-2])
    total = 2 * rows[0] + rows[1]
    vmem = pl.BlockSpec(memory_space=pltpu.VMEM)
    kernel = functools.partial(query_sum_kernel, rows=rows)
    outs = pl.pallas_call(
        lambda *refs: kernel(*refs[:9], *refs[9 + len(deps) :]),
        in_specs=[ANY] * 3 + [vmem] * 6 + [ANY] * len(deps),
        out_specs=[vmem] * 4,
        out_shape=[sds((2, 4, total, LANES), BF)] * 4,
        scratch_shapes=[
            *[pltpu.VMEM(shape, BF) for shape in shapes],
            pltpu.VMEM((2, 2, 4, total, LANES), BF),
            pltpu.VMEM((2, 2, 4, total, LANES), BF),
            pltpu.SemaphoreType.DMA((2, 6)),
            pltpu.SemaphoreType.DMA((6,)),
        ],
        compiler_params=pltpu.CompilerParams(collective_id=collective, has_side_effects=True, vmem_limit_bytes=VMEM_BYTES),
        name="query_sum",
    )(*patch_grads, normed, cot, att, branch, act, dact, *deps)
    return [out.reshape(8, total, LANES) for out in outs]


ORDERS = (("y", "x", "low", "high"), ("x", "y", "low", "high"))
PLACES = {"x": BIT_X, "y": BIT_Y, "low": BIT_LOW, "high": BIT_HIGH}


def across(array, name):
    axis, weight = {"x": ("page", 2), "y": ("strip", 1), "low": ("strip", 2), "high": ("strip", 4)}[name]
    return lax.ppermute(array, axis, [(i, i ^ weight) for i in range(lax.axis_size(axis))])


def halve_add_kernel(s_ref, *refs):
    for k in range(4):
        keep, got, out = refs[2 * k], refs[2 * k + 1], refs[8 + k]
        out[...] = (keep[...].astype(F32) + got[...].astype(F32)).astype(BF)


def halve_add(scalars, kept, got, stage, deps):
    ins, outs = [], []
    for order in range(2):
        size = kept[order].shape[0] // 2
        shape = kept[order].shape[1:]
        place = PLACES[ORDERS[order][stage]]
        for flip in (1, 0):
            spec = pl.BlockSpec(
                (1, *shape),
                lambda i, s, place=place, flip=flip, size=size: ((1 - s[place] if flip else s[place]) * size + i, 0, 0),
            )
            ins += [(kept[order], spec), (got[order], spec)]
            outs.append(((size, *shape), BF, pl.BlockSpec((1, *shape), lambda i, s: (i, 0, 0))))
    return call(
        halve_add_kernel, "halve_add", ins, outs, grid=(size,), scalars=scalars, deps=deps, work=(1e6, 6 * size * 1296 * 512, 0)
    )


def late_sum_kernel(*refs, lots, arrays, early_rows):
    grads = refs[:arrays]
    early = refs[arrays : arrays + 4]
    own, got = refs[arrays + 4 : arrays + 6], refs[arrays + 6 : arrays + 8]
    sums, first_held = refs[arrays + 8 : arrays + 10], refs[arrays + 10 : arrays + 12]
    held = [refs[arrays + 12 : arrays + 16], refs[arrays + 16 : arrays + 20]]
    done, loaded, early_held = refs[arrays + 20 : arrays + 22], refs[arrays + 22 : arrays + 26], refs[arrays + 26 : arrays + 28]
    remote, near = refs[arrays + 28 :]
    core, core_mate, orders = coordinates()
    meet([core_mate] + [mate for _, mate in orders[0]])
    numbers, local_numbers = iter(range(1000)), iter(range(1000))
    jobs = []
    for order, at, members in lots:
        copies, first = [], at
        for member, start, rows in members:
            there, span = pl.ds(start, rows), pl.ds(first, rows)
            first += rows
            copies.append(
                send(grads[member].at[1 - core, :, there, :], first_held[order].at[:, span, :], remote, next(numbers), core_mate)
            )
            copy = pltpu.make_async_copy(
                grads[member].at[core, :, there, :], sums[order].at[:, span, :], near.at[next(local_numbers)]
            )
            copy.start()
            copies.append(copy)
        jobs.append((order, at, first - at, copies))
    loads = []
    for k in range(4):
        copy = pltpu.make_async_copy(early[k], loaded[k], near.at[next(local_numbers)])
        copy.start()
        loads.append(copy)
    for copy in loads:
        copy.wait()
    early_flights = []
    for order in range(2):
        bit, mate = orders[order][3]
        kept = loaded[2 * order]
        add_rows(kept, 1 - bit, loaded[2 * order + 1], 1 - bit, 1, 0, early_rows)
        early_flights.append(send(kept.at[1 - bit], early_held[order], remote, next(numbers), mate))
        add_rows(kept, bit, loaded[2 * order + 1], bit, 1, 0, early_rows)
    bases = [0] * len(jobs)
    flights = [None] * len(jobs)
    first_exchange = []
    for stage in range(4):
        size = 8 >> stage
        for n, (order, at, rows, copies) in enumerate(jobs):
            source = first_held[order] if stage == 0 else held[order][stage - 1]
            for copy in copies if stage == 0 else [flights[n]]:
                copy.wait()
            bit, mate = orders[order][stage]
            out, keep = size * (1 - bit), size * bit
            base = bases[n]
            add_rows(sums[order], base + out, source, out, size, at, rows)
            flights[n] = send(
                sums[order].at[pl.ds(base + out, size), pl.ds(at, rows), :],
                held[order][stage].at[:, pl.ds(at, rows), :],
                remote,
                next(numbers),
                mate,
            )
            add_rows(sums[order], base + keep, source, keep, size, at, rows)
            bases[n] = base + keep
        if stage == 2:
            for order in range(2):
                early_flights[order].wait()
                total = loaded[2 * order][orders[order][3][0]].astype(F32) + early_held[order][...].astype(F32)
                own[order][:early_rows, :] = total.astype(BF)
                span = pl.ds(0, early_rows)
                first_exchange.append(send(own[order].at[span, :], done[order].at[span, :], remote, next(numbers), core_mate))
    exchange = []
    for n, (order, at, rows, _) in enumerate(jobs):
        flights[n].wait()
        value = sums[order][bases[n], pl.ds(at, rows), :].astype(F32) + held[order][3][0, pl.ds(at, rows), :].astype(F32)
        span = pl.ds(early_rows + at, rows)
        own[order][span, :] = value.astype(BF)
        exchange.append(send(own[order].at[span, :], done[order].at[span, :], remote, next(numbers), core_mate))
    for copy in first_exchange + exchange:
        copy.wait()
    for order in range(2):
        got[order][...] = done[order][...]


def late_sum(grads, lots, rows, early, collective, deps):
    grads = [g.reshape(2, 16, *g.shape[-2:]) for g in grads]
    arrays = len(grads)
    members = sum(len(lot[2]) for lot in lots)
    early_rows = early[0].shape[1]
    share = [sds((early_rows + r, LANES), BF) for r in rows]
    vmem = lambda *shape: pltpu.VMEM(shape, BF)
    kernel = functools.partial(late_sum_kernel, lots=lots, arrays=arrays, early_rows=early_rows)
    first = arrays + 4
    return pl.pallas_call(
        lambda *refs: kernel(*refs[:first], *refs[first + len(deps) :]),
        in_specs=[ANY] * (first + len(deps)),
        out_specs=[pl.BlockSpec(memory_space=pltpu.VMEM)] * 4,
        out_shape=share + share,
        scratch_shapes=[
            *[vmem(16, r, LANES) for r in rows],
            *[vmem(16, r, LANES) for r in rows],
            *[vmem(8 >> k, rows[0], LANES) for k in range(4)],
            *[vmem(8 >> k, rows[1], LANES) for k in range(4)],
            *[vmem(early_rows + r, LANES) for r in rows],
            *[vmem(2, early_rows, LANES)] * 4,
            *[vmem(early_rows, LANES)] * 2,
            pltpu.SemaphoreType.DMA((2, members + 5 * len(lots) + 4)),
            pltpu.SemaphoreType.DMA((members + 4,)),
        ],
        compiler_params=pltpu.CompilerParams(collective_id=collective, has_side_effects=True, vmem_limit_bytes=VMEM_BYTES),
        name="late_sum",
    )(*grads, *early, *deps)


def finish_kernel(core_ref, own0, own1, got0, got1, gain_ref, *outs, plan):
    first = core_ref[0] == 0
    owns, gots = (own0, own1), (got0, got1)
    lane = iota((1, LANES), 1)
    left = lane < 64

    def tile(order, at, size, part):
        mine = owns[order][at : at + size, :].astype(F32)
        theirs = gots[order][at : at + size, :].astype(F32)
        return jnp.where(first == (part == 0), mine, theirs)

    for out, (size, tiles, flipped) in zip(outs, plan):
        count = len(tiles)
        for part in range(2):
            rows = slice(part * size, (part + 1) * size)
            values = [tile(order, at, size, part) for order, at in tiles]
            if count % 2 == 0:
                for t in range(count // 2):
                    out[rows, t * LANES : (t + 1) * LANES] = jnp.where(first, values[t], values[t + count // 2])
                continue
            turned = [pltpu.roll(v, 64, 1) for v in values[count // 2 :]]
            whole_tiles = [
                jnp.where(first, values[t], jnp.where(left, turned[t], turned[t + 1])) for t in range(count // 2)
            ]
            rest = jnp.where(first, values[count // 2], turned[-1])
            if flipped:
                for t, value in enumerate(whole_tiles):
                    for at in range(0, size, 64):
                        column = part * size + at
                        out[t * LANES : (t + 1) * LANES, column : column + 64] = value[at : at + 64].T
                for at in range(0, size, 64):
                    column = part * size + at
                    out[count // 2 * LANES :, column : column + 64] = rest[at : at + 64].T[:64]
                continue
            for t, value in enumerate(whole_tiles):
                out[rows, t * LANES : (t + 1) * LANES] = value
            out[rows, count // 2 * LANES :] = rest[:, :64]
    size = gain_ref.shape[1] // 2
    at = own0.shape[0] - size
    gain = jnp.concatenate([tile(0, at, size, part) for part in range(2)], axis=0).T
    gain_ref[...] = jnp.where(first, gain[0:1], gain[1:2])


def finish(core, shares, shapes, plan, gain_rows):
    vmem = pl.BlockSpec(memory_space=pltpu.VMEM)
    outs = [shape[::-1] if flipped else shape for shape, (_, _, flipped) in zip(shapes, plan)]
    gain, *found = pl.pallas_call(
        functools.partial(finish_kernel, plan=plan),
        in_specs=[pl.BlockSpec(memory_space=pltpu.SMEM)] + [vmem] * 4,
        out_specs=[vmem] * (1 + len(outs)),
        out_shape=[sds((1, gain_rows), F32)] + [sds(shape, F32) for shape in outs],
        compiler_params=pltpu.CompilerParams(vmem_limit_bytes=VMEM_BYTES),
        name="finish",
    )(core, *shares)
    return gain.T, *[f.T if flipped else f for f, (_, _, flipped) in zip(found, plan)]


def from_ahead(array, count, distance):
    return lax.ppermute(array, "strip", [(i, (i - distance) % count) for i in range(count)])


def from_partner(array, count):
    return lax.ppermute(array, "strip", [(i, i ^ 1) for i in range(count)])


def scattered(grad):
    strips, pages = lax.axis_size("strip"), lax.axis_size("page")
    rows, cols = grad.shape
    part = lax.psum_scatter(grad, "strip", scatter_dimension=0, tiled=True)
    part = part.reshape(rows // strips, pages, cols // pages).transpose(1, 0, 2)
    return lax.psum_scatter(part, "page", scatter_dimension=0, tiled=False).astype(F32)


def local(
    visual_in, query_in, row_valid, segment_ids, slot_valid, col_shift, row_shifted, norm_gains,
    w_vqkv, w_vout, w_up, w_down, w_qqkv, w_xkv, w_qout, w_qup, w_qdown, visual_cot, query_cot,
):
    pages, strip_rows, columns, width = visual_in.shape
    own_slots, all_slots = query_in.shape[1], segment_ids.shape[1]
    count = lax.axis_size("strip")
    tiled = count == 8
    group = count // 2
    half = strip_rows * columns
    slots = 2 * own_slots
    window = WIN * WIN
    form = (strip_rows, columns)
    place, page = lax.axis_index("strip"), lax.axis_index("page")
    odd = place % 2
    up = jnp.where(odd == 1, 1 - row_shifted[0], row_shifted[0])
    down = 1 - up
    pick = lambda array, which: lax.dynamic_index_in_dim(array, which, 0, keepdims=False)
    scalars = jnp.stack([up, pick(col_shift, up), odd, page % 2, page // 2, odd, place // 2 % 2, place // 4, (place // 2) * slots]).astype(jnp.int32)

    visual, cot = visual_in.reshape(pages, half, width), visual_cot.reshape(pages, half, width)
    query_sent, patch_sent = pack(scalars, [(query_in, slot_valid), (visual, row_valid)])
    query_theirs = from_partner(query_sent, count)
    patch_sent = held_back(patch_sent, [query_theirs])
    patch_other = from_ahead(patch_sent, count, 1)
    gains = jnp.pad(norm_gains.T, ((0, 4), (0, 0)))

    order = [-1] + list(range(group - 1))
    blocks = forward_blocks(group if tiled else 1, slots, group)
    near_block = next(block for block, near in blocks if near)

    def gather(array):
        pieces = [array if k == 0 else from_ahead(array, count, 2 * k) for k in order]
        return pieces if tiled else [jnp.concatenate(pieces, axis=0)]

    def give_back(arrays):
        if not tiled:
            arrays = [arrays[0][n * slots : (n + 1) * slots] for n in range(group)]
        return [piece if k == 0 else from_ahead(piece, count, -2 * k) for piece, k in zip(arrays, order)]

    x_query, normed_three, q_own, slot_kv, same, turned = query_in_call(
        scalars, segment_ids, slot_valid, query_in, query_theirs, gains, w_qqkv, [patch_sent]
    )
    qs = gather(q_own)
    x, normed_one, qkv, cross, key_bias = patch_in(
        scalars, row_valid, visual, patch_other, gains, w_vqkv, w_xkv, form, [q_own]
    )
    att = window_forward(qkv, window, [])
    cot_sent, cot_q_sent = pack_two(scalars, cot, query_cot, [att, *qs])
    cot_other, cot_theirs = from_ahead(cot_sent, count, 1), from_partner(cot_q_sent, count)
    q_out = query_forward(qs, cross, slot_kv, key_bias, same, blocks, [cot_q_sent])
    out_parts = give_back(q_out)
    (vis_own, vis_other, grad_after, grad_att, g_vout, g_up, g_down, gain_two) = patch_ffn(
        scalars, att, x, cot, cot_other, gains, w_vout, w_up, w_down, tiled, form, [q_out[0]]
    )
    vis_came = from_ahead(vis_other, count, -1)
    (q_res, q_res_other, grad_q, send_q, att_q, normed_four, act_q, dact_q, branch_q, cot_q, gain_four) = query_ffn(
        scalars, out_parts, x_query, query_cot, cot_theirs, gains, w_qout, w_qup, w_qdown, tiled, [gain_two]
    )
    gos = gather(send_q)
    res_came = from_partner(q_res_other, count)
    if tiled:
        out_0, keep_0, out_1, keep_1 = query_sum(
            [g_up, g_down, g_vout], normed_four, cot_q, att_q, branch_q, act_q, dact_q, 0, []
        )
        got = [across(out_0, "y"), across(out_1, "x")]
        last = keep_0
    else:
        g_qout, g_qup, g_qdown = query_weights(normed_four, cot_q, att_q, branch_q, act_q, dact_q, tiled, [])
        last = g_qout
    g_proj = window_backward(qkv, grad_att, window, [last, vis_came])
    last = [g_proj, res_came]
    dqs, dks, dvs, dsks, dsvs = [], [], [], [], []
    for part in range(2):
        dq, dk, dv, dsk, dsv = query_backward(qs, gos, cross, slot_kv, key_bias, turned, near_block, part, last)
        last = [dk] if part == 0 else [dk, *dqs[0]]
        dqs.append(give_back(dq))
        dks.append(dk)
        dvs.append(dv)
        dsks.append(dsk)
        dsvs.append(dsv)
        if tiled:
            out_0, keep_0, out_1, keep_1 = halve_add(scalars, [keep_0, keep_1], got, part + 1, last)
            got = [across(out_0, ORDERS[0][part + 1]), across(out_1, ORDERS[1][part + 1])]
            last = [keep_0]
    vin_own, vin_other, gain_rows, g_vqkv, *g_xkv = patch_back(
        scalars, g_proj, w_vqkv, dks, dvs, normed_one, x, grad_after, gains, w_xkv, gain_two, gain_four, pages, tiled, form, last
    )
    qin_own, qin_other, g_qqkv, gain_grads = query_out(
        scalars, dqs, dsks, dsvs, normed_three, x_query, grad_q, gains, w_qqkv, gain_rows, pages, tiled, got if tiled else []
    )

    vin_came = from_ahead(vin_other, count, -1)
    qin_came = from_partner(qin_other, count)

    weights = (w_vqkv, w_vout, w_up, w_down, w_qqkv, w_xkv, w_qout, w_qup, w_qdown)
    if tiled:
        size = lambda g: g.shape[-2]
        a, b, c, d, e = g_vqkv, g_xkv[0], gain_grads, g_qqkv, g_xkv[1]
        cut = (size(a) // 2 + 15) // 16 * 16
        lots = [
            (0, 0, [(0, 0, cut)]),
            (1, 0, [(3, 0, cut)]),
            (0, cut, [(0, cut, size(a) - cut)]),
            (1, cut, [(3, cut, size(d) - cut)]),
            (0, size(a), [(1, 0, size(b)), (2, 0, size(c))]),
            (1, size(d), [(4, 0, size(e))]),
        ]
        late_rows = [size(a) + size(b) + size(c), size(d) + size(e)]
        shares = late_sum([a, b, c, d, e], lots, late_rows, [keep_0, got[0], keep_1, got[1]], 1, [])
        tall, flat = g_up.shape[-2], g_vout.shape[-2]
        end = 2 * tall + flat
        where = {2: (0, 0), 7: (0, tall), 1: (0, 2 * tall), 0: (0, end), 5: (0, end + size(a))}
        where.update({3: (1, 0), 8: (1, tall), 6: (1, 2 * tall), 4: (1, end)})
        plan, shapes = [], []
        for number, weight in enumerate(weights):
            rows, cols = weight.shape
            step, tiles = rows // 16, cols // 256
            which, at = where[number]
            spots = [(which, at + t * step) for t in range(tiles)]
            if number == 5:
                spots = spots[:3] + [(1, end + size(d) + t * step) for t in range(3)]
            flipped = rows > 2 * cols and tiles % 2 == 1
            plan.append((step, spots, flipped))
            shapes.append((rows // 8, cols // lax.axis_size("page")))
        last = shares[0]
        gain_part, *parts = finish(scalars[CORE:CORE + 1], shares, shapes, plan, width // 8)
    else:
        last = gain_rows
        parts = [scattered(g) for g in (g_vqkv, g_vout, g_up, g_down, g_qqkv, g_xkv[0], g_qout, g_qup, g_qdown)]
        gain_part = lax.psum_scatter(gain_grads[:4], "page", scatter_dimension=0, tiled=True)
        gain_part = lax.psum_scatter(gain_part, "strip", scatter_dimension=1, tiled=True).reshape(-1, 1)
    visual_out, query_out_rows, visual_in_grad, query_in_grad = put(
        scalars, [vis_own, q_res, vin_own, qin_own], [vis_came, res_came, vin_came, qin_came], [last]
    )
    shape = (pages, strip_rows, columns, width)
    visual_out, visual_in_grad = visual_out.reshape(shape), visual_in_grad.reshape(shape)
    return (visual_out, query_out_rows, visual_in_grad, query_in_grad, gain_part, *parts)


def solution(mesh):
    tokens, slots, table = P("page", "strip", None, None), P("page", "strip", None), P("page", "strip")
    tile = P("strip", "page")
    return jax.shard_map(
        local,
        mesh=mesh,
        in_specs=(tokens, slots, table, P("page", None), table, P("page"), P("page")) + (P(),) * 10 + (tokens, slots),
        out_specs=(tokens, slots, tokens, slots) + (tile,) * 10,
        check_vma=False,
    )
```

```python
import functools

import jax
import jax.numpy as jnp
from jax import lax
from jax.experimental import pallas as pl
from jax.experimental.pallas import tpu as pltpu
from jax.sharding import PartitionSpec as P

HEADS = 12
WIN = 12
EPS = 1e-05
MASKED = -1e9
SCALE = 0.125
BF = jnp.bfloat16
F32 = jnp.float32
LANES = 128
VMEM_BYTES = 65400 * 1024


def dot(left, right, left_dim=1, right_dim=0):
    return lax.dot_general(
        left, right, (((left_dim,), (right_dim,)), ((), ())), preferred_element_type=F32
    )


def iota(shape, dim):
    return lax.broadcasted_iota(jnp.int32, shape, dim)


def norm_stats(rows):
    offset = rows - jnp.mean(rows, axis=-1, keepdims=True)
    spread = lax.rsqrt(jnp.mean(offset * offset, axis=-1, keepdims=True) + EPS)
    return offset * spread, spread


def norm_back(unit, spread, gain, grad):
    product = grad * unit
    scaled = grad * gain
    centre = jnp.mean(scaled, axis=-1, keepdims=True)
    slope = jnp.mean(scaled * unit, axis=-1, keepdims=True)
    return spread * (scaled - centre - unit * slope), jnp.sum(product, axis=0, keepdims=True)


def gelu_pair(t):
    square = t * t
    plus = 0.5 * jnp.tanh(t * (0.7978845608 + 0.0356774081 * square)) + 0.5
    value = t * plus
    return value, plus + value * (1.0 - plus) * (1.5957691216 + 0.2140644488 * square)


def three_parts(value):
    high = value.astype(BF).astype(F32)
    rest = value - high
    middle = rest.astype(BF).astype(F32)
    low = (rest - middle).astype(BF).astype(F32)
    return high, middle, low


def place_lanes(column, lane, first):
    high, middle, low = three_parts(column)
    return (
        jnp.where(lane == first, high, 0.0)
        + jnp.where(lane == first + 16, middle, 0.0)
        + jnp.where(lane == first + 32, low, 0.0)
    )


def join_lanes(stats, first):
    total = stats
    rolled = []
    for part in range(3):
        amount = (first + 16 * part) % LANES
        rolled.append(total if amount == 0 else pltpu.roll(total, LANES - amount, 1))
    return rolled[0] + rolled[1] + rolled[2]


def spread_heads(values, width):
    head_dim = width // HEADS
    pick = (iota((LANES, width), 0) == iota((LANES, width), 1) // head_dim).astype(BF)
    high, middle, low = three_parts(values)
    return dot(high.astype(BF), pick) + dot(middle.astype(BF), pick) + dot(low.astype(BF), pick)


def whole(shape, single=False):
    mode = pl.Buffered(1) if single else None
    return pl.BlockSpec(shape, lambda *_: (0,) * len(shape), pipeline_mode=mode)


def sds(shape, kind):
    return jax.ShapeDtypeStruct(shape, kind)


ANY = pl.BlockSpec(memory_space=pl.ANY)


def call(kernel, name, ins, outs, grid=(1,), scratch=(), scalars=None, deps=(), work=(0, 0, 0), aliases={}):
    first = len(ins) + (scalars is not None)

    def body(*refs):
        kernel(*refs[:first], *refs[first + len(deps) :])

    return pl.pallas_call(
        body,
        grid_spec=pltpu.PrefetchScalarGridSpec(
            num_scalar_prefetch=int(scalars is not None),
            grid=grid,
            in_specs=[spec for _, spec in ins] + [ANY] * len(deps),
            out_specs=[spec for *_, spec in outs],
            scratch_shapes=list(scratch),
        ),
        out_shape=[sds(shape, kind) for shape, kind, _ in outs],
        input_output_aliases=aliases,
        compiler_params=pltpu.CompilerParams(vmem_limit_bytes=VMEM_BYTES),
        cost_estimate=pl.CostEstimate(flops=int(3 * work[0]), bytes_accessed=int(work[1]), transcendentals=int(work[2])),
        name=name,
    )(*([] if scalars is None else [scalars]), *[array for array, _ in ins], *deps)


UP, SHIFT, ODD, CORE, BIT_X, BIT_Y, BIT_LOW, BIT_HIGH, BASE = range(9)


def page_block(shape):
    return pl.BlockSpec((1, *shape[1:]), lambda *at: (at[-1][UP],) + (0,) * (len(shape) - 1))


def steps_below(value, size, count):
    total = jnp.zeros_like(value)
    for k in range(1, count):
        total = total + jnp.where(value >= size * k, 1, 0)
    return total


def into_windows(own, other, shift, strip_rows, columns):
    half, part = strip_rows * columns, strip_rows * WIN
    token = iota((half, 1), 0)
    window = steps_below(token, part, columns // WIN)
    inside = token - part * window
    row = steps_below(inside, WIN, strip_rows)
    column = inside - WIN * row + WIN * window + shift
    column = jnp.where(column >= columns, column - columns, column)
    onehot = (iota((half, half), 1) == row * columns + column).astype(F32).astype(BF)
    turned = [dot(onehot, own), dot(onehot, other)]
    pieces = [turned[side][w * part : (w + 1) * part] for w in range(columns // WIN) for side in range(2)]
    return jnp.concatenate(pieces, axis=0)


def out_of_windows(shift, strip_rows, columns):
    half = strip_rows * columns
    token = iota((half, 1), 0)
    row = steps_below(token, columns, strip_rows)
    column = token - columns * row - shift
    column = jnp.where(column < 0, column + columns, column)
    window = steps_below(column, WIN, columns // WIN)
    spot = window * (strip_rows * WIN) + row * WIN + column - WIN * window
    return (iota((half, half), 1) == spot).astype(F32).astype(BF)


def tile_index(strip, half, order):
    y = strip % 2
    lead = (y, half) if order == 0 else (half, y)
    return lead + ((strip // 2 % 2) * 2 + strip // 4,)


def tile_shape(rows, cols):
    return (2, 2, 2, 4, cols // 256 * (rows // 16), LANES)


def store_all(ref, value, order):
    rows, cols = value.shape
    size, tiles = rows // 16, cols // 256
    for strip in range(8):
        for core in range(2):
            at = (2 * strip + core) * size
            for half in range(2):
                lead = tile_index(strip, half, order)
                for t in range(tiles):
                    lanes = (half * tiles + t) * LANES
                    ref[(core, *lead, slice(t * size, (t + 1) * size), slice(None))] = value[at : at + size, lanes : lanes + LANES]


def store_columns(ref, value, order, half=0, first=0):
    size = value.shape[0] // 16
    for strip in range(8):
        for core in range(2):
            at = (2 * strip + core) * size
            lead = tile_index(strip, half, order)
            for t in range(value.shape[1] // LANES):
                rows = slice((first + t) * size, (first + t + 1) * size)
                ref[(core, *lead, rows, slice(None))] = value[at : at + size, t * LANES : (t + 1) * LANES]


def store_strips(ref, value, order, z=0):
    size, tiles = value.shape[0] // 4, value.shape[1] // 256
    for y in range(2):
        for core in range(2):
            for half in range(2):
                lead = (y, half) if order == 0 else (half, y)
                for t in range(tiles):
                    lanes = (half * tiles + t) * LANES
                    at = (2 * y + core) * size
                    ref[(core, *lead, z, slice(t * size, (t + 1) * size), slice(None))] = value[at : at + size, lanes : lanes + LANES]


def columns_spec(rows, chunk, per_half, order, at):
    block = (2, 2, 1, 4) if order == 0 else (2, 1, 2, 4)
    lead = lambda half: (0, 0, half, 0) if order == 0 else (0, half, 0, 0)
    return pl.BlockSpec(
        (*block, chunk // LANES * (rows // 16), LANES), lambda j, *_: (*lead(at(j) // per_half), at(j) % per_half, 0)
    )


def strips_spec(rows, cols):
    return pl.BlockSpec(
        (2, 2, 2, 1, cols // 256 * (rows // 16), LANES), lambda j, *_: (0, 0, 0, (j % 2) * 2 + j // 2, 0, 0)
    )


def grad_forms(width, hidden, chunk, tiled, wo_order):
    if not tiled:
        return [
            ((width, width), BF, whole((width, width))),
            ((width, hidden), BF, pl.BlockSpec((width, chunk), lambda j, *_: (0, j))),
            ((hidden, width), BF, pl.BlockSpec((chunk, width), lambda j, *_: (j, 0))),
        ]
    shapes = [tile_shape(width, width), tile_shape(width, hidden), tile_shape(hidden, width)]
    specs = [
        whole(shapes[0]),
        columns_spec(width, chunk, hidden // 2 // chunk, 0, lambda j: j),
        strips_spec(hidden, width),
    ]
    return [(shape, BF, spec) for shape, spec in zip(shapes, specs)]


def put_grad(ref, value, store, order, tiled):
    if tiled:
        store(ref, value, order)
    else:
        ref[...] = value


def patch_in_kernel(s_ref, ok_ref, own_ref, other_ref, gain_ref, wq_ref, wx_ref, x_ref, n_ref, qkv_ref, cross_ref, bias_ref, turned, *, form):
    strip_rows, half = form[0], own_ref.shape[1]
    row = steps_below(iota((WIN * WIN, 1), 0), WIN, WIN)
    valid = jnp.zeros((WIN * WIN, 1), F32)
    for r in range(strip_rows):
        mine = jnp.where(ok_ref[s_ref[UP], r] == 1, 1.0, 0.0)
        theirs = other_ref[half : half + 1, r : r + 1].astype(F32)
        valid = valid + jnp.where(row == r, mine, 0.0) + jnp.where(row == strip_rows + r, theirs, 0.0)
    bias = jnp.broadcast_to(jnp.where(valid > 0.5, 0.0, MASKED).astype(BF), (WIN * WIN, LANES))
    for k in range(2):
        bias_ref[k * WIN * WIN : (k + 1) * WIN * WIN, :] = bias
    @pl.when(pl.program_id(0) == 0)
    def _():
        turned[...] = into_windows(own_ref[0], other_ref[:half, :], s_ref[SHIFT], *form).astype(BF)

    step = x_ref.shape[0]
    x = turned[pl.ds(pl.multiple_of(pl.program_id(0) * step, step), step), :].astype(F32)
    x_ref[...] = x.astype(BF)
    unit, _ = norm_stats(x)
    normed = (unit * gain_ref[0:1, :]).astype(BF)
    n_ref[...] = normed
    qkv_ref[...] = dot(normed, wq_ref[...]).astype(BF)
    cross_ref[...] = dot(normed, wx_ref[...]).astype(BF)


def patch_in(scalars, rows_ok, visual, other, gains, wq, wx, form, deps):
    _, half, width = visual.shape
    tokens = 2 * half
    step = 4 * form[0] * WIN
    rows = lambda w: ((tokens, w), BF, pl.BlockSpec((step, w), lambda i, *_: (i, 0)))
    return call(
        functools.partial(patch_in_kernel, form=form),
        "patch_in",
        [(rows_ok, pl.BlockSpec(memory_space=pltpu.SMEM)), (visual, page_block(visual.shape))]
        + [(a, whole(a.shape, True)) for a in (other, gains, wq, wx)],
        [rows(width), rows(width), rows(wq.shape[1]), rows(wx.shape[1]), rows(LANES)],
        grid=(tokens // step,),
        scratch=[pltpu.VMEM((tokens, width), BF)],
        scalars=scalars,
        deps=deps,
        work=(2 * tokens * width * (wq.shape[1] + wx.shape[1]), 2e7, 0),
    )


def pack_kernel(s_ref, ok_a_ref, a_ref, ok_b_ref, b_ref, a_out, b_out):
    for ok_ref, rows_ref, out_ref in ((ok_a_ref, a_ref, a_out), (ok_b_ref, b_ref, b_out)):
        count, flags = rows_ref.shape[1], ok_ref.shape[1]
        out_ref[:count, :] = rows_ref[0]
        out_ref[count:, :] = jnp.zeros_like(out_ref[count:, :])
        theirs = jnp.where(s_ref[UP] == 0, ok_ref[1:2, :], ok_ref[0:1, :]).astype(F32).astype(BF)
        out_ref[count:, :flags] = jnp.broadcast_to(theirs, (out_ref.shape[0] - count, flags))


def other_page(shape):
    return pl.BlockSpec((1, *shape[1:]), lambda *at: (1 - at[-1][UP],) + (0,) * (len(shape) - 1))


def pack(scalars, arrays):
    ins, outs = [], []
    for rows, flags in arrays:
        ins += [(flags, whole(flags.shape)), (rows, other_page(rows.shape))]
        shape = (rows.shape[1] + 16, rows.shape[2])
        outs.append((shape, BF, whole(shape)))
    return call(pack_kernel, "pack", ins, outs, scalars=scalars)


def held_back(array, deps):
    [out] = call(lambda a_ref, out_ref: None, "held_back", [(array, ANY)], [(array.shape, array.dtype, ANY)], deps=deps, aliases={0: 0})
    return out


def pack_two_kernel(s_ref, a_ref, b_ref, a_out, b_out):
    a_out[...] = a_ref[0]
    b_out[...] = b_ref[0]


def pack_two(scalars, a, b, deps):
    return call(
        pack_two_kernel,
        "pack_two",
        [(x, other_page(x.shape)) for x in (a, b)],
        [(x.shape[1:], BF, whole(x.shape[1:])) for x in (a, b)],
        scalars=scalars,
        deps=deps,
    )


def put_kernel(s_ref, *refs):
    count = len(refs) // 3
    for came, out in zip(refs[count : 2 * count], refs[2 * count :]):
        out[0] = came[...].astype(out.dtype)


def put(scalars, arrays, came, deps):
    return call(
        put_kernel,
        "put",
        [(a, ANY) for a in arrays] + [(c, whole(c.shape)) for c in came],
        [(a.shape, a.dtype, other_page(a.shape)) for a in arrays],
        scalars=scalars,
        deps=deps,
        aliases={k + 1: k for k in range(len(arrays))},
    )


def head_masks():
    lane = iota((1, LANES), 1)
    left = lane < 64
    return left, [left.astype(F32).astype(BF), (~left).astype(F32).astype(BF)]


def stack(parts, axis=0):
    return jnp.concatenate(parts, axis=axis)


def window_kernel(qkv_ref, out_ref):
    tokens, width = out_ref.shape
    left, masks = head_masks()
    for pair in range(HEADS // 2):
        at = pair * LANES
        q = qkv_ref[:, at : at + LANES] * SCALE
        k = qkv_ref[:, width + at : width + at + LANES]
        v = qkv_ref[:, 2 * width + at : 2 * width + at + LANES]
        scores = dot(stack([q * masks[0], q * masks[1]]), k, 1, 1)
        raised = jnp.exp(scores - jnp.max(scores, axis=-1, keepdims=True))
        total = jnp.sum(raised, axis=-1, keepdims=True)
        mixed = dot(raised.astype(BF), v) * (1.0 / total)
        out_ref[:, at : at + LANES] = jnp.where(left, mixed[:tokens], mixed[tokens:]).astype(BF)


def window_forward(qkv, tokens, deps):
    total, width3 = qkv.shape
    width = width3 // 3
    rows = lambda w: pl.BlockSpec((tokens, w), lambda i: (i, 0))
    [att] = call(
        window_kernel,
        "window_forward",
        [(qkv, rows(width3))],
        [((total, width), BF, rows(width))],
        grid=(total // tokens,),
        deps=deps,
        work=(16 * total * tokens * width, 8e6, total * tokens * HEADS),
    )
    return att


def window_back_kernel(qkv_ref, go_ref, out_ref):
    tokens, width = go_ref.shape
    left, masks = head_masks()
    for pair in range(HEADS // 2):
        at = pair * LANES
        q = qkv_ref[:, at : at + LANES]
        k = qkv_ref[:, width + at : width + at + LANES]
        v = qkv_ref[:, 2 * width + at : 2 * width + at + LANES]
        g = go_ref[:, at : at + LANES]
        scaled = q * SCALE
        all_scores = [dot(k * masks[side], scaled, 1, 1) for side in range(2)]
        all_grads = [dot(v * masks[side], g, 1, 1) for side in range(2)]
        parts = []
        for scores, grads in zip(all_scores, all_grads):
            raised = jnp.exp(scores - jnp.max(scores, axis=0, keepdims=True))
            inverse = 1.0 / jnp.sum(raised, axis=0, keepdims=True)
            probs = raised * inverse
            inner = jnp.sum(probs * grads, axis=0, keepdims=True)
            dscore = (probs * (grads - inner)).astype(BF)
            parts.append((dot(dscore, k, 0, 0), dot(dscore, q), dot(probs.astype(BF), g)))
        for index, factor in ((0, SCALE), (1, SCALE), (2, 1.0)):
            joined = jnp.where(left, parts[0][index], parts[1][index]) * factor
            out_ref[:, index * width + at : index * width + at + LANES] = joined.astype(BF)


def window_backward(qkv, go, tokens, deps):
    total, width3 = qkv.shape
    width = width3 // 3
    rows = lambda w: pl.BlockSpec((tokens, w), lambda i: (i, 0))
    [out] = call(
        window_back_kernel,
        "window_backward",
        [(qkv, rows(width3)), (go, rows(width))],
        [((total, width3), BF, rows(width3))],
        grid=(total // tokens,),
        deps=deps,
        work=(40 * total * tokens * width, 1.3e7, total * tokens * HEADS),
    )
    return out


def split_halves(rows, part):
    count = rows.shape[0] // (2 * part)
    return [
        jnp.concatenate([rows[(2 * w + s) * part : (2 * w + s + 1) * part] for w in range(count)], axis=0)
        for s in range(2)
    ]


def patch_ffn_kernel(
    s_ref, att_ref, x_ref, own_ref, other_ref, gain_ref, wo_ref, up_ref, down_ref,
    out_own_ref, out_other_ref, after_grad_ref, att_grad_ref, wo_grad_ref, up_grad_ref, down_grad_ref, gain_grad_ref,
    after, normed, cot, total, acts, dacts,
    *, tiled, form,
):
    step = pl.program_id(0)
    tokens, width = att_ref.shape
    part = form[0] * WIN
    block = 4 * part
    back = after_grad_ref
    blocks = [slice(b * block, (b + 1) * block) for b in range(tokens // block)]

    @pl.when(step == 0)
    def _():
        cot[...] = into_windows(own_ref[0], other_ref[...], s_ref[SHIFT], *form).astype(BF)
        for rows in blocks:
            value = x_ref[rows, :].astype(F32) + dot(att_ref[rows, :], wo_ref[...])
            after[rows, :] = value
            unit, _ = norm_stats(value)
            normed[rows, :] = (unit * gain_ref[1:2, :]).astype(BF)

    def products(first):
        enter = lambda rows: (dot(normed[rows, :], up_ref[...]), dot(cot[rows, :], down_ref[...], 1, 1))
        ahead = enter(blocks[0])
        for b, rows in enumerate(blocks):
            pre, grads = ahead
            if b + 1 < len(blocks):
                ahead = enter(blocks[b + 1])
            value, slope = gelu_pair(pre)
            act = value.astype(BF)
            acts[rows, :] = act
            dact = (slope * grads).astype(BF)
            dacts[rows, :] = dact
            if first:
                total[rows, :] = dot(act, down_ref[...])
                back[rows, :] = dot(dact, up_ref[...], 1, 1)
            else:
                total[rows, :] += dot(act, down_ref[...])
                back[rows, :] += dot(dact, up_ref[...], 1, 1)

    @pl.when(step == 0)
    def _():
        products(True)

    @pl.when(step > 0)
    def _():
        products(False)

    put_grad(up_grad_ref, dot(normed[...], dacts[...], 0, 0).astype(BF), store_columns, 0, tiled)
    put_grad(down_grad_ref, dot(acts[...], cot[...], 0, 0).astype(BF), store_strips, 1, tiled)

    @pl.when(step == pl.num_programs(0) - 1)
    def _():
        gain_sum = jnp.zeros((1, width), F32)
        for rows in blocks:
            unit, spread = norm_stats(after[rows, :])
            grad, gain_part = norm_back(unit, spread, gain_ref[1:2, :], back[rows, :])
            gain_sum = gain_sum + gain_part
            grad = cot[rows, :].astype(F32) + grad
            after_grad_ref[rows, :] = grad
            branch = grad.astype(BF)
            normed[rows, :] = branch
            att_grad_ref[rows, :] = dot(branch, wo_ref[...], 1, 1).astype(BF)
        gain_grad_ref[...] = jnp.broadcast_to(gain_sum, gain_grad_ref.shape)
        put_grad(wo_grad_ref, dot(att_ref[...], normed[...], 0, 0).astype(BF), store_all, 0, tiled)
        halves = split_halves(after[...] + total[...], part)
        onehot = out_of_windows(s_ref[SHIFT], *form)
        out_own_ref[0] = dot(onehot, halves[0].astype(BF)).astype(BF)
        out_other_ref[...] = dot(onehot, halves[1].astype(BF)).astype(BF)


def patch_ffn(scalars, att, x, cot, cot_other, gains, wo, up, down, tiled, form, deps, chunk=768):
    tokens, width = att.shape
    half = tokens // 2
    hidden = up.shape[1]
    single = lambda a: (a, whole(a.shape, True))
    return call(
        functools.partial(patch_ffn_kernel, tiled=tiled, form=form),
        "patch_ffn",
        [
            single(att), single(x), (cot, page_block(cot.shape)), single(cot_other), single(gains), single(wo),
            (up, pl.BlockSpec((width, chunk), lambda j, *_: (0, j))),
            (down, pl.BlockSpec((chunk, width), lambda j, *_: (j, 0))),
        ],
        [
            (cot.shape, BF, page_block(cot.shape)),
            ((half, width), BF, whole((half, width))),
            ((tokens, width), F32, whole((tokens, width))),
            ((tokens, width), BF, whole((tokens, width))),
            *grad_forms(width, hidden, chunk, tiled, 0),
            ((8, width), F32, whole((8, width))),
        ],
        grid=(hidden // chunk,),
        scratch=[
            pltpu.VMEM((tokens, width), F32),
            pltpu.VMEM((tokens, width), BF),
            pltpu.VMEM((tokens, width), BF),
            pltpu.VMEM((tokens, width), F32),
            pltpu.VMEM((tokens, chunk), BF),
            pltpu.VMEM((tokens, chunk), BF),
        ],
        scalars=scalars,
        deps=deps,
        work=(12 * tokens * width * hidden, 4e7, tokens * hidden),
    )


def patch_back_kernel(
    s_ref, gp_ref, wq_ref, gk0_ref, gk1_ref, gv0_ref, gv1_ref, n_ref, x_ref, after_ref, gain_ref, wx_ref, g2_ref, g4_ref,
    own_ref, other_ref, gain_grad_ref, wq_grad_ref, *rest,
    tiled, form,
):
    step = pl.program_id(0)
    half, width = other_ref.shape
    tokens = 2 * half
    part = form[0] * WIN
    block = 4 * part
    back = rest[-1]

    def query_part(first):
        term = dot(gp_ref[...], wq_ref[...], 1, 1)
        back[...] = term if first else back[...] + term
        put_grad(wq_grad_ref, dot(n_ref[...], gp_ref[...], 0, 0).astype(BF), store_columns, 0, tiled)

    def cross_part(grad):
        back[...] += dot(grad, wx_ref[...], 1, 1)
        w_grad = dot(n_ref[...], grad, 0, 0).astype(BF)
        if not tiled:
            rest[0][...] = w_grad
            return
        store_columns(rest[0], w_grad[:, : width // 2], 0)
        store_columns(rest[1], w_grad[:, width // 2 :], 1)

    @pl.when(step == 0)
    def _():
        query_part(True)

    @pl.when(step == 1)
    def _():
        query_part(False)

    @pl.when(step == 2)
    def _():
        cross_part(jnp.concatenate([gk0_ref[...], gk1_ref[...]], axis=1))

    @pl.when(step == 3)
    def _():
        cross_part(jnp.concatenate([gv0_ref[...], gv1_ref[...]], axis=1))
        gain_sum = jnp.zeros((1, width), F32)
        for b in range(tokens // block):
            rows = slice(b * block, (b + 1) * block)
            unit, spread = norm_stats(x_ref[rows, :].astype(F32))
            grad, gain_part = norm_back(unit, spread, gain_ref[0:1, :], back[rows, :])
            gain_sum = gain_sum + gain_part
            back[rows, :] = after_ref[rows, :] + grad
        row = iota((8, width), 0)
        gain_grad_ref[...] = jnp.where(row == 0, gain_sum, jnp.where(row == 1, g2_ref[...], jnp.where(row == 3, g4_ref[...], 0.0)))
        halves = split_halves(back[...], part)
        onehot = out_of_windows(s_ref[SHIFT], *form)
        high = halves[0].astype(BF)
        low = (halves[0] - high.astype(F32)).astype(BF)
        own_ref[0] = dot(onehot, high) + dot(onehot, low)
        other_ref[...] = dot(onehot, halves[1].astype(BF)).astype(BF)


def patch_back(scalars, gp, wq, gks, gvs, normed, x, after, gains, wx, g2, g4, pages, tiled, form, deps):
    tokens, width = x.shape
    half = tokens // 2
    cols = wx.shape[1]
    chunk = wq.shape[1] // 2
    at_q, at_x = (lambda j: jnp.minimum(j, 1)), (lambda j: jnp.maximum(j - 2, 0))
    if tiled:
        shape = tile_shape(width, cols // 2)
        grads = [(tile_shape(width, wq.shape[1]), BF, columns_spec(width, chunk, 1, 0, at_q))]
        grads += [(shape, BF, columns_spec(width, width // 2, 1, order, at_x)) for order in (0, 1)]
    else:
        grads = [
            (wq.shape, BF, pl.BlockSpec((width, chunk), lambda j, *_: (0, at_q(j)))),
            (wx.shape, BF, pl.BlockSpec((width, width), lambda j, *_: (0, at_x(j)))),
        ]
    single = lambda a: (a, whole(a.shape, True))
    own_shape = (pages, half, width)
    return call(
        functools.partial(patch_back_kernel, tiled=tiled, form=form),
        "patch_back",
        [
            (gp, pl.BlockSpec((tokens, chunk), lambda j, *_: (0, at_q(j)))),
            (wq, pl.BlockSpec((width, chunk), lambda j, *_: (0, at_q(j)))),
            *[single(a) for a in (*gks, *gvs, normed, x, after, gains)],
            (wx, pl.BlockSpec((width, width), lambda j, *_: (0, at_x(j)))),
            single(g2),
            single(g4),
        ],
        [
            (own_shape, F32, page_block(own_shape)),
            ((half, width), BF, whole((half, width))),
            ((8, width), F32, whole((8, width))),
            *grads,
        ],
        grid=(4,),
        scratch=[pltpu.VMEM((tokens, width), F32)],
        scalars=scalars,
        deps=deps,
        work=(4 * tokens * width * (cols + wq.shape[1]), 4e7, 0),
    )


def pair_rows(own, theirs, odd):
    return jnp.where(odd == 1, jnp.concatenate([theirs, own], axis=0), jnp.concatenate([own, theirs], axis=0))


def query_in_kernel(
    s_ref, seg_ref, ok_ref, own_ref, theirs_ref, gain_ref, w_ref, x_ref, n_ref, q_ref, kv_ref, same_ref, turned_ref
):
    own_slots = own_ref.shape[1]
    x = pair_rows(own_ref[0].astype(F32), theirs_ref[:own_slots, :].astype(F32), s_ref[ODD])
    slots, total = 2 * own_slots, seg_ref.shape[1]
    reach = slots + 64
    first = s_ref[UP] == 0
    segments = jnp.where(first, seg_ref[0:1, :], seg_ref[1:2, :]).astype(F32)
    amount = 32 - s_ref[BASE]
    near = pltpu.roll(jnp.broadcast_to(segments, (8, total)), jnp.where(amount < 0, amount + total, amount), 1)
    mine = jnp.where(first, ok_ref[0:1, :], ok_ref[1:2, :]).astype(F32)
    theirs = theirs_ref[own_slots : own_slots + 1, :own_slots].astype(F32)
    valid = jnp.where(s_ref[ODD] == 1, jnp.concatenate([theirs, mine], axis=1), jnp.concatenate([mine, theirs], axis=1))
    own = pltpu.roll(near, total - 32, 1)[0:1, :slots]
    own = jnp.where(valid > 0.5, own, -1.0)
    padded = -(-reach // LANES) * LANES
    column = near[:, :padded].T[:reach, 0:1]
    same = jnp.where(column == own, 1.0, 0.0)
    same_ref[...] = same.astype(BF)
    turned_ref[...] = same.T.astype(BF)
    x_ref[...] = x.astype(BF)
    unit, _ = norm_stats(x)
    normed = (unit * gain_ref[2:3, :]).astype(BF)
    n_ref[...] = normed
    width = x.shape[1]
    q_ref[...] = dot(normed, w_ref[:, :width]).astype(BF)
    kv_ref[...] = dot(normed, w_ref[:, width:]).astype(BF)


def query_in_call(scalars, segments, slots_ok, queries, theirs, gains, w, deps):
    _, own_slots, width = queries.shape
    slots = 2 * own_slots
    reach = slots + 64
    rows = lambda w: ((slots, w), BF, whole((slots, w)))
    return call(
        query_in_kernel,
        "query_in",
        [(segments, whole(segments.shape)), (slots_ok, whole(slots_ok.shape)), (queries, page_block(queries.shape))]
        + [(a, whole(a.shape)) for a in (theirs, gains, w)],
        [rows(width), rows(width), rows(width), rows(2 * width)]
        + [(shape, BF, whole(shape)) for shape in ((reach, slots), (slots, reach))],
        deps=deps,
        scalars=scalars,
        work=(2 * slots * width * w.shape[1], 5e6, 0),
    )


def forward_blocks(pieces, slots, group):
    if pieces > 1:
        blocks = [([(0, 0, slots - 32)], False), ([(0, slots - 32, 32), (1, 0, slots), (2, 0, 32)], True)]
        blocks.append(([(2, 32, slots - 32)], False))
        return blocks + [([(k, 0, slots)], False) for k in range(3, pieces)]
    blocks = [([(0, slots - 32, slots + 64)], True)]
    if slots > 32:
        blocks.append(([(0, 0, slots - 32)], False))
    at, total = 2 * slots + 32, slots * group
    while at < total:
        size = min(256, total - at)
        blocks.append(([(0, at, size)], False))
        at += size
    return blocks


def take(refs, block):
    parts = [refs[p][at : at + size, :] for p, at, size in block]
    return parts[0] if len(parts) == 1 else jnp.concatenate([p.astype(F32) for p in parts], axis=0).astype(parts[0].dtype)


def give(refs, block, value):
    done = 0
    for p, at, size in block:
        refs[p][at : at + size, :] = value[done : done + size].astype(refs[p].dtype)
        done += size


def query_forward_kernel(*refs, pieces, blocks):
    qs = refs[:pieces]
    k_ref, v_ref, sk_ref, sv_ref, kb_ref, same_ref = refs[pieces : pieces + 6]
    outs, held = refs[pieces + 6 : 2 * pieces + 6], refs[2 * pieces + 6 :]
    pair = pl.program_id(0)
    left, masks = head_masks()
    lane = iota((1, LANES), 1)

    @pl.when(pair == 0)
    def _():
        for h in held:
            h[...] = jnp.zeros_like(h)

    @pl.when(pair < HEADS // 2)
    def _():
        keys = [jnp.where(lane == 64 * (1 - side), kb_ref[...], k_ref[...]) for side in range(2)]
        marks = [jnp.where(lane == 64 * (1 - side), 1.0, 0.0).astype(BF) for side in range(2)]
        for block, near in blocks:
            q = take(qs, block) * SCALE
            size = q.shape[0]
            all_scores = [dot(q * masks[side] + marks[side], keys[side], 1, 1) for side in range(2)]
            if near:
                same = same_ref[...].astype(F32) > 0.5
                extras = [jnp.where(same, dot(q * masks[side], sk_ref[...], 1, 1), MASKED) for side in range(2)]
            mixed, columns = [], jnp.zeros((size, LANES), F32)
            for side in range(2):
                scores = all_scores[side]
                peak = jnp.max(scores, axis=-1, keepdims=True)
                if near:
                    peak = jnp.maximum(peak, jnp.max(extras[side], axis=-1, keepdims=True))
                raised = jnp.exp(scores - peak)
                total = jnp.sum(raised, axis=-1, keepdims=True)
                value = dot(raised.astype(BF), v_ref[...])
                if near:
                    raised = jnp.exp(extras[side] - peak)
                    total = total + jnp.sum(raised, axis=-1, keepdims=True)
                    value = value + dot(raised.astype(BF), sv_ref[...])
                mixed.append(value * (1.0 / total))
                columns = columns + place_lanes(peak + jnp.log(total), lane, 2 * pair + side)
            give(outs, block, jnp.where(left, mixed[0], mixed[1]))
            done = 0
            for p, at, rows in block:
                held[p][at : at + rows, :] += columns[done : done + rows]
                done += rows

    @pl.when(pair == HEADS // 2)
    def _():
        for out, h in zip(outs, held):
            out[...] = h[...].astype(BF)


def query_forward(qs, cross, slot_kv, key_bias, same, blocks, deps):
    width = qs[0].shape[1]
    patches, slots = cross.shape[0], slot_kv.shape[0]
    pairs = HEADS // 2
    total = sum(q.shape[0] for q in qs)
    col = lambda rows, first: pl.BlockSpec((rows, LANES), lambda p: (0, first + jnp.minimum(p, pairs - 1)))
    return call(
        functools.partial(query_forward_kernel, pieces=len(qs), blocks=blocks),
        "query_forward",
        [(q, col(q.shape[0], 0)) for q in qs]
        + [(cross, col(patches, 0)), (cross, col(patches, pairs)), (slot_kv, col(slots, 0)), (slot_kv, col(slots, pairs))]
        + [(a, whole(a.shape)) for a in (key_bias, same)],
        [((q.shape[0], width + LANES), BF, pl.BlockSpec((q.shape[0], LANES), lambda p: (0, p))) for q in qs],
        grid=(pairs + 1,),
        scratch=[pltpu.VMEM((q.shape[0], LANES), F32) for q in qs],
        deps=deps,
        work=(16 * total * patches * width, 1e7, total * patches * HEADS),
    )


def stat_lanes(stats, pair):
    shape = (LANES, 2 * LANES)
    row, col = iota(shape, 0), iota(shape, 1)
    group, lane = col // LANES, col % LANES
    side, place = lane // 4, lane % 4
    hit = (row == 48 * group + 2 * pair + side + 16 * place) & (side < 2) & (place < 3)
    return dot(stats, jnp.where(hit, -1.0, 0.0).astype(BF)).astype(BF)


def query_back_kernel(*refs, pieces, blocks, near_block, first_pair):
    qs, gos, stats = refs[:pieces], refs[pieces : 2 * pieces], refs[2 * pieces : 3 * pieces]
    k_ref, v_ref, sk_ref, sv_ref, kb_ref, same_ref = refs[3 * pieces : 3 * pieces + 6]
    dqs = refs[3 * pieces + 6 : 4 * pieces + 6]
    dk_ref, dv_ref, dsk_ref, dsv_ref, sum_k, sum_v = refs[4 * pieces + 6 : 4 * pieces + 12]
    near_dqs = refs[4 * pieces + 12 :]
    pair = pl.program_id(0) + first_pair
    left, masks = head_masks()
    lane = iota((1, LANES), 1)
    patches, slots = k_ref.shape[0], sk_ref.shape[0]
    ones = [jnp.where((lane >= 4 * k) & (lane < 4 * k + 3), 1.0, 0.0).astype(BF) for k in range(2)]
    plain = jnp.where(lane == 8, 1.0, 0.0).astype(BF)

    def both_heads(rows, bias=None):
        extra = [jnp.broadcast_to(ones[k], rows.shape) for k in range(2)]
        if bias is not None:
            extra = [jnp.where(lane == 8, bias, e) for e in extra]
        return stack([stack([rows * masks[k], extra[k]], 1) for k in range(2)])

    keys, values = both_heads(k_ref[...], kb_ref[...]), both_heads(v_ref[...])

    def sides(block):
        q, g, st = take(qs, block), take(gos, block), take(stats, block)
        lanes = stat_lanes(st, pair)
        return q, g, stack([q * SCALE, lanes[:, :LANES] + plain], 1), stack([g, lanes[:, LANES:]], 1)

    for ref in near_dqs:
        ref[...] = jnp.zeros_like(ref)
    q, g, shifted, lowered = sides(near_block)
    same = same_ref[...].astype(F32)
    scores = dot(both_heads(sk_ref[...]), shifted, 1, 1)
    probs = jnp.exp(jnp.where(stack([same, same]) > 0.5, scores, MASKED))
    dscore = (probs * dot(both_heads(sv_ref[...]), lowered, 1, 1)).astype(BF)
    dsk, dsv = dot(dscore, q), dot(probs.astype(BF), g)
    moved = [dot(dscore[k * slots : (k + 1) * slots], sk_ref[...], 0, 0) for k in range(2)]
    give(near_dqs, near_block, jnp.where(left, moved[0], moved[1]))
    dsk_ref[...] = (jnp.where(left, dsk[:slots], dsk[slots:]) * SCALE).astype(BF)
    dsv_ref[...] = jnp.where(left, dsv[:slots], dsv[slots:]).astype(BF)

    for number, block in enumerate(blocks):
        q, g, shifted, lowered = sides(block)
        size = q.shape[0]
        probs = jnp.exp(dot(keys, shifted, 1, 1))
        dscore = (probs * dot(values, lowered, 1, 1)).astype(BF)
        dv = dot(probs.astype(BF), g)
        dk = dot(dscore, q)
        dq = dot(stack([dscore[:patches], dscore[patches:]], 1), k_ref[...], 0, 0)
        near = take(near_dqs, block)
        give(dqs, block, (jnp.where(left, dq[:size], dq[size:]) + near) * SCALE)
        if number == 0:
            sum_k[...] = jnp.where(left, dk[:patches], dk[patches:])
            sum_v[...] = jnp.where(left, dv[:patches], dv[patches:])
        else:
            sum_k[...] += jnp.where(left, dk[:patches], dk[patches:])
            sum_v[...] += jnp.where(left, dv[:patches], dv[patches:])
    dk_ref[...] = (sum_k[...] * SCALE).astype(BF)
    dv_ref[...] = sum_v[...].astype(BF)


def query_backward(qs, gos, cross, slot_kv, key_bias, same, near_block, part, deps):
    patches, slots = cross.shape[0], slot_kv.shape[0]
    pairs = HEADS // 2
    count = pairs // 2
    width = count * LANES
    total = sum(q.shape[0] for q in qs)
    blocks = []
    for number, q in enumerate(qs):
        step = min(256, q.shape[0])
        blocks += [[(number, at, step)] for at in range(0, q.shape[0], step)]
    col = lambda rows, first: pl.BlockSpec((rows, LANES), lambda p: (0, first + part * count + p))
    out = lambda rows: ((rows, width), BF, pl.BlockSpec((rows, LANES), lambda p: (0, p)))
    found = call(
        functools.partial(
            query_back_kernel, pieces=len(qs), blocks=blocks, near_block=near_block, first_pair=part * count
        ),
        "query_backward",
        [(q, col(q.shape[0], 0)) for q in qs]
        + [(g, col(g.shape[0], 0)) for g in gos]
        + [(g, pl.BlockSpec((g.shape[0], LANES), lambda p: (0, pairs))) for g in gos]
        + [(cross, col(patches, 0)), (cross, col(patches, pairs)), (slot_kv, col(slots, 0)), (slot_kv, col(slots, pairs))]
        + [(a, whole(a.shape)) for a in (key_bias, same)],
        [out(q.shape[0]) for q in qs] + [out(patches), out(patches), out(slots), out(slots)],
        grid=(count,),
        scratch=[pltpu.VMEM((patches, LANES), F32)] * 2 + [pltpu.VMEM((q.shape[0], LANES), F32) for q in qs],
        deps=deps,
        work=(20 * total * patches * width, 1.5e7, total * patches * HEADS // 2),
    )
    return found[: len(qs)], *found[len(qs) :]


def query_ffn_kernel(s_ref, *refs, parts, tiled):
    outs = refs[:parts]
    x_ref, own_ref, theirs_ref, gain_ref, wo_ref, up_ref, down_ref = refs[parts : parts + 7]
    (
        out_own_ref, out_other_ref, grad_ref, send_ref, att_ref, normed_ref, act_ref, dact_ref, branch_ref, cot_ref,
        gain_grad_ref, mixed, after, total, back, joint,
    ) = refs[parts + 7 :]
    step = pl.program_id(0)
    width = x_ref.shape[1]

    @pl.when(step == 0)
    def _():
        each = [join_lanes(o[:, width:].astype(F32), 0) for o in outs]
        peak = functools.reduce(jnp.maximum, each)
        weights = [jnp.exp(e - peak) for e in each]
        weight_sum = functools.reduce(jnp.add, weights)
        joint[...] = peak + jnp.log(weight_sum)
        value = None
        for o, w in zip(outs, weights):
            term = o[:, :width].astype(F32) * spread_heads(w / weight_sum, width)
            value = term if value is None else value + term
        mixed[...] = value
        att_ref[...] = value.astype(BF)
        rows = x_ref[...].astype(F32) + dot(att_ref[...], wo_ref[...])
        after[...] = rows
        unit, _ = norm_stats(rows)
        normed_ref[...] = (unit * gain_ref[3:4, :]).astype(BF)
        cot_ref[...] = pair_rows(own_ref[0].astype(F32), theirs_ref[...].astype(F32), s_ref[ODD]).astype(BF)
        total[...] = jnp.zeros_like(total)
        back[...] = jnp.zeros_like(back)

    grads = dot(cot_ref[...], down_ref[...], 1, 1)
    value, slope = gelu_pair(dot(normed_ref[...], up_ref[...]))
    dact = (slope * grads).astype(BF)
    dact_ref[...] = dact
    back[...] += dot(dact, up_ref[...], 1, 1)
    act = value.astype(BF)
    act_ref[...] = act
    total[...] += dot(act, down_ref[...])

    @pl.when(step == pl.num_programs(0) - 1)
    def _():
        rows = after[...] + total[...]
        own_slots = rows.shape[0] // 2
        low, high = rows[:own_slots], rows[own_slots:]
        odd = s_ref[ODD] == 1
        out_own_ref[0] = jnp.where(odd, high, low).astype(BF)
        out_other_ref[...] = jnp.where(odd, low, high).astype(BF)
        unit, spread = norm_stats(after[...])
        grad, gain_part = norm_back(unit, spread, gain_ref[3:4, :], back[...])
        gain_grad_ref[...] = jnp.broadcast_to(gain_part, gain_grad_ref.shape)
        grad = cot_ref[...].astype(F32) + grad
        grad_ref[...] = grad
        branch = grad.astype(BF)
        branch_ref[...] = branch
        sent = dot(branch, wo_ref[...], 1, 1).astype(BF)
        send_ref[:, :width] = sent
        pick = (iota((width, LANES), 0) // (width // HEADS) == iota((width, LANES), 1)).astype(F32).astype(BF)
        high, middle, low = three_parts(sent.astype(F32) * mixed[...])
        inner = dot(high.astype(BF), pick) + dot(middle.astype(BF), pick) + dot(low.astype(BF), pick)
        lane = iota((1, LANES), 1)
        packed = jnp.zeros(inner.shape, F32)
        for source, first in ((joint[...], 0), (inner, 48)):
            kept = jnp.where(lane < HEADS, source, 0.0)
            for number, piece in enumerate(three_parts(kept)):
                amount = first + 16 * number
                packed = packed + (piece if amount == 0 else pltpu.roll(piece, amount, 1))
        send_ref[:, width:] = packed.astype(BF)


def query_ffn(scalars, outs, x, cot, cot_theirs, gains, wo, up, down, tiled, deps, chunk=768):
    slots, width = x.shape
    hidden = up.shape[1]
    rows = lambda w, kind: ((slots, w), kind, whole((slots, w)))
    chunks = ((slots, hidden), BF, pl.BlockSpec((slots, chunk), lambda j, *_: (0, j)))
    half = (slots // 2, width)
    return call(
        functools.partial(query_ffn_kernel, parts=len(outs), tiled=tiled),
        "query_ffn",
        [(a, whole(a.shape)) for a in (*outs, x)]
        + [(cot, page_block(cot.shape))]
        + [(a, whole(a.shape)) for a in (cot_theirs, gains, wo)]
        + [
            (up, pl.BlockSpec((width, chunk), lambda j, *_: (0, j))),
            (down, pl.BlockSpec((chunk, width), lambda j, *_: (j, 0))),
        ],
        [
            (cot.shape, BF, page_block(cot.shape)), (half, BF, whole(half)), rows(width, F32), rows(width + LANES, BF),
            rows(width, BF), rows(width, BF), chunks, chunks, rows(width, BF), rows(width, BF), ((8, width), F32, whole((8, width))),
        ],
        grid=(hidden // chunk,),
        scratch=[pltpu.VMEM((slots, width), F32)] * 4 + [pltpu.VMEM((slots, LANES), F32)],
        scalars=scalars,
        deps=deps,
        work=(8 * slots * width * hidden, 2e7, slots * hidden),
    )


def query_weights_kernel(normed_ref, cot_ref, att_ref, branch_ref, act_ref, dact_ref, wo_ref, up_ref, down_ref, *, tiled):
    put_grad(up_ref, dot(normed_ref[...], dact_ref[...], 0, 0).astype(BF), store_columns, 0, tiled)
    put_grad(down_ref, dot(act_ref[...], cot_ref[...], 0, 0).astype(BF), store_strips, 1, tiled)

    @pl.when(pl.program_id(0) == 0)
    def _():
        put_grad(wo_ref, dot(att_ref[...], branch_ref[...], 0, 0).astype(BF), store_all, 1, tiled)


def query_weights(normed, cot, att, branch, act, dact, tiled, deps, chunk=768):
    slots, width = normed.shape
    hidden = act.shape[1]
    return call(
        functools.partial(query_weights_kernel, tiled=tiled),
        "query_weights",
        [(a, whole((slots, width))) for a in (normed, cot, att, branch)]
        + [(a, pl.BlockSpec((slots, chunk), lambda j: (0, j))) for a in (act, dact)],
        grad_forms(width, hidden, chunk, tiled, 1),
        grid=(hidden // chunk,),
        deps=deps,
        work=(4 * slots * width * hidden, 1.6e7, 0),
    )


def query_out_kernel(s_ref, *refs, parts, tiled):
    halves = [refs[:parts], refs[parts : 2 * parts]]
    others = refs[2 * parts : 2 * parts + 4]
    n_ref, x_ref, grad_ref, gain_ref, w_ref, rows_ref = refs[2 * parts + 4 : 2 * parts + 10]
    own_ref, other_ref, w_grad_ref, gain_grad_ref = refs[2 * parts + 10 : 2 * parts + 14]
    width = x_ref.shape[1]
    sums = []
    for dqs in halves:
        value = dqs[0][...].astype(F32)
        for d in dqs[1:]:
            value = value + d[...].astype(F32)
        sums.append(value.astype(BF))
    join = lambda a, b: jnp.concatenate([a, b], axis=1)
    pieces = [join(*sums), join(others[0][...], others[1][...]), join(others[2][...], others[3][...])]
    back = None
    for number, piece in enumerate(pieces):
        cols = slice(number * width, (number + 1) * width)
        term = dot(piece, w_ref[:, cols], 1, 1)
        back = term if back is None else back + term
        (refs[-1] if tiled else w_grad_ref)[:, cols] = dot(n_ref[...], piece, 0, 0).astype(BF)
    if tiled:
        store_all(w_grad_ref, refs[-1][...], 1)
    unit, spread = norm_stats(x_ref[...].astype(F32))
    grad, gain_part = norm_back(unit, spread, gain_ref[2:3, :], back)
    rows = grad_ref[...] + grad
    own_slots = rows.shape[0] // 2
    low, high = rows[:own_slots], rows[own_slots:]
    odd = s_ref[ODD] == 1
    own_ref[0] = jnp.where(odd, high, low)
    other_ref[...] = jnp.where(odd, low, high).astype(BF)
    gain_rows = rows_ref[...] + jnp.where(iota((8, width), 0) == 2, gain_part, 0.0)
    if not tiled:
        gain_grad_ref[...] = gain_rows
        return
    turned = gain_rows.T
    size = width // 16
    lane = iota((1, LANES), 1)
    for half in range(2):
        tile = jnp.where(lane == 0, turned[:, 2 * half : 2 * half + 1], 0.0)
        tile = jnp.where(lane == 1, turned[:, 2 * half + 1 : 2 * half + 2], tile).astype(BF)
        for strip in range(8):
            for core in range(2):
                at = (2 * strip + core) * size
                gain_grad_ref[(core, *tile_index(strip, half, 0), slice(None), slice(None))] = tile[at : at + size]


def query_out(scalars, dqs, dks, dvs, normed, x, grad, gains, w, gain_rows, pages, tiled, deps):
    slots, width = x.shape
    own_shape = (pages, slots // 2, width)
    w_shape = tile_shape(width, w.shape[1]) if tiled else w.shape
    g_shape, g_kind = (tile_shape(width, 256), BF) if tiled else ((8, width), F32)
    ins = (*dqs[0], *dqs[1], *dks, *dvs, normed, x, grad, gains, w, gain_rows)
    return call(
        functools.partial(query_out_kernel, parts=len(dqs[0]), tiled=tiled),
        "query_out",
        [(a, whole(a.shape, True)) for a in ins],
        [
            (own_shape, F32, page_block(own_shape)),
            ((slots // 2, width), BF, whole((slots // 2, width))),
            (w_shape, BF, whole(w_shape)),
            (g_shape, g_kind, whole(g_shape)),
        ],
        scratch=[pltpu.VMEM(w.shape, BF)] if tiled else [],
        scalars=scalars,
        deps=deps,
        work=(4 * slots * width * w.shape[1], 1e7, 0),
    )


PAIR = pl.DeviceIdType.MESH


def coordinates():
    page, strip = lax.axis_index("page"), lax.axis_index("strip")
    core, x = lax.rem(page, 2), page // 2
    y, z_low, z_high = lax.rem(strip, 2), lax.rem(strip // 2, 2), strip // 4
    flip = lambda index, bit, weight: index + weight - 2 * weight * bit
    core_mate = (flip(page, core, 1), strip)
    mates = {
        "x": (x, (flip(page, x, 2), strip)),
        "y": (y, (page, flip(strip, y, 1))),
        "low": (z_low, (page, flip(strip, z_low, 2))),
        "high": (z_high, (page, flip(strip, z_high, 4))),
    }
    return core, core_mate, [[mates[k] for k in ("y", "x", "low", "high")], [mates[k] for k in ("x", "y", "low", "high")]]


def meet(mates):
    barrier = pltpu.get_barrier_semaphore()
    for mate in mates:
        pl.semaphore_signal(barrier, inc=1, device_id=mate, device_id_type=PAIR)
    pl.semaphore_wait(barrier, len(mates))


def send(source, target, sems, number, mate):
    copy = pltpu.make_async_remote_copy(
        src_ref=source,
        dst_ref=target,
        send_sem=sems.at[0, number],
        recv_sem=sems.at[1, number],
        device_id=mate,
        device_id_type=PAIR,
    )
    copy.start()
    return copy


def add_rows(target, first, source, start, length, at, rows):
    span = pl.ds(at, rows)

    def step(i, carry):
        total = target[first + i, span, :].astype(F32) + source[start + i, span, :].astype(F32)
        target[first + i, span, :] = total.astype(BF)
        return carry

    lax.fori_loop(0, length, step, 0)


def query_sum_kernel(*refs, rows):
    up_ref, down_ref, wo_ref, normed_ref, cot_ref, att_ref, branch_ref, act_ref, dact_ref = refs[:9]
    outs = refs[9:13]
    own_up, own_down, own_wo, held_0, held_1, remote, near = refs[13:]
    held = (held_0, held_1)
    core, core_mate, orders = coordinates()
    meet([core_mate])
    wide, small = rows
    far, mine = [], []
    for number, (grad, order, at, size) in enumerate(((up_ref, 0, 0, wide), (down_ref, 1, 0, wide), (wo_ref, 0, 2 * wide, small))):
        span, bit = pl.ds(at, size), orders[order][0][0]
        far.append(send(grad.at[1 - core], held[order].at[:, :, :, span, :], remote, number, core_mate))
        for which in range(2):
            first = bit if which else 1 - bit
            copy = pltpu.make_async_copy(
                grad.at[core, first], outs[2 * order + which].at[:, :, span, :], near.at[2 * number + which]
            )
            copy.start()
            mine.append(copy)
    width = normed_ref.shape[1]
    own_rows = ((own_up, 0, wide, wide), (own_down, 1, wide, wide), (own_wo, 1, 2 * wide, small))
    store_all(own_wo, dot(att_ref[...], branch_ref[...], 0, 0).astype(BF), 1)
    for j in range(act_ref.shape[1] // width):
        cols = slice(j * width, (j + 1) * width)
        store_columns(own_up, dot(normed_ref[...], dact_ref[:, cols], 0, 0).astype(BF), 0, j // 2, (j % 2) * (width // LANES))
        store_strips(own_down, dot(act_ref[:, cols], cot_ref[...], 0, 0).astype(BF), 1, (j % 2) * 2 + j // 2)
    later = []
    for number, (grad, order, at, size) in enumerate(own_rows):
        later.append(send(grad.at[1 - core], held[order].at[:, :, :, pl.ds(at, size), :], remote, 3 + number, core_mate))
    for copy in far + mine:
        copy.wait()

    def add(order, at, size, own):
        bit = orders[order][0][0]
        span = pl.ds(at, size)
        for which in range(2):
            out, first = outs[2 * order + which], bit if which else 1 - bit
            for i in range(2):

                def step(z, carry, out=out, first=first, i=i):
                    mine = out[i, z, span, :] if own is None else own[core, first, i, z]
                    out[i, z, span, :] = (mine.astype(F32) + held[order][first, i, z, span, :].astype(F32)).astype(BF)
                    return carry

                lax.fori_loop(0, 4, step, 0)

    for order, at, size in ((0, 0, wide), (1, 0, wide), (0, 2 * wide, small)):
        add(order, at, size, None)
    for copy, (grad, order, at, size) in zip(later, own_rows):
        copy.wait()
        add(order, at, size, grad)


def query_sum(patch_grads, normed, cot, att, branch, act, dact, collective, deps):
    width, hidden = normed.shape[1], act.shape[1]
    shapes = [tile_shape(width, hidden), tile_shape(hidden, width), tile_shape(width, width)]
    rows = (shapes[0][-2], shapes[2][-2])
    total = 2 * rows[0] + rows[1]
    vmem = pl.BlockSpec(memory_space=pltpu.VMEM)
    kernel = functools.partial(query_sum_kernel, rows=rows)
    outs = pl.pallas_call(
        lambda *refs: kernel(*refs[:9], *refs[9 + len(deps) :]),
        in_specs=[ANY] * 3 + [vmem] * 6 + [ANY] * len(deps),
        out_specs=[vmem] * 4,
        out_shape=[sds((2, 4, total, LANES), BF)] * 4,
        scratch_shapes=[
            *[pltpu.VMEM(shape, BF) for shape in shapes],
            pltpu.VMEM((2, 2, 4, total, LANES), BF),
            pltpu.VMEM((2, 2, 4, total, LANES), BF),
            pltpu.SemaphoreType.DMA((2, 6)),
            pltpu.SemaphoreType.DMA((6,)),
        ],
        compiler_params=pltpu.CompilerParams(collective_id=collective, has_side_effects=True, vmem_limit_bytes=VMEM_BYTES),
        name="query_sum",
    )(*patch_grads, normed, cot, att, branch, act, dact, *deps)
    return [out.reshape(8, total, LANES) for out in outs]


ORDERS = (("y", "x", "low", "high"), ("x", "y", "low", "high"))
PLACES = {"x": BIT_X, "y": BIT_Y, "low": BIT_LOW, "high": BIT_HIGH}


def across(array, name):
    axis, weight = {"x": ("page", 2), "y": ("strip", 1), "low": ("strip", 2), "high": ("strip", 4)}[name]
    return lax.ppermute(array, axis, [(i, i ^ weight) for i in range(lax.axis_size(axis))])


def halve_add_kernel(s_ref, *refs):
    for k in range(4):
        keep, got, out = refs[2 * k], refs[2 * k + 1], refs[8 + k]
        out[...] = (keep[...].astype(F32) + got[...].astype(F32)).astype(BF)


def halve_add(scalars, kept, got, stage, deps):
    ins, outs = [], []
    for order in range(2):
        size = kept[order].shape[0] // 2
        shape = kept[order].shape[1:]
        place = PLACES[ORDERS[order][stage]]
        for flip in (1, 0):
            spec = pl.BlockSpec(
                (1, *shape),
                lambda i, s, place=place, flip=flip, size=size: ((1 - s[place] if flip else s[place]) * size + i, 0, 0),
            )
            ins += [(kept[order], spec), (got[order], spec)]
            outs.append(((size, *shape), BF, pl.BlockSpec((1, *shape), lambda i, s: (i, 0, 0))))
    return call(
        halve_add_kernel, "halve_add", ins, outs, grid=(size,), scalars=scalars, deps=deps, work=(1e6, 6 * size * 1296 * 512, 0)
    )


def late_sum_kernel(*refs, lots, arrays, early_rows):
    grads = refs[:arrays]
    early = refs[arrays : arrays + 4]
    own, got = refs[arrays + 4 : arrays + 6], refs[arrays + 6 : arrays + 8]
    sums, first_held = refs[arrays + 8 : arrays + 10], refs[arrays + 10 : arrays + 12]
    held = [refs[arrays + 12 : arrays + 16], refs[arrays + 16 : arrays + 20]]
    done, loaded, early_held = refs[arrays + 20 : arrays + 22], refs[arrays + 22 : arrays + 26], refs[arrays + 26 : arrays + 28]
    remote, near = refs[arrays + 28 :]
    core, core_mate, orders = coordinates()
    meet([core_mate] + [mate for _, mate in orders[0]])
    numbers, local_numbers = iter(range(1000)), iter(range(1000))
    jobs = []
    for order, at, members in lots:
        copies, first = [], at
        for member, start, rows in members:
            there, span = pl.ds(start, rows), pl.ds(first, rows)
            first += rows
            copies.append(
                send(grads[member].at[1 - core, :, there, :], first_held[order].at[:, span, :], remote, next(numbers), core_mate)
            )
            copy = pltpu.make_async_copy(
                grads[member].at[core, :, there, :], sums[order].at[:, span, :], near.at[next(local_numbers)]
            )
            copy.start()
            copies.append(copy)
        jobs.append((order, at, first - at, copies))
    loads = []
    for k in range(4):
        copy = pltpu.make_async_copy(early[k], loaded[k], near.at[next(local_numbers)])
        copy.start()
        loads.append(copy)
    early_flights = []
    bases = [0] * len(jobs)
    flights = [None] * len(jobs)
    first_exchange = []
    for stage in range(4):
        size = 8 >> stage
        for n, (order, at, rows, copies) in enumerate(jobs):
            source = first_held[order] if stage == 0 else held[order][stage - 1]
            for copy in copies if stage == 0 else [flights[n]]:
                copy.wait()
            bit, mate = orders[order][stage]
            out, keep = size * (1 - bit), size * bit
            base = bases[n]
            add_rows(sums[order], base + out, source, out, size, at, rows)
            flights[n] = send(
                sums[order].at[pl.ds(base + out, size), pl.ds(at, rows), :],
                held[order][stage].at[:, pl.ds(at, rows), :],
                remote,
                next(numbers),
                mate,
            )
            add_rows(sums[order], base + keep, source, keep, size, at, rows)
            bases[n] = base + keep
        if stage == 0:
            for copy in loads:
                copy.wait()
            for order in range(2):
                bit, mate = orders[order][3]
                kept = loaded[2 * order]
                add_rows(kept, 1 - bit, loaded[2 * order + 1], 1 - bit, 1, 0, early_rows)
                early_flights.append(send(kept.at[1 - bit], early_held[order], remote, next(numbers), mate))
                add_rows(kept, bit, loaded[2 * order + 1], bit, 1, 0, early_rows)
        if stage == 2:
            for order in range(2):
                early_flights[order].wait()
                total = loaded[2 * order][orders[order][3][0]].astype(F32) + early_held[order][...].astype(F32)
                own[order][:early_rows, :] = total.astype(BF)
                span = pl.ds(0, early_rows)
                first_exchange.append(send(own[order].at[span, :], done[order].at[span, :], remote, next(numbers), core_mate))
    exchange = []
    for n, (order, at, rows, _) in enumerate(jobs):
        flights[n].wait()
        value = sums[order][bases[n], pl.ds(at, rows), :].astype(F32) + held[order][3][0, pl.ds(at, rows), :].astype(F32)
        span = pl.ds(early_rows + at, rows)
        own[order][span, :] = value.astype(BF)
        exchange.append(send(own[order].at[span, :], done[order].at[span, :], remote, next(numbers), core_mate))
    for copy in first_exchange + exchange:
        copy.wait()
    for order in range(2):
        got[order][...] = done[order][...]


def late_sum(grads, lots, rows, early, collective, deps):
    grads = [g.reshape(2, 16, *g.shape[-2:]) for g in grads]
    arrays = len(grads)
    members = sum(len(lot[2]) for lot in lots)
    early_rows = early[0].shape[1]
    share = [sds((early_rows + r, LANES), BF) for r in rows]
    vmem = lambda *shape: pltpu.VMEM(shape, BF)
    kernel = functools.partial(late_sum_kernel, lots=lots, arrays=arrays, early_rows=early_rows)
    first = arrays + 4
    return pl.pallas_call(
        lambda *refs: kernel(*refs[:first], *refs[first + len(deps) :]),
        in_specs=[ANY] * (first + len(deps)),
        out_specs=[pl.BlockSpec(memory_space=pltpu.VMEM)] * 4,
        out_shape=share + share,
        scratch_shapes=[
            *[vmem(16, r, LANES) for r in rows],
            *[vmem(16, r, LANES) for r in rows],
            *[vmem(8 >> k, rows[0], LANES) for k in range(4)],
            *[vmem(8 >> k, rows[1], LANES) for k in range(4)],
            *[vmem(early_rows + r, LANES) for r in rows],
            *[vmem(2, early_rows, LANES)] * 4,
            *[vmem(early_rows, LANES)] * 2,
            pltpu.SemaphoreType.DMA((2, members + 5 * len(lots) + 4)),
            pltpu.SemaphoreType.DMA((members + 4,)),
        ],
        compiler_params=pltpu.CompilerParams(collective_id=collective, has_side_effects=True, vmem_limit_bytes=VMEM_BYTES),
        name="late_sum",
    )(*grads, *early, *deps)


def finish_kernel(s_ref, own0, own1, got0, got1, *refs, plan, puts):
    came, gain_ref = refs[puts : 2 * puts], refs[2 * puts]
    outs, put_outs = refs[2 * puts + 1 : 2 * puts + 1 + len(plan)], refs[2 * puts + 1 + len(plan) :]
    for c, out in zip(came, put_outs):
        out[0] = c[...].astype(out.dtype)
    first = s_ref[CORE] == 0
    owns, gots = (own0, own1), (got0, got1)
    lane = iota((1, LANES), 1)
    left = lane < 64

    def tile(order, at, size, part):
        mine = owns[order][at : at + size, :].astype(F32)
        theirs = gots[order][at : at + size, :].astype(F32)
        return jnp.where(first == (part == 0), mine, theirs)

    for out, (size, tiles, flipped) in zip(outs, plan):
        count = len(tiles)
        for part in range(2):
            rows = slice(part * size, (part + 1) * size)
            values = [tile(order, at, size, part) for order, at in tiles]
            if count % 2 == 0:
                for t in range(count // 2):
                    out[rows, t * LANES : (t + 1) * LANES] = jnp.where(first, values[t], values[t + count // 2])
                continue
            turned = [pltpu.roll(v, 64, 1) for v in values[count // 2 :]]
            whole_tiles = [
                jnp.where(first, values[t], jnp.where(left, turned[t], turned[t + 1])) for t in range(count // 2)
            ]
            rest = jnp.where(first, values[count // 2], turned[-1])
            if flipped:
                for t, value in enumerate(whole_tiles):
                    for at in range(0, size, 64):
                        column = part * size + at
                        out[t * LANES : (t + 1) * LANES, column : column + 64] = value[at : at + 64].T
                for at in range(0, size, 64):
                    column = part * size + at
                    out[count // 2 * LANES :, column : column + 64] = rest[at : at + 64].T[:64]
                continue
            for t, value in enumerate(whole_tiles):
                out[rows, t * LANES : (t + 1) * LANES] = value
            out[rows, count // 2 * LANES :] = rest[:, :64]
    size = gain_ref.shape[1] // 2
    at = own0.shape[0] - size
    gain = jnp.concatenate([tile(0, at, size, part) for part in range(2)], axis=0).T
    gain_ref[...] = jnp.where(first, gain[0:1], gain[1:2])


def finish(scalars, shares, shapes, plan, gain_rows, arrays, came):
    outs = [shape[::-1] if flipped else shape for shape, (_, _, flipped) in zip(shapes, plan)]
    gain, *found = call(
        functools.partial(finish_kernel, plan=plan, puts=len(arrays)),
        "finish",
        [(a, whole(a.shape)) for a in shares] + [(a, ANY) for a in arrays] + [(c, whole(c.shape)) for c in came],
        [((1, gain_rows), F32, whole((1, gain_rows)))]
        + [(shape, F32, whole(shape)) for shape in outs]
        + [(a.shape, a.dtype, other_page(a.shape)) for a in arrays],
        scalars=scalars,
        aliases={1 + len(shares) + k: 1 + len(outs) + k for k in range(len(arrays))},
    )
    weights = [f.T if flipped else f for f, (_, _, flipped) in zip(found, plan)]
    return gain.T, weights, found[len(outs) :]


def from_ahead(array, count, distance):
    return lax.ppermute(array, "strip", [(i, (i - distance) % count) for i in range(count)])


def from_partner(array, count):
    return lax.ppermute(array, "strip", [(i, i ^ 1) for i in range(count)])


def scattered(grad):
    strips, pages = lax.axis_size("strip"), lax.axis_size("page")
    rows, cols = grad.shape
    part = lax.psum_scatter(grad, "strip", scatter_dimension=0, tiled=True)
    part = part.reshape(rows // strips, pages, cols // pages).transpose(1, 0, 2)
    return lax.psum_scatter(part, "page", scatter_dimension=0, tiled=False).astype(F32)


def local(
    visual_in, query_in, row_valid, segment_ids, slot_valid, col_shift, row_shifted, norm_gains,
    w_vqkv, w_vout, w_up, w_down, w_qqkv, w_xkv, w_qout, w_qup, w_qdown, visual_cot, query_cot,
):
    pages, strip_rows, columns, width = visual_in.shape
    own_slots, all_slots = query_in.shape[1], segment_ids.shape[1]
    count = lax.axis_size("strip")
    tiled = count == 8
    group = count // 2
    half = strip_rows * columns
    slots = 2 * own_slots
    window = WIN * WIN
    form = (strip_rows, columns)
    place, page = lax.axis_index("strip"), lax.axis_index("page")
    odd = place % 2
    up = jnp.where(odd == 1, 1 - row_shifted[0], row_shifted[0])
    down = 1 - up
    pick = lambda array, which: lax.dynamic_index_in_dim(array, which, 0, keepdims=False)
    shift = jnp.where(up == 0, col_shift[0], col_shift[1])
    scalars = jnp.stack([up, shift, odd, page % 2, page // 2, odd, place // 2 % 2, place // 4, (place // 2) * slots]).astype(jnp.int32)

    visual, cot = visual_in.reshape(pages, half, width), visual_cot.reshape(pages, half, width)
    query_sent, patch_sent = pack(scalars, [(query_in, slot_valid), (visual, row_valid)])
    query_theirs = from_partner(query_sent, count)
    patch_sent = held_back(patch_sent, [query_theirs])
    patch_other = from_ahead(patch_sent, count, 1)
    gains = jnp.pad(norm_gains.T, ((0, 4), (0, 0)))

    order = [-1] + list(range(group - 1))
    blocks = forward_blocks(group if tiled else 1, slots, group)
    near_block = next(block for block, near in blocks if near)

    def gather(array):
        pieces = [array if k == 0 else from_ahead(array, count, 2 * k) for k in order]
        return pieces if tiled else [jnp.concatenate(pieces, axis=0)]

    def give_back(arrays):
        if not tiled:
            arrays = [arrays[0][n * slots : (n + 1) * slots] for n in range(group)]
        return [piece if k == 0 else from_ahead(piece, count, -2 * k) for piece, k in zip(arrays, order)]

    x_query, normed_three, q_own, slot_kv, same, turned = query_in_call(
        scalars, segment_ids, slot_valid, query_in, query_theirs, gains, w_qqkv, [patch_sent]
    )
    qs = gather(q_own)
    x, normed_one, qkv, cross, key_bias = patch_in(
        scalars, row_valid, visual, patch_other, gains, w_vqkv, w_xkv, form, [q_own]
    )
    att = window_forward(qkv, window, [])
    cot_sent, cot_q_sent = pack_two(scalars, cot, query_cot, [att, *qs])
    cot_other, cot_theirs = from_ahead(cot_sent, count, 1), from_partner(cot_q_sent, count)
    q_out = query_forward(qs, cross, slot_kv, key_bias, same, blocks, [cot_q_sent])
    out_parts = give_back(q_out)
    (vis_own, vis_other, grad_after, grad_att, g_vout, g_up, g_down, gain_two) = patch_ffn(
        scalars, att, x, cot, cot_other, gains, w_vout, w_up, w_down, tiled, form, [q_out[0]]
    )
    vis_came = from_ahead(vis_other, count, -1)
    (q_res, q_res_other, grad_q, send_q, att_q, normed_four, act_q, dact_q, branch_q, cot_q, gain_four) = query_ffn(
        scalars, out_parts, x_query, query_cot, cot_theirs, gains, w_qout, w_qup, w_qdown, tiled, [gain_two]
    )
    gos = gather(send_q)
    res_came = from_partner(q_res_other, count)
    if tiled:
        out_0, keep_0, out_1, keep_1 = query_sum(
            [g_up, g_down, g_vout], normed_four, cot_q, att_q, branch_q, act_q, dact_q, 0, []
        )
        got = [across(out_0, "y"), across(out_1, "x")]
        last = keep_0
    else:
        g_qout, g_qup, g_qdown = query_weights(normed_four, cot_q, att_q, branch_q, act_q, dact_q, tiled, [])
        last = g_qout
    g_proj = window_backward(qkv, grad_att, window, [last, vis_came])
    last = [g_proj, res_came]
    dqs, dks, dvs, dsks, dsvs = [], [], [], [], []
    for part in range(2):
        dq, dk, dv, dsk, dsv = query_backward(qs, gos, cross, slot_kv, key_bias, turned, near_block, part, last)
        last = [dk] if part == 0 else [dk, *dqs[0]]
        dqs.append(give_back(dq))
        dks.append(dk)
        dvs.append(dv)
        dsks.append(dsk)
        dsvs.append(dsv)
        if tiled:
            out_0, keep_0, out_1, keep_1 = halve_add(scalars, [keep_0, keep_1], got, part + 1, last)
            got = [across(out_0, ORDERS[0][part + 1]), across(out_1, ORDERS[1][part + 1])]
            last = [keep_0]
    vin_own, vin_other, gain_rows, g_vqkv, *g_xkv = patch_back(
        scalars, g_proj, w_vqkv, dks, dvs, normed_one, x, grad_after, gains, w_xkv, gain_two, gain_four, pages, tiled, form, last
    )
    qin_own, qin_other, g_qqkv, gain_grads = query_out(
        scalars, dqs, dsks, dsvs, normed_three, x_query, grad_q, gains, w_qqkv, gain_rows, pages, tiled, got if tiled else []
    )

    vin_came = from_ahead(vin_other, count, -1)
    qin_came = from_partner(qin_other, count)
    arrays, came = [vis_own, q_res, vin_own, qin_own], [vis_came, res_came, vin_came, qin_came]

    weights = (w_vqkv, w_vout, w_up, w_down, w_qqkv, w_xkv, w_qout, w_qup, w_qdown)
    if tiled:
        size = lambda g: g.shape[-2]
        a, b, c, d, e = g_vqkv, g_xkv[0], gain_grads, g_qqkv, g_xkv[1]
        cut = (size(a) // 2 + 15) // 16 * 16
        lots = [
            (0, 0, [(0, 0, cut)]),
            (1, 0, [(3, 0, cut)]),
            (0, cut, [(0, cut, size(a) - cut)]),
            (1, cut, [(3, cut, size(d) - cut)]),
            (0, size(a), [(1, 0, size(b)), (2, 0, size(c))]),
            (1, size(d), [(4, 0, size(e))]),
        ]
        late_rows = [size(a) + size(b) + size(c), size(d) + size(e)]
        shares = late_sum([a, b, c, d, e], lots, late_rows, [keep_0, got[0], keep_1, got[1]], 1, [])
        tall, flat = g_up.shape[-2], g_vout.shape[-2]
        end = 2 * tall + flat
        where = {2: (0, 0), 7: (0, tall), 1: (0, 2 * tall), 0: (0, end), 5: (0, end + size(a))}
        where.update({3: (1, 0), 8: (1, tall), 6: (1, 2 * tall), 4: (1, end)})
        plan, shapes = [], []
        for number, weight in enumerate(weights):
            rows, cols = weight.shape
            step, tiles = rows // 16, cols // 256
            which, at = where[number]
            spots = [(which, at + t * step) for t in range(tiles)]
            if number == 5:
                spots = spots[:3] + [(1, end + size(d) + t * step) for t in range(3)]
            flipped = rows > 2 * cols and tiles % 2 == 1
            plan.append((step, spots, flipped))
            shapes.append((rows // 8, cols // lax.axis_size("page")))
        gain_part, parts, placed = finish(scalars, shares, shapes, plan, width // 8, arrays, came)
    else:
        placed = put(scalars, arrays, came, [gain_rows])
        parts = [scattered(g) for g in (g_vqkv, g_vout, g_up, g_down, g_qqkv, g_xkv[0], g_qout, g_qup, g_qdown)]
        gain_part = lax.psum_scatter(gain_grads[:4], "page", scatter_dimension=0, tiled=True)
        gain_part = lax.psum_scatter(gain_part, "strip", scatter_dimension=1, tiled=True).reshape(-1, 1)
    visual_out, query_out_rows, visual_in_grad, query_in_grad = placed
    shape = (pages, strip_rows, columns, width)
    visual_out, visual_in_grad = visual_out.reshape(shape), visual_in_grad.reshape(shape)
    return (visual_out, query_out_rows, visual_in_grad, query_in_grad, gain_part, *parts)


def solution(mesh):
    tokens, slots, table = P("page", "strip", None, None), P("page", "strip", None), P("page", "strip")
    tile = P("strip", "page")
    return jax.shard_map(
        local,
        mesh=mesh,
        in_specs=(tokens, slots, table, P("page", None), table, P("page"), P("page")) + (P(),) * 10 + (tokens, slots),
        out_specs=(tokens, slots, tokens, slots) + (tile,) * 10,
        check_vma=False,
    )
```
